32 devices in a mesh: ex: 4 (over z), ey: 4 (over x, core), ez: 2 (over y).
Axes of the slice: x: 2, y: 2, z: 4, core: 2. Of those that a mesh axis runs over, the one named last changes fastest.
Arguments:
- load_raw: float32 [8, 8, 8, 32, 384], P('ex', 'ey', 'ez'), may hold values from -8 to 8
- scaling: float32 [8, 8, 8, 384], P('ex', 'ey', 'ez'), may hold values from 0.6 to 1.8
- fine_matrix: float32 [384, 384], replicated
- fine_inverse: float32 [384, 384], replicated
- prolong_four: float32 [384, 98], replicated
- coarse_four: float32 [98, 98], replicated
- prolong_two: float32 [384, 26], replicated
- coarse_two: float32 [26, 26], replicated
- orient: int32 [3, 8, 8, 8], P(None, 'ex', 'ey', 'ez'), may hold values from 0 to 3
- boundary: int32 [6, 8, 8, 8], P(None, 'ex', 'ey', 'ez'), may hold values from 0 to 1
Outputs:
- solution: float32 [8, 8, 8, 32, 384], P('ex', 'ey', 'ez')
The draws below stay inside these ranges and needn't reach their ends.
All inputs are finite; a program needn't handle non-finite values.
Results may differ from the reference program's by a relative error of at most 0.0001.
Values sent between devices are 32-bit elements; how exact they have to be, the bound alone decides.
No kernel may reach another device: no remote copies, remote signals or barrier semaphores. Data moves between devices by JAX's collectives and lax.ppermute only.
A program may use at most 64 MiB of HBM per device.

```python
import math
import jax
import jax.numpy as jnp
from jax import lax

SPECIES = 32
FACE_SIDE = 8
NODES = 384
C4 = 98
C2 = 26
CYCLES = 2
GX = 8
GY = 8
GZ = 8


def shared_matrices(key):
    base = jax.random.fold_in(key, 7)
    keys = jax.random.split(base, 4)
    spread = 0.5
    gauss = jax.random.normal(keys[0], (NODES, NODES), jnp.float32) * spread / jnp.sqrt(jnp.float32(NODES))
    offdiag = (gauss + gauss.T) * (1.0 - jnp.eye(NODES, dtype=jnp.float32))
    diagonal = jnp.sum(jnp.abs(offdiag), axis=1) + jax.random.uniform(keys[1], (NODES,), jnp.float32, 0.5, 2.0)
    matrix = (offdiag + jnp.diag(diagonal)) / 8.0
    inverse = jnp.linalg.inv(matrix)
    prolong_four = jax.random.normal(keys[2], (NODES, C4), jnp.float32) / jnp.sqrt(jnp.float32(C4))
    prolong_two = jax.random.normal(keys[3], (NODES, C2), jnp.float32) / jnp.sqrt(jnp.float32(C2))
    galerkin_four = jnp.dot(jnp.dot(prolong_four.T, matrix, precision=lax.Precision.HIGHEST), prolong_four, precision=lax.Precision.HIGHEST)
    galerkin_two = jnp.dot(jnp.dot(prolong_two.T, matrix, precision=lax.Precision.HIGHEST), prolong_two, precision=lax.Precision.HIGHEST)
    return (matrix, inverse, prolong_four, jnp.linalg.inv(galerkin_four), prolong_two, jnp.linalg.inv(galerkin_two))


def draw_fine_matrix(key, part):
    return shared_matrices(key)[0]


def draw_fine_inverse(key, part):
    return shared_matrices(key)[1]


def draw_prolong_four(key, part):
    return shared_matrices(key)[2]


def draw_coarse_four(key, part):
    return shared_matrices(key)[3]


def draw_prolong_two(key, part):
    return shared_matrices(key)[4]


def draw_coarse_two(key, part):
    return shared_matrices(key)[5]


def plant(values, key, least, top_value):
    longest = values.shape.index(max(values.shape))
    spots = []
    for shift in (0, 1):
        where = [jax.random.randint(jax.random.fold_in(key, axis), (), 0, length) for axis, length in enumerate(values.shape)]
        where[longest] = (where[longest] + shift) % values.shape[longest]
        spots.append(tuple(where))
    return values.at[spots[0]].set(least).at[spots[1]].set(top_value)


def shard_levels(stream_key, extent, cuts, low, top_value):
    def one(dim, blocks):
        draws = jax.random.uniform(jax.random.fold_in(jax.random.fold_in(stream_key, 6), dim), (blocks,), jnp.float32, low / len(cuts), top_value / len(cuts))
        return jnp.repeat(jnp.exp(draws), extent[dim] // blocks).reshape((-1,) + (1,) * (len(extent) - dim - 1))

    gain = one(*cuts[0])
    for cut in cuts[1:]:
        gain = gain * one(*cut)
    return gain


def bell_draw(rng, shape, scale, limit, cuts=(), kind=jnp.bfloat16):
    level = shard_levels(rng, shape, cuts, -0.22, 0.18) if cuts else 1.0
    result = jax.random.normal(rng, shape, jnp.float32) * scale * level
    return jnp.minimum(jnp.maximum(result, -limit), limit).astype(kind)


def setup_inputs(seed: int = 0) -> dict:
    arg_keys = jax.random.split(jax.random.key(seed), 11)
    return {
        "load_raw": bell_draw(arg_keys[0], (GX, GY, GZ, SPECIES, NODES), 1.0, 8.0, ((0, 4), (1, 4), (2, 2)), jnp.float32),
        "scaling": jnp.clip(jnp.exp(math.log(1.8) - 1.0986122 * jax.random.uniform(arg_keys[1], (GX, GY, GZ, NODES), jnp.float32) ** shard_levels(arg_keys[1], (GX, GY, GZ, NODES), ((0, 4), (1, 4), (2, 2)), -0.2, 0.2)), 0.6, 1.8),
        "fine_matrix": draw_fine_matrix(jax.random.fold_in(arg_keys[10], 71), 0),
        "fine_inverse": draw_fine_inverse(jax.random.fold_in(arg_keys[10], 71), 0),
        "prolong_four": draw_prolong_four(jax.random.fold_in(arg_keys[10], 71), 0),
        "coarse_four": draw_coarse_four(jax.random.fold_in(arg_keys[10], 71), 0),
        "prolong_two": draw_prolong_two(jax.random.fold_in(arg_keys[10], 71), 0),
        "coarse_two": draw_coarse_two(jax.random.fold_in(arg_keys[10], 71), 0),
        "orient": plant(jax.random.randint(arg_keys[8], (3, GX, GY, GZ), 0, 4), jax.random.fold_in(arg_keys[8], 1), 0, 3).astype(jnp.int32),
        "boundary": plant(jax.random.randint(arg_keys[9], (6, GX, GY, GZ), 0, 2), jax.random.fold_in(arg_keys[9], 1), 0, 1).astype(jnp.int32),
    }


fine_weight = 0.5
coarse_weight = 0.5

def flip_face(face_data, face_code):
    reshaped = face_data.reshape(face_data.shape[:-1] + (FACE_SIDE, FACE_SIDE))
    codes_full = face_code[:, :, :, None, None, None]
    reshaped = jnp.where(codes_full % 2 == 1, jnp.flip(reshaped, -2), reshaped)
    reshaped = jnp.where(codes_full // 2 == 1, jnp.flip(reshaped, -1), reshaped)
    return reshaped.reshape(face_data.shape)

def keep_factors(boundary, dim_index, count_along):
    position = lax.broadcasted_iota(jnp.int32, boundary.shape[1:], dim_index)
    keep_low = 1 - jnp.where(position == 0, boundary[2 * dim_index], 0)
    keep_top = 1 - jnp.where(position == count_along - 1, boundary[2 * dim_index + 1], 0)
    return (keep_low.astype(jnp.float32), keep_top.astype(jnp.float32))

def assemble(element_data, orient, boundary):
    face_nodes = FACE_SIDE * FACE_SIDE
    face_list = [element_data[..., face_index * face_nodes:(face_index + 1) * face_nodes] for face_index in range(6)]
    pieces = []
    for dim_index in range(3):
        low_face = face_list[2 * dim_index]
        top_face = face_list[2 * dim_index + 1]
        face_code = orient[dim_index]
        count_along = low_face.shape[dim_index]
        sent_low = flip_face(low_face, face_code)
        zero_slab = jnp.zeros_like(lax.slice_in_dim(low_face, 0, 1, axis=dim_index))
        above = jnp.concatenate([lax.slice_in_dim(sent_low, 1, count_along, axis=dim_index), zero_slab], dim_index)
        below = flip_face(jnp.concatenate([zero_slab, lax.slice_in_dim(top_face, 0, count_along - 1, axis=dim_index)], dim_index), face_code)
        keep_low, keep_top = keep_factors(boundary, dim_index, count_along)
        pieces.append((low_face + below) * keep_low[:, :, :, None, None])
        pieces.append((top_face + above) * keep_top[:, :, :, None, None])
    return jnp.concatenate(pieces, -1)

def product(left, right):
    return jnp.dot(left.astype(jnp.float32), right.astype(jnp.float32), precision=lax.Precision.HIGHEST, preferred_element_type=jnp.float32)

def apply_operator(solution, scaling, fine_matrix):
    scaled = solution * scaling[:, :, :, None, :]
    row_block = product(scaled.reshape(-1, NODES), fine_matrix).reshape(solution.shape)
    return row_block * scaling[:, :, :, None, :]

def smooth_terms(residual, scaling, fine_inverse, prolong_four, coarse_four, prolong_two, coarse_two):
    scaled = (residual / scaling[:, :, :, None, :]).reshape(-1, NODES)
    fine_term = fine_weight * product(scaled, fine_inverse)
    four_term = coarse_weight * product(product(product(scaled, prolong_four), coarse_four), prolong_four.T)
    two_term = coarse_weight * product(product(product(scaled, prolong_two), coarse_two), prolong_two.T)
    inverse_scale = 1.0 / scaling[:, :, :, None, :]
    return (fine_term.reshape(residual.shape) * inverse_scale, four_term.reshape(residual.shape) * inverse_scale, two_term.reshape(residual.shape) * inverse_scale)

def reference(load_raw, scaling, fine_matrix, fine_inverse, prolong_four, coarse_four, prolong_two, coarse_two, orient, boundary):
    assembled = assemble(load_raw, orient, boundary)
    solution = jnp.zeros_like(load_raw)
    for cycle_index in range(CYCLES):
        if cycle_index == 0:
            residual = assembled
        else:
            residual = assembled - assemble(apply_operator(solution, scaling, fine_matrix), orient, boundary)
        terms = smooth_terms(residual, scaling, fine_inverse, prolong_four, coarse_four, prolong_two, coarse_two)
        solution = solution + assemble(terms[0] + terms[1] + terms[2], orient, boundary)
    return solution
```

```python
import functools

import jax
import jax.numpy as jnp
from jax import lax
from jax.experimental import pallas as pl
from jax.experimental.pallas import tpu as pltpu
from jax.sharding import PartitionSpec as P

FACE_SIDE = 8
AXES = ("ex", "ey", "ez")
VMEM_LIMIT = 24 * 1024 * 1024


def strip(ref, rows, dim):
    width = 2 * FACE_SIDE * FACE_SIDE
    return ref[rows, dim * width : (dim + 1) * width]


class Layout:
    def __init__(self, counts, species, sizes):
        self.counts = counts
        self.species = species
        self.sizes = sizes
        self.face = FACE_SIDE * FACE_SIDE

    def number(self, element):
        return (element[0] * self.counts[1] + element[1]) * self.counts[2] + element[2]

    def rows(self, element):
        start = self.number(element) * self.species
        return slice(start, start + self.species)

    def layer(self, dim, position):
        spans = [range(count) for count in self.counts]
        spans[dim] = range(position, position + 1)
        return [(i, j, k) for i in spans[0] for j in spans[1] for k in spans[2]]

    def pairs(self, dim):
        return (len(self.layer(dim, 0)) + 1) // 2

    def turns(self):
        return [
            (dim, parity)
            for dim in range(3)
            for parity in range(2)
            if self.sizes[dim] > 1 + parity
        ]

    def message(self, dim):
        return jax.ShapeDtypeStruct((self.pairs(dim) * self.species, 2 * self.face), jnp.float32)


def lanes_of(layout):
    return lax.broadcasted_iota(jnp.int32, (layout.species, 2 * layout.face), 1)


def picked(value, index):
    return jnp.take_along_axis(value, index, axis=1, mode="promise_in_bounds")


def flip_mask(code):
    reach = FACE_SIDE - 1
    first = jnp.where(code % 2 == 1, reach * FACE_SIDE, 0)
    return first + jnp.where(code // 2 == 1, reach, 0)


def pack(layout, load_block, orient_ref, outs):
    lane = lanes_of(layout)
    low = lane < layout.face
    turns = layout.turns()
    for dim in range(3):
        if layout.sizes[dim] == 1:
            continue
        even = lax.rem(lax.axis_index(AXES[dim]), 2) == 0
        first = layout.layer(dim, 0)
        last = layout.layer(dim, layout.counts[dim] - 1)
        for pair in range(layout.pairs(dim)):
            sides = []
            for half in range(2):
                where = min(2 * pair + half, len(first) - 1)
                upper = load_block(last[where], dim)
                lower = load_block(first[where], dim)
                code = orient_ref[(dim,) + first[where]]
                lower = picked(lower, lane ^ (flip_mask(code) + half * layout.face))
                if half == 0:
                    upper = pltpu.roll(upper, layout.face, 1)
                sides.append((upper, lower))
            up = jnp.where(low, sides[0][0], sides[1][0])
            down = jnp.where(low, sides[0][1], sides[1][1])
            rows = slice(pair * layout.species, (pair + 1) * layout.species)
            for parity in range(2):
                if (dim, parity) in turns:
                    is_lower = even if parity == 0 else jnp.logical_not(even)
                    outs[turns.index((dim, parity))][rows, :] = jnp.where(is_lower, up, down)


def received(layout, dim, where, refs, want_low):
    turns = layout.turns()
    rows = slice((where // 2) * layout.species, (where // 2 + 1) * layout.species)
    even = lax.rem(lax.axis_index(AXES[dim]), 2) == 0
    from_pair = [
        refs[turns.index((dim, parity))][rows, :] if (dim, parity) in turns else None
        for parity in range(2)
    ]
    zero = jnp.zeros((layout.species, 2 * layout.face), jnp.float32)
    first = zero if from_pair[0] is None else from_pair[0]
    second = zero if from_pair[1] is None else from_pair[1]
    if want_low:
        return jnp.where(even, second, first)
    return jnp.where(even, first, second)


def assemble(layout, load_block, messages, orient_ref, boundary_ref, emit):
    lane = lanes_of(layout)
    low = lane < layout.face
    for dim in range(3):
        count = layout.counts[dim]
        here = lax.axis_index(AXES[dim])
        at_start = here == 0
        at_end = here == layout.sizes[dim] - 1
        for where, start in enumerate(layout.layer(dim, 0)):
            line = [start[:dim] + (step,) + start[dim + 1 :] for step in range(count)]
            blocks = [load_block(element, dim) for element in line]
            half = (where % 2) * layout.face
            turned = []
            for step, element in enumerate(line):
                mask = flip_mask(orient_ref[(dim,) + element])
                if step == 0:
                    from_below = received(layout, dim, where, messages, True)
                    turned.append(picked(from_below, lane ^ (mask + half)))
                else:
                    shared = jnp.where(low, blocks[step], blocks[step - 1])
                    turned.append(picked(shared, lane ^ (mask + layout.face)))
            from_above = received(layout, dim, where, messages, False)
            if half == 0:
                from_above = pltpu.roll(from_above, layout.face, 1)
            turned.append(from_above)
            for step, element in enumerate(line):
                value = blocks[step] + jnp.where(low, turned[step], turned[step + 1])
                if step == 0:
                    fixed = jnp.where(at_start, boundary_ref[(2 * dim,) + element], 0)
                    value = jnp.where(low & (fixed == 1), 0.0, value)
                if step == count - 1:
                    fixed = jnp.where(at_end, boundary_ref[(2 * dim + 1,) + element], 0)
                    value = jnp.where(jnp.logical_not(low) & (fixed == 1), 0.0, value)
                emit(element, dim, value)


def halves(value):
    high = value.astype(jnp.bfloat16)
    return high, (value - high.astype(jnp.float32)).astype(jnp.bfloat16)


def dot(left, right):
    return jnp.dot(left, right, preferred_element_type=jnp.float32)


def split_product(high, rest, matrix_ref):
    return (
        dot(high[...], matrix_ref[0]) + dot(high[...], matrix_ref[1]) + dot(rest[...], matrix_ref[0])
    )


def matrices_kernel(fine, inverse, four, coarse_four, two, coarse_two, operator, smoother):
    operator[0], operator[1] = halves(fine[...])

    def full(left, right, contract):
        return lax.dot_general(
            left,
            right,
            (((1,), (contract,)), ((), ())),
            precision=lax.Precision.HIGHEST,
            preferred_element_type=jnp.float32,
        )

    total = inverse[...]
    total += full(full(four[...], coarse_four[...], 0), four[...], 1)
    total += full(full(two[...], coarse_two[...], 0), two[...], 1)
    smoother[0], smoother[1] = halves(0.5 * total)


def first_kernel(layout, load, orient, *outs):
    pack(layout, lambda element, dim: strip(load, layout.rows(element), dim), orient, outs)


def stage_kernel(layout, kind, *refs):
    turns = len(layout.turns())
    refs = list(refs)
    value, messages = refs[0], refs[1 : 1 + turns]
    refs = refs[1 + turns :]
    orient, boundary = refs[:2]
    refs = refs[2:]

    def block(element, dim):
        return strip(value, layout.rows(element), dim)

    width = 2 * layout.face
    if kind == "last":
        (out,) = refs

        def emit(element, dim, result):
            out[layout.rows(element), dim * width : (dim + 1) * width] = result

        assemble(layout, block, messages, orient, boundary, emit)
        return

    scaling, matrix = refs[:2]
    refs = refs[2:]
    other = None
    if kind != "smooth":
        other, refs = refs[0], refs[1:]
    out, sent, (high, rest, scale) = refs[0], refs[1 : 1 + turns], refs[1 + turns :]
    scale[...] = scaling[...] if kind == "operator" else 1.0 / scaling[...]

    def factor(element, dim):
        return scale[element[0], element[1], element[2] : element[2] + 1, dim * width : (dim + 1) * width]

    def emit(element, dim, result):
        at = (layout.rows(element), slice(dim * width, (dim + 1) * width))
        high[at], rest[at] = halves(result * factor(element, dim))

    assemble(layout, block, messages, orient, boundary, emit)
    out[...] = split_product(high, rest, matrix)
    spans = [range(count) for count in layout.counts]
    for element in [(i, j, k) for i in spans[0] for j in spans[1] for k in spans[2]]:
        for dim in range(3):
            at = (layout.rows(element), slice(dim * width, (dim + 1) * width))
            scaled = out[at] * factor(element, dim)
            if kind == "operator":
                scaled = other[at] - scaled
            elif kind == "smooth_more":
                scaled = other[at] + scaled
            out[at] = scaled
    pack(layout, lambda element, dim: strip(out, layout.rows(element), dim), orient, sent)


def in_vmem(count):
    return [pl.BlockSpec(memory_space=pltpu.VMEM)] * count


def in_smem(count):
    return [pl.BlockSpec(memory_space=pltpu.SMEM)] * count


PARAMS = pltpu.CompilerParams(vmem_limit_bytes=VMEM_LIMIT)


def exchange(layout, messages):
    results = []
    for (dim, parity), message in zip(layout.turns(), messages):
        size = layout.sizes[dim]
        pairs = []
        for lower in range(parity, size - 1, 2):
            pairs += [(lower, lower + 1), (lower + 1, lower)]
        results.append(lax.ppermute(message, AXES[dim], pairs))
    return results


def body(
    load_raw,
    scaling,
    fine_matrix,
    fine_inverse,
    prolong_four,
    coarse_four,
    prolong_two,
    coarse_two,
    orient,
    boundary,
):
    counts, species, nodes = load_raw.shape[:3], load_raw.shape[3], load_raw.shape[4]
    layout = Layout(counts, species, tuple(lax.axis_size(axis) for axis in AXES))
    load = load_raw.reshape(-1, nodes)
    turns = layout.turns()
    message_shapes = [layout.message(dim) for dim, _ in turns]
    whole = jax.ShapeDtypeStruct(load.shape, jnp.float32)
    split_matrix = jax.ShapeDtypeStruct((2,) + fine_matrix.shape, jnp.bfloat16)

    operator, smoother = pl.pallas_call(
        matrices_kernel,
        out_shape=(split_matrix, split_matrix),
        in_specs=in_vmem(6),
        out_specs=tuple(in_vmem(2)),
        compiler_params=PARAMS,
        name="matrices",
    )(fine_matrix, fine_inverse, prolong_four, coarse_four, prolong_two, coarse_two)

    sent = pl.pallas_call(
        functools.partial(first_kernel, layout),
        out_shape=tuple(message_shapes),
        in_specs=in_vmem(1) + in_smem(1),
        out_specs=tuple(in_vmem(len(turns))),
        compiler_params=PARAMS,
        name="pack",
    )(load, orient)

    def stage(kind, value, messages, matrix, other):
        extra = () if other is None else (other,)
        results = pl.pallas_call(
            functools.partial(stage_kernel, layout, kind),
            out_shape=(whole,) + tuple(message_shapes),
            in_specs=in_vmem(1 + len(turns)) + in_smem(2) + in_vmem(2 + len(extra)),
            out_specs=tuple(in_vmem(1 + len(turns))),
            scratch_shapes=[
                pltpu.VMEM(load.shape, jnp.bfloat16),
                pltpu.VMEM(load.shape, jnp.bfloat16),
                pltpu.VMEM(scaling.shape, jnp.float32),
            ],
            compiler_params=PARAMS,
            name=kind,
        )(value, *messages, orient, boundary, scaling, matrix, *extra)
        return results[0], results[1:]

    first, sent = stage("smooth", load, exchange(layout, sent), smoother, None)
    left, sent = stage("operator", first, exchange(layout, sent), operator, load)
    total, sent = stage("smooth_more", left, exchange(layout, sent), smoother, first)
    result = pl.pallas_call(
        functools.partial(stage_kernel, layout, "last"),
        out_shape=whole,
        in_specs=in_vmem(1 + len(turns)) + in_smem(2),
        out_specs=in_vmem(1)[0],
        compiler_params=PARAMS,
        name="last",
    )(total, *exchange(layout, sent), orient, boundary)
    return result.reshape(load_raw.shape)


def solution(mesh):
    in_specs = (
        P("ex", "ey", "ez", None, None),
        P("ex", "ey", "ez", None),
        P(),
        P(),
        P(),
        P(),
        P(),
        P(),
        P(None, "ex", "ey", "ez"),
        P(None, "ex", "ey", "ez"),
    )
    out_specs = P("ex", "ey", "ez", None, None)
    return jax.shard_map(body, mesh=mesh, in_specs=in_specs, out_specs=out_specs, check_vma=False)
```

```python
import functools

import jax
import jax.numpy as jnp
from jax import lax
from jax.experimental import pallas as pl
from jax.experimental.pallas import tpu as pltpu
from jax.sharding import PartitionSpec as P

FACE_SIDE = 8
AXES = ("ex", "ey", "ez")
VMEM_LIMIT = 24 * 1024 * 1024


def strip(ref, rows, dim):
    width = 2 * FACE_SIDE * FACE_SIDE
    return ref[rows, dim * width : (dim + 1) * width]


class Layout:
    def __init__(self, counts, species, sizes):
        self.counts = counts
        self.species = species
        self.sizes = sizes
        self.face = FACE_SIDE * FACE_SIDE

    def number(self, element):
        return (element[0] * self.counts[1] + element[1]) * self.counts[2] + element[2]

    def rows(self, element):
        start = self.number(element) * self.species
        return slice(start, start + self.species)

    def layer(self, dim, position):
        spans = [range(count) for count in self.counts]
        spans[dim] = range(position, position + 1)
        return [(i, j, k) for i in spans[0] for j in spans[1] for k in spans[2]]

    def pairs(self, dim):
        return (len(self.layer(dim, 0)) + 1) // 2

    def turns(self):
        order = [(0, 0), (0, 1), (1, 1), (2, 0), (2, 1), (1, 0)]
        return [(dim, parity) for dim, parity in order if self.sizes[dim] > 1 + parity]

    def message(self, dim):
        return jax.ShapeDtypeStruct((self.pairs(dim) * self.species, 2 * self.face), jnp.float32)


def lanes_of(layout):
    return lax.broadcasted_iota(jnp.int32, (layout.species, 2 * layout.face), 1)


def picked(value, index):
    return jnp.take_along_axis(value, index, axis=1, mode="promise_in_bounds")


def flip_mask(code):
    reach = FACE_SIDE - 1
    return (code & 1) * (reach * FACE_SIDE) + (code >> 1) * reach


def places():
    return [lax.axis_index(axis) for axis in AXES]


def pack(layout, here, load_block, orient_ref, outs):
    lane = lanes_of(layout)
    low = lane < layout.face
    turns = layout.turns()
    for dim in range(3):
        if layout.sizes[dim] == 1:
            continue
        even = (here[dim] & 1) == 0
        first = layout.layer(dim, 0)
        last = layout.layer(dim, layout.counts[dim] - 1)
        for pair in range(layout.pairs(dim)):
            sides = []
            for half in range(2):
                where = min(2 * pair + half, len(first) - 1)
                upper = load_block(last[where], dim)
                lower = load_block(first[where], dim)
                code = orient_ref[(dim,) + first[where]]
                lower = picked(lower, lane ^ (flip_mask(code) + half * layout.face))
                if half == 0:
                    upper = pltpu.roll(upper, layout.face, 1)
                sides.append((upper, lower))
            up = jnp.where(low, sides[0][0], sides[1][0])
            down = jnp.where(low, sides[0][1], sides[1][1])
            rows = slice(pair * layout.species, (pair + 1) * layout.species)
            for parity in range(2):
                if (dim, parity) in turns:
                    is_lower = even if parity == 0 else jnp.logical_not(even)
                    outs[turns.index((dim, parity))][rows, :] = jnp.where(is_lower, up, down)


def received(layout, here, dim, refs):
    turns = layout.turns()
    even = (here[dim] & 1) == 0
    at_start = here[dim] == 0
    at_end = here[dim] == layout.sizes[dim] - 1
    zero = jnp.zeros((layout.species, 2 * layout.face), jnp.float32)
    found = []
    for pair in range(layout.pairs(dim)):
        rows = slice(pair * layout.species, (pair + 1) * layout.species)
        first, second = [
            refs[turns.index((dim, parity))][rows, :] if (dim, parity) in turns else zero
            for parity in range(2)
        ]
        below = jnp.where(at_start, 0.0, jnp.where(even, second, first))
        above = jnp.where(at_end, 0.0, jnp.where(even, first, second))
        found.append((below, above))
    return found


def assemble(layout, here, load_block, messages, orient_ref, boundary_ref, emit):
    lane = lanes_of(layout)
    low = lane < layout.face
    for dim in range(3):
        count = layout.counts[dim]
        at_start = here[dim] == 0
        at_end = here[dim] == layout.sizes[dim] - 1
        outside = received(layout, here, dim, messages)
        for where, start in enumerate(layout.layer(dim, 0)):
            line = [start[:dim] + (step,) + start[dim + 1 :] for step in range(count)]
            blocks = [load_block(element, dim) for element in line]
            half = (where % 2) * layout.face
            below, above = outside[where // 2]
            turned = []
            for step, element in enumerate(line):
                mask = flip_mask(orient_ref[(dim,) + element])
                if step == 0:
                    turned.append(picked(below, lane ^ (mask + half)))
                else:
                    shared = jnp.where(low, blocks[step], blocks[step - 1])
                    turned.append(picked(shared, lane ^ (mask + layout.face)))
            turned.append(pltpu.roll(above, layout.face, 1) if half == 0 else above)
            for step, element in enumerate(line):
                value = blocks[step] + jnp.where(low, turned[step], turned[step + 1])
                if step == 0:
                    fixed = jnp.where(at_start, boundary_ref[element + (2 * dim,)], 0)
                    value = jnp.where(low & (fixed == 1), 0.0, value)
                if step == count - 1:
                    fixed = jnp.where(at_end, boundary_ref[element + (2 * dim + 1,)], 0)
                    value = jnp.where(jnp.logical_not(low) & (fixed == 1), 0.0, value)
                emit(element, dim, value)


def halves(value):
    high = value.astype(jnp.bfloat16)
    return high, (value - high.astype(jnp.float32)).astype(jnp.bfloat16)


def stacked(value, out):
    high, rest = halves(value)
    size = value.shape[0]
    out[:size, :] = high
    out[size : 2 * size, :] = rest
    out[2 * size :, :] = high


def matrices_kernel(fine, inverse, four, coarse_four, two, coarse_two, operator, smoother):
    stacked(fine[...], operator)

    def full(left, right, contract):
        return lax.dot_general(
            left,
            right,
            (contract, ((), ())),
            precision=lax.Precision.HIGHEST,
            preferred_element_type=jnp.float32,
        )

    total = inverse[...]
    for prolong, coarse in ((four, coarse_four), (two, coarse_two)):
        total += full(prolong[...], full(coarse[...], prolong[...], ((1,), (0,))), ((0,), (0,)))
    stacked(0.5 * total, smoother)


def first_kernel(layout, load, orient, *outs):
    pack(layout, places(), lambda element, dim: strip(load, layout.rows(element), dim), orient, outs)


def stage_kernel(layout, kind, *refs):
    turns = len(layout.turns())
    refs = list(refs)
    value, messages = refs[0], refs[1 : 1 + turns]
    refs = refs[1 + turns :]
    orient, boundary = refs[:2]
    refs = refs[2:]
    here = places()

    def block(element, dim):
        return strip(value, layout.rows(element), dim)

    width = 2 * layout.face
    if kind == "last":
        (out,) = refs

        def emit(element, dim, result):
            out[layout.rows(element), dim * width : (dim + 1) * width] = result

        assemble(layout, here, block, messages, orient, boundary, emit)
        return

    scaling, matrix = refs[:2]
    refs = refs[2:]
    other = None
    if kind != "smooth":
        other, refs = refs[0], refs[1:]
    out, sent, (split, scale) = refs[0], refs[1 : 1 + turns], refs[1 + turns :]
    nodes = value.shape[1]
    scale[...] = scaling[...] if kind == "operator" else 1.0 / scaling[...]

    def factor(element, dim):
        return scale[element[0], element[1], element[2] : element[2] + 1, dim * width : (dim + 1) * width]

    def emit(element, dim, result):
        high, rest = halves(result * factor(element, dim))
        for part, piece in enumerate((high, high, rest)):
            start = part * nodes + dim * width
            split[layout.rows(element), start : start + width] = piece

    assemble(layout, here, block, messages, orient, boundary, emit)
    out[...] = jnp.dot(split[...], matrix[...], preferred_element_type=jnp.float32)
    spans = [range(count) for count in layout.counts]
    for element in [(i, j, k) for i in spans[0] for j in spans[1] for k in spans[2]]:
        for dim in range(3):
            at = (layout.rows(element), slice(dim * width, (dim + 1) * width))
            scaled = out[at] * factor(element, dim)
            if kind == "operator":
                scaled = other[at] - scaled
            elif kind == "smooth_more":
                scaled = other[at] + scaled
            out[at] = scaled
    pack(layout, here, lambda element, dim: strip(out, layout.rows(element), dim), orient, sent)


def in_vmem(count):
    return [pl.BlockSpec(memory_space=pltpu.VMEM)] * count


def in_smem(count):
    return [pl.BlockSpec(memory_space=pltpu.SMEM)] * count


PARAMS = pltpu.CompilerParams(vmem_limit_bytes=VMEM_LIMIT)


def exchange(layout, messages):
    results = []
    for (dim, parity), message in zip(layout.turns(), messages):
        size = layout.sizes[dim]
        partner = list(range(size))
        for lower in range(parity, size - 1, 2):
            partner[lower], partner[lower + 1] = lower + 1, lower
        pairs = list(enumerate(partner))
        results.append(lax.ppermute(message, AXES[dim], pairs))
    return results


def body(
    load_raw,
    scaling,
    fine_matrix,
    fine_inverse,
    prolong_four,
    coarse_four,
    prolong_two,
    coarse_two,
    orient,
    boundary,
):
    counts, species, nodes = load_raw.shape[:3], load_raw.shape[3], load_raw.shape[4]
    layout = Layout(counts, species, tuple(lax.axis_size(axis) for axis in AXES))
    load = load_raw.reshape(-1, nodes)
    turns = layout.turns()
    message_shapes = [layout.message(dim) for dim, _ in turns]
    whole = jax.ShapeDtypeStruct(load.shape, jnp.float32)
    split_matrix = jax.ShapeDtypeStruct((3 * nodes, nodes), jnp.bfloat16)
    boundary = jnp.transpose(boundary, (1, 2, 3, 0))

    operator, smoother = pl.pallas_call(
        matrices_kernel,
        out_shape=(split_matrix, split_matrix),
        in_specs=in_vmem(6),
        out_specs=tuple(in_vmem(2)),
        compiler_params=PARAMS,
        name="matrices",
    )(fine_matrix, fine_inverse, prolong_four.T, coarse_four, prolong_two.T, coarse_two)

    sent = pl.pallas_call(
        functools.partial(first_kernel, layout),
        out_shape=tuple(message_shapes),
        in_specs=in_vmem(1) + in_smem(1),
        out_specs=tuple(in_vmem(len(turns))),
        compiler_params=PARAMS,
        name="pack",
    )(load, orient)

    def stage(kind, value, messages, matrix, other):
        extra = () if other is None else (other,)
        results = pl.pallas_call(
            functools.partial(stage_kernel, layout, kind),
            out_shape=(whole,) + tuple(message_shapes),
            in_specs=in_vmem(1 + len(turns)) + in_smem(2) + in_vmem(2 + len(extra)),
            out_specs=tuple(in_vmem(1 + len(turns))),
            scratch_shapes=[
                pltpu.VMEM((load.shape[0], 3 * nodes), jnp.bfloat16),
                pltpu.VMEM(scaling.shape, jnp.float32),
            ],
            compiler_params=PARAMS,
            name=kind,
        )(value, *messages, orient, boundary, scaling, matrix, *extra)
        return results[0], results[1:]

    first, sent = stage("smooth", load, exchange(layout, sent), smoother, None)
    left, sent = stage("operator", first, exchange(layout, sent), operator, load)
    total, sent = stage("smooth_more", left, exchange(layout, sent), smoother, first)
    result = pl.pallas_call(
        functools.partial(stage_kernel, layout, "last"),
        out_shape=whole,
        in_specs=in_vmem(1 + len(turns)) + in_smem(2),
        out_specs=in_vmem(1)[0],
        compiler_params=PARAMS,
        name="last",
    )(total, *exchange(layout, sent), orient, boundary)
    return result.reshape(load_raw.shape)


def solution(mesh):
    in_specs = (
        P("ex", "ey", "ez", None, None),
        P("ex", "ey", "ez", None),
        P(),
        P(),
        P(),
        P(),
        P(),
        P(),
        P(None, "ex", "ey", "ez"),
        P(None, "ex", "ey", "ez"),
    )
    out_specs = P("ex", "ey", "ez", None, None)
    return jax.shard_map(body, mesh=mesh, in_specs=in_specs, out_specs=out_specs, check_vma=False)
```

```python
import functools

import jax
import jax.numpy as jnp
from jax import lax
from jax.experimental import pallas as pl
from jax.experimental.pallas import tpu as pltpu
from jax.sharding import PartitionSpec as P

FACE_SIDE = 8
AXES = ("ex", "ey", "ez")
VMEM_LIMIT = 24 * 1024 * 1024


def strip(ref, rows, dim):
    width = 2 * FACE_SIDE * FACE_SIDE
    return ref[rows, dim * width : (dim + 1) * width]


class Layout:
    def __init__(self, counts, species, sizes):
        self.counts = counts
        self.species = species
        self.sizes = sizes
        self.face = FACE_SIDE * FACE_SIDE

    def number(self, element):
        return (element[0] * self.counts[1] + element[1]) * self.counts[2] + element[2]

    def rows(self, element):
        start = self.number(element) * self.species
        return slice(start, start + self.species)

    def layer(self, dim, position):
        spans = [range(count) for count in self.counts]
        spans[dim] = range(position, position + 1)
        return [(i, j, k) for i in spans[0] for j in spans[1] for k in spans[2]]

    def pairs(self, dim):
        return (len(self.layer(dim, 0)) + 1) // 2

    def turns(self):
        order = [(0, 0), (0, 1), (1, 1), (2, 0), (2, 1), (1, 0)]
        return [(dim, parity) for dim, parity in order if self.sizes[dim] > 1 + parity]

    def message(self, dim):
        return jax.ShapeDtypeStruct((self.pairs(dim) * self.species, 2 * self.face), jnp.float32)


def lanes_of(layout):
    return lax.broadcasted_iota(jnp.int32, (layout.species, 2 * layout.face), 1)


def picked(value, index):
    return jnp.take_along_axis(value, index, axis=1, mode="promise_in_bounds")


def flip_mask(code):
    reach = FACE_SIDE - 1
    return (code & 1) * (reach * FACE_SIDE) + (code >> 1) * reach


def places():
    return [lax.axis_index(axis) for axis in AXES]


def pack(layout, here, load_block, orient_ref, outs):
    lane = lanes_of(layout)
    low = lane < layout.face
    turns = layout.turns()
    for dim in range(3):
        if layout.sizes[dim] == 1:
            continue
        even = (here[dim] & 1) == 0
        first = layout.layer(dim, 0)
        last = layout.layer(dim, layout.counts[dim] - 1)
        for pair in range(layout.pairs(dim)):
            sides = []
            for half in range(2):
                where = min(2 * pair + half, len(first) - 1)
                upper = load_block(last[where], dim)
                lower = load_block(first[where], dim)
                code = orient_ref[(dim,) + first[where]]
                lower = picked(lower, lane ^ (flip_mask(code) + half * layout.face))
                if half == 0:
                    upper = pltpu.roll(upper, layout.face, 1)
                sides.append((upper, lower))
            up = jnp.where(low, sides[0][0], sides[1][0])
            down = jnp.where(low, sides[0][1], sides[1][1])
            rows = slice(pair * layout.species, (pair + 1) * layout.species)
            for parity in range(2):
                if (dim, parity) in turns:
                    is_lower = even if parity == 0 else jnp.logical_not(even)
                    outs[turns.index((dim, parity))][rows, :] = jnp.where(is_lower, up, down)


def received(layout, here, dim, refs):
    turns = layout.turns()
    even = (here[dim] & 1) == 0
    at_start = here[dim] == 0
    at_end = here[dim] == layout.sizes[dim] - 1
    zero = jnp.zeros((layout.species, 2 * layout.face), jnp.float32)
    found = []
    for pair in range(layout.pairs(dim)):
        rows = slice(pair * layout.species, (pair + 1) * layout.species)
        first, second = [
            refs[turns.index((dim, parity))][rows, :] if (dim, parity) in turns else zero
            for parity in range(2)
        ]
        below = jnp.where(at_start, 0.0, jnp.where(even, second, first))
        above = jnp.where(at_end, 0.0, jnp.where(even, first, second))
        found.append((below, above))
    return found


def assemble(layout, here, load_block, messages, orient_ref, boundary_ref, emit):
    lane = lanes_of(layout)
    low = lane < layout.face
    for dim in range(3):
        count = layout.counts[dim]
        at_start = here[dim] == 0
        at_end = here[dim] == layout.sizes[dim] - 1
        outside = received(layout, here, dim, messages)
        for where, start in enumerate(layout.layer(dim, 0)):
            line = [start[:dim] + (step,) + start[dim + 1 :] for step in range(count)]
            blocks = [load_block(element, dim) for element in line]
            half = (where % 2) * layout.face
            below, above = outside[where // 2]
            turned = []
            for step, element in enumerate(line):
                mask = flip_mask(orient_ref[(dim,) + element])
                if step == 0:
                    turned.append(picked(below, lane ^ (mask + half)))
                else:
                    shared = jnp.where(low, blocks[step], blocks[step - 1])
                    turned.append(picked(shared, lane ^ (mask + layout.face)))
            turned.append(pltpu.roll(above, layout.face, 1) if half == 0 else above)
            for step, element in enumerate(line):
                value = blocks[step] + jnp.where(low, turned[step], turned[step + 1])
                if step == 0:
                    fixed = jnp.where(at_start, boundary_ref[element + (2 * dim,)], 0)
                    value = jnp.where(low & (fixed == 1), 0.0, value)
                if step == count - 1:
                    fixed = jnp.where(at_end, boundary_ref[element + (2 * dim + 1,)], 0)
                    value = jnp.where(jnp.logical_not(low) & (fixed == 1), 0.0, value)
                emit(element, dim, value)


def halves(value):
    high = value.astype(jnp.bfloat16)
    return high, (value - high.astype(jnp.float32)).astype(jnp.bfloat16)


def stacked(value, out):
    high, rest = halves(value)
    size = value.shape[0]
    out[:size, :] = high
    out[size : 2 * size, :] = rest
    out[2 * size :, :] = high


def matrices_kernel(fine, inverse, four, coarse_four, two, coarse_two, operator, smoother):
    stacked(fine[...], operator)

    def full(left, right, contract):
        return lax.dot_general(
            left,
            right,
            (contract, ((), ())),
            precision=lax.Precision.HIGHEST,
            preferred_element_type=jnp.float32,
        )

    total = inverse[...]
    for prolong, coarse in ((four, coarse_four), (two, coarse_two)):
        total += full(prolong[...], full(coarse[...], prolong[...], ((1,), (0,))), ((0,), (0,)))
    stacked(0.5 * total, smoother)


def first_kernel(layout, load, orient, *outs):
    pack(layout, places(), lambda element, dim: strip(load, layout.rows(element), dim), orient, outs)


def stage_kernel(layout, kind, *refs):
    turns = len(layout.turns())
    refs = list(refs)
    value, messages = refs[0], refs[1 : 1 + turns]
    refs = refs[1 + turns :]
    orient, boundary = refs[:2]
    refs = refs[2:]
    here = places()

    def block(element, dim):
        return strip(value, layout.rows(element), dim)

    width = 2 * layout.face
    if kind == "last":
        (out,) = refs

        def emit(element, dim, result):
            out[layout.rows(element), dim * width : (dim + 1) * width] = result

        assemble(layout, here, block, messages, orient, boundary, emit)
        return

    scaling, matrix = refs[:2]
    refs = refs[2:]
    other = None
    if kind != "smooth":
        other, refs = refs[0], refs[1:]
    out, sent, (split, scale) = refs[0], refs[1 : 1 + turns], refs[1 + turns :]
    nodes = value.shape[1]
    scale[...] = scaling[...] if kind == "operator" else 1.0 / scaling[...]

    def factor(element, dim):
        return scale[element[0], element[1], element[2] : element[2] + 1, dim * width : (dim + 1) * width]

    def emit(element, dim, result):
        high, rest = halves(result * factor(element, dim))
        for part, piece in enumerate((high, high, rest)):
            start = part * nodes + dim * width
            split[layout.rows(element), start : start + width] = piece

    assemble(layout, here, block, messages, orient, boundary, emit)
    out[...] = jnp.dot(split[...], matrix[...], preferred_element_type=jnp.float32)
    spans = [range(count) for count in layout.counts]
    for element in [(i, j, k) for i in spans[0] for j in spans[1] for k in spans[2]]:
        for dim in range(3):
            at = (layout.rows(element), slice(dim * width, (dim + 1) * width))
            scaled = out[at] * factor(element, dim)
            if kind == "operator":
                scaled = other[at] - scaled
            elif kind == "smooth_more":
                scaled = other[at] + scaled
            out[at] = scaled
    pack(layout, here, lambda element, dim: strip(out, layout.rows(element), dim), orient, sent)


def in_vmem(count):
    return [pl.BlockSpec(memory_space=pltpu.VMEM)] * count


def in_smem(count):
    return [pl.BlockSpec(memory_space=pltpu.SMEM)] * count


PARAMS = pltpu.CompilerParams(vmem_limit_bytes=VMEM_LIMIT)


def exchange(layout, messages):
    results = []
    for (dim, parity), message in zip(layout.turns(), messages):
        size = layout.sizes[dim]
        partner = list(range(size))
        for lower in range(parity, size - 1, 2):
            partner[lower], partner[lower + 1] = lower + 1, lower
        if size > 2 and size % 2 == 0 and parity == 1:
            partner[0], partner[-1] = size - 1, 0
        pairs = list(enumerate(partner))
        results.append(lax.ppermute(message, AXES[dim], pairs))
    return results


def body(
    load_raw,
    scaling,
    fine_matrix,
    fine_inverse,
    prolong_four,
    coarse_four,
    prolong_two,
    coarse_two,
    orient,
    boundary,
):
    counts, species, nodes = load_raw.shape[:3], load_raw.shape[3], load_raw.shape[4]
    layout = Layout(counts, species, tuple(lax.axis_size(axis) for axis in AXES))
    load = load_raw.reshape(-1, nodes)
    turns = layout.turns()
    message_shapes = [layout.message(dim) for dim, _ in turns]
    whole = jax.ShapeDtypeStruct(load.shape, jnp.float32)
    split_matrix = jax.ShapeDtypeStruct((3 * nodes, nodes), jnp.bfloat16)
    boundary = jnp.transpose(boundary, (1, 2, 3, 0))

    operator, smoother = pl.pallas_call(
        matrices_kernel,
        out_shape=(split_matrix, split_matrix),
        in_specs=in_vmem(6),
        out_specs=tuple(in_vmem(2)),
        compiler_params=PARAMS,
        name="matrices",
    )(fine_matrix, fine_inverse, prolong_four.T, coarse_four, prolong_two.T, coarse_two)

    sent = pl.pallas_call(
        functools.partial(first_kernel, layout),
        out_shape=tuple(message_shapes),
        in_specs=in_vmem(1) + in_smem(1),
        out_specs=tuple(in_vmem(len(turns))),
        compiler_params=PARAMS,
        name="pack",
    )(load, orient)

    def stage(kind, value, messages, matrix, other):
        extra = () if other is None else (other,)
        results = pl.pallas_call(
            functools.partial(stage_kernel, layout, kind),
            out_shape=(whole,) + tuple(message_shapes),
            in_specs=in_vmem(1 + len(turns)) + in_smem(2) + in_vmem(2 + len(extra)),
            out_specs=tuple(in_vmem(1 + len(turns))),
            scratch_shapes=[
                pltpu.VMEM((load.shape[0], 3 * nodes), jnp.bfloat16),
                pltpu.VMEM(scaling.shape, jnp.float32),
            ],
            compiler_params=PARAMS,
            name=kind,
        )(value, *messages, orient, boundary, scaling, matrix, *extra)
        return results[0], results[1:]

    first, sent = stage("smooth", load, exchange(layout, sent), smoother, None)
    left, sent = stage("operator", first, exchange(layout, sent), operator, load)
    total, sent = stage("smooth_more", left, exchange(layout, sent), smoother, first)
    result = pl.pallas_call(
        functools.partial(stage_kernel, layout, "last"),
        out_shape=whole,
        in_specs=in_vmem(1 + len(turns)) + in_smem(2),
        out_specs=in_vmem(1)[0],
        compiler_params=PARAMS,
        name="last",
    )(total, *exchange(layout, sent), orient, boundary)
    return result.reshape(load_raw.shape)


def solution(mesh):
    in_specs = (
        P("ex", "ey", "ez", None, None),
        P("ex", "ey", "ez", None),
        P(),
        P(),
        P(),
        P(),
        P(),
        P(),
        P(None, "ex", "ey", "ez"),
        P(None, "ex", "ey", "ez"),
    )
    out_specs = P("ex", "ey", "ez", None, None)
    return jax.shard_map(body, mesh=mesh, in_specs=in_specs, out_specs=out_specs, check_vma=False)
```

```python
import functools

import jax
import jax.numpy as jnp
from jax import lax
from jax.experimental import pallas as pl
from jax.experimental.pallas import tpu as pltpu
from jax.sharding import PartitionSpec as P

FACE_SIDE = 8
FACE = FACE_SIDE * FACE_SIDE
WIDTH = 2 * FACE
AXES = ("ex", "ey", "ez")
EARLY = (0, 1)
LATE = (2,)
VMEM_LIMIT = 24 * 1024 * 1024


class Layout:
    def __init__(self, counts, species, sizes):
        self.counts = counts
        self.species = species
        self.sizes = sizes

    def elements(self):
        spans = [range(count) for count in self.counts]
        return [(i, j, k) for i in spans[0] for j in spans[1] for k in spans[2]]

    def number(self, element):
        return (element[0] * self.counts[1] + element[1]) * self.counts[2] + element[2]

    def rows(self, element):
        start = self.number(element) * self.species
        return slice(start, start + self.species)

    def layer(self, dim, position):
        return [element for element in self.elements() if element[dim] == position]

    def pairs(self, dim):
        return (len(self.layer(dim, 0)) + 1) // 2

    def pair_rows(self, pair):
        return slice(pair * self.species, (pair + 1) * self.species)

    def turns(self, dims=EARLY + LATE):
        order = [(0, 0), (0, 1), (1, 1), (1, 0), (2, 0), (2, 1)]
        return [
            (dim, parity) for dim, parity in order if self.sizes[dim] > 1 + parity and dim in dims
        ]

    def message(self, dim):
        return jax.ShapeDtypeStruct((self.pairs(dim) * self.species, WIDTH), jnp.float32)


def columns(dim):
    return slice(dim * WIDTH, (dim + 1) * WIDTH)


def lanes(layout):
    return lax.broadcasted_iota(jnp.int32, (layout.species, WIDTH), 1)


def picked(value, index):
    return jnp.take_along_axis(value, index, axis=1, mode="promise_in_bounds")


def flip_mask(code):
    reach = FACE_SIDE - 1
    return (code & 1) * (reach * FACE_SIDE) + (code >> 1) * reach


def places():
    return [lax.axis_index(axis) for axis in AXES]


def pack(layout, here, dim, load_block, mask_of, outs):
    turns = [(turn, out) for turn, out in zip(layout.turns(), outs) if turn[0] == dim]
    if not turns:
        return
    lane = lanes(layout)
    low = lane < FACE
    even = (here[dim] & 1) == 0
    first = layout.layer(dim, 0)
    last = layout.layer(dim, layout.counts[dim] - 1)
    for pair in range(layout.pairs(dim)):
        sides = []
        for half in range(2):
            where = min(2 * pair + half, len(first) - 1)
            upper = load_block(last[where], dim)
            lower = load_block(first[where], dim)
            lower = picked(lower, lane ^ mask_of(first[where], dim) ^ (half * FACE))
            if half == 0:
                upper = pltpu.roll(upper, FACE, 1)
            sides.append((upper, lower))
        up = jnp.where(low, sides[0][0], sides[1][0])
        down = jnp.where(low, sides[0][1], sides[1][1])
        for (_, parity), out in turns:
            is_lower = even if parity == 0 else jnp.logical_not(even)
            out[layout.pair_rows(pair), :] = jnp.where(is_lower, up, down)


def received(layout, here, dim, messages):
    even = (here[dim] & 1) == 0
    at_start = here[dim] == 0
    at_end = here[dim] == layout.sizes[dim] - 1
    zero = jnp.zeros((layout.species, WIDTH), jnp.float32)
    found = []
    for pair in range(layout.pairs(dim)):
        first, second = [
            messages[dim, parity][layout.pair_rows(pair), :] if (dim, parity) in messages else zero
            for parity in range(2)
        ]
        below = jnp.where(at_start, 0.0, jnp.where(even, second, first))
        above = jnp.where(at_end, 0.0, jnp.where(even, first, second))
        found.append((below, above))
    return found


def assemble(layout, here, dim, load_block, messages, mask_of, keep_of, emit):
    lane = lanes(layout)
    low = lane < FACE
    count = layout.counts[dim]
    outside = received(layout, here, dim, messages)
    for where, start in enumerate(layout.layer(dim, 0)):
        line = [start[:dim] + (step,) + start[dim + 1 :] for step in range(count)]
        blocks = [load_block(element, dim) for element in line]
        half = (where % 2) * FACE
        below, above = outside[where // 2]
        turned = []
        for step, element in enumerate(line):
            index = lane ^ mask_of(element, dim)
            if step == 0:
                turned.append(picked(below, index ^ half))
            else:
                shared = jnp.where(low, blocks[step], blocks[step - 1])
                turned.append(picked(shared, index ^ FACE))
        turned.append(pltpu.roll(above, FACE, 1) if half == 0 else above)
        for step, element in enumerate(line):
            value = blocks[step] + jnp.where(low, turned[step], turned[step + 1])
            if step in (0, count - 1):
                value = value * keep_of(element, dim)
            emit(element, value)


def halves(value):
    high = value.astype(jnp.bfloat16)
    return high, (value - high.astype(jnp.float32)).astype(jnp.bfloat16)


def dot(left, right, contract=((1,), (0,))):
    return lax.dot_general(left, right, (contract, ((), ())), preferred_element_type=jnp.float32)


def split_dot(left, right, contract):
    left_high, left_rest = halves(left)
    right_high, right_rest = halves(right)
    return (
        dot(left_high, right_high, contract)
        + dot(left_high, right_rest, contract)
        + dot(left_rest, right_high, contract)
    )


def stacked(value, early, late):
    high, rest = halves(value)
    cut = WIDTH * len(EARLY)
    for out, rows in ((early, slice(0, cut)), (late, slice(cut, None))):
        size = out.shape[0] // 3
        for part, piece in enumerate((high, rest, high)):
            out[part * size : (part + 1) * size, :] = piece[rows, :]


def prepare_kernel(layout, *refs):
    sources, refs = refs[:8], refs[8:]
    outs, masks, keeps, refs = refs[:4], refs[4], refs[5], refs[6:]
    staged, arrived = refs[:8], refs[8]
    copies = [
        pltpu.make_async_copy(source, stage, arrived.at[number])
        for number, (source, stage) in enumerate(zip(sources, staged))
    ]
    for copy in copies:
        copy.start()
    for copy in copies[:2]:
        copy.wait()
    orient, boundary = staged[:2]
    low = lax.broadcasted_iota(jnp.int32, (1, WIDTH), 1) < FACE
    here = places()
    for element in layout.elements():
        number = layout.number(element)
        for dim in range(3):
            mask = flip_mask(orient[(dim,) + element])
            masks[number : number + 1, columns(dim)] = jnp.full((1, WIDTH), mask, jnp.int32)
            at_start = (here[dim] == 0) & (element[dim] == 0)
            at_end = (here[dim] == layout.sizes[dim] - 1) & (element[dim] == layout.counts[dim] - 1)
            fixed_low = jnp.where(at_start, boundary[element + (2 * dim,)], 0)
            fixed_top = jnp.where(at_end, boundary[element + (2 * dim + 1,)], 0)
            fixed = jnp.where(low, fixed_low, fixed_top)
            keeps[number : number + 1, columns(dim)] = 1.0 - fixed.astype(jnp.float32)
    for copy in copies[2:]:
        copy.wait()
    fine, inverse, four, coarse_four, two, coarse_two = [stage[...] for stage in staged[2:]]
    stacked(fine, outs[0], outs[1])
    total = inverse
    for prolong, coarse in ((four, coarse_four), (two, coarse_two)):
        total += split_dot(prolong, split_dot(coarse, prolong, ((1,), (0,))), ((0,), (0,)))
    stacked(0.5 * total, outs[2], outs[3])


def first_kernel(layout, load, orient, *refs):
    turns = len(layout.turns())
    outs, (staged, codes, arrived) = refs[:turns], refs[turns:]
    copies = [
        pltpu.make_async_copy(load.at[:, columns(dim)], staged.at[:, columns(dim)], arrived.at[dim])
        for dim in range(3)
    ]
    code_copy = pltpu.make_async_copy(orient, codes, arrived.at[3])
    code_copy.start()
    for copy in copies:
        copy.start()
    here = places()
    code_copy.wait()
    for dim in range(3):
        copies[dim].wait()
        pack(
            layout,
            here,
            dim,
            lambda element, dim: staged[layout.rows(element), columns(dim)],
            lambda element, dim: flip_mask(codes[(dim,) + element]),
            outs,
        )


def table(layout, ref):
    def row(element, dim):
        number = layout.number(element)
        return ref[number : number + 1, columns(dim)]

    return row


def scales(layout, kind, ref):
    def row(element, dim):
        value = ref[element[0], element[1], element[2] : element[2] + 1, columns(dim)]
        return value if kind == "operator" else 1.0 / value

    return row


def scaled_product(layout, kind, dims, here, value, messages, masks, keeps, scaling, matrix, split):
    factor = scales(layout, kind, scaling)
    size = len(dims) * WIDTH
    for place, dim in enumerate(dims):

        def emit(element, result):
            high, rest = halves(result * factor(element, dim))
            for part, piece in enumerate((high, high, rest)):
                start = part * size + place * WIDTH
                split[layout.rows(element), start : start + WIDTH] = piece

        assemble(
            layout,
            here,
            dim,
            lambda element, dim: value[layout.rows(element), columns(dim)],
            messages,
            table(layout, masks),
            table(layout, keeps),
            emit,
        )
    return dot(split[...], matrix[...])


def taken(layout, dims, refs):
    turns = layout.turns(dims)
    return dict(zip(turns, refs)), refs[len(turns) :]


def early_kernel(layout, kind, value, *refs):
    messages, refs = taken(layout, EARLY, refs)
    masks, keeps, scaling, matrix, out, split = refs
    out[...] = scaled_product(
        layout, kind, EARLY, places(), value, messages, masks, keeps, scaling, matrix, split
    )


def late_kernel(layout, kind, value, *refs):
    messages, refs = taken(layout, LATE, refs)
    masks, keeps, scaling, matrix, begun, refs = *refs[:5], refs[5:]
    other = None
    if kind != "smooth":
        other, refs = refs[0], refs[1:]
    turns = len(layout.turns())
    out, sent, (split, summed) = refs[0], refs[1 : 1 + turns], refs[1 + turns :]
    here = places()
    summed[...] = begun[...] + scaled_product(
        layout, kind, LATE, here, value, messages, masks, keeps, scaling, matrix, split
    )
    factor = scales(layout, kind, scaling)
    for dim in range(3):
        for element in layout.elements():
            at = (layout.rows(element), columns(dim))
            result = summed[at] * factor(element, dim)
            if kind == "operator":
                result = other[at] - result
            elif kind == "smooth_more":
                result = other[at] + result
            out[at] = result
        pack(
            layout,
            here,
            dim,
            lambda element, dim: out[layout.rows(element), columns(dim)],
            table(layout, masks),
            sent,
        )


def last_kernel(layout, dims, value, *refs):
    messages, refs = taken(layout, dims, refs)
    masks, keeps = refs[:2]
    out, ready, left = refs[-3:]
    copies = []
    for place, dim in enumerate(dims):

        def emit(element, result):
            ready[layout.rows(element), place * WIDTH : (place + 1) * WIDTH] = result

        assemble(
            layout,
            places(),
            dim,
            lambda element, dim: value[layout.rows(element), columns(dim)],
            messages,
            table(layout, masks),
            table(layout, keeps),
            emit,
        )
        copy = pltpu.make_async_copy(
            ready.at[:, place * WIDTH : (place + 1) * WIDTH],
            out.at[:, columns(dim)],
            left.at[place],
        )
        copy.start()
        copies.append(copy)
    for copy in copies:
        copy.wait()


def in_vmem(count):
    return [pl.BlockSpec(memory_space=pltpu.VMEM)] * count


def in_hbm(count):
    return [pl.BlockSpec(memory_space=pltpu.HBM)] * count


PARAMS = pltpu.CompilerParams(vmem_limit_bytes=VMEM_LIMIT)


def kept_in_hbm(*values):
    return [pltpu.with_memory_space_constraint(value, pltpu.HBM) for value in values]


def cost(flops, size):
    return pl.CostEstimate(flops=flops, bytes_accessed=size, transcendentals=0)


def exchange(layout, messages):
    results = {}
    for (dim, parity), message in zip(layout.turns(), messages):
        size = layout.sizes[dim]
        partner = list(range(size))
        for lower in range(parity, size - 1, 2):
            partner[lower], partner[lower + 1] = lower + 1, lower
        if size > 2 and size % 2 == 0 and parity == 1:
            partner[0], partner[-1] = size - 1, 0
        results[dim, parity] = lax.ppermute(message, AXES[dim], list(enumerate(partner)))
    return results


def body(
    load_raw,
    scaling,
    fine_matrix,
    fine_inverse,
    prolong_four,
    coarse_four,
    prolong_two,
    coarse_two,
    orient,
    boundary,
):
    counts, species, nodes = load_raw.shape[:3], load_raw.shape[3], load_raw.shape[4]
    layout = Layout(counts, species, tuple(lax.axis_size(axis) for axis in AXES))
    load = load_raw.reshape(-1, nodes)
    rows = load.shape[0]
    turns = layout.turns()
    message_shapes = tuple(layout.message(dim) for dim, _ in turns)
    whole = jax.ShapeDtypeStruct(load.shape, jnp.float32)
    matrix_shapes = tuple(
        jax.ShapeDtypeStruct((3 * WIDTH * len(dims), nodes), jnp.bfloat16) for dims in (EARLY, LATE)
    )
    elements = len(layout.elements())

    sent = pl.pallas_call(
        functools.partial(first_kernel, layout),
        out_shape=message_shapes,
        in_specs=in_hbm(2),
        out_specs=tuple(in_vmem(len(turns))),
        scratch_shapes=[
            pltpu.VMEM(load.shape, jnp.float32),
            pltpu.SMEM(orient.shape, jnp.int32),
            pltpu.SemaphoreType.DMA((4,)),
        ],
        compiler_params=PARAMS,
        name="pack",
    )(*kept_in_hbm(load, orient))

    sources = (orient, jnp.transpose(boundary, (1, 2, 3, 0)), fine_matrix, fine_inverse)
    sources += (prolong_four.T, coarse_four, prolong_two.T, coarse_two)
    *matrices, masks, keeps = pl.pallas_call(
        functools.partial(prepare_kernel, layout),
        out_shape=matrix_shapes
        + matrix_shapes
        + (
            jax.ShapeDtypeStruct((elements, nodes), jnp.int32),
            jax.ShapeDtypeStruct((elements, nodes), jnp.float32),
        ),
        in_specs=in_hbm(8),
        out_specs=tuple(in_vmem(6)),
        scratch_shapes=[pltpu.SMEM(source.shape, source.dtype) for source in sources[:2]]
        + [pltpu.VMEM(source.shape, source.dtype) for source in sources[2:]]
        + [pltpu.SemaphoreType.DMA((8,))],
        compiler_params=PARAMS,
        cost_estimate=cost(2 * nodes * nodes * nodes, 8 * nodes * nodes),
        name="prepare",
    )(*kept_in_hbm(*sources))
    operator, smoother = matrices[:2], matrices[2:]

    def stage(kind, value, messages, matrix, other):
        early = [messages[turn] for turn in layout.turns(EARLY)]
        late = [messages[turn] for turn in layout.turns(LATE)]
        extra = () if other is None else (other,)
        begun = pl.pallas_call(
            functools.partial(early_kernel, layout, kind),
            out_shape=whole,
            in_specs=in_vmem(5 + len(early)),
            out_specs=in_vmem(1)[0],
            scratch_shapes=[pltpu.VMEM((rows, matrix[0].shape[0]), jnp.bfloat16)],
            compiler_params=PARAMS,
            cost_estimate=cost(2 * rows * matrix[0].shape[0] * nodes, 8 * rows * nodes),
            name=kind + "_early",
        )(value, *early, masks, keeps, scaling, matrix[0])
        results = pl.pallas_call(
            functools.partial(late_kernel, layout, kind),
            out_shape=(whole,) + message_shapes,
            in_specs=in_vmem(6 + len(late) + len(extra)),
            out_specs=tuple(in_vmem(1 + len(turns))),
            scratch_shapes=[
                pltpu.VMEM((rows, matrix[1].shape[0]), jnp.bfloat16),
                pltpu.VMEM(load.shape, jnp.float32),
            ],
            compiler_params=PARAMS,
            cost_estimate=cost(2 * rows * matrix[1].shape[0] * nodes, 12 * rows * nodes),
            name=kind + "_late",
        )(value, *late, masks, keeps, scaling, matrix[1], begun, *extra)
        return results[0], results[1:]

    first, sent = stage("smooth", load, exchange(layout, sent), smoother, None)
    left, sent = stage("operator", first, exchange(layout, sent), operator, load)
    total, sent = stage("smooth_more", left, exchange(layout, sent), smoother, first)
    messages = exchange(layout, sent)
    result = None
    for dims in (EARLY, LATE):
        mine = [messages[turn] for turn in layout.turns(dims)]
        begun = () if result is None else (result,)
        result = pl.pallas_call(
            functools.partial(last_kernel, layout, dims),
            out_shape=whole,
            in_specs=in_vmem(3 + len(mine)) + in_hbm(len(begun)),
            out_specs=in_hbm(1)[0],
            input_output_aliases={3 + len(mine): 0} if begun else {},
            scratch_shapes=[
                pltpu.VMEM((rows, len(dims) * WIDTH), jnp.float32),
                pltpu.SemaphoreType.DMA((len(dims),)),
            ],
            compiler_params=PARAMS,
            cost_estimate=cost(0, 12 * rows * len(dims) * WIDTH),
            name="last_early" if dims == EARLY else "last_late",
        )(total, *mine, masks, keeps, *begun)
    return result.reshape(load_raw.shape)


def solution(mesh):
    in_specs = (
        P("ex", "ey", "ez", None, None),
        P("ex", "ey", "ez", None),
        P(),
        P(),
        P(),
        P(),
        P(),
        P(),
        P(None, "ex", "ey", "ez"),
        P(None, "ex", "ey", "ez"),
    )
    out_specs = P("ex", "ey", "ez", None, None)
    return jax.shard_map(body, mesh=mesh, in_specs=in_specs, out_specs=out_specs, check_vma=False)
```

```python
import functools

import jax
import jax.numpy as jnp
from jax import lax
from jax.experimental import pallas as pl
from jax.experimental.pallas import tpu as pltpu
import numpy as np
from jax.sharding import PartitionSpec as P

FACE_SIDE = 8
FACE = FACE_SIDE * FACE_SIDE
WIDTH = 2 * FACE
AXES = ("ex", "ey", "ez")
EARLY = (0, 1)
LATE = (2,)
VMEM_LIMIT = 24 * 1024 * 1024


class Layout:
    def __init__(self, counts, species, sizes):
        self.counts = counts
        self.species = species
        self.sizes = sizes

    def elements(self):
        spans = [range(count) for count in self.counts]
        return [(i, j, k) for i in spans[0] for j in spans[1] for k in spans[2]]

    def number(self, element):
        return (element[0] * self.counts[1] + element[1]) * self.counts[2] + element[2]

    def rows(self, element):
        start = self.number(element) * self.species
        return slice(start, start + self.species)

    def layer(self, dim, position):
        return [element for element in self.elements() if element[dim] == position]

    def pairs(self, dim):
        return (len(self.layer(dim, 0)) + 1) // 2

    def pair_rows(self, pair):
        return slice(pair * self.species, (pair + 1) * self.species)

    def turns(self, dims=EARLY + LATE):
        order = [(0, 1), (0, 0), (1, 1), (1, 0), (2, 1), (2, 0)]
        return [
            (dim, parity) for dim, parity in order if self.sizes[dim] > 1 + parity and dim in dims
        ]

    def message(self, dim):
        return jax.ShapeDtypeStruct((self.pairs(dim) * self.species, WIDTH), jnp.float32)


def columns(dim):
    return slice(dim * WIDTH, (dim + 1) * WIDTH)


def lanes(layout):
    return lax.broadcasted_iota(jnp.int32, (layout.species, WIDTH), 1)


def picked(value, index):
    return jnp.take_along_axis(value, index, axis=1, mode="promise_in_bounds")


def flip_mask(code):
    reach = FACE_SIDE - 1
    return (code & 1) * (reach * FACE_SIDE) + (code >> 1) * reach


def places():
    return [lax.axis_index(axis) for axis in AXES]


def pack(layout, here, dim, load_block, mask_of, outs):
    turns = [(turn, out) for turn, out in zip(layout.turns(), outs) if turn[0] == dim]
    if not turns:
        return
    lane = lanes(layout)
    low = lane < FACE
    even = (here[dim] & 1) == 0
    first = layout.layer(dim, 0)
    last = layout.layer(dim, layout.counts[dim] - 1)
    for pair in range(layout.pairs(dim)):
        sides = []
        for half in range(2):
            where = min(2 * pair + half, len(first) - 1)
            upper = load_block(last[where], dim)
            lower = load_block(first[where], dim)
            lower = picked(lower, lane ^ mask_of(first[where], dim) ^ (half * FACE))
            if half == 0:
                upper = pltpu.roll(upper, FACE, 1)
            sides.append((upper, lower))
        up = jnp.where(low, sides[0][0], sides[1][0])
        down = jnp.where(low, sides[0][1], sides[1][1])
        for (_, parity), out in turns:
            is_lower = even if parity == 0 else jnp.logical_not(even)
            out[layout.pair_rows(pair), :] = jnp.where(is_lower, up, down)


def received(layout, here, dim, messages):
    even = (here[dim] & 1) == 0
    at_start = here[dim] == 0
    at_end = here[dim] == layout.sizes[dim] - 1
    zero = jnp.zeros((layout.species, WIDTH), jnp.float32)
    found = []
    for pair in range(layout.pairs(dim)):
        first, second = [
            messages[dim, parity][layout.pair_rows(pair), :] if (dim, parity) in messages else zero
            for parity in range(2)
        ]
        below = jnp.where(at_start, 0.0, jnp.where(even, second, first))
        above = jnp.where(at_end, 0.0, jnp.where(even, first, second))
        found.append((below, above))
    return found


def assemble(layout, here, dim, load_block, messages, mask_of, keep_of, emit):
    lane = lanes(layout)
    low = lane < FACE
    count = layout.counts[dim]
    outside = received(layout, here, dim, messages)
    for where, start in enumerate(layout.layer(dim, 0)):
        line = [start[:dim] + (step,) + start[dim + 1 :] for step in range(count)]
        blocks = [load_block(element, dim) for element in line]
        half = (where % 2) * FACE
        below, above = outside[where // 2]
        turned = []
        for step, element in enumerate(line):
            index = lane ^ mask_of(element, dim)
            if step == 0:
                turned.append(picked(below, index ^ half))
            else:
                shared = jnp.where(low, blocks[step], blocks[step - 1])
                turned.append(picked(shared, index ^ FACE))
        turned.append(pltpu.roll(above, FACE, 1) if half == 0 else above)
        for step, element in enumerate(line):
            value = blocks[step] + jnp.where(low, turned[step], turned[step + 1])
            if step in (0, count - 1):
                value = value * keep_of(element, dim)
            emit(element, value)


def halves(value):
    high = value.astype(jnp.bfloat16)
    return high, (value - high.astype(jnp.float32)).astype(jnp.bfloat16)


def dot(left, right, contract=((1,), (0,))):
    return lax.dot_general(left, right, (contract, ((), ())), preferred_element_type=jnp.float32)


def split_dot(left, right, contract):
    left_high, left_rest = halves(left)
    right_high, right_rest = halves(right)
    return (
        dot(left_high, right_high, contract)
        + dot(left_high, right_rest, contract)
        + dot(left_rest, right_high, contract)
    )


def stacked(value, early, late):
    high, rest = halves(value)
    cut = WIDTH * len(EARLY)
    for out, rows in ((early, slice(0, cut)), (late, slice(cut, None))):
        size = out.shape[0] // 3
        for part, piece in enumerate((high, rest, high)):
            out[part * size : (part + 1) * size, :] = piece[rows, :]


def operator_kernel(fine, early, late):
    stacked(fine[...], early, late)


def smoother_kernel(layout, *refs):
    sources, (early, late, masks, keeps), refs = refs[:7], refs[7:11], refs[11:]
    staged, (right, left, arrived) = refs[:7], refs[7:]
    copies = [
        pltpu.make_async_copy(source, stage, arrived.at[number])
        for number, (source, stage) in enumerate(zip(sources, staged))
    ]
    for copy in copies:
        copy.start()
    right[...] = jnp.zeros_like(right)
    left[...] = jnp.zeros_like(left)
    low = lax.broadcasted_iota(jnp.int32, (1, WIDTH), 1) < FACE
    here = places()
    for copy in copies[:2]:
        copy.wait()
    orient, boundary, four, coarse_four, two, coarse_two, inverse = staged
    for element in layout.elements():
        number = layout.number(element)
        for dim in range(3):
            mask = flip_mask(orient[(dim,) + element])
            masks[number : number + 1, columns(dim)] = jnp.full((1, WIDTH), mask, jnp.int32)
            at_start = (here[dim] == 0) & (element[dim] == 0)
            at_end = (here[dim] == layout.sizes[dim] - 1) & (element[dim] == layout.counts[dim] - 1)
            fixed_low = jnp.where(at_start, boundary[element + (2 * dim,)], 0)
            fixed_top = jnp.where(at_end, boundary[element + (2 * dim + 1,)], 0)
            fixed = jnp.where(low, fixed_low, fixed_top)
            keeps[number : number + 1, columns(dim)] = 1.0 - fixed.astype(jnp.float32)
    for copy in copies[2:6]:
        copy.wait()
    start = 0
    for prolong, coarse in ((four, coarse_four), (two, coarse_two)):
        rows = slice(start, start + prolong.shape[0])
        left[rows, :] = prolong[...]
        right[rows, :] = split_dot(coarse[...], prolong[...], ((1,), (0,)))
        start += rounded(prolong.shape[0])
    corrections = split_dot(left[...], right[...], ((0,), (0,)))
    copies[6].wait()
    stacked(0.5 * (inverse[...] + corrections), early, late)


def rounded(count):
    return (count + 7) // 8 * 8


def first_kernel(layout, load, orient, *refs):
    turns = len(layout.turns())
    outs, (staged, codes, arrived) = refs[:turns], refs[turns:]
    copies = [
        pltpu.make_async_copy(load.at[:, columns(dim)], staged.at[:, columns(dim)], arrived.at[dim])
        for dim in range(3)
    ]
    code_copy = pltpu.make_async_copy(orient, codes, arrived.at[3])
    code_copy.start()
    for copy in copies:
        copy.start()
    here = places()
    code_copy.wait()
    for dim in range(3):
        copies[dim].wait()
        pack(
            layout,
            here,
            dim,
            lambda element, dim: staged[layout.rows(element), columns(dim)],
            lambda element, dim: flip_mask(codes[(dim,) + element]),
            outs,
        )


def table(layout, ref):
    def row(element, dim):
        number = layout.number(element)
        return ref[number : number + 1, columns(dim)]

    return row


def scales(layout, kind, ref):
    def row(element, dim):
        value = ref[element[0], element[1], element[2] : element[2] + 1, columns(dim)]
        return value if kind == "operator" else 1.0 / value

    return row


def scaled_product(layout, kind, dims, here, value, messages, masks, keeps, scaling, matrix, split):
    factor = scales(layout, kind, scaling)
    size = len(dims) * WIDTH
    for place, dim in enumerate(dims):

        def emit(element, result):
            high, rest = halves(result * factor(element, dim))
            for part, piece in enumerate((high, high, rest)):
                start = part * size + place * WIDTH
                split[layout.rows(element), start : start + WIDTH] = piece

        assemble(
            layout,
            here,
            dim,
            lambda element, dim: value[layout.rows(element), columns(dim)],
            messages,
            table(layout, masks),
            table(layout, keeps),
            emit,
        )
    return dot(split[...], matrix[...])


def taken(layout, dims, refs):
    turns = layout.turns(dims)
    return dict(zip(turns, refs)), refs[len(turns) :]


def early_kernel(layout, kind, value, *refs):
    messages, refs = taken(layout, EARLY, refs)
    masks, keeps, scaling, matrix, out, split = refs
    out[...] = scaled_product(
        layout, kind, EARLY, places(), value, messages, masks, keeps, scaling, matrix, split
    )


def late_kernel(layout, kind, value, *refs):
    messages, refs = taken(layout, LATE, refs)
    masks, keeps, scaling, matrix, begun, refs = *refs[:5], refs[5:]
    other = None
    if kind != "smooth":
        other, refs = refs[0], refs[1:]
    turns = len(layout.turns())
    out, sent, (split, summed) = refs[0], refs[1 : 1 + turns], refs[1 + turns :]
    here = places()
    summed[...] = begun[...] + scaled_product(
        layout, kind, LATE, here, value, messages, masks, keeps, scaling, matrix, split
    )
    factor = scales(layout, kind, scaling)
    for dim in range(3):
        for element in layout.elements():
            at = (layout.rows(element), columns(dim))
            result = summed[at] * factor(element, dim)
            if kind == "operator":
                result = other[at] - result
            elif kind == "smooth_more":
                result = other[at] + result
            out[at] = result
        pack(
            layout,
            here,
            dim,
            lambda element, dim: out[layout.rows(element), columns(dim)],
            table(layout, masks),
            sent,
        )


def assembled_strips(layout, dims, value, messages, masks, keeps, ready):
    for place, dim in enumerate(dims):

        def emit(element, result):
            ready[layout.rows(element), place * WIDTH : (place + 1) * WIDTH] = result

        assemble(
            layout,
            places(),
            dim,
            lambda element, dim: value[layout.rows(element), columns(dim)],
            messages,
            table(layout, masks),
            table(layout, keeps),
            emit,
        )


def last_early_kernel(layout, value, *refs):
    messages, (masks, keeps, ready) = taken(layout, EARLY, refs)
    assembled_strips(layout, EARLY, value, messages, masks, keeps, ready)


def last_late_kernel(layout, begun, value, *refs):
    messages, (masks, keeps, out, ready, left) = taken(layout, LATE, refs)
    cut = begun.shape[1]
    first = pltpu.make_async_copy(begun, out.at[:, :cut], left.at[0])
    first.start()
    assembled_strips(layout, LATE, value, messages, masks, keeps, ready)
    second = pltpu.make_async_copy(ready, out.at[:, cut:], left.at[1])
    second.start()
    first.wait()
    second.wait()


def in_vmem(count):
    return [pl.BlockSpec(memory_space=pltpu.VMEM)] * count


def in_hbm(count):
    return [pl.BlockSpec(memory_space=pltpu.HBM)] * count


PARAMS = pltpu.CompilerParams(vmem_limit_bytes=VMEM_LIMIT)


def kept_in_hbm(*values):
    return [pltpu.with_memory_space_constraint(value, pltpu.HBM) for value in values]


def cost(flops, size):
    return pl.CostEstimate(flops=flops, bytes_accessed=size, transcendentals=0)


def partners(layout, dim, parity):
    sizes = layout.sizes
    swap = {}
    for place in np.ndindex(*sizes):
        other = list(place)
        lower = place[dim] % 2 == parity
        at = place[dim] + (1 if lower else -1)
        if 0 <= at < sizes[dim]:
            other[dim] = at
        elif dim != 1 and sizes[1] % 2 == 0:
            other[1] = place[1] ^ 1
        elif sizes[dim] % 2 == 0:
            other[dim] = sizes[dim] - 1 - place[dim]
        swap[place] = tuple(other)
    return [
        (int(np.ravel_multi_index(place, sizes)), int(np.ravel_multi_index(other, sizes)))
        for place, other in swap.items()
    ]


def exchange(layout, messages):
    return {
        turn: lax.ppermute(message, AXES, partners(layout, *turn))
        for turn, message in zip(layout.turns(), messages)
    }


def body(
    load_raw,
    scaling,
    fine_matrix,
    fine_inverse,
    prolong_four,
    coarse_four,
    prolong_two,
    coarse_two,
    orient,
    boundary,
):
    counts, species, nodes = load_raw.shape[:3], load_raw.shape[3], load_raw.shape[4]
    layout = Layout(counts, species, tuple(lax.axis_size(axis) for axis in AXES))
    load = load_raw.reshape(-1, nodes)
    rows = load.shape[0]
    turns = layout.turns()
    message_shapes = tuple(layout.message(dim) for dim, _ in turns)
    whole = jax.ShapeDtypeStruct(load.shape, jnp.float32)
    matrix_shapes = tuple(
        jax.ShapeDtypeStruct((3 * WIDTH * len(dims), nodes), jnp.bfloat16) for dims in (EARLY, LATE)
    )
    elements = len(layout.elements())

    sent = pl.pallas_call(
        functools.partial(first_kernel, layout),
        out_shape=message_shapes,
        in_specs=in_hbm(2),
        out_specs=tuple(in_vmem(len(turns))),
        scratch_shapes=[
            pltpu.VMEM(load.shape, jnp.float32),
            pltpu.SMEM(orient.shape, jnp.int32),
            pltpu.SemaphoreType.DMA((4,)),
        ],
        compiler_params=PARAMS,
        name="pack",
    )(*kept_in_hbm(load, orient))

    sources = (orient, jnp.transpose(boundary, (1, 2, 3, 0)))
    sources += (prolong_four.T, coarse_four, prolong_two.T, coarse_two, fine_inverse)
    stack = (rounded(prolong_four.shape[1]) + rounded(prolong_two.shape[1]), nodes)
    *smoother, masks, keeps = pl.pallas_call(
        functools.partial(smoother_kernel, layout),
        out_shape=matrix_shapes
        + (
            jax.ShapeDtypeStruct((elements, nodes), jnp.int32),
            jax.ShapeDtypeStruct((elements, nodes), jnp.float32),
        ),
        in_specs=in_hbm(7),
        out_specs=tuple(in_vmem(4)),
        scratch_shapes=[pltpu.SMEM(source.shape, source.dtype) for source in sources[:2]]
        + [pltpu.VMEM(source.shape, source.dtype) for source in sources[2:]]
        + [pltpu.VMEM(stack, jnp.float32), pltpu.VMEM(stack, jnp.float32)]
        + [pltpu.SemaphoreType.DMA((7,))],
        compiler_params=PARAMS,
        cost_estimate=cost(2 * nodes * nodes * nodes, 8 * nodes * nodes),
        name="smoother",
    )(*kept_in_hbm(*sources))
    operator = pl.pallas_call(
        operator_kernel,
        out_shape=matrix_shapes,
        in_specs=in_vmem(1),
        out_specs=tuple(in_vmem(2)),
        compiler_params=PARAMS,
        cost_estimate=cost(0, 10 * nodes * nodes),
        name="operator",
    )(fine_matrix)

    def stage(kind, value, messages, matrix, other):
        early = [messages[turn] for turn in layout.turns(EARLY)]
        late = [messages[turn] for turn in layout.turns(LATE)]
        extra = () if other is None else (other,)
        begun = pl.pallas_call(
            functools.partial(early_kernel, layout, kind),
            out_shape=whole,
            in_specs=in_vmem(5 + len(early)),
            out_specs=in_vmem(1)[0],
            scratch_shapes=[pltpu.VMEM((rows, matrix[0].shape[0]), jnp.bfloat16)],
            compiler_params=PARAMS,
            cost_estimate=cost(2 * rows * matrix[0].shape[0] * nodes, 8 * rows * nodes),
            name=kind + "_early",
        )(value, *early, masks, keeps, scaling, matrix[0])
        results = pl.pallas_call(
            functools.partial(late_kernel, layout, kind),
            out_shape=(whole,) + message_shapes,
            in_specs=in_vmem(6 + len(late) + len(extra)),
            out_specs=tuple(in_vmem(1 + len(turns))),
            scratch_shapes=[
                pltpu.VMEM((rows, matrix[1].shape[0]), jnp.bfloat16),
                pltpu.VMEM(load.shape, jnp.float32),
            ],
            compiler_params=PARAMS,
            cost_estimate=cost(2 * rows * matrix[1].shape[0] * nodes, 12 * rows * nodes),
            name=kind + "_late",
        )(value, *late, masks, keeps, scaling, matrix[1], begun, *extra)
        return results[0], results[1:]

    first, sent = stage("smooth", load, exchange(layout, sent), smoother, None)
    left, sent = stage("operator", first, exchange(layout, sent), operator, load)
    total, sent = stage("smooth_more", left, exchange(layout, sent), smoother, first)
    messages = exchange(layout, sent)
    early = [messages[turn] for turn in layout.turns(EARLY)]
    late = [messages[turn] for turn in layout.turns(LATE)]
    cut = len(EARLY) * WIDTH
    begun = pl.pallas_call(
        functools.partial(last_early_kernel, layout),
        out_shape=jax.ShapeDtypeStruct((rows, cut), jnp.float32),
        in_specs=in_vmem(3 + len(early)),
        out_specs=in_vmem(1)[0],
        compiler_params=PARAMS,
        cost_estimate=cost(0, 8 * rows * cut),
        name="last_early",
    )(total, *early, masks, keeps)
    result = pl.pallas_call(
        functools.partial(last_late_kernel, layout),
        out_shape=whole,
        in_specs=in_vmem(4 + len(late)),
        out_specs=in_hbm(1)[0],
        scratch_shapes=[
            pltpu.VMEM((rows, nodes - cut), jnp.float32),
            pltpu.SemaphoreType.DMA((2,)),
        ],
        compiler_params=PARAMS,
        cost_estimate=cost(0, 8 * rows * nodes),
        name="last_late",
    )(begun, total, *late, masks, keeps)
    return result.reshape(load_raw.shape)


def solution(mesh):
    in_specs = (
        P("ex", "ey", "ez", None, None),
        P("ex", "ey", "ez", None),
        P(),
        P(),
        P(),
        P(),
        P(),
        P(),
        P(None, "ex", "ey", "ez"),
        P(None, "ex", "ey", "ez"),
    )
    out_specs = P("ex", "ey", "ez", None, None)
    return jax.shard_map(body, mesh=mesh, in_specs=in_specs, out_specs=out_specs, check_vma=False)
```

```python
import functools

import jax
import jax.numpy as jnp
from jax import lax
from jax.experimental import pallas as pl
from jax.experimental.pallas import tpu as pltpu
import numpy as np
from jax.sharding import PartitionSpec as P

FACE_SIDE = 8
FACE = FACE_SIDE * FACE_SIDE
WIDTH = 2 * FACE
AXES = ("ex", "ey", "ez")
EARLY = (0, 1)
LATE = (2,)
VMEM_LIMIT = 24 * 1024 * 1024


class Layout:
    def __init__(self, counts, species, sizes):
        self.counts = counts
        self.species = species
        self.sizes = sizes

    def elements(self):
        spans = [range(count) for count in self.counts]
        return [(i, j, k) for i in spans[0] for j in spans[1] for k in spans[2]]

    def number(self, element):
        return (element[0] * self.counts[1] + element[1]) * self.counts[2] + element[2]

    def rows(self, element):
        start = self.number(element) * self.species
        return slice(start, start + self.species)

    def layer(self, dim, position):
        return [element for element in self.elements() if element[dim] == position]

    def pairs(self, dim):
        return (len(self.layer(dim, 0)) + 1) // 2

    def pair_rows(self, pair):
        return slice(pair * self.species, (pair + 1) * self.species)

    def turns(self, dims=EARLY + LATE):
        order = [(0, 1), (0, 0), (1, 1), (1, 0), (2, 1), (2, 0)]
        return [
            (dim, parity) for dim, parity in order if self.sizes[dim] > 1 + parity and dim in dims
        ]

    def message(self, dim):
        return jax.ShapeDtypeStruct((self.pairs(dim) * self.species, WIDTH), jnp.float32)


def columns(dim):
    return slice(dim * WIDTH, (dim + 1) * WIDTH)


def lanes(layout):
    return lax.broadcasted_iota(jnp.int32, (layout.species, WIDTH), 1)


def picked(value, index):
    return jnp.take_along_axis(value, index, axis=1, mode="promise_in_bounds")


def flip_mask(code):
    reach = FACE_SIDE - 1
    return (code & 1) * (reach * FACE_SIDE) + (code >> 1) * reach


def places():
    return [lax.axis_index(axis) for axis in AXES]


def pack(layout, here, dim, load_block, mask_of, outs):
    turns = [(turn, out) for turn, out in zip(layout.turns(), outs) if turn[0] == dim]
    if not turns:
        return
    lane = lanes(layout)
    low = lane < FACE
    even = (here[dim] & 1) == 0
    first = layout.layer(dim, 0)
    last = layout.layer(dim, layout.counts[dim] - 1)
    for pair in range(layout.pairs(dim)):
        sides = []
        for half in range(2):
            where = min(2 * pair + half, len(first) - 1)
            upper = load_block(last[where], dim)
            lower = load_block(first[where], dim)
            lower = picked(lower, lane ^ mask_of(first[where], dim) ^ (half * FACE))
            if half == 0:
                upper = pltpu.roll(upper, FACE, 1)
            sides.append((upper, lower))
        up = jnp.where(low, sides[0][0], sides[1][0])
        down = jnp.where(low, sides[0][1], sides[1][1])
        for (_, parity), out in turns:
            is_lower = even if parity == 0 else jnp.logical_not(even)
            out[layout.pair_rows(pair), :] = jnp.where(is_lower, up, down)


def message_part(layout, dim, message, pair, even):
    rows = layout.pair_rows(pair)
    if layout.sizes[dim] != 2:
        return message[rows, :]
    size = layout.message(dim).shape[0]
    return jnp.where(even, message[size + rows.start : size + rows.stop, :], message[rows, :])


def received(layout, here, dim, messages):
    even = (here[dim] & 1) == 0
    at_start = here[dim] == 0
    at_end = here[dim] == layout.sizes[dim] - 1
    zero = jnp.zeros((layout.species, WIDTH), jnp.float32)
    found = []
    for pair in range(layout.pairs(dim)):
        first, second = [
            message_part(layout, dim, messages[dim, parity], pair, even)
            if (dim, parity) in messages
            else zero
            for parity in range(2)
        ]
        below = jnp.where(at_start, 0.0, jnp.where(even, second, first))
        above = jnp.where(at_end, 0.0, jnp.where(even, first, second))
        found.append((below, above))
    return found


def assemble(layout, here, dim, load_block, messages, mask_of, keep_of, emit):
    lane = lanes(layout)
    low = lane < FACE
    count = layout.counts[dim]
    outside = received(layout, here, dim, messages)
    for where, start in enumerate(layout.layer(dim, 0)):
        line = [start[:dim] + (step,) + start[dim + 1 :] for step in range(count)]
        blocks = [load_block(element, dim) for element in line]
        half = (where % 2) * FACE
        below, above = outside[where // 2]
        turned = []
        for step, element in enumerate(line):
            index = lane ^ mask_of(element, dim)
            if step == 0:
                turned.append(picked(below, index ^ half))
            else:
                shared = jnp.where(low, blocks[step], blocks[step - 1])
                turned.append(picked(shared, index ^ FACE))
        turned.append(pltpu.roll(above, FACE, 1) if half == 0 else above)
        for step, element in enumerate(line):
            value = blocks[step] + jnp.where(low, turned[step], turned[step + 1])
            if step in (0, count - 1):
                value = value * keep_of(element, dim)
            emit(element, value)


def halves(value):
    high = value.astype(jnp.bfloat16)
    return high, (value - high.astype(jnp.float32)).astype(jnp.bfloat16)


def dot(left, right, contract=((1,), (0,))):
    return lax.dot_general(left, right, (contract, ((), ())), preferred_element_type=jnp.float32)


def split_dot(left, right, contract):
    left_high, left_rest = halves(left)
    right_high, right_rest = halves(right)
    return (
        dot(left_high, right_high, contract)
        + dot(left_high, right_rest, contract)
        + dot(left_rest, right_high, contract)
    )


def stacked(value, early, late):
    high, rest = halves(value)
    cut = WIDTH * len(EARLY)
    for out, rows in ((early, slice(0, cut)), (late, slice(cut, None))):
        size = out.shape[0] // 3
        for part, piece in enumerate((high, rest, high)):
            out[part * size : (part + 1) * size, :] = piece[rows, :]


def operator_kernel(fine, early, late):
    stacked(fine[...], early, late)


def smoother_kernel(layout, *refs):
    sources, (early, late, masks, keeps), refs = refs[:7], refs[7:11], refs[11:]
    staged, (right, left, arrived) = refs[:7], refs[7:]
    copies = [
        pltpu.make_async_copy(source, stage, arrived.at[number])
        for number, (source, stage) in enumerate(zip(sources, staged))
    ]
    for copy in copies:
        copy.start()
    right[...] = jnp.zeros_like(right)
    left[...] = jnp.zeros_like(left)
    low = lax.broadcasted_iota(jnp.int32, (1, WIDTH), 1) < FACE
    here = places()
    for copy in copies[:2]:
        copy.wait()
    orient, boundary, four, coarse_four, two, coarse_two, inverse = staged
    for element in layout.elements():
        number = layout.number(element)
        for dim in range(3):
            mask = flip_mask(orient[(dim,) + element])
            masks[number : number + 1, columns(dim)] = jnp.full((1, WIDTH), mask, jnp.int32)
            at_start = (here[dim] == 0) & (element[dim] == 0)
            at_end = (here[dim] == layout.sizes[dim] - 1) & (element[dim] == layout.counts[dim] - 1)
            fixed_low = jnp.where(at_start, boundary[element + (2 * dim,)], 0)
            fixed_top = jnp.where(at_end, boundary[element + (2 * dim + 1,)], 0)
            fixed = jnp.where(low, fixed_low, fixed_top)
            keeps[number : number + 1, columns(dim)] = 1.0 - fixed.astype(jnp.float32)
    for copy in copies[2:6]:
        copy.wait()
    start = 0
    for prolong, coarse in ((four, coarse_four), (two, coarse_two)):
        rows = slice(start, start + prolong.shape[0])
        left[rows, :] = prolong[...]
        right[rows, :] = split_dot(coarse[...], prolong[...], ((1,), (0,)))
        start += rounded(prolong.shape[0])
    corrections = split_dot(left[...], right[...], ((0,), (0,)))
    copies[6].wait()
    stacked(0.5 * (inverse[...] + corrections), early, late)


def rounded(count):
    return (count + 7) // 8 * 8


def first_kernel(layout, load, orient, *refs):
    turns = len(layout.turns())
    outs, (staged, codes, arrived) = refs[:turns], refs[turns:]
    copies = [
        pltpu.make_async_copy(load.at[:, columns(dim)], staged.at[:, columns(dim)], arrived.at[dim])
        for dim in range(3)
    ]
    code_copy = pltpu.make_async_copy(orient, codes, arrived.at[3])
    code_copy.start()
    for copy in copies:
        copy.start()
    here = places()
    code_copy.wait()
    for dim in range(3):
        copies[dim].wait()
        pack(
            layout,
            here,
            dim,
            lambda element, dim: staged[layout.rows(element), columns(dim)],
            lambda element, dim: flip_mask(codes[(dim,) + element]),
            outs,
        )


def table(layout, ref):
    def row(element, dim):
        number = layout.number(element)
        return ref[number : number + 1, columns(dim)]

    return row


def scales(layout, kind, ref):
    def row(element, dim):
        value = ref[element[0], element[1], element[2] : element[2] + 1, columns(dim)]
        return value if kind == "operator" else 1.0 / value

    return row


def scaled_product(layout, kind, dims, here, value, messages, masks, keeps, scaling, matrix, split):
    factor = scales(layout, kind, scaling)
    size = len(dims) * WIDTH
    for place, dim in enumerate(dims):

        def emit(element, result):
            high, rest = halves(result * factor(element, dim))
            for part, piece in enumerate((high, high, rest)):
                start = part * size + place * WIDTH
                split[layout.rows(element), start : start + WIDTH] = piece

        assemble(
            layout,
            here,
            dim,
            lambda element, dim: value[layout.rows(element), columns(dim)],
            messages,
            table(layout, masks),
            table(layout, keeps),
            emit,
        )
    return dot(split[...], matrix[...])


def taken(layout, dims, refs):
    turns = layout.turns(dims)
    return dict(zip(turns, refs)), refs[len(turns) :]


def early_kernel(layout, kind, value, *refs):
    messages, refs = taken(layout, EARLY, refs)
    masks, keeps, scaling, matrix, out, split = refs
    out[...] = scaled_product(
        layout, kind, EARLY, places(), value, messages, masks, keeps, scaling, matrix, split
    )


def late_kernel(layout, kind, value, *refs):
    messages, refs = taken(layout, LATE, refs)
    masks, keeps, scaling, matrix, begun, refs = *refs[:5], refs[5:]
    other = None
    if kind != "smooth":
        other, refs = refs[0], refs[1:]
    turns = len(layout.turns())
    out, sent, (split, summed) = refs[0], refs[1 : 1 + turns], refs[1 + turns :]
    here = places()
    summed[...] = begun[...] + scaled_product(
        layout, kind, LATE, here, value, messages, masks, keeps, scaling, matrix, split
    )
    factor = scales(layout, kind, scaling)
    for dim in range(3):
        for element in layout.elements():
            at = (layout.rows(element), columns(dim))
            result = summed[at] * factor(element, dim)
            if kind == "operator":
                result = other[at] - result
            elif kind == "smooth_more":
                result = other[at] + result
            out[at] = result
        pack(
            layout,
            here,
            dim,
            lambda element, dim: out[layout.rows(element), columns(dim)],
            table(layout, masks),
            sent,
        )


def assembled_strips(layout, dims, value, messages, masks, keeps, ready):
    for place, dim in enumerate(dims):

        def emit(element, result):
            ready[layout.rows(element), place * WIDTH : (place + 1) * WIDTH] = result

        assemble(
            layout,
            places(),
            dim,
            lambda element, dim: value[layout.rows(element), columns(dim)],
            messages,
            table(layout, masks),
            table(layout, keeps),
            emit,
        )


def last_early_kernel(layout, value, *refs):
    messages, (masks, keeps, ready) = taken(layout, EARLY, refs)
    assembled_strips(layout, EARLY, value, messages, masks, keeps, ready)


def last_late_kernel(layout, begun, value, *refs):
    messages, (masks, keeps, out, ready, left) = taken(layout, LATE, refs)
    cut = begun.shape[1]
    first = pltpu.make_async_copy(begun, out.at[:, :cut], left.at[0])
    first.start()
    assembled_strips(layout, LATE, value, messages, masks, keeps, ready)
    second = pltpu.make_async_copy(ready, out.at[:, cut:], left.at[1])
    second.start()
    first.wait()
    second.wait()


def in_vmem(count):
    return [pl.BlockSpec(memory_space=pltpu.VMEM)] * count


def in_hbm(count):
    return [pl.BlockSpec(memory_space=pltpu.HBM)] * count


PARAMS = pltpu.CompilerParams(vmem_limit_bytes=VMEM_LIMIT)


def kept_in_hbm(*values):
    return [pltpu.with_memory_space_constraint(value, pltpu.HBM) for value in values]


def cost(flops, size):
    return pl.CostEstimate(flops=flops, bytes_accessed=size, transcendentals=0)


def partners(layout, dim, parity):
    sizes = layout.sizes
    swap = {}
    for place in np.ndindex(*sizes):
        other = list(place)
        lower = place[dim] % 2 == parity
        at = place[dim] + (1 if lower else -1)
        if 0 <= at < sizes[dim]:
            other[dim] = at
        elif dim != 1 and sizes[1] % 2 == 0:
            other[1] = place[1] ^ 1
        elif sizes[dim] % 2 == 0:
            other[dim] = sizes[dim] - 1 - place[dim]
        swap[place] = tuple(other)
    return [
        (int(np.ravel_multi_index(place, sizes)), int(np.ravel_multi_index(other, sizes)))
        for place, other in swap.items()
    ]


def exchange(layout, messages):
    results = {}
    for (dim, parity), message in zip(layout.turns(), messages):
        if layout.sizes[dim] == 2:
            result = lax.all_gather(message, AXES[dim], tiled=True)
        else:
            result = lax.ppermute(message, AXES, partners(layout, dim, parity))
        results[dim, parity] = result
    return results


def body(
    load_raw,
    scaling,
    fine_matrix,
    fine_inverse,
    prolong_four,
    coarse_four,
    prolong_two,
    coarse_two,
    orient,
    boundary,
):
    counts, species, nodes = load_raw.shape[:3], load_raw.shape[3], load_raw.shape[4]
    layout = Layout(counts, species, tuple(lax.axis_size(axis) for axis in AXES))
    load = load_raw.reshape(-1, nodes)
    rows = load.shape[0]
    turns = layout.turns()
    message_shapes = tuple(layout.message(dim) for dim, _ in turns)
    whole = jax.ShapeDtypeStruct(load.shape, jnp.float32)
    matrix_shapes = tuple(
        jax.ShapeDtypeStruct((3 * WIDTH * len(dims), nodes), jnp.bfloat16) for dims in (EARLY, LATE)
    )
    elements = len(layout.elements())

    sent = pl.pallas_call(
        functools.partial(first_kernel, layout),
        out_shape=message_shapes,
        in_specs=in_hbm(2),
        out_specs=tuple(in_vmem(len(turns))),
        scratch_shapes=[
            pltpu.VMEM(load.shape, jnp.float32),
            pltpu.SMEM(orient.shape, jnp.int32),
            pltpu.SemaphoreType.DMA((4,)),
        ],
        compiler_params=PARAMS,
        name="pack",
    )(*kept_in_hbm(load, orient))

    sources = (orient, jnp.transpose(boundary, (1, 2, 3, 0)))
    sources += (prolong_four.T, coarse_four, prolong_two.T, coarse_two, fine_inverse)
    stack = (rounded(prolong_four.shape[1]) + rounded(prolong_two.shape[1]), nodes)
    *smoother, masks, keeps = pl.pallas_call(
        functools.partial(smoother_kernel, layout),
        out_shape=matrix_shapes
        + (
            jax.ShapeDtypeStruct((elements, nodes), jnp.int32),
            jax.ShapeDtypeStruct((elements, nodes), jnp.float32),
        ),
        in_specs=in_hbm(7),
        out_specs=tuple(in_vmem(4)),
        scratch_shapes=[pltpu.SMEM(source.shape, source.dtype) for source in sources[:2]]
        + [pltpu.VMEM(source.shape, source.dtype) for source in sources[2:]]
        + [pltpu.VMEM(stack, jnp.float32), pltpu.VMEM(stack, jnp.float32)]
        + [pltpu.SemaphoreType.DMA((7,))],
        compiler_params=PARAMS,
        cost_estimate=cost(2 * nodes * nodes * nodes, 8 * nodes * nodes),
        name="smoother",
    )(*kept_in_hbm(*sources))
    operator = pl.pallas_call(
        operator_kernel,
        out_shape=matrix_shapes,
        in_specs=in_vmem(1),
        out_specs=tuple(in_vmem(2)),
        compiler_params=PARAMS,
        cost_estimate=cost(0, 10 * nodes * nodes),
        name="operator",
    )(fine_matrix)

    def stage(kind, value, messages, matrix, other):
        early = [messages[turn] for turn in layout.turns(EARLY)]
        late = [messages[turn] for turn in layout.turns(LATE)]
        extra = () if other is None else (other,)
        begun = pl.pallas_call(
            functools.partial(early_kernel, layout, kind),
            out_shape=whole,
            in_specs=in_vmem(5 + len(early)),
            out_specs=in_vmem(1)[0],
            scratch_shapes=[pltpu.VMEM((rows, matrix[0].shape[0]), jnp.bfloat16)],
            compiler_params=PARAMS,
            cost_estimate=cost(2 * rows * matrix[0].shape[0] * nodes, 8 * rows * nodes),
            name=kind + "_early",
        )(value, *early, masks, keeps, scaling, matrix[0])
        results = pl.pallas_call(
            functools.partial(late_kernel, layout, kind),
            out_shape=(whole,) + message_shapes,
            in_specs=in_vmem(6 + len(late) + len(extra)),
            out_specs=tuple(in_vmem(1 + len(turns))),
            scratch_shapes=[
                pltpu.VMEM((rows, matrix[1].shape[0]), jnp.bfloat16),
                pltpu.VMEM(load.shape, jnp.float32),
            ],
            compiler_params=PARAMS,
            cost_estimate=cost(2 * rows * matrix[1].shape[0] * nodes, 12 * rows * nodes),
            name=kind + "_late",
        )(value, *late, masks, keeps, scaling, matrix[1], begun, *extra)
        return results[0], results[1:]

    first, sent = stage("smooth", load, exchange(layout, sent), smoother, None)
    left, sent = stage("operator", first, exchange(layout, sent), operator, load)
    total, sent = stage("smooth_more", left, exchange(layout, sent), smoother, first)
    messages = exchange(layout, sent)
    early = [messages[turn] for turn in layout.turns(EARLY)]
    late = [messages[turn] for turn in layout.turns(LATE)]
    cut = len(EARLY) * WIDTH
    begun = pl.pallas_call(
        functools.partial(last_early_kernel, layout),
        out_shape=jax.ShapeDtypeStruct((rows, cut), jnp.float32),
        in_specs=in_vmem(3 + len(early)),
        out_specs=in_vmem(1)[0],
        compiler_params=PARAMS,
        cost_estimate=cost(0, 8 * rows * cut),
        name="last_early",
    )(total, *early, masks, keeps)
    result = pl.pallas_call(
        functools.partial(last_late_kernel, layout),
        out_shape=whole,
        in_specs=in_vmem(4 + len(late)),
        out_specs=in_hbm(1)[0],
        scratch_shapes=[
            pltpu.VMEM((rows, nodes - cut), jnp.float32),
            pltpu.SemaphoreType.DMA((2,)),
        ],
        compiler_params=PARAMS,
        cost_estimate=cost(0, 8 * rows * nodes),
        name="last_late",
    )(begun, total, *late, masks, keeps)
    return result.reshape(load_raw.shape)


def solution(mesh):
    in_specs = (
        P("ex", "ey", "ez", None, None),
        P("ex", "ey", "ez", None),
        P(),
        P(),
        P(),
        P(),
        P(),
        P(),
        P(None, "ex", "ey", "ez"),
        P(None, "ex", "ey", "ez"),
    )
    out_specs = P("ex", "ey", "ez", None, None)
    return jax.shard_map(body, mesh=mesh, in_specs=in_specs, out_specs=out_specs, check_vma=False)
```

```python
import functools

import jax
import jax.numpy as jnp
from jax import lax
from jax.experimental import pallas as pl
from jax.experimental.pallas import tpu as pltpu
import numpy as np
from jax.sharding import PartitionSpec as P

FACE_SIDE = 8
FACE = FACE_SIDE * FACE_SIDE
WIDTH = 2 * FACE
AXES = ("ex", "ey", "ez")
EARLY = (0, 1)
LATE = (2,)
VMEM_LIMIT = 24 * 1024 * 1024


class Layout:
    def __init__(self, counts, species, sizes):
        self.counts = counts
        self.species = species
        self.sizes = sizes

    def elements(self):
        spans = [range(count) for count in self.counts]
        return [(i, j, k) for i in spans[0] for j in spans[1] for k in spans[2]]

    def number(self, element):
        return (element[0] * self.counts[1] + element[1]) * self.counts[2] + element[2]

    def rows(self, element):
        start = self.number(element) * self.species
        return slice(start, start + self.species)

    def layer(self, dim, position):
        return [element for element in self.elements() if element[dim] == position]

    def pairs(self, dim):
        return (len(self.layer(dim, 0)) + 1) // 2

    def pair_rows(self, pair):
        return slice(pair * self.species, (pair + 1) * self.species)

    def turns(self, dims=EARLY + LATE):
        order = [(0, 1), (0, 0), (1, 1), (1, 0), (2, 1), (2, 0)]
        return [
            (dim, parity) for dim, parity in order if self.sizes[dim] > 1 + parity and dim in dims
        ]

    def message(self, dim):
        return jax.ShapeDtypeStruct((self.pairs(dim) * self.species, WIDTH), jnp.float32)


def columns(dim):
    return slice(dim * WIDTH, (dim + 1) * WIDTH)


def lanes(layout):
    return lax.broadcasted_iota(jnp.int32, (layout.species, WIDTH), 1)


def picked(value, index):
    return jnp.take_along_axis(value, index, axis=1, mode="promise_in_bounds")


def flip_mask(code):
    reach = FACE_SIDE - 1
    return (code & 1) * (reach * FACE_SIDE) + (code >> 1) * reach


def places():
    return [lax.axis_index(axis) for axis in AXES]


def pack(layout, here, dim, load_block, mask_of, outs):
    turns = [(turn, out) for turn, out in zip(layout.turns(), outs) if turn[0] == dim]
    if not turns:
        return
    lane = lanes(layout)
    low = lane < FACE
    even = (here[dim] & 1) == 0
    first = layout.layer(dim, 0)
    last = layout.layer(dim, layout.counts[dim] - 1)
    for pair in range(layout.pairs(dim)):
        sides = []
        for half in range(2):
            where = min(2 * pair + half, len(first) - 1)
            upper = load_block(last[where], dim)
            lower = load_block(first[where], dim)
            lower = picked(lower, lane ^ mask_of(first[where], dim) ^ (half * FACE))
            if half == 0:
                upper = pltpu.roll(upper, FACE, 1)
            sides.append((upper, lower))
        up = jnp.where(low, sides[0][0], sides[1][0])
        down = jnp.where(low, sides[0][1], sides[1][1])
        for (_, parity), out in turns:
            is_lower = even if parity == 0 else jnp.logical_not(even)
            out[layout.pair_rows(pair), :] = jnp.where(is_lower, up, down)


def received(layout, here, dim, messages):
    even = (here[dim] & 1) == 0
    at_start = here[dim] == 0
    at_end = here[dim] == layout.sizes[dim] - 1
    zero = jnp.zeros((layout.species, WIDTH), jnp.float32)
    found = []
    for pair in range(layout.pairs(dim)):
        first, second = [
            messages[dim, parity][layout.pair_rows(pair), :] if (dim, parity) in messages else zero
            for parity in range(2)
        ]
        below = jnp.where(at_start, 0.0, jnp.where(even, second, first))
        above = jnp.where(at_end, 0.0, jnp.where(even, first, second))
        found.append((below, above))
    return found


def assemble(layout, here, dim, load_block, messages, mask_of, keep_of, emit, slab=None):
    lane = lanes(layout)
    low = lane < FACE
    count = layout.counts[dim]
    outside = received(layout, here, dim, messages)
    for where, start in enumerate(layout.layer(dim, 0)):
        if slab not in (None, start[0]):
            continue
        line = [start[:dim] + (step,) + start[dim + 1 :] for step in range(count)]
        blocks = [load_block(element, dim) for element in line]
        half = (where % 2) * FACE
        below, above = outside[where // 2]
        turned = []
        for step, element in enumerate(line):
            index = lane ^ mask_of(element, dim)
            if step == 0:
                turned.append(picked(below, index ^ half))
            else:
                shared = jnp.where(low, blocks[step], blocks[step - 1])
                turned.append(picked(shared, index ^ FACE))
        turned.append(pltpu.roll(above, FACE, 1) if half == 0 else above)
        for step, element in enumerate(line):
            value = blocks[step] + jnp.where(low, turned[step], turned[step + 1])
            if step in (0, count - 1):
                value = value * keep_of(element, dim)
            emit(element, value)


def halves(value):
    high = value.astype(jnp.bfloat16)
    return high, (value - high.astype(jnp.float32)).astype(jnp.bfloat16)


def dot(left, right, contract=((1,), (0,))):
    return lax.dot_general(left, right, (contract, ((), ())), preferred_element_type=jnp.float32)


def split_dot(left, right, contract):
    left_high, left_rest = halves(left)
    right_high, right_rest = halves(right)
    return (
        dot(left_high, right_high, contract)
        + dot(left_high, right_rest, contract)
        + dot(left_rest, right_high, contract)
    )


def stacked(value, early, late):
    high, rest = halves(value)
    cut = WIDTH * len(EARLY)
    for out, rows in ((early, slice(0, cut)), (late, slice(cut, None))):
        size = out.shape[0] // 3
        for part, piece in enumerate((high, rest, high)):
            out[part * size : (part + 1) * size, :] = piece[rows, :]


def operator_kernel(fine, early, late):
    stacked(fine[...], early, late)


def smoother_kernel(layout, *refs):
    inverse, *sources = refs[:7]
    (early, late, masks, keeps), refs = refs[7:11], refs[11:]
    staged, (right, left, arrived) = refs[:6], refs[6:]
    copies = [
        pltpu.make_async_copy(source, stage, arrived.at[number])
        for number, (source, stage) in enumerate(zip(sources, staged))
    ]
    for copy in copies:
        copy.start()
    right[...] = jnp.zeros_like(right)
    left[...] = jnp.zeros_like(left)
    low = lax.broadcasted_iota(jnp.int32, (1, WIDTH), 1) < FACE
    here = places()
    for copy in copies[:2]:
        copy.wait()
    orient, boundary, four, coarse_four, two, coarse_two = staged
    for element in layout.elements():
        number = layout.number(element)
        for dim in range(3):
            mask = flip_mask(orient[(dim,) + element])
            masks[number : number + 1, columns(dim)] = jnp.full((1, WIDTH), mask, jnp.int32)
            at_start = (here[dim] == 0) & (element[dim] == 0)
            at_end = (here[dim] == layout.sizes[dim] - 1) & (element[dim] == layout.counts[dim] - 1)
            fixed_low = jnp.where(at_start, boundary[element + (2 * dim,)], 0)
            fixed_top = jnp.where(at_end, boundary[element + (2 * dim + 1,)], 0)
            fixed = jnp.where(low, fixed_low, fixed_top)
            keeps[number : number + 1, columns(dim)] = 1.0 - fixed.astype(jnp.float32)
    for copy in copies[2:]:
        copy.wait()
    start = 0
    for prolong, coarse in ((four, coarse_four), (two, coarse_two)):
        rows = slice(start, start + prolong.shape[0])
        left[rows, :] = prolong[...]
        right[rows, :] = split_dot(coarse[...], prolong[...], ((1,), (0,)))
        start += rounded(prolong.shape[0])
    corrections = split_dot(left[...], right[...], ((0,), (0,)))
    stacked(0.5 * (inverse[...] + corrections), early, late)


def rounded(count):
    return (count + 7) // 8 * 8


def first_kernel(layout, load, orient, *refs):
    turns = len(layout.turns())
    outs, (staged, codes, arrived) = refs[:turns], refs[turns:]
    copies = [
        pltpu.make_async_copy(load.at[:, columns(dim)], staged.at[:, columns(dim)], arrived.at[dim])
        for dim in range(3)
    ]
    code_copy = pltpu.make_async_copy(orient, codes, arrived.at[3])
    code_copy.start()
    for copy in copies:
        copy.start()
    here = places()
    code_copy.wait()
    for dim in range(3):
        copies[dim].wait()
        pack(
            layout,
            here,
            dim,
            lambda element, dim: staged[layout.rows(element), columns(dim)],
            lambda element, dim: flip_mask(codes[(dim,) + element]),
            outs,
        )


def table(layout, ref):
    def row(element, dim):
        number = layout.number(element)
        return ref[number : number + 1, columns(dim)]

    return row


def scales(layout, kind, ref):
    def row(element, dim):
        value = ref[element[0], element[1], element[2] : element[2] + 1, columns(dim)]
        return value if kind == "operator" else 1.0 / value

    return row


def scaled_products(
    layout, kind, dims, here, value, messages, masks, keeps, scaling, matrix, split
):
    factor = scales(layout, kind, scaling)
    size = len(dims) * WIDTH

    def strip(place, dim, slab):
        def emit(element, result):
            high, rest = halves(result * factor(element, dim))
            for part, piece in enumerate((high, high, rest)):
                start = part * size + place * WIDTH
                split[layout.rows(element), start : start + WIDTH] = piece

        assemble(
            layout,
            here,
            dim,
            lambda element, dim: value[layout.rows(element), columns(dim)],
            messages,
            table(layout, masks),
            table(layout, keeps),
            emit,
            slab,
        )

    for place, dim in enumerate(dims):
        if dim == 0:
            strip(place, dim, None)
    count = layout.counts[0]
    height = value.shape[0] // count
    for slab in range(count):
        for place, dim in enumerate(dims):
            if dim != 0:
                strip(place, dim, slab)
        rows = slice(slab * height, (slab + 1) * height)
        yield slab, rows, dot(split[rows, :], matrix[...])


def taken(layout, dims, refs):
    turns = layout.turns(dims)
    return dict(zip(turns, refs)), refs[len(turns) :]


def early_kernel(layout, kind, value, *refs):
    messages, refs = taken(layout, EARLY, refs)
    masks, keeps, scaling, matrix, out, split = refs
    for _, rows, product in scaled_products(
        layout, kind, EARLY, places(), value, messages, masks, keeps, scaling, matrix, split
    ):
        out[rows, :] = product


def late_kernel(layout, kind, value, *refs):
    messages, refs = taken(layout, LATE, refs)
    masks, keeps, scaling, matrix, begun, refs = *refs[:5], refs[5:]
    other = None
    if kind != "smooth":
        other, refs = refs[0], refs[1:]
    turns = len(layout.turns())
    out, sent, (split, summed) = refs[0], refs[1 : 1 + turns], refs[1 + turns :]
    here = places()
    factor = scales(layout, kind, scaling)
    for slab, rows, product in scaled_products(
        layout, kind, LATE, here, value, messages, masks, keeps, scaling, matrix, split
    ):
        summed[rows, :] = begun[rows, :] + product
        for element in layout.elements():
            if element[0] != slab:
                continue
            for dim in range(3):
                at = (layout.rows(element), columns(dim))
                result = summed[at] * factor(element, dim)
                if kind == "operator":
                    result = other[at] - result
                elif kind == "smooth_more":
                    result = other[at] + result
                out[at] = result
    for dim in range(3):
        pack(
            layout,
            here,
            dim,
            lambda element, dim: out[layout.rows(element), columns(dim)],
            table(layout, masks),
            sent,
        )


def assembled_strips(layout, dims, value, messages, masks, keeps, ready):
    for place, dim in enumerate(dims):

        def emit(element, result):
            ready[layout.rows(element), place * WIDTH : (place + 1) * WIDTH] = result

        assemble(
            layout,
            places(),
            dim,
            lambda element, dim: value[layout.rows(element), columns(dim)],
            messages,
            table(layout, masks),
            table(layout, keeps),
            emit,
        )


def last_early_kernel(layout, value, *refs):
    messages, (masks, keeps, ready) = taken(layout, EARLY, refs)
    assembled_strips(layout, EARLY, value, messages, masks, keeps, ready)


def last_late_kernel(layout, begun, value, *refs):
    messages, (masks, keeps, out, ready, left) = taken(layout, LATE, refs)
    cut = begun.shape[1]
    first = pltpu.make_async_copy(begun, out.at[:, :cut], left.at[0])
    first.start()
    assembled_strips(layout, LATE, value, messages, masks, keeps, ready)
    second = pltpu.make_async_copy(ready, out.at[:, cut:], left.at[1])
    second.start()
    first.wait()
    second.wait()


def in_vmem(count):
    return [pl.BlockSpec(memory_space=pltpu.VMEM)] * count


def in_hbm(count):
    return [pl.BlockSpec(memory_space=pltpu.HBM)] * count


PARAMS = pltpu.CompilerParams(vmem_limit_bytes=VMEM_LIMIT)


def kept_in_hbm(*values):
    return [pltpu.with_memory_space_constraint(value, pltpu.HBM) for value in values]


def cost(flops, size):
    return pl.CostEstimate(flops=flops, bytes_accessed=size, transcendentals=0)


def partners(layout, dim, parity):
    sizes = layout.sizes
    swap = {}
    for place in np.ndindex(*sizes):
        other = list(place)
        lower = place[dim] % 2 == parity
        at = place[dim] + (1 if lower else -1)
        if 0 <= at < sizes[dim]:
            other[dim] = at
        elif dim != 1 and sizes[1] % 2 == 0:
            other[1] = place[1] ^ 1
        elif sizes[dim] % 2 == 0:
            other[dim] = sizes[dim] - 1 - place[dim]
        swap[place] = tuple(other)
    return [
        (int(np.ravel_multi_index(place, sizes)), int(np.ravel_multi_index(other, sizes)))
        for place, other in swap.items()
    ]


def exchange(layout, messages):
    return {
        turn: lax.ppermute(message, AXES, partners(layout, *turn))
        for turn, message in zip(layout.turns(), messages)
    }


def body(
    load_raw,
    scaling,
    fine_matrix,
    fine_inverse,
    prolong_four,
    coarse_four,
    prolong_two,
    coarse_two,
    orient,
    boundary,
):
    counts, species, nodes = load_raw.shape[:3], load_raw.shape[3], load_raw.shape[4]
    layout = Layout(counts, species, tuple(lax.axis_size(axis) for axis in AXES))
    load = load_raw.reshape(-1, nodes)
    rows = load.shape[0]
    turns = layout.turns()
    message_shapes = tuple(layout.message(dim) for dim, _ in turns)
    whole = jax.ShapeDtypeStruct(load.shape, jnp.float32)
    matrix_shapes = tuple(
        jax.ShapeDtypeStruct((3 * WIDTH * len(dims), nodes), jnp.bfloat16) for dims in (EARLY, LATE)
    )
    elements = len(layout.elements())

    sent = pl.pallas_call(
        functools.partial(first_kernel, layout),
        out_shape=message_shapes,
        in_specs=in_hbm(2),
        out_specs=tuple(in_vmem(len(turns))),
        scratch_shapes=[
            pltpu.VMEM(load.shape, jnp.float32),
            pltpu.SMEM(orient.shape, jnp.int32),
            pltpu.SemaphoreType.DMA((4,)),
        ],
        compiler_params=PARAMS,
        name="pack",
    )(*kept_in_hbm(load, orient))

    sources = (orient, jnp.transpose(boundary, (1, 2, 3, 0)))
    sources += (prolong_four.T, coarse_four, prolong_two.T, coarse_two)
    stack = (rounded(prolong_four.shape[1]) + rounded(prolong_two.shape[1]), nodes)
    *smoother, masks, keeps = pl.pallas_call(
        functools.partial(smoother_kernel, layout),
        out_shape=matrix_shapes
        + (
            jax.ShapeDtypeStruct((elements, nodes), jnp.int32),
            jax.ShapeDtypeStruct((elements, nodes), jnp.float32),
        ),
        in_specs=in_vmem(1) + in_hbm(6),
        out_specs=tuple(in_vmem(4)),
        scratch_shapes=[pltpu.SMEM(source.shape, source.dtype) for source in sources[:2]]
        + [pltpu.VMEM(source.shape, source.dtype) for source in sources[2:]]
        + [pltpu.VMEM(stack, jnp.float32), pltpu.VMEM(stack, jnp.float32)]
        + [pltpu.SemaphoreType.DMA((6,))],
        compiler_params=PARAMS,
        cost_estimate=cost(2 * nodes * nodes * nodes, 8 * nodes * nodes),
        name="smoother",
    )(fine_inverse, *kept_in_hbm(*sources))
    operator = pl.pallas_call(
        operator_kernel,
        out_shape=matrix_shapes,
        in_specs=in_vmem(1),
        out_specs=tuple(in_vmem(2)),
        compiler_params=PARAMS,
        cost_estimate=cost(0, 10 * nodes * nodes),
        name="operator",
    )(fine_matrix)

    def stage(kind, value, messages, matrix, other):
        early = [messages[turn] for turn in layout.turns(EARLY)]
        late = [messages[turn] for turn in layout.turns(LATE)]
        extra = () if other is None else (other,)
        begun = pl.pallas_call(
            functools.partial(early_kernel, layout, kind),
            out_shape=whole,
            in_specs=in_vmem(5 + len(early)),
            out_specs=in_vmem(1)[0],
            scratch_shapes=[pltpu.VMEM((rows, matrix[0].shape[0]), jnp.bfloat16)],
            compiler_params=PARAMS,
            cost_estimate=cost(2 * rows * matrix[0].shape[0] * nodes, 8 * rows * nodes),
            name=kind + "_early",
        )(value, *early, masks, keeps, scaling, matrix[0])
        results = pl.pallas_call(
            functools.partial(late_kernel, layout, kind),
            out_shape=(whole,) + message_shapes,
            in_specs=in_vmem(6 + len(late) + len(extra)),
            out_specs=tuple(in_vmem(1 + len(turns))),
            scratch_shapes=[
                pltpu.VMEM((rows, matrix[1].shape[0]), jnp.bfloat16),
                pltpu.VMEM(load.shape, jnp.float32),
            ],
            compiler_params=PARAMS,
            cost_estimate=cost(2 * rows * matrix[1].shape[0] * nodes, 12 * rows * nodes),
            name=kind + "_late",
        )(value, *late, masks, keeps, scaling, matrix[1], begun, *extra)
        return results[0], results[1:]

    first, sent = stage("smooth", load, exchange(layout, sent), smoother, None)
    left, sent = stage("operator", first, exchange(layout, sent), operator, load)
    total, sent = stage("smooth_more", left, exchange(layout, sent), smoother, first)
    messages = exchange(layout, sent)
    early = [messages[turn] for turn in layout.turns(EARLY)]
    late = [messages[turn] for turn in layout.turns(LATE)]
    cut = len(EARLY) * WIDTH
    begun = pl.pallas_call(
        functools.partial(last_early_kernel, layout),
        out_shape=jax.ShapeDtypeStruct((rows, cut), jnp.float32),
        in_specs=in_vmem(3 + len(early)),
        out_specs=in_vmem(1)[0],
        compiler_params=PARAMS,
        cost_estimate=cost(0, 8 * rows * cut),
        name="last_early",
    )(total, *early, masks, keeps)
    result = pl.pallas_call(
        functools.partial(last_late_kernel, layout),
        out_shape=whole,
        in_specs=in_vmem(4 + len(late)),
        out_specs=in_hbm(1)[0],
        scratch_shapes=[
            pltpu.VMEM((rows, nodes - cut), jnp.float32),
            pltpu.SemaphoreType.DMA((2,)),
        ],
        compiler_params=PARAMS,
        cost_estimate=cost(0, 8 * rows * nodes),
        name="last_late",
    )(begun, total, *late, masks, keeps)
    return result.reshape(load_raw.shape)


def solution(mesh):
    in_specs = (
        P("ex", "ey", "ez", None, None),
        P("ex", "ey", "ez", None),
        P(),
        P(),
        P(),
        P(),
        P(),
        P(),
        P(None, "ex", "ey", "ez"),
        P(None, "ex", "ey", "ez"),
    )
    out_specs = P("ex", "ey", "ez", None, None)
    return jax.shard_map(body, mesh=mesh, in_specs=in_specs, out_specs=out_specs, check_vma=False)
```

```python
import functools

import jax
import jax.numpy as jnp
from jax import lax
from jax.experimental import pallas as pl
from jax.experimental.pallas import tpu as pltpu
import numpy as np
from jax.sharding import PartitionSpec as P

FACE_SIDE = 8
FACE = FACE_SIDE * FACE_SIDE
WIDTH = 2 * FACE
AXES = ("ex", "ey", "ez")
GROUPS = ((0,), (2,), (1,))
ORDER = sum(GROUPS, ())
VMEM_LIMIT = 24 * 1024 * 1024


class Layout:
    def __init__(self, counts, species, sizes):
        self.counts = counts
        self.species = species
        self.sizes = sizes

    def elements(self):
        spans = [range(count) for count in self.counts]
        return [(i, j, k) for i in spans[0] for j in spans[1] for k in spans[2]]

    def number(self, element):
        return (element[0] * self.counts[1] + element[1]) * self.counts[2] + element[2]

    def rows(self, element):
        start = self.number(element) * self.species
        return slice(start, start + self.species)

    def layer(self, dim, position):
        return [element for element in self.elements() if element[dim] == position]

    def pairs(self, dim):
        return (len(self.layer(dim, 0)) + 1) // 2

    def pair_rows(self, pair):
        return slice(pair * self.species, (pair + 1) * self.species)

    def turns(self, dims=ORDER):
        return [(dim, parity) for dim in dims for parity in (1, 0) if self.sizes[dim] > 1 + parity]

    def message(self):
        pairs = max(self.pairs(each) for each in range(3))
        return jax.ShapeDtypeStruct((pairs * self.species, WIDTH), jnp.float32)


def columns(dim):
    return slice(dim * WIDTH, (dim + 1) * WIDTH)


def lanes(layout):
    return lax.broadcasted_iota(jnp.int32, (layout.species, WIDTH), 1)


def picked(value, index):
    return jnp.take_along_axis(value, index, axis=1, mode="promise_in_bounds")


def flip_mask(code):
    reach = FACE_SIDE - 1
    return (code & 1) * (reach * FACE_SIDE) + (code >> 1) * reach


def places():
    return [lax.axis_index(axis) for axis in AXES]


def pack(layout, here, dim, load_block, mask_of, outs):
    turns = [(turn, out) for turn, out in zip(layout.turns(), outs) if turn[0] == dim]
    if not turns:
        return
    lane = lanes(layout)
    low = lane < FACE
    even = (here[dim] & 1) == 0
    first = layout.layer(dim, 0)
    last = layout.layer(dim, layout.counts[dim] - 1)
    used = layout.pairs(dim) * layout.species
    for _, out in turns:
        if used < out.shape[0]:
            out[used:, :] = jnp.zeros((out.shape[0] - used, WIDTH), jnp.float32)
    for pair in range(layout.pairs(dim)):
        sides = []
        for half in range(2):
            where = min(2 * pair + half, len(first) - 1)
            upper = load_block(last[where], dim)
            lower = load_block(first[where], dim)
            lower = picked(lower, lane ^ mask_of(first[where], dim) ^ (half * FACE))
            if half == 0:
                upper = pltpu.roll(upper, FACE, 1)
            sides.append((upper, lower))
        up = jnp.where(low, sides[0][0], sides[1][0])
        down = jnp.where(low, sides[0][1], sides[1][1])
        for (_, parity), out in turns:
            is_lower = even if parity == 0 else jnp.logical_not(even)
            out[layout.pair_rows(pair), :] = jnp.where(is_lower, up, down)


def received(layout, here, dim, messages):
    even = (here[dim] & 1) == 0
    at_start = here[dim] == 0
    at_end = here[dim] == layout.sizes[dim] - 1
    zero = jnp.zeros((layout.species, WIDTH), jnp.float32)
    found = []
    for pair in range(layout.pairs(dim)):
        first, second = [
            messages[dim, parity][layout.pair_rows(pair), :] if (dim, parity) in messages else zero
            for parity in range(2)
        ]
        below = jnp.where(at_start, 0.0, jnp.where(even, second, first))
        above = jnp.where(at_end, 0.0, jnp.where(even, first, second))
        found.append((below, above))
    return found


def assemble(layout, here, dim, load_block, messages, mask_of, keep_of, emit, slab=None):
    lane = lanes(layout)
    low = lane < FACE
    count = layout.counts[dim]
    outside = received(layout, here, dim, messages)
    for where, start in enumerate(layout.layer(dim, 0)):
        if slab not in (None, start[0]):
            continue
        line = [start[:dim] + (step,) + start[dim + 1 :] for step in range(count)]
        blocks = [load_block(element, dim) for element in line]
        half = (where % 2) * FACE
        below, above = outside[where // 2]
        turned = []
        for step, element in enumerate(line):
            index = lane ^ mask_of(element, dim)
            if step == 0:
                turned.append(picked(below, index ^ half))
            else:
                shared = jnp.where(low, blocks[step], blocks[step - 1])
                turned.append(picked(shared, index ^ FACE))
        turned.append(pltpu.roll(above, FACE, 1) if half == 0 else above)
        for step, element in enumerate(line):
            value = blocks[step] + jnp.where(low, turned[step], turned[step + 1])
            if step in (0, count - 1):
                value = value * keep_of(element, dim)
            emit(element, value)


def halves(value):
    high = value.astype(jnp.bfloat16)
    return high, (value - high.astype(jnp.float32)).astype(jnp.bfloat16)


def dot(left, right, contract=((1,), (0,))):
    return lax.dot_general(left, right, (contract, ((), ())), preferred_element_type=jnp.float32)


def split_dot(left, right, contract):
    left_high, left_rest = halves(left)
    right_high, right_rest = halves(right)
    return (
        dot(left_high, right_high, contract)
        + dot(left_high, right_rest, contract)
        + dot(left_rest, right_high, contract)
    )


def stacked(value, outs):
    high, rest = halves(value)
    for out, dims in zip(outs, GROUPS):
        size = len(dims) * WIDTH
        for part, piece in enumerate((high, rest, high)):
            for place, dim in enumerate(dims):
                start = part * size + place * WIDTH
                out[start : start + WIDTH, :] = piece[columns(dim), :]


def operator_kernel(fine, *outs):
    stacked(fine[...], outs)


def smoother_kernel(layout, *refs):
    inverse, *sources = refs[:7]
    outs, refs = refs[7 : 7 + len(GROUPS)], refs[7 + len(GROUPS) :]
    (masks, keeps), refs = refs[:2], refs[2:]
    staged, (right, left, arrived) = refs[:6], refs[6:]
    copies = [
        pltpu.make_async_copy(source, stage, arrived.at[number])
        for number, (source, stage) in enumerate(zip(sources, staged))
    ]
    for copy in copies:
        copy.start()
    right[...] = jnp.zeros_like(right)
    left[...] = jnp.zeros_like(left)
    low = lax.broadcasted_iota(jnp.int32, (1, WIDTH), 1) < FACE
    here = places()
    for copy in copies[:2]:
        copy.wait()
    orient, boundary, four, coarse_four, two, coarse_two = staged
    for element in layout.elements():
        number = layout.number(element)
        for dim in range(3):
            mask = flip_mask(orient[(dim,) + element])
            masks[number : number + 1, columns(dim)] = jnp.full((1, WIDTH), mask, jnp.int32)
            at_start = (here[dim] == 0) & (element[dim] == 0)
            at_end = (here[dim] == layout.sizes[dim] - 1) & (element[dim] == layout.counts[dim] - 1)
            fixed_low = jnp.where(at_start, boundary[element + (2 * dim,)], 0)
            fixed_top = jnp.where(at_end, boundary[element + (2 * dim + 1,)], 0)
            fixed = jnp.where(low, fixed_low, fixed_top)
            keeps[number : number + 1, columns(dim)] = 1.0 - fixed.astype(jnp.float32)
    for copy in copies[2:]:
        copy.wait()
    start = 0
    for prolong, coarse in ((four, coarse_four), (two, coarse_two)):
        rows = slice(start, start + prolong.shape[0])
        left[rows, :] = prolong[...]
        right[rows, :] = split_dot(coarse[...], prolong[...], ((1,), (0,)))
        start += rounded(prolong.shape[0])
    corrections = split_dot(left[...], right[...], ((0,), (0,)))
    stacked(0.5 * (inverse[...] + corrections), outs)


def rounded(count):
    return (count + 7) // 8 * 8


def first_kernel(layout, load, orient, *refs):
    turns = len(layout.turns())
    outs, (staged, codes, arrived) = refs[:turns], refs[turns:]
    copies = [
        pltpu.make_async_copy(load.at[:, columns(dim)], staged.at[:, columns(dim)], arrived.at[dim])
        for dim in range(3)
    ]
    code_copy = pltpu.make_async_copy(orient, codes, arrived.at[3])
    code_copy.start()
    for copy in copies:
        copy.start()
    here = places()
    code_copy.wait()
    for dim in range(3):
        copies[dim].wait()
        pack(
            layout,
            here,
            dim,
            lambda element, dim: staged[layout.rows(element), columns(dim)],
            lambda element, dim: flip_mask(codes[(dim,) + element]),
            outs,
        )


def table(layout, ref):
    def row(element, dim):
        number = layout.number(element)
        return ref[number : number + 1, columns(dim)]

    return row


def scales(layout, kind, ref):
    def row(element, dim):
        value = ref[element[0], element[1], element[2] : element[2] + 1, columns(dim)]
        return value if kind == "operator" else 1.0 / value

    return row


def scaled_products(
    layout, kind, dims, here, value, messages, masks, keeps, scaling, matrix, split
):
    factor = scales(layout, kind, scaling)
    size = len(dims) * WIDTH

    def strip(place, dim, slab):
        def emit(element, result):
            high, rest = halves(result * factor(element, dim))
            for part, piece in enumerate((high, high, rest)):
                start = part * size + place * WIDTH
                split[layout.rows(element), start : start + WIDTH] = piece

        assemble(
            layout,
            here,
            dim,
            lambda element, dim: value[layout.rows(element), columns(dim)],
            messages,
            table(layout, masks),
            table(layout, keeps),
            emit,
            slab,
        )

    for place, dim in enumerate(dims):
        if dim == 0:
            strip(place, dim, None)
    count = layout.counts[0]
    height = value.shape[0] // count
    for slab in range(count):
        for place, dim in enumerate(dims):
            if dim != 0:
                strip(place, dim, slab)
        rows = slice(slab * height, (slab + 1) * height)
        yield slab, rows, dot(split[rows, :], matrix[...])


def taken(layout, dims, refs):
    turns = layout.turns(dims)
    return dict(zip(turns, refs)), refs[len(turns) :]


def stage_kernel(layout, kind, group, value, *refs):
    dims = GROUPS[group]
    messages, refs = taken(layout, dims, refs)
    masks, keeps, scaling, matrix, refs = *refs[:4], refs[4:]
    begun = None
    if group > 0 or kind != "smooth":
        begun, refs = refs[0], refs[1:]
    out, *sent, split, summed = refs
    here = places()
    factor = scales(layout, kind, scaling)
    for slab, rows, product in scaled_products(
        layout, kind, dims, here, value, messages, masks, keeps, scaling, matrix, split
    ):
        summed[rows, :] = product
        for element in layout.elements():
            if element[0] != slab:
                continue
            for dim in range(3):
                at = (layout.rows(element), columns(dim))
                result = summed[at] * factor(element, dim)
                if begun is None:
                    out[at] = result
                elif kind == "operator":
                    out[at] = begun[at] - result
                else:
                    out[at] = begun[at] + result
    if sent:
        for dim in ORDER:
            pack(
                layout,
                here,
                dim,
                lambda element, dim: out[layout.rows(element), columns(dim)],
                table(layout, masks),
                sent,
            )


def assembled_strips(layout, dims, value, messages, masks, keeps, ready):
    for place, dim in enumerate(dims):

        def emit(element, result):
            ready[layout.rows(element), place * WIDTH : (place + 1) * WIDTH] = result

        assemble(
            layout,
            places(),
            dim,
            lambda element, dim: value[layout.rows(element), columns(dim)],
            messages,
            table(layout, masks),
            table(layout, keeps),
            emit,
        )


def last_early_kernel(layout, dims, value, *refs):
    messages, (masks, keeps, ready) = taken(layout, dims, refs)
    assembled_strips(layout, dims, value, messages, masks, keeps, ready)


def last_late_kernel(layout, begun, value, *refs):
    dims = GROUPS[-1]
    messages, (masks, keeps, out, ready, left) = taken(layout, dims, refs)

    def copies(source, done, first):
        return [
            pltpu.make_async_copy(
                source.at[:, place * WIDTH : (place + 1) * WIDTH],
                out.at[:, columns(dim)],
                left.at[first + place],
            )
            for place, dim in enumerate(done)
        ]

    before = ORDER[: -len(dims)]
    started = copies(begun, before, 0)
    for copy in started:
        copy.start()
    assembled_strips(layout, dims, value, messages, masks, keeps, ready)
    rest = copies(ready, dims, len(before))
    for copy in rest:
        copy.start()
    for copy in started + rest:
        copy.wait()


def in_vmem(count):
    return [pl.BlockSpec(memory_space=pltpu.VMEM)] * count


def in_hbm(count):
    return [pl.BlockSpec(memory_space=pltpu.HBM)] * count


PARAMS = pltpu.CompilerParams(vmem_limit_bytes=VMEM_LIMIT)


def kept_in_hbm(*values):
    return [pltpu.with_memory_space_constraint(value, pltpu.HBM) for value in values]


def cost(flops, size):
    return pl.CostEstimate(flops=flops, bytes_accessed=size, transcendentals=0)


def partners(layout, dim, parity):
    sizes = layout.sizes
    swap = {}
    for place in np.ndindex(*sizes):
        other = list(place)
        lower = place[dim] % 2 == parity
        at = place[dim] + (1 if lower else -1)
        if 0 <= at < sizes[dim]:
            other[dim] = at
        elif dim != 1 and sizes[1] % 2 == 0:
            other[1] = place[1] ^ 1
        elif sizes[dim] % 2 == 0:
            other[dim] = sizes[dim] - 1 - place[dim]
        swap[place] = tuple(other)
    return [
        (int(np.ravel_multi_index(place, sizes)), int(np.ravel_multi_index(other, sizes)))
        for place, other in swap.items()
    ]


def exchange(layout, messages):
    return {
        turn: lax.ppermute(message, AXES, partners(layout, *turn))
        for turn, message in zip(layout.turns(), messages)
    }


def body(
    load_raw,
    scaling,
    fine_matrix,
    fine_inverse,
    prolong_four,
    coarse_four,
    prolong_two,
    coarse_two,
    orient,
    boundary,
):
    counts, species, nodes = load_raw.shape[:3], load_raw.shape[3], load_raw.shape[4]
    layout = Layout(counts, species, tuple(lax.axis_size(axis) for axis in AXES))
    load = load_raw.reshape(-1, nodes)
    rows = load.shape[0]
    turns = layout.turns()
    message_shapes = tuple(layout.message() for _ in turns)
    whole = jax.ShapeDtypeStruct(load.shape, jnp.float32)
    matrix_shapes = tuple(
        jax.ShapeDtypeStruct((3 * WIDTH * len(dims), nodes), jnp.bfloat16) for dims in GROUPS
    )
    elements = len(layout.elements())

    sent = pl.pallas_call(
        functools.partial(first_kernel, layout),
        out_shape=message_shapes,
        in_specs=in_hbm(2),
        out_specs=tuple(in_vmem(len(turns))),
        scratch_shapes=[
            pltpu.VMEM(load.shape, jnp.float32),
            pltpu.SMEM(orient.shape, jnp.int32),
            pltpu.SemaphoreType.DMA((4,)),
        ],
        compiler_params=PARAMS,
        name="pack",
    )(*kept_in_hbm(load, orient))

    sources = (orient, jnp.transpose(boundary, (1, 2, 3, 0)))
    sources += (prolong_four.T, coarse_four, prolong_two.T, coarse_two)
    stack = (rounded(prolong_four.shape[1]) + rounded(prolong_two.shape[1]), nodes)
    *smoother, masks, keeps = pl.pallas_call(
        functools.partial(smoother_kernel, layout),
        out_shape=matrix_shapes
        + (
            jax.ShapeDtypeStruct((elements, nodes), jnp.int32),
            jax.ShapeDtypeStruct((elements, nodes), jnp.float32),
        ),
        in_specs=in_vmem(1) + in_hbm(6),
        out_specs=tuple(in_vmem(len(GROUPS) + 2)),
        scratch_shapes=[pltpu.SMEM(source.shape, source.dtype) for source in sources[:2]]
        + [pltpu.VMEM(source.shape, source.dtype) for source in sources[2:]]
        + [pltpu.VMEM(stack, jnp.float32), pltpu.VMEM(stack, jnp.float32)]
        + [pltpu.SemaphoreType.DMA((6,))],
        compiler_params=PARAMS,
        cost_estimate=cost(2 * nodes * nodes * nodes, 8 * nodes * nodes),
        name="smoother",
    )(fine_inverse, *kept_in_hbm(*sources))
    operator = pl.pallas_call(
        operator_kernel,
        out_shape=matrix_shapes,
        in_specs=in_vmem(1),
        out_specs=tuple(in_vmem(len(GROUPS))),
        compiler_params=PARAMS,
        cost_estimate=cost(0, 10 * nodes * nodes),
        name="operator",
    )(fine_matrix)

    def stage(kind, value, messages, matrix, begun):
        for group, dims in enumerate(GROUPS):
            mine = [messages[turn] for turn in layout.turns(dims)]
            before = () if begun is None else (begun,)
            ends = group == len(GROUPS) - 1
            depth = matrix[group].shape[0]
            begun, *sent = pl.pallas_call(
                functools.partial(stage_kernel, layout, kind, group),
                out_shape=(whole,) + (message_shapes if ends else ()),
                in_specs=in_vmem(5 + len(mine) + len(before)),
                out_specs=tuple(in_vmem(1 + (len(turns) if ends else 0))),
                scratch_shapes=[
                    pltpu.VMEM((rows, depth), jnp.bfloat16),
                    pltpu.VMEM(load.shape, jnp.float32),
                ],
                compiler_params=PARAMS,
                cost_estimate=cost(2 * rows * depth * nodes, 8 * rows * nodes),
                name="{}_{}".format(kind, group),
            )(value, *mine, masks, keeps, scaling, matrix[group], *before)
        return begun, sent

    first, sent = stage("smooth", load, exchange(layout, sent), smoother, None)
    left, sent = stage("operator", first, exchange(layout, sent), operator, load)
    total, sent = stage("smooth_more", left, exchange(layout, sent), smoother, first)
    messages = exchange(layout, sent)
    early_dims, late_dims = ORDER[: -len(GROUPS[-1])], GROUPS[-1]
    early = [messages[turn] for turn in layout.turns(early_dims)]
    late = [messages[turn] for turn in layout.turns(late_dims)]
    cut = len(early_dims) * WIDTH
    begun = pl.pallas_call(
        functools.partial(last_early_kernel, layout, early_dims),
        out_shape=jax.ShapeDtypeStruct((rows, cut), jnp.float32),
        in_specs=in_vmem(3 + len(early)),
        out_specs=in_vmem(1)[0],
        compiler_params=PARAMS,
        cost_estimate=cost(0, 8 * rows * cut),
        name="last_early",
    )(total, *early, masks, keeps)
    result = pl.pallas_call(
        functools.partial(last_late_kernel, layout),
        out_shape=whole,
        in_specs=in_vmem(4 + len(late)),
        out_specs=in_hbm(1)[0],
        scratch_shapes=[
            pltpu.VMEM((rows, nodes - cut), jnp.float32),
            pltpu.SemaphoreType.DMA((3,)),
        ],
        compiler_params=PARAMS,
        cost_estimate=cost(0, 8 * rows * nodes),
        name="last_late",
    )(begun, total, *late, masks, keeps)
    return result.reshape(load_raw.shape)


def solution(mesh):
    in_specs = (
        P("ex", "ey", "ez", None, None),
        P("ex", "ey", "ez", None),
        P(),
        P(),
        P(),
        P(),
        P(),
        P(),
        P(None, "ex", "ey", "ez"),
        P(None, "ex", "ey", "ez"),
    )
    out_specs = P("ex", "ey", "ez", None, None)
    return jax.shard_map(body, mesh=mesh, in_specs=in_specs, out_specs=out_specs, check_vma=False)
```

```python
import functools

import jax
import jax.numpy as jnp
from jax import lax
from jax.experimental import pallas as pl
from jax.experimental.pallas import tpu as pltpu
import numpy as np
from jax.sharding import PartitionSpec as P

FACE_SIDE = 8
FACE = FACE_SIDE * FACE_SIDE
WIDTH = 2 * FACE
AXES = ("ex", "ey", "ez")
TURNS = ((1, 1), (0, 1), (0, 0), (1, 0), (2, 1), (2, 0))
EARLY = (1, 0)
LATE = 2
VMEM_LIMIT = 24 * 1024 * 1024


class Layout:
    def __init__(self, counts, species, sizes):
        self.counts = counts
        self.species = species
        self.sizes = sizes

    def elements(self):
        spans = [range(count) for count in self.counts]
        return [(i, j, k) for i in spans[0] for j in spans[1] for k in spans[2]]

    def number(self, element):
        return (element[0] * self.counts[1] + element[1]) * self.counts[2] + element[2]

    def rows(self, element):
        start = self.number(element) * self.species
        return slice(start, start + self.species)

    def layer(self, dim, position):
        return [element for element in self.elements() if element[dim] == position]

    def pairs(self, dim):
        return (len(self.layer(dim, 0)) + 1) // 2

    def pair_rows(self, pair):
        return slice(pair * self.species, (pair + 1) * self.species)

    def turns(self, dims=(0, 1, 2)):
        return [
            (dim, parity) for dim, parity in TURNS if dim in dims and self.sizes[dim] > 1 + parity
        ]

    def edge(self, dim):
        ends = (0, self.counts[dim] - 1)
        return [element for element in self.elements() if element[dim] in ends]

    def message(self, dim):
        return jax.ShapeDtypeStruct((self.pairs(dim) * self.species, WIDTH), jnp.float32)


def columns(dim):
    return slice(dim * WIDTH, (dim + 1) * WIDTH)


def lanes(layout):
    return lax.broadcasted_iota(jnp.int32, (layout.species, WIDTH), 1)


def picked(value, index):
    return jnp.take_along_axis(value, index, axis=1, mode="promise_in_bounds")


def flip_mask(code):
    reach = FACE_SIDE - 1
    return (code & 1) * (reach * FACE_SIDE) + (code >> 1) * reach


def places():
    return [lax.axis_index(axis) for axis in AXES]


def pack(layout, here, dim, load_block, mask_of, outs):
    turns = [(turn, out) for turn, out in zip(layout.turns(), outs) if turn[0] == dim]
    if not turns:
        return
    lane = lanes(layout)
    low = lane < FACE
    even = (here[dim] & 1) == 0
    first = layout.layer(dim, 0)
    last = layout.layer(dim, layout.counts[dim] - 1)
    for pair in range(layout.pairs(dim)):
        sides = []
        for half in range(2):
            where = min(2 * pair + half, len(first) - 1)
            upper = load_block(last[where], dim)
            lower = load_block(first[where], dim)
            lower = picked(lower, lane ^ mask_of(first[where], dim) ^ (half * FACE))
            if half == 0:
                upper = pltpu.roll(upper, FACE, 1)
            sides.append((upper, lower))
        up = jnp.where(low, sides[0][0], sides[1][0])
        down = jnp.where(low, sides[0][1], sides[1][1])
        for (_, parity), out in turns:
            is_lower = even if parity == 0 else jnp.logical_not(even)
            out[layout.pair_rows(pair), :] = jnp.where(is_lower, up, down)


def received(layout, here, dim, messages):
    even = (here[dim] & 1) == 0
    at_start = here[dim] == 0
    at_end = here[dim] == layout.sizes[dim] - 1
    zero = jnp.zeros((layout.species, WIDTH), jnp.float32)
    found = []
    for pair in range(layout.pairs(dim)):
        first, second = [
            messages[dim, parity][layout.pair_rows(pair), :] if (dim, parity) in messages else zero
            for parity in range(2)
        ]
        below = jnp.where(at_start, 0.0, jnp.where(even, second, first))
        above = jnp.where(at_end, 0.0, jnp.where(even, first, second))
        found.append((below, above))
    return found


def unpacked(lane, outside, where, mask):
    below, above = outside[where // 2]
    half = (where % 2) * FACE
    from_below = picked(below, lane ^ mask ^ half)
    from_above = pltpu.roll(above, FACE, 1) if half == 0 else above
    return from_below, from_above


def assemble(layout, here, dim, load_block, messages, mask_of, keep_of, emit, slab=None):
    lane = lanes(layout)
    low = lane < FACE
    count = layout.counts[dim]
    outside = None if messages is None else received(layout, here, dim, messages)
    zero = jnp.zeros((layout.species, WIDTH), jnp.float32)
    for where, start in enumerate(layout.layer(dim, 0)):
        if slab not in (None, start[0]):
            continue
        line = [start[:dim] + (step,) + start[dim + 1 :] for step in range(count)]
        blocks = [load_block(element, dim) for element in line]
        if outside is None:
            from_below, from_above = zero, zero
        else:
            from_below, from_above = unpacked(lane, outside, where, mask_of(start, dim))
        turned = [from_below]
        for step, element in list(enumerate(line))[1:]:
            shared = jnp.where(low, blocks[step], blocks[step - 1])
            turned.append(picked(shared, lane ^ mask_of(element, dim) ^ FACE))
        turned.append(from_above)
        for step, element in enumerate(line):
            value = blocks[step] + jnp.where(low, turned[step], turned[step + 1])
            if step in (0, count - 1):
                value = value * keep_of(element, dim)
            emit(element, value)


def halves(value):
    high = value.astype(jnp.bfloat16)
    return high, (value - high.astype(jnp.float32)).astype(jnp.bfloat16)


def dot(left, right, contract=((1,), (0,))):
    return lax.dot_general(left, right, (contract, ((), ())), preferred_element_type=jnp.float32)


def split_dot(left, right, contract):
    left_high, left_rest = halves(left)
    right_high, right_rest = halves(right)
    return (
        dot(left_high, right_high, contract)
        + dot(left_high, right_rest, contract)
        + dot(left_rest, right_high, contract)
    )


def stacked(value, outs):
    high, rest = halves(value)
    for dim, out in enumerate(outs):
        for part, piece in enumerate((high, rest, high)):
            out[part * WIDTH : (part + 1) * WIDTH, :] = piece[columns(dim), :]


def operator_kernel(fine, *outs):
    stacked(fine[...], outs)


def smoother_kernel(inverse, four, coarse_four, two, coarse_two, *refs):
    *outs, right, left = refs
    right[...] = jnp.zeros_like(right)
    left[...] = jnp.zeros_like(left)
    start = 0
    for prolong, coarse in ((four, coarse_four), (two, coarse_two)):
        rows = slice(start, start + prolong.shape[0])
        left[rows, :] = prolong[...]
        right[rows, :] = split_dot(coarse[...], prolong[...], ((1,), (0,)))
        start += rounded(prolong.shape[0])
    corrections = split_dot(left[...], right[...], ((0,), (0,)))
    stacked(0.5 * (inverse[...] + corrections), outs)


def rounded(count):
    return (count + 7) // 8 * 8


def first_kernel(layout, load, orient, boundary, *refs):
    turns = len(layout.turns())
    weights, refs = refs[:4], refs[4:]
    outs, (masks, keeps), fetched, refs = refs[:turns], refs[turns : turns + 2], *cut_at(refs, turns)
    staged, codes, fixed, arrived = refs
    small = [
        pltpu.make_async_copy(source, target, arrived.at[number])
        for number, (source, target) in enumerate(((orient, codes), (boundary, fixed)))
    ]
    strips = [
        pltpu.make_async_copy(
            load.at[:, columns(dim)], staged.at[:, columns(dim)], arrived.at[2 + dim]
        )
        for dim in range(3)
    ]
    fetches = [
        pltpu.make_async_copy(source, target, arrived.at[5 + number])
        for number, (source, target) in enumerate(zip(weights, fetched))
    ]
    for copy in small + strips + fetches:
        copy.start()
    here = places()
    for copy in small:
        copy.wait()
    tabulate(layout, here, codes, fixed, masks, keeps)
    for dim in range(3):
        strips[dim].wait()
        pack(
            layout,
            here,
            dim,
            lambda element, dim: staged[layout.rows(element), columns(dim)],
            table(layout, masks),
            outs,
        )
    for copy in fetches:
        copy.wait()


def cut_at(refs, turns):
    return refs[turns + 2 : turns + 6], refs[turns + 6 :]


def tabulate(layout, here, codes, boundary, masks, keeps):
    low = lax.broadcasted_iota(jnp.int32, (1, WIDTH), 1) < FACE
    for element in layout.elements():
        number = layout.number(element)
        for dim in range(3):
            mask = flip_mask(codes[(dim,) + element])
            masks[number : number + 1, columns(dim)] = jnp.full((1, WIDTH), mask, jnp.int32)
            at_start = (here[dim] == 0) & (element[dim] == 0)
            at_end = (here[dim] == layout.sizes[dim] - 1) & (element[dim] == layout.counts[dim] - 1)
            fixed_low = jnp.where(at_start, boundary[element + (2 * dim,)], 0)
            fixed_top = jnp.where(at_end, boundary[element + (2 * dim + 1,)], 0)
            fixed = jnp.where(low, fixed_low, fixed_top)
            keeps[number : number + 1, columns(dim)] = 1.0 - fixed.astype(jnp.float32)


def table(layout, ref):
    def row(element, dim):
        number = layout.number(element)
        return ref[number : number + 1, columns(dim)]

    return row


def scales(layout, kind, ref):
    def row(element, dim):
        value = ref[element[0], element[1], element[2] : element[2] + 1, columns(dim)]
        return value if kind == "operator" else 1.0 / value

    return row


def put_split(split, rows, value):
    high, rest = halves(value)
    for part, piece in enumerate((high, high, rest)):
        split[rows, part * WIDTH : (part + 1) * WIDTH] = piece


def taken(layout, dims, refs):
    turns = layout.turns(dims)
    return dict(zip(turns, refs)), refs[len(turns) :]


def combined(kind, begun, result):
    if begun is None:
        return result
    return begun - result if kind == "operator" else begun + result


def strip_kernel(layout, kind, dim, local, value, *refs):
    messages, refs = (None, refs) if local else taken(layout, (dim,), refs)
    masks, keeps, scaling, matrix, *before, out, split, summed = refs
    begun = before[0] if before else None
    here = places()
    factor = scales(layout, kind, scaling)

    def emit(element, result):
        put_split(split, layout.rows(element), result * factor(element, dim))

    def assembled(slab):
        assemble(
            layout,
            here,
            dim,
            lambda element, dim: value[layout.rows(element), columns(dim)],
            messages,
            table(layout, masks),
            table(layout, keeps),
            emit,
            slab,
        )

    if dim == 0:
        assembled(None)
    count = layout.counts[0]
    height = value.shape[0] // count
    for slab in range(count):
        if dim != 0:
            assembled(slab)
        rows = slice(slab * height, (slab + 1) * height)
        summed[rows, :] = dot(split[rows, :], matrix[...])
        for element in layout.layer(0, slab):
            for each in range(3):
                at = (layout.rows(element), columns(each))
                result = summed[at] * factor(element, each)
                out[at] = combined(kind, None if begun is None else begun[at], result)


def faces_kernel(layout, kind, *refs):
    messages, refs = taken(layout, (LATE,), refs)
    masks, scaling, matrix, begun, *refs = refs
    out, *sent, split, summed = refs
    here = places()
    factor = scales(layout, kind, scaling)
    lane = lanes(layout)
    low = lane < FACE
    outside = received(layout, here, LATE, messages)
    mask_of = table(layout, masks)
    edge = layout.edge(LATE)
    for number, element in enumerate(edge):
        start = element[:LATE] + (0,) + element[LATE + 1 :]
        where = layout.layer(LATE, 0).index(start)
        from_below, from_above = unpacked(lane, outside, where, mask_of(start, LATE))
        lower = from_below if element[LATE] == 0 else 0.0
        upper = from_above if element[LATE] == layout.counts[LATE] - 1 else 0.0
        rows = slice(number * layout.species, (number + 1) * layout.species)
        put_split(split, rows, jnp.where(low, lower, upper) * factor(element, LATE))
    summed[...] = dot(split[...], matrix[...])
    for element in layout.elements():
        for dim in range(3):
            at = (layout.rows(element), columns(dim))
            if element in edge:
                number = edge.index(element)
                rows = slice(number * layout.species, (number + 1) * layout.species)
                result = summed[rows, columns(dim)] * factor(element, dim)
                out[at] = combined(kind, begun[at], result)
            else:
                out[at] = begun[at]
    for dim in range(3):
        pack(
            layout,
            here,
            dim,
            lambda element, dim: out[layout.rows(element), columns(dim)],
            mask_of,
            sent,
        )


def assembled_strips(layout, dims, value, messages, masks, keeps, ready):
    for place, dim in enumerate(dims):

        def emit(element, result):
            ready[layout.rows(element), place * WIDTH : (place + 1) * WIDTH] = result

        assemble(
            layout,
            places(),
            dim,
            lambda element, dim: value[layout.rows(element), columns(dim)],
            messages,
            table(layout, masks),
            table(layout, keeps),
            emit,
        )


def last_early_kernel(layout, value, *refs):
    messages, (masks, keeps, ready) = taken(layout, EARLY, refs)
    assembled_strips(layout, EARLY, value, messages, masks, keeps, ready)


def last_late_kernel(layout, begun, value, *refs):
    messages, (masks, keeps, out, ready, left) = taken(layout, (LATE,), refs)

    def copies(source, done, first):
        return [
            pltpu.make_async_copy(
                source.at[:, place * WIDTH : (place + 1) * WIDTH],
                out.at[:, columns(dim)],
                left.at[first + place],
            )
            for place, dim in enumerate(done)
        ]

    started = copies(begun, EARLY, 0)
    for copy in started:
        copy.start()
    assembled_strips(layout, (LATE,), value, messages, masks, keeps, ready)
    rest = copies(ready, (LATE,), len(EARLY))
    for copy in rest:
        copy.start()
    for copy in started + rest:
        copy.wait()


def in_vmem(count):
    return [pl.BlockSpec(memory_space=pltpu.VMEM)] * count


def in_hbm(count):
    return [pl.BlockSpec(memory_space=pltpu.HBM)] * count


PARAMS = pltpu.CompilerParams(vmem_limit_bytes=VMEM_LIMIT)


def kept_in_hbm(*values):
    return [pltpu.with_memory_space_constraint(value, pltpu.HBM) for value in values]


def cost(flops, size):
    return pl.CostEstimate(flops=flops, bytes_accessed=size, transcendentals=0)


def partners(layout, dim, parity):
    sizes = layout.sizes
    swap = {}
    for place in np.ndindex(*sizes):
        other = list(place)
        lower = place[dim] % 2 == parity
        at = place[dim] + (1 if lower else -1)
        if 0 <= at < sizes[dim]:
            other[dim] = at
        elif dim != 1 and sizes[1] % 2 == 0:
            other[1] = place[1] ^ 1
        elif sizes[dim] % 2 == 0:
            other[dim] = sizes[dim] - 1 - place[dim]
        swap[place] = tuple(other)
    return [
        (int(np.ravel_multi_index(place, sizes)), int(np.ravel_multi_index(other, sizes)))
        for place, other in swap.items()
    ]


def exchange(layout, messages):
    return {
        turn: lax.ppermute(message, AXES, partners(layout, *turn))
        for turn, message in zip(layout.turns(), messages)
    }


def body(
    load_raw,
    scaling,
    fine_matrix,
    fine_inverse,
    prolong_four,
    coarse_four,
    prolong_two,
    coarse_two,
    orient,
    boundary,
):
    counts, species, nodes = load_raw.shape[:3], load_raw.shape[3], load_raw.shape[4]
    layout = Layout(counts, species, tuple(lax.axis_size(axis) for axis in AXES))
    load = load_raw.reshape(-1, nodes)
    rows = load.shape[0]
    turns = layout.turns()
    message_shapes = tuple(layout.message(dim) for dim, _ in turns)
    whole = jax.ShapeDtypeStruct(load.shape, jnp.float32)
    matrix_shapes = (jax.ShapeDtypeStruct((3 * WIDTH, nodes), jnp.bfloat16),) * 3
    elements = len(layout.elements())
    tables = tuple(jax.ShapeDtypeStruct((elements, nodes), kind) for kind in (jnp.int32, jnp.float32))
    weights = (prolong_four.T, coarse_four, prolong_two.T, coarse_two)
    sides = jnp.transpose(boundary, (1, 2, 3, 0))

    sent = pl.pallas_call(
        functools.partial(first_kernel, layout),
        out_shape=message_shapes
        + tables
        + tuple(jax.ShapeDtypeStruct(weight.shape, weight.dtype) for weight in weights),
        in_specs=in_hbm(7),
        out_specs=tuple(in_vmem(len(turns) + 6)),
        scratch_shapes=[
            pltpu.VMEM(load.shape, jnp.float32),
            pltpu.SMEM(orient.shape, jnp.int32),
            pltpu.SMEM(sides.shape, jnp.int32),
            pltpu.SemaphoreType.DMA((9,)),
        ],
        compiler_params=PARAMS,
        name="pack",
    )(*kept_in_hbm(load, orient, sides, *weights))
    masks, keeps, *weights = sent[len(turns) :]

    stack = (rounded(prolong_four.shape[1]) + rounded(prolong_two.shape[1]), nodes)
    smoother = pl.pallas_call(
        smoother_kernel,
        out_shape=matrix_shapes,
        in_specs=in_vmem(5),
        out_specs=tuple(in_vmem(3)),
        scratch_shapes=[pltpu.VMEM(stack, jnp.float32), pltpu.VMEM(stack, jnp.float32)],
        compiler_params=PARAMS,
        cost_estimate=cost(2 * nodes * nodes * nodes, 8 * nodes * nodes),
        name="smoother",
    )(fine_inverse, *weights)
    operator = pl.pallas_call(
        operator_kernel,
        out_shape=matrix_shapes,
        in_specs=in_vmem(1),
        out_specs=tuple(in_vmem(3)),
        compiler_params=PARAMS,
        cost_estimate=cost(0, 10 * nodes * nodes),
        name="operator",
    )(fine_matrix)

    def stage(kind, value, messages, matrix, begun):
        estimate = cost(6 * rows * WIDTH * nodes, 8 * rows * nodes)
        for dim, local in ((LATE, True),) + tuple((dim, False) for dim in EARLY):
            mine = [] if local else [messages[turn] for turn in layout.turns((dim,))]
            before = () if begun is None else (begun,)
            begun = pl.pallas_call(
                functools.partial(strip_kernel, layout, kind, dim, local),
                out_shape=whole,
                in_specs=in_vmem(5 + len(mine) + len(before)),
                out_specs=in_vmem(1)[0],
                scratch_shapes=[
                    pltpu.VMEM((rows, 3 * WIDTH), jnp.bfloat16),
                    pltpu.VMEM(load.shape, jnp.float32),
                ],
                compiler_params=PARAMS,
                cost_estimate=estimate,
                name="{}_{}".format(kind, dim),
            )(value, *mine, masks, keeps, scaling, matrix[dim], *before)
        mine = [messages[turn] for turn in layout.turns((LATE,))]
        height = len(layout.edge(LATE)) * species
        result, *sent = pl.pallas_call(
            functools.partial(faces_kernel, layout, kind),
            out_shape=(whole,) + message_shapes,
            in_specs=in_vmem(4 + len(mine)),
            out_specs=tuple(in_vmem(1 + len(turns))),
            scratch_shapes=[
                pltpu.VMEM((height, 3 * WIDTH), jnp.bfloat16),
                pltpu.VMEM((height, nodes), jnp.float32),
            ],
            compiler_params=PARAMS,
            cost_estimate=estimate,
            name="{}_faces".format(kind),
        )(*mine, masks, scaling, matrix[LATE], begun)
        return result, sent

    first, sent = stage("smooth", load, exchange(layout, sent), smoother, None)
    left, sent = stage("operator", first, exchange(layout, sent), operator, load)
    total, sent = stage("smooth_more", left, exchange(layout, sent), smoother, first)
    messages = exchange(layout, sent)
    early = [messages[turn] for turn in layout.turns(EARLY)]
    late = [messages[turn] for turn in layout.turns((LATE,))]
    cut = len(EARLY) * WIDTH
    begun = pl.pallas_call(
        functools.partial(last_early_kernel, layout),
        out_shape=jax.ShapeDtypeStruct((rows, cut), jnp.float32),
        in_specs=in_vmem(3 + len(early)),
        out_specs=in_vmem(1)[0],
        compiler_params=PARAMS,
        cost_estimate=cost(0, 8 * rows * cut),
        name="last_early",
    )(total, *early, masks, keeps)
    result = pl.pallas_call(
        functools.partial(last_late_kernel, layout),
        out_shape=whole,
        in_specs=in_vmem(4 + len(late)),
        out_specs=in_hbm(1)[0],
        scratch_shapes=[
            pltpu.VMEM((rows, nodes - cut), jnp.float32),
            pltpu.SemaphoreType.DMA((3,)),
        ],
        compiler_params=PARAMS,
        cost_estimate=cost(0, 8 * rows * nodes),
        name="last_late",
    )(begun, total, *late, masks, keeps)
    return result.reshape(load_raw.shape)


def solution(mesh):
    in_specs = (
        P("ex", "ey", "ez", None, None),
        P("ex", "ey", "ez", None),
        P(),
        P(),
        P(),
        P(),
        P(),
        P(),
        P(None, "ex", "ey", "ez"),
        P(None, "ex", "ey", "ez"),
    )
    out_specs = P("ex", "ey", "ez", None, None)
    return jax.shard_map(body, mesh=mesh, in_specs=in_specs, out_specs=out_specs, check_vma=False)
```

```python
import functools

import jax
import jax.numpy as jnp
from jax import lax
from jax.experimental import pallas as pl
from jax.experimental.pallas import tpu as pltpu
import numpy as np
from jax.sharding import PartitionSpec as P

FACE_SIDE = 8
FACE = FACE_SIDE * FACE_SIDE
WIDTH = 2 * FACE
AXES = ("ex", "ey", "ez")
TURNS = ((1, 1), (0, 1), (0, 0), (1, 0), (2, 1), (2, 0))
EARLY = 1
LATE = (0, 2)
VMEM_LIMIT = 24 * 1024 * 1024


class Layout:
    def __init__(self, counts, species, sizes):
        self.counts = counts
        self.species = species
        self.sizes = sizes

    def elements(self):
        spans = [range(count) for count in self.counts]
        return [(i, j, k) for i in spans[0] for j in spans[1] for k in spans[2]]

    def number(self, element):
        return (element[0] * self.counts[1] + element[1]) * self.counts[2] + element[2]

    def rows(self, element):
        start = self.number(element) * self.species
        return slice(start, start + self.species)

    def layer(self, dim, position):
        return [element for element in self.elements() if element[dim] == position]

    def pairs(self, dim):
        return (len(self.layer(dim, 0)) + 1) // 2

    def pair_rows(self, pair):
        return slice(pair * self.species, (pair + 1) * self.species)

    def turns(self, dims=(0, 1, 2)):
        return [
            (dim, parity) for dim, parity in TURNS if dim in dims and self.sizes[dim] > 1 + parity
        ]

    def sides(self, dim):
        return self.layer(dim, 0), self.layer(dim, self.counts[dim] - 1)

    def message(self, dim):
        return jax.ShapeDtypeStruct((self.pairs(dim) * self.species, WIDTH), jnp.float32)


def columns(dim):
    return slice(dim * WIDTH, (dim + 1) * WIDTH)


def lanes(layout):
    return lax.broadcasted_iota(jnp.int32, (layout.species, WIDTH), 1)


def picked(value, index):
    return jnp.take_along_axis(value, index, axis=1, mode="promise_in_bounds")


def flip_mask(code):
    reach = FACE_SIDE - 1
    return (code & 1) * (reach * FACE_SIDE) + (code >> 1) * reach


def places():
    return [lax.axis_index(axis) for axis in AXES]


def pack(layout, here, dim, load_block, mask_of, outs):
    turns = [(turn, out) for turn, out in zip(layout.turns(), outs) if turn[0] == dim]
    if not turns:
        return
    lane = lanes(layout)
    low = lane < FACE
    even = (here[dim] & 1) == 0
    first = layout.layer(dim, 0)
    last = layout.layer(dim, layout.counts[dim] - 1)
    for pair in range(layout.pairs(dim)):
        sides = []
        for half in range(2):
            where = min(2 * pair + half, len(first) - 1)
            upper = load_block(last[where], dim)
            lower = load_block(first[where], dim)
            lower = picked(lower, lane ^ mask_of(first[where], dim) ^ (half * FACE))
            if half == 0:
                upper = pltpu.roll(upper, FACE, 1)
            sides.append((upper, lower))
        up = jnp.where(low, sides[0][0], sides[1][0])
        down = jnp.where(low, sides[0][1], sides[1][1])
        for (_, parity), out in turns:
            is_lower = even if parity == 0 else jnp.logical_not(even)
            out[layout.pair_rows(pair), :] = jnp.where(is_lower, up, down)


def received(layout, here, dim, messages):
    even = (here[dim] & 1) == 0
    at_start = here[dim] == 0
    at_end = here[dim] == layout.sizes[dim] - 1
    zero = jnp.zeros((layout.species, WIDTH), jnp.float32)
    found = []
    for pair in range(layout.pairs(dim)):
        first, second = [
            messages[dim, parity][layout.pair_rows(pair), :] if (dim, parity) in messages else zero
            for parity in range(2)
        ]
        below = jnp.where(at_start, 0.0, jnp.where(even, second, first))
        above = jnp.where(at_end, 0.0, jnp.where(even, first, second))
        found.append((below, above))
    return found


def unpacked(lane, outside, where, mask):
    below, above = outside[where // 2]
    half = (where % 2) * FACE
    inside = lane & (FACE - 1)
    return picked(below, (inside ^ mask) + half), picked(above, inside + half)


def assemble(layout, here, dim, load_block, messages, mask_of, keep_of, emit, slab=None):
    lane = lanes(layout)
    low = lane < FACE
    count = layout.counts[dim]
    outside = None if messages is None else received(layout, here, dim, messages)
    zero = jnp.zeros((layout.species, WIDTH), jnp.float32)
    for where, start in enumerate(layout.layer(dim, 0)):
        if slab not in (None, start[0]):
            continue
        line = [start[:dim] + (step,) + start[dim + 1 :] for step in range(count)]
        blocks = [load_block(element, dim) for element in line]
        if outside is None:
            from_below, from_above = zero, zero
        else:
            from_below, from_above = unpacked(lane, outside, where, mask_of(start, dim))
        turned = [from_below]
        for step, element in list(enumerate(line))[1:]:
            shared = jnp.where(low, blocks[step], blocks[step - 1])
            turned.append(picked(shared, lane ^ mask_of(element, dim) ^ FACE))
        turned.append(from_above)
        for step, element in enumerate(line):
            value = blocks[step] + jnp.where(low, turned[step], turned[step + 1])
            if step in (0, count - 1):
                value = value * keep_of(element, dim)
            emit(element, value)


def halves(value):
    high = value.astype(jnp.bfloat16)
    return high, (value - high.astype(jnp.float32)).astype(jnp.bfloat16)


def dot(left, right, contract=((1,), (0,))):
    return lax.dot_general(left, right, (contract, ((), ())), preferred_element_type=jnp.float32)


def split_dot(left, right, contract):
    left_high, left_rest = halves(left)
    right_high, right_rest = halves(right)
    return (
        dot(left_high, right_high, contract)
        + dot(left_high, right_rest, contract)
        + dot(left_rest, right_high, contract)
    )


def stacked(value, local, early, faces):
    high, rest = halves(value)
    for out, dims in ((local, LATE), (early, (EARLY,))):
        size = len(dims) * WIDTH
        for part, piece in enumerate((high, rest, high)):
            for place, dim in enumerate(dims):
                start = part * size + place * WIDTH
                out[start : start + WIDTH, :] = piece[columns(dim), :]
    for number in range(faces.shape[0]):
        start = LATE[number // 2] * WIDTH + (number % 2) * FACE
        rows = slice(start, start + FACE)
        for part, piece in enumerate((high, high, rest)):
            faces[number, part * FACE : (part + 1) * FACE, :] = piece[rows, :]
        faces[number, 3 * FACE :, :] = jnp.zeros((FACE, value.shape[1]), jnp.bfloat16)


def matrices_kernel(fine, inverse, four, coarse_four, two, coarse_two, *refs):
    *outs, right, left = refs
    stacked(fine[...], *outs[:3])
    right[...] = jnp.zeros_like(right)
    left[...] = jnp.zeros_like(left)
    start = 0
    for prolong, coarse in ((four, coarse_four), (two, coarse_two)):
        rows = slice(start, start + prolong.shape[0])
        left[rows, :] = prolong[...]
        right[rows, :] = split_dot(coarse[...], prolong[...], ((1,), (0,)))
        start += rounded(prolong.shape[0])
    corrections = split_dot(left[...], right[...], ((0,), (0,)))
    stacked(0.5 * (inverse[...] + corrections), *outs[3:])


def rounded(count):
    return (count + 7) // 8 * 8


def first_kernel(layout, load, orient, boundary, *refs):
    turns = len(layout.turns())
    weights, refs = refs[:4], refs[4:]
    outs, (masks, keeps), fetched, refs = refs[:turns], refs[turns : turns + 2], *cut_at(refs, turns)
    staged, codes, fixed, arrived = refs
    small = [
        pltpu.make_async_copy(source, target, arrived.at[number])
        for number, (source, target) in enumerate(((orient, codes), (boundary, fixed)))
    ]
    strips = [
        pltpu.make_async_copy(
            load.at[:, columns(dim)], staged.at[:, columns(dim)], arrived.at[2 + dim]
        )
        for dim in range(3)
    ]
    fetches = [
        pltpu.make_async_copy(source, target, arrived.at[5 + number])
        for number, (source, target) in enumerate(zip(weights, fetched))
    ]
    for copy in small + strips + fetches:
        copy.start()
    here = places()
    for copy in small:
        copy.wait()
    tabulate(layout, here, codes, fixed, masks, keeps)
    for dim in range(3):
        strips[dim].wait()
        pack(
            layout,
            here,
            dim,
            lambda element, dim: staged[layout.rows(element), columns(dim)],
            table(layout, masks),
            outs,
        )
    for copy in fetches:
        copy.wait()


def cut_at(refs, turns):
    return refs[turns + 2 : turns + 6], refs[turns + 6 :]


def tabulate(layout, here, codes, boundary, masks, keeps):
    low = lax.broadcasted_iota(jnp.int32, (1, WIDTH), 1) < FACE
    for element in layout.elements():
        number = layout.number(element)
        for dim in range(3):
            mask = flip_mask(codes[(dim,) + element])
            masks[number : number + 1, columns(dim)] = jnp.full((1, WIDTH), mask, jnp.int32)
            at_start = (here[dim] == 0) & (element[dim] == 0)
            at_end = (here[dim] == layout.sizes[dim] - 1) & (element[dim] == layout.counts[dim] - 1)
            fixed_low = jnp.where(at_start, boundary[element + (2 * dim,)], 0)
            fixed_top = jnp.where(at_end, boundary[element + (2 * dim + 1,)], 0)
            fixed = jnp.where(low, fixed_low, fixed_top)
            keeps[number : number + 1, columns(dim)] = 1.0 - fixed.astype(jnp.float32)


def table(layout, ref):
    def row(element, dim):
        number = layout.number(element)
        return ref[number : number + 1, columns(dim)]

    return row


def scales(layout, kind, ref):
    def row(element, dim):
        value = ref[element[0], element[1], element[2] : element[2] + 1, columns(dim)]
        return value if kind == "operator" else 1.0 / value

    return row


def put_split(split, rows, place, count, value):
    high, rest = halves(value)
    for part, piece in enumerate((high, high, rest)):
        start = (part * count + place) * WIDTH
        split[rows, start : start + WIDTH] = piece


def taken(layout, dims, refs):
    turns = layout.turns(dims)
    return dict(zip(turns, refs)), refs[len(turns) :]


def combined(kind, begun, result):
    if begun is None:
        return result
    return begun - result if kind == "operator" else begun + result


def strips_kernel(layout, kind, dims, local, value, *refs):
    messages, refs = (None, refs) if local else taken(layout, dims, refs)
    masks, keeps, scaling, matrix, *before, out, split, summed = refs
    begun = before[0] if before else None
    here = places()
    factor = scales(layout, kind, scaling)

    def assembled(place, slab):
        dim = dims[place]

        def emit(element, result):
            scaled = result * factor(element, dim)
            put_split(split, layout.rows(element), place, len(dims), scaled)

        assemble(
            layout,
            here,
            dim,
            lambda element, dim: value[layout.rows(element), columns(dim)],
            messages,
            table(layout, masks),
            table(layout, keeps),
            emit,
            slab,
        )

    if 0 in dims:
        assembled(dims.index(0), None)
    count = layout.counts[0]
    height = value.shape[0] // count
    for slab in range(count):
        for place, dim in enumerate(dims):
            if dim != 0:
                assembled(place, slab)
        rows = slice(slab * height, (slab + 1) * height)
        summed[rows, :] = dot(split[rows, :], matrix[...])
        for element in layout.layer(0, slab):
            for each in range(3):
                at = (layout.rows(element), columns(each))
                result = summed[at] * factor(element, each)
                out[at] = combined(kind, None if begun is None else begun[at], result)


def combined(kind, begun, result):
    if begun is None:
        return result
    return begun - result if kind == "operator" else begun + result


def outside_faces(layout, here, messages, masks):
    lane = lanes(layout)
    for order, dim in enumerate(LATE):
        outside = received(layout, here, dim, messages)
        lower, upper = layout.sides(dim)
        for where, element in enumerate(lower):
            mask = table(layout, masks)(element, dim)
            from_below, from_above = unpacked(lane, outside, where, mask)
            yield 2 * order, where, element, from_below
            yield 2 * order + 1, where, upper[where], from_above


def faces_kernel(layout, kind, *refs):
    messages, refs = taken(layout, LATE, refs)
    masks, scaling, faces, begun, *refs = refs
    turns = len(layout.turns())
    out, sent, scratch = refs[0], refs[1 : 1 + turns], refs[1 + turns :]
    splits, sums = scratch[:4], scratch[4:]
    here = places()
    factor = scales(layout, kind, scaling)
    lane = lanes(layout)
    low = lane < FACE
    row_low = low[:1]

    def both(row, side):
        turned = pltpu.roll(row, FACE, 1)
        return jnp.where(row_low, turned, row) if side else jnp.where(row_low, row, turned)

    share = {}
    for number, where, element, face in outside_faces(layout, here, messages, masks):
        value = face * both(factor(element, LATE[number // 2]), number % 2)
        high = value.astype(jnp.bfloat16).astype(jnp.float32)
        rows = layout.pair_rows(where)
        splits[number][rows, :WIDTH] = jnp.where(low, high, value - high).astype(jnp.bfloat16)
        splits[number][rows, WIDTH:] = jnp.where(low, high, 0.0).astype(jnp.bfloat16)
        share.setdefault(element, []).append((number, rows))
    for number in range(4):
        sums[number][...] = dot(splits[number][...], faces[number])
    for element in layout.elements():
        for dim in range(3):
            at = (layout.rows(element), columns(dim))
            parts = [sums[number][rows, columns(dim)] for number, rows in share.get(element, ())]
            if parts:
                result = sum(parts[1:], parts[0]) * factor(element, dim)
                out[at] = combined(kind, begun[at], result)
            else:
                out[at] = begun[at]
    for dim in range(3):
        pack(
            layout,
            here,
            dim,
            lambda element, dim: out[layout.rows(element), columns(dim)],
            table(layout, masks),
            sent,
        )


def last_early_kernel(layout, value, *refs):
    messages, (masks, keeps, ready) = taken(layout, (EARLY,), refs)

    for dim in range(3):

        def emit(element, result):
            ready[layout.rows(element), columns(dim)] = result

        assemble(
            layout,
            places(),
            dim,
            lambda element, dim: value[layout.rows(element), columns(dim)],
            messages if dim == EARLY else None,
            table(layout, masks),
            table(layout, keeps),
            emit,
        )


def last_late_kernel(layout, begun, *refs):
    messages, (masks, out, ready, left) = taken(layout, LATE, refs)
    low = lanes(layout) < FACE

    def copy(source, dim):
        return pltpu.make_async_copy(
            source.at[:, columns(dim)], out.at[:, columns(dim)], left.at[dim]
        )

    started = [copy(begun, EARLY)]
    started[0].start()
    faces = {}
    for number, _, element, face in outside_faces(layout, places(), messages, masks):
        faces[element, number] = face
    for order, dim in enumerate(LATE):
        for element in layout.elements():
            at = (layout.rows(element), columns(dim))
            value = begun[at]
            lower = faces.get((element, 2 * order))
            upper = faces.get((element, 2 * order + 1))
            if lower is not None:
                value += jnp.where(low, lower, 0.0)
            if upper is not None:
                value += jnp.where(low, 0.0, upper)
            ready[at] = value
        started.append(copy(ready, dim))
        started[-1].start()
    for each in started:
        each.wait()


def in_vmem(count):
    return [pl.BlockSpec(memory_space=pltpu.VMEM)] * count


def in_hbm(count):
    return [pl.BlockSpec(memory_space=pltpu.HBM)] * count


PARAMS = pltpu.CompilerParams(vmem_limit_bytes=VMEM_LIMIT)


def kept_in_hbm(*values):
    return [pltpu.with_memory_space_constraint(value, pltpu.HBM) for value in values]


def cost(flops, size):
    return pl.CostEstimate(flops=flops, bytes_accessed=size, transcendentals=0)


def partners(layout, dim, parity):
    sizes = layout.sizes
    swap = {}
    for place in np.ndindex(*sizes):
        other = list(place)
        lower = place[dim] % 2 == parity
        at = place[dim] + (1 if lower else -1)
        if 0 <= at < sizes[dim]:
            other[dim] = at
        elif dim != 1 and sizes[1] % 2 == 0:
            other[1] = place[1] ^ 1
        elif sizes[dim] % 2 == 0:
            other[dim] = sizes[dim] - 1 - place[dim]
        swap[place] = tuple(other)
    return [
        (int(np.ravel_multi_index(place, sizes)), int(np.ravel_multi_index(other, sizes)))
        for place, other in swap.items()
    ]


def exchange(layout, messages):
    return {
        turn: lax.ppermute(message, AXES, partners(layout, *turn))
        for turn, message in zip(layout.turns(), messages)
    }


def body(
    load_raw,
    scaling,
    fine_matrix,
    fine_inverse,
    prolong_four,
    coarse_four,
    prolong_two,
    coarse_two,
    orient,
    boundary,
):
    counts, species, nodes = load_raw.shape[:3], load_raw.shape[3], load_raw.shape[4]
    layout = Layout(counts, species, tuple(lax.axis_size(axis) for axis in AXES))
    load = load_raw.reshape(-1, nodes)
    rows = load.shape[0]
    turns = layout.turns()
    message_shapes = tuple(layout.message(dim) for dim, _ in turns)
    whole = jax.ShapeDtypeStruct(load.shape, jnp.float32)
    matrix_shapes = tuple(
        jax.ShapeDtypeStruct(shape, jnp.bfloat16)
        for shape in (
            (3 * len(LATE) * WIDTH, nodes),
            (3 * WIDTH, nodes),
            (2 * len(LATE), 4 * FACE, nodes),
        )
    )
    elements = len(layout.elements())
    tables = tuple(jax.ShapeDtypeStruct((elements, nodes), kind) for kind in (jnp.int32, jnp.float32))
    weights = (prolong_four.T, coarse_four, prolong_two.T, coarse_two)
    sides = jnp.transpose(boundary, (1, 2, 3, 0))

    sent = pl.pallas_call(
        functools.partial(first_kernel, layout),
        out_shape=message_shapes
        + tables
        + tuple(jax.ShapeDtypeStruct(weight.shape, weight.dtype) for weight in weights),
        in_specs=in_hbm(7),
        out_specs=tuple(in_vmem(len(turns) + 6)),
        scratch_shapes=[
            pltpu.VMEM(load.shape, jnp.float32),
            pltpu.SMEM(orient.shape, jnp.int32),
            pltpu.SMEM(sides.shape, jnp.int32),
            pltpu.SemaphoreType.DMA((9,)),
        ],
        compiler_params=PARAMS,
        name="pack",
    )(*kept_in_hbm(load, orient, sides, *weights))
    masks, keeps, *weights = sent[len(turns) :]

    stack = (rounded(prolong_four.shape[1]) + rounded(prolong_two.shape[1]), nodes)
    matrices = pl.pallas_call(
        matrices_kernel,
        out_shape=matrix_shapes * 2,
        in_specs=in_vmem(6),
        out_specs=tuple(in_vmem(6)),
        scratch_shapes=[pltpu.VMEM(stack, jnp.float32), pltpu.VMEM(stack, jnp.float32)],
        compiler_params=PARAMS,
        cost_estimate=cost(2 * nodes * nodes * nodes, 8 * nodes * nodes),
        name="matrices",
    )(fine_matrix, fine_inverse, *weights)
    operator, smoother = matrices[:3], matrices[3:]

    def stage(kind, value, messages, matrix, begun):
        for dims, local, factor in ((LATE, True, matrix[0]), ((EARLY,), False, matrix[1])):
            mine = [] if local else [messages[turn] for turn in layout.turns(dims)]
            before = () if begun is None else (begun,)
            begun = pl.pallas_call(
                functools.partial(strips_kernel, layout, kind, dims, local),
                out_shape=whole,
                in_specs=in_vmem(5 + len(mine) + len(before)),
                out_specs=in_vmem(1)[0],
                scratch_shapes=[
                    pltpu.VMEM((rows, factor.shape[0]), jnp.bfloat16),
                    pltpu.VMEM(load.shape, jnp.float32),
                ],
                compiler_params=PARAMS,
                cost_estimate=cost(2 * rows * factor.shape[0] * nodes, 8 * rows * nodes),
                name=kind + ("_local" if local else "_early"),
            )(value, *mine, masks, keeps, scaling, factor, *before)
        mine = [messages[turn] for turn in layout.turns(LATE)]
        heights = [len(side) * species for dim in LATE for side in layout.sides(dim)]
        result, *sent = pl.pallas_call(
            functools.partial(faces_kernel, layout, kind),
            out_shape=(whole,) + message_shapes,
            in_specs=in_vmem(4 + len(mine)),
            out_specs=tuple(in_vmem(1 + len(turns))),
            scratch_shapes=[pltpu.VMEM((height, 4 * FACE), jnp.bfloat16) for height in heights]
            + [pltpu.VMEM((height, nodes), jnp.float32) for height in heights],
            compiler_params=PARAMS,
            cost_estimate=cost(8 * FACE * sum(heights) * nodes, 12 * rows * nodes),
            name=kind + "_faces",
        )(*mine, masks, scaling, matrix[2], begun)
        return result, sent

    first, sent = stage("smooth", load, exchange(layout, sent), smoother, None)
    left, sent = stage("operator", first, exchange(layout, sent), operator, load)
    total, sent = stage("smooth_more", left, exchange(layout, sent), smoother, first)
    messages = exchange(layout, sent)
    early = [messages[turn] for turn in layout.turns((EARLY,))]
    late = [messages[turn] for turn in layout.turns(LATE)]
    begun = pl.pallas_call(
        functools.partial(last_early_kernel, layout),
        out_shape=whole,
        in_specs=in_vmem(3 + len(early)),
        out_specs=in_vmem(1)[0],
        compiler_params=PARAMS,
        cost_estimate=cost(0, 8 * rows * nodes),
        name="last_early",
    )(total, *early, masks, keeps)
    result = pl.pallas_call(
        functools.partial(last_late_kernel, layout),
        out_shape=whole,
        in_specs=in_vmem(2 + len(late)),
        out_specs=in_hbm(1)[0],
        scratch_shapes=[pltpu.VMEM((rows, nodes), jnp.float32), pltpu.SemaphoreType.DMA((3,))],
        compiler_params=PARAMS,
        cost_estimate=cost(0, 8 * rows * nodes),
        name="last_late",
    )(begun, *late, masks)
    return result.reshape(load_raw.shape)


def solution(mesh):
    in_specs = (
        P("ex", "ey", "ez", None, None),
        P("ex", "ey", "ez", None),
        P(),
        P(),
        P(),
        P(),
        P(),
        P(),
        P(None, "ex", "ey", "ez"),
        P(None, "ex", "ey", "ez"),
    )
    out_specs = P("ex", "ey", "ez", None, None)
    return jax.shard_map(body, mesh=mesh, in_specs=in_specs, out_specs=out_specs, check_vma=False)
```

```python
import functools

import jax
import jax.numpy as jnp
from jax import lax
from jax.experimental import pallas as pl
from jax.experimental.pallas import tpu as pltpu
import numpy as np
from jax.sharding import PartitionSpec as P

FACE_SIDE = 8
FACE = FACE_SIDE * FACE_SIDE
WIDTH = 2 * FACE
AXES = ("ex", "ey", "ez")
TURNS = ((0, 1), (0, 0), (1, 1), (2, 1), (2, 0), (1, 0))
EARLY = 0
LATE = (1, 2)
VMEM_LIMIT = 24 * 1024 * 1024


class Layout:
    def __init__(self, counts, species, sizes):
        self.counts = counts
        self.species = species
        self.sizes = sizes

    def elements(self):
        spans = [range(count) for count in self.counts]
        return [(i, j, k) for i in spans[0] for j in spans[1] for k in spans[2]]

    def number(self, element):
        return (element[0] * self.counts[1] + element[1]) * self.counts[2] + element[2]

    def rows(self, element):
        start = self.number(element) * self.species
        return slice(start, start + self.species)

    def layer(self, dim, position):
        return [element for element in self.elements() if element[dim] == position]

    def pairs(self, dim):
        return (len(self.layer(dim, 0)) + 1) // 2

    def pair_rows(self, pair):
        return slice(pair * self.species, (pair + 1) * self.species)

    def turns(self, dims=(0, 1, 2)):
        return [
            (dim, parity) for dim, parity in TURNS if dim in dims and self.sizes[dim] > 1 + parity
        ]

    def sides(self, dim):
        return self.layer(dim, 0), self.layer(dim, self.counts[dim] - 1)

    def message(self):
        pairs = max(self.pairs(dim) for dim in range(3))
        return jax.ShapeDtypeStruct((pairs * self.species, WIDTH), jnp.float32)


def columns(dim):
    return slice(dim * WIDTH, (dim + 1) * WIDTH)


def lanes(layout):
    return lax.broadcasted_iota(jnp.int32, (layout.species, WIDTH), 1)


def picked(value, index):
    return jnp.take_along_axis(value, index, axis=1, mode="promise_in_bounds")


def flip_mask(code):
    reach = FACE_SIDE - 1
    return (code & 1) * (reach * FACE_SIDE) + (code >> 1) * reach


def places():
    return [lax.axis_index(axis) for axis in AXES]


def pack(layout, here, dim, load_block, mask_of, outs):
    turns = [(turn, out) for turn, out in zip(layout.turns(), outs) if turn[0] == dim]
    if not turns:
        return
    lane = lanes(layout)
    low = lane < FACE
    even = (here[dim] & 1) == 0
    first = layout.layer(dim, 0)
    last = layout.layer(dim, layout.counts[dim] - 1)
    used = layout.pairs(dim) * layout.species
    for _, out in turns:
        if used < out.shape[0]:
            out[used:, :] = jnp.zeros((out.shape[0] - used, WIDTH), jnp.float32)
    for pair in range(layout.pairs(dim)):
        sides = []
        for half in range(2):
            where = min(2 * pair + half, len(first) - 1)
            upper = load_block(last[where], dim)
            lower = load_block(first[where], dim)
            lower = picked(lower, lane ^ mask_of(first[where], dim) ^ (half * FACE))
            if half == 0:
                upper = pltpu.roll(upper, FACE, 1)
            sides.append((upper, lower))
        up = jnp.where(low, sides[0][0], sides[1][0])
        down = jnp.where(low, sides[0][1], sides[1][1])
        for (_, parity), out in turns:
            is_lower = even if parity == 0 else jnp.logical_not(even)
            out[layout.pair_rows(pair), :] = jnp.where(is_lower, up, down)


def received(layout, here, dim, messages):
    even = (here[dim] & 1) == 0
    at_start = here[dim] == 0
    at_end = here[dim] == layout.sizes[dim] - 1
    zero = jnp.zeros((layout.species, WIDTH), jnp.float32)
    found = []
    for pair in range(layout.pairs(dim)):
        first, second = [
            messages[dim, parity][layout.pair_rows(pair), :] if (dim, parity) in messages else zero
            for parity in range(2)
        ]
        below = jnp.where(at_start, 0.0, jnp.where(even, second, first))
        above = jnp.where(at_end, 0.0, jnp.where(even, first, second))
        found.append((below, above))
    return found


def unpacked(lane, outside, where, mask):
    below, above = outside[where // 2]
    half = (where % 2) * FACE
    inside = lane & (FACE - 1)
    return picked(below, (inside ^ mask) + half), picked(above, inside + half)


def assemble(layout, here, dim, load_block, messages, mask_of, keep_of, emit, slab=None):
    lane = lanes(layout)
    low = lane < FACE
    count = layout.counts[dim]
    outside = None if messages is None else received(layout, here, dim, messages)
    zero = jnp.zeros((layout.species, WIDTH), jnp.float32)
    for where, start in enumerate(layout.layer(dim, 0)):
        if slab not in (None, start[0]):
            continue
        line = [start[:dim] + (step,) + start[dim + 1 :] for step in range(count)]
        blocks = [load_block(element, dim) for element in line]
        if outside is None:
            from_below, from_above = zero, zero
        else:
            from_below, from_above = unpacked(lane, outside, where, mask_of(start, dim))
        turned = [from_below]
        for step, element in list(enumerate(line))[1:]:
            shared = jnp.where(low, blocks[step], blocks[step - 1])
            turned.append(picked(shared, lane ^ mask_of(element, dim) ^ FACE))
        turned.append(from_above)
        for step, element in enumerate(line):
            value = blocks[step] + jnp.where(low, turned[step], turned[step + 1])
            if step in (0, count - 1):
                value = value * keep_of(element, dim)
            emit(element, value)


def halves(value):
    high = value.astype(jnp.bfloat16)
    return high, (value - high.astype(jnp.float32)).astype(jnp.bfloat16)


def dot(left, right, contract=((1,), (0,))):
    return lax.dot_general(left, right, (contract, ((), ())), preferred_element_type=jnp.float32)


def split_dot(left, right, contract):
    left_high, left_rest = halves(left)
    right_high, right_rest = halves(right)
    return (
        dot(left_high, right_high, contract)
        + dot(left_high, right_rest, contract)
        + dot(left_rest, right_high, contract)
    )


def stacked(value, local, early, faces):
    high, rest = halves(value)
    for out, dims in ((local, LATE), (early, (EARLY,))):
        size = len(dims) * WIDTH
        for part, piece in enumerate((high, rest, high)):
            for place, dim in enumerate(dims):
                start = part * size + place * WIDTH
                out[start : start + WIDTH, :] = piece[columns(dim), :]
    for number in range(faces.shape[0]):
        start = LATE[number // 2] * WIDTH + (number % 2) * FACE
        rows = slice(start, start + FACE)
        for part, piece in enumerate((high, high, rest)):
            faces[number, part * FACE : (part + 1) * FACE, :] = piece[rows, :]
        faces[number, 3 * FACE :, :] = jnp.zeros((FACE, value.shape[1]), jnp.bfloat16)


def operator_kernel(fine, *outs):
    stacked(fine[...], *outs)


def smoother_kernel(inverse, four, coarse_four, two, coarse_two, *refs):
    *outs, right, left = refs
    right[...] = jnp.zeros_like(right)
    left[...] = jnp.zeros_like(left)
    start = 0
    for prolong, coarse in ((four, coarse_four), (two, coarse_two)):
        rows = slice(start, start + prolong.shape[0])
        left[rows, :] = prolong[...]
        right[rows, :] = split_dot(coarse[...], prolong[...], ((1,), (0,)))
        start += rounded(prolong.shape[0])
    corrections = split_dot(left[...], right[...], ((0,), (0,)))
    stacked(0.5 * (inverse[...] + corrections), *outs)


def rounded(count):
    return (count + 7) // 8 * 8


def first_kernel(layout, load, orient, boundary, *refs):
    turns = len(layout.turns())
    weights, refs = refs[:4], refs[4:]
    outs, (masks, keeps), fetched, refs = refs[:turns], refs[turns : turns + 2], *cut_at(refs, turns)
    staged, codes, fixed, arrived = refs
    small = [
        pltpu.make_async_copy(source, target, arrived.at[number])
        for number, (source, target) in enumerate(((orient, codes), (boundary, fixed)))
    ]
    strips = [
        pltpu.make_async_copy(
            load.at[:, columns(dim)], staged.at[:, columns(dim)], arrived.at[2 + dim]
        )
        for dim in range(3)
    ]
    fetches = [
        pltpu.make_async_copy(source, target, arrived.at[5 + number])
        for number, (source, target) in enumerate(zip(weights, fetched))
    ]
    for copy in small + strips + fetches:
        copy.start()
    here = places()
    for copy in small:
        copy.wait()
    tabulate(layout, here, codes, fixed, masks, keeps)
    for dim in range(3):
        strips[dim].wait()
        pack(
            layout,
            here,
            dim,
            lambda element, dim: staged[layout.rows(element), columns(dim)],
            table(layout, masks),
            outs,
        )
    for copy in fetches:
        copy.wait()


def cut_at(refs, turns):
    return refs[turns + 2 : turns + 6], refs[turns + 6 :]


def tabulate(layout, here, codes, boundary, masks, keeps):
    low = lax.broadcasted_iota(jnp.int32, (1, WIDTH), 1) < FACE
    for element in layout.elements():
        number = layout.number(element)
        for dim in range(3):
            mask = flip_mask(codes[(dim,) + element])
            masks[number : number + 1, columns(dim)] = jnp.full((1, WIDTH), mask, jnp.int32)
            at_start = (here[dim] == 0) & (element[dim] == 0)
            at_end = (here[dim] == layout.sizes[dim] - 1) & (element[dim] == layout.counts[dim] - 1)
            fixed_low = jnp.where(at_start, boundary[element + (2 * dim,)], 0)
            fixed_top = jnp.where(at_end, boundary[element + (2 * dim + 1,)], 0)
            fixed = jnp.where(low, fixed_low, fixed_top)
            keeps[number : number + 1, columns(dim)] = 1.0 - fixed.astype(jnp.float32)


def table(layout, ref):
    def row(element, dim):
        number = layout.number(element)
        return ref[number : number + 1, columns(dim)]

    return row


def scales(layout, kind, ref):
    def row(element, dim):
        value = ref[element[0], element[1], element[2] : element[2] + 1, columns(dim)]
        return value if kind == "operator" else 1.0 / value

    return row


def put_split(split, rows, place, count, value):
    high, rest = halves(value)
    for part, piece in enumerate((high, high, rest)):
        start = (part * count + place) * WIDTH
        split[rows, start : start + WIDTH] = piece


def taken(layout, dims, refs):
    turns = layout.turns(dims)
    return dict(zip(turns, refs)), refs[len(turns) :]


def combined(kind, begun, result):
    if begun is None:
        return result
    return begun - result if kind == "operator" else begun + result


def strips_kernel(layout, kind, dims, local, value, *refs):
    messages, refs = (None, refs) if local else taken(layout, dims, refs)
    masks, keeps, scaling, matrix, *before, out, split, summed = refs
    begun = before[0] if before else None
    here = places()
    factor = scales(layout, kind, scaling)

    def assembled(place, slab):
        dim = dims[place]

        def emit(element, result):
            scaled = result * factor(element, dim)
            put_split(split, layout.rows(element), place, len(dims), scaled)

        assemble(
            layout,
            here,
            dim,
            lambda element, dim: value[layout.rows(element), columns(dim)],
            messages,
            table(layout, masks),
            table(layout, keeps),
            emit,
            slab,
        )

    if 0 in dims:
        assembled(dims.index(0), None)
    count = layout.counts[0]
    height = value.shape[0] // count
    for slab in range(count):
        for place, dim in enumerate(dims):
            if dim != 0:
                assembled(place, slab)
        rows = slice(slab * height, (slab + 1) * height)
        summed[rows, :] = dot(split[rows, :], matrix[...])
        for element in layout.layer(0, slab):
            for each in range(3):
                at = (layout.rows(element), columns(each))
                result = summed[at] * factor(element, each)
                out[at] = combined(kind, None if begun is None else begun[at], result)


def combined(kind, begun, result):
    if begun is None:
        return result
    return begun - result if kind == "operator" else begun + result


def outside_faces(layout, here, messages, masks):
    lane = lanes(layout)
    for order, dim in enumerate(LATE):
        outside = received(layout, here, dim, messages)
        lower, upper = layout.sides(dim)
        for where, element in enumerate(lower):
            mask = table(layout, masks)(element, dim)
            from_below, from_above = unpacked(lane, outside, where, mask)
            yield 2 * order, where, element, from_below
            yield 2 * order + 1, where, upper[where], from_above


def faces_kernel(layout, kind, *refs):
    messages, refs = taken(layout, LATE, refs)
    masks, scaling, faces, begun, *refs = refs
    turns = len(layout.turns())
    out, sent, scratch = refs[0], refs[1 : 1 + turns], refs[1 + turns :]
    splits, sums = scratch[:4], scratch[4:]
    here = places()
    factor = scales(layout, kind, scaling)
    lane = lanes(layout)
    low = lane < FACE
    row_low = low[:1]

    def both(row, side):
        turned = pltpu.roll(row, FACE, 1)
        return jnp.where(row_low, turned, row) if side else jnp.where(row_low, row, turned)

    share = {}
    for number, where, element, face in outside_faces(layout, here, messages, masks):
        value = face * both(factor(element, LATE[number // 2]), number % 2)
        high = value.astype(jnp.bfloat16).astype(jnp.float32)
        rows = layout.pair_rows(where)
        splits[number][rows, :WIDTH] = jnp.where(low, high, value - high).astype(jnp.bfloat16)
        splits[number][rows, WIDTH:] = jnp.where(low, high, 0.0).astype(jnp.bfloat16)
        share.setdefault(element, []).append((number, rows))
    for number in range(4):
        sums[number][...] = dot(splits[number][...], faces[number])
    for element in layout.elements():
        for dim in range(3):
            at = (layout.rows(element), columns(dim))
            parts = [sums[number][rows, columns(dim)] for number, rows in share.get(element, ())]
            if parts:
                result = sum(parts[1:], parts[0]) * factor(element, dim)
                out[at] = combined(kind, begun[at], result)
            else:
                out[at] = begun[at]
    for dim in range(3):
        pack(
            layout,
            here,
            dim,
            lambda element, dim: out[layout.rows(element), columns(dim)],
            table(layout, masks),
            sent,
        )


def last_early_kernel(layout, value, *refs):
    messages, (masks, keeps, ready) = taken(layout, (EARLY,), refs)

    for dim in range(3):

        def emit(element, result):
            ready[layout.rows(element), columns(dim)] = result

        assemble(
            layout,
            places(),
            dim,
            lambda element, dim: value[layout.rows(element), columns(dim)],
            messages if dim == EARLY else None,
            table(layout, masks),
            table(layout, keeps),
            emit,
        )


def last_late_kernel(layout, begun, *refs):
    messages, (masks, out, ready, left) = taken(layout, LATE, refs)
    low = lanes(layout) < FACE

    def copy(source, dim):
        return pltpu.make_async_copy(
            source.at[:, columns(dim)], out.at[:, columns(dim)], left.at[dim]
        )

    started = [copy(begun, EARLY)]
    started[0].start()
    faces = {}
    for number, _, element, face in outside_faces(layout, places(), messages, masks):
        faces[element, number] = face
    for order, dim in enumerate(LATE):
        for element in layout.elements():
            at = (layout.rows(element), columns(dim))
            value = begun[at]
            lower = faces.get((element, 2 * order))
            upper = faces.get((element, 2 * order + 1))
            if lower is not None:
                value += jnp.where(low, lower, 0.0)
            if upper is not None:
                value += jnp.where(low, 0.0, upper)
            ready[at] = value
        started.append(copy(ready, dim))
        started[-1].start()
    for each in started:
        each.wait()


def in_vmem(count):
    return [pl.BlockSpec(memory_space=pltpu.VMEM)] * count


def in_hbm(count):
    return [pl.BlockSpec(memory_space=pltpu.HBM)] * count


PARAMS = pltpu.CompilerParams(vmem_limit_bytes=VMEM_LIMIT)


def kept_in_hbm(*values):
    return [pltpu.with_memory_space_constraint(value, pltpu.HBM) for value in values]


def cost(flops, size):
    return pl.CostEstimate(flops=flops, bytes_accessed=size, transcendentals=0)


def partners(layout, dim, parity):
    sizes = layout.sizes
    swap = {}
    for place in np.ndindex(*sizes):
        other = list(place)
        lower = place[dim] % 2 == parity
        at = place[dim] + (1 if lower else -1)
        if 0 <= at < sizes[dim]:
            other[dim] = at
        elif dim != 1 and sizes[1] % 2 == 0:
            other[1] = place[1] ^ 1
        elif sizes[dim] % 2 == 0:
            other[dim] = sizes[dim] - 1 - place[dim]
        swap[place] = tuple(other)
    return [
        (int(np.ravel_multi_index(place, sizes)), int(np.ravel_multi_index(other, sizes)))
        for place, other in swap.items()
    ]


def exchange(layout, messages):
    return {
        turn: lax.ppermute(message, AXES, partners(layout, *turn))
        for turn, message in zip(layout.turns(), messages)
    }


def body(
    load_raw,
    scaling,
    fine_matrix,
    fine_inverse,
    prolong_four,
    coarse_four,
    prolong_two,
    coarse_two,
    orient,
    boundary,
):
    counts, species, nodes = load_raw.shape[:3], load_raw.shape[3], load_raw.shape[4]
    layout = Layout(counts, species, tuple(lax.axis_size(axis) for axis in AXES))
    load = load_raw.reshape(-1, nodes)
    rows = load.shape[0]
    turns = layout.turns()
    message_shapes = tuple(layout.message() for _ in turns)
    whole = jax.ShapeDtypeStruct(load.shape, jnp.float32)
    matrix_shapes = tuple(
        jax.ShapeDtypeStruct(shape, jnp.bfloat16)
        for shape in (
            (3 * len(LATE) * WIDTH, nodes),
            (3 * WIDTH, nodes),
            (2 * len(LATE), 4 * FACE, nodes),
        )
    )
    elements = len(layout.elements())
    tables = tuple(jax.ShapeDtypeStruct((elements, nodes), kind) for kind in (jnp.int32, jnp.float32))
    weights = (prolong_four.T, coarse_four, prolong_two.T, coarse_two)
    sides = jnp.transpose(boundary, (1, 2, 3, 0))

    sent = pl.pallas_call(
        functools.partial(first_kernel, layout),
        out_shape=message_shapes
        + tables
        + tuple(jax.ShapeDtypeStruct(weight.shape, weight.dtype) for weight in weights),
        in_specs=in_hbm(7),
        out_specs=tuple(in_vmem(len(turns) + 6)),
        scratch_shapes=[
            pltpu.VMEM(load.shape, jnp.float32),
            pltpu.SMEM(orient.shape, jnp.int32),
            pltpu.SMEM(sides.shape, jnp.int32),
            pltpu.SemaphoreType.DMA((9,)),
        ],
        compiler_params=PARAMS,
        name="pack",
    )(*kept_in_hbm(load, orient, sides, *weights))
    masks, keeps, *weights = sent[len(turns) :]

    stack = (rounded(prolong_four.shape[1]) + rounded(prolong_two.shape[1]), nodes)
    smoother = pl.pallas_call(
        smoother_kernel,
        out_shape=matrix_shapes,
        in_specs=in_vmem(5),
        out_specs=tuple(in_vmem(3)),
        scratch_shapes=[pltpu.VMEM(stack, jnp.float32), pltpu.VMEM(stack, jnp.float32)],
        compiler_params=PARAMS,
        cost_estimate=cost(2 * nodes * nodes * nodes, 8 * nodes * nodes),
        name="smoother",
    )(fine_inverse, *weights)
    operator = pl.pallas_call(
        operator_kernel,
        out_shape=matrix_shapes,
        in_specs=in_vmem(1),
        out_specs=tuple(in_vmem(3)),
        compiler_params=PARAMS,
        cost_estimate=cost(0, 10 * nodes * nodes),
        name="operator",
    )(fine_matrix)

    def stage(kind, value, messages, matrix, begun):
        for dims, local, factor in ((LATE, True, matrix[0]), ((EARLY,), False, matrix[1])):
            mine = [] if local else [messages[turn] for turn in layout.turns(dims)]
            before = () if begun is None else (begun,)
            begun = pl.pallas_call(
                functools.partial(strips_kernel, layout, kind, dims, local),
                out_shape=whole,
                in_specs=in_vmem(5 + len(mine) + len(before)),
                out_specs=in_vmem(1)[0],
                scratch_shapes=[
                    pltpu.VMEM((rows, factor.shape[0]), jnp.bfloat16),
                    pltpu.VMEM(load.shape, jnp.float32),
                ],
                compiler_params=PARAMS,
                cost_estimate=cost(2 * rows * factor.shape[0] * nodes, 8 * rows * nodes),
                name=kind + ("_local" if local else "_early"),
            )(value, *mine, masks, keeps, scaling, factor, *before)
        mine = [messages[turn] for turn in layout.turns(LATE)]
        heights = [len(side) * species for dim in LATE for side in layout.sides(dim)]
        result, *sent = pl.pallas_call(
            functools.partial(faces_kernel, layout, kind),
            out_shape=(whole,) + message_shapes,
            in_specs=in_vmem(4 + len(mine)),
            out_specs=tuple(in_vmem(1 + len(turns))),
            scratch_shapes=[pltpu.VMEM((height, 4 * FACE), jnp.bfloat16) for height in heights]
            + [pltpu.VMEM((height, nodes), jnp.float32) for height in heights],
            compiler_params=PARAMS,
            cost_estimate=cost(8 * FACE * sum(heights) * nodes, 12 * rows * nodes),
            name=kind + "_faces",
        )(*mine, masks, scaling, matrix[2], begun)
        return result, sent

    first, sent = stage("smooth", load, exchange(layout, sent), smoother, None)
    left, sent = stage("operator", first, exchange(layout, sent), operator, load)
    total, sent = stage("smooth_more", left, exchange(layout, sent), smoother, first)
    messages = exchange(layout, sent)
    early = [messages[turn] for turn in layout.turns((EARLY,))]
    late = [messages[turn] for turn in layout.turns(LATE)]
    begun = pl.pallas_call(
        functools.partial(last_early_kernel, layout),
        out_shape=whole,
        in_specs=in_vmem(3 + len(early)),
        out_specs=in_vmem(1)[0],
        compiler_params=PARAMS,
        cost_estimate=cost(0, 8 * rows * nodes),
        name="last_early",
    )(total, *early, masks, keeps)
    result = pl.pallas_call(
        functools.partial(last_late_kernel, layout),
        out_shape=whole,
        in_specs=in_vmem(2 + len(late)),
        out_specs=in_hbm(1)[0],
        scratch_shapes=[pltpu.VMEM((rows, nodes), jnp.float32), pltpu.SemaphoreType.DMA((3,))],
        compiler_params=PARAMS,
        cost_estimate=cost(0, 8 * rows * nodes),
        name="last_late",
    )(begun, *late, masks)
    return result.reshape(load_raw.shape)


def solution(mesh):
    in_specs = (
        P("ex", "ey", "ez", None, None),
        P("ex", "ey", "ez", None),
        P(),
        P(),
        P(),
        P(),
        P(),
        P(),
        P(None, "ex", "ey", "ez"),
        P(None, "ex", "ey", "ez"),
    )
    out_specs = P("ex", "ey", "ez", None, None)
    return jax.shard_map(body, mesh=mesh, in_specs=in_specs, out_specs=out_specs, check_vma=False)
```

```python
import functools

import jax
import jax.numpy as jnp
from jax import lax
from jax.experimental import pallas as pl
from jax.experimental.pallas import tpu as pltpu
import numpy as np
from jax.sharding import PartitionSpec as P

FACE_SIDE = 8
FACE = FACE_SIDE * FACE_SIDE
WIDTH = 2 * FACE
AXES = ("ex", "ey", "ez")
TURNS = ((1, 1), (0, 1), (0, 0), (1, 0), (2, 1), (2, 0))
EARLY = (1, 0)
LATE = 2
LAST_TURNS = ((1, 1), (1, 0), (2, 1), (2, 0), (0, 0), (0, 1))
LAST_EARLY = (1, 2)
LAST_LATE = 0
VMEM_LIMIT = 24 * 1024 * 1024


class Layout:
    def __init__(self, counts, species, sizes):
        self.counts = counts
        self.species = species
        self.sizes = sizes

    def elements(self):
        spans = [range(count) for count in self.counts]
        return [(i, j, k) for i in spans[0] for j in spans[1] for k in spans[2]]

    def number(self, element):
        return (element[0] * self.counts[1] + element[1]) * self.counts[2] + element[2]

    def rows(self, element):
        start = self.number(element) * self.species
        return slice(start, start + self.species)

    def layer(self, dim, position):
        return [element for element in self.elements() if element[dim] == position]

    def pairs(self, dim):
        return (len(self.layer(dim, 0)) + 1) // 2

    def pair_rows(self, pair):
        return slice(pair * self.species, (pair + 1) * self.species)

    def turns(self, dims=(0, 1, 2), order=TURNS):
        return [
            (dim, parity) for dim, parity in order if dim in dims and self.sizes[dim] > 1 + parity
        ]

    def edge(self, dim):
        ends = (0, self.counts[dim] - 1)
        return [element for element in self.elements() if element[dim] in ends]

    def message(self, dim, level=False):
        pairs = max(self.pairs(each) for each in range(3)) if level else self.pairs(dim)
        return jax.ShapeDtypeStruct((pairs * self.species, WIDTH), jnp.float32)


def columns(dim):
    return slice(dim * WIDTH, (dim + 1) * WIDTH)


def lanes(layout):
    return lax.broadcasted_iota(jnp.int32, (layout.species, WIDTH), 1)


def picked(value, index):
    return jnp.take_along_axis(value, index, axis=1, mode="promise_in_bounds")


def flip_mask(code):
    reach = FACE_SIDE - 1
    return (code & 1) * (reach * FACE_SIDE) + (code >> 1) * reach


def places():
    return [lax.axis_index(axis) for axis in AXES]


def pack(layout, here, dim, load_block, mask_of, outs):
    turns = [(turn, out) for turn, out in zip(layout.turns(), outs) if turn[0] == dim]
    if not turns:
        return
    lane = lanes(layout)
    low = lane < FACE
    even = (here[dim] & 1) == 0
    first = layout.layer(dim, 0)
    last = layout.layer(dim, layout.counts[dim] - 1)
    used = layout.pairs(dim) * layout.species
    for _, out in turns:
        if used < out.shape[0]:
            out[used:, :] = jnp.zeros((out.shape[0] - used, WIDTH), jnp.float32)
    for pair in range(layout.pairs(dim)):
        sides = []
        for half in range(2):
            where = min(2 * pair + half, len(first) - 1)
            upper = load_block(last[where], dim)
            lower = load_block(first[where], dim)
            lower = picked(lower, lane ^ mask_of(first[where], dim) ^ (half * FACE))
            if half == 0:
                upper = pltpu.roll(upper, FACE, 1)
            sides.append((upper, lower))
        up = jnp.where(low, sides[0][0], sides[1][0])
        down = jnp.where(low, sides[0][1], sides[1][1])
        for (_, parity), out in turns:
            is_lower = even if parity == 0 else jnp.logical_not(even)
            out[layout.pair_rows(pair), :] = jnp.where(is_lower, up, down)


def received(layout, here, dim, messages):
    even = (here[dim] & 1) == 0
    at_start = here[dim] == 0
    at_end = here[dim] == layout.sizes[dim] - 1
    zero = jnp.zeros((layout.species, WIDTH), jnp.float32)
    found = []
    for pair in range(layout.pairs(dim)):
        first, second = [
            messages[dim, parity][layout.pair_rows(pair), :] if (dim, parity) in messages else zero
            for parity in range(2)
        ]
        below = jnp.where(at_start, 0.0, jnp.where(even, second, first))
        above = jnp.where(at_end, 0.0, jnp.where(even, first, second))
        found.append((below, above))
    return found


def unpacked(lane, outside, where, mask):
    below, above = outside[where // 2]
    half = (where % 2) * FACE
    from_below = picked(below, lane ^ mask ^ half)
    from_above = pltpu.roll(above, FACE, 1) if half == 0 else above
    return from_below, from_above


def assemble(layout, here, dim, load_block, messages, mask_of, keep_of, emit, slab=None):
    lane = lanes(layout)
    low = lane < FACE
    count = layout.counts[dim]
    outside = None if messages is None else received(layout, here, dim, messages)
    zero = jnp.zeros((layout.species, WIDTH), jnp.float32)
    for where, start in enumerate(layout.layer(dim, 0)):
        if slab not in (None, start[0]):
            continue
        line = [start[:dim] + (step,) + start[dim + 1 :] for step in range(count)]
        blocks = [load_block(element, dim) for element in line]
        if outside is None:
            from_below, from_above = zero, zero
        else:
            from_below, from_above = unpacked(lane, outside, where, mask_of(start, dim))
        turned = [from_below]
        for step, element in list(enumerate(line))[1:]:
            shared = jnp.where(low, blocks[step], blocks[step - 1])
            turned.append(picked(shared, lane ^ mask_of(element, dim) ^ FACE))
        turned.append(from_above)
        for step, element in enumerate(line):
            value = blocks[step] + jnp.where(low, turned[step], turned[step + 1])
            if step in (0, count - 1):
                value = value * keep_of(element, dim)
            emit(element, value)


def halves(value):
    high = value.astype(jnp.bfloat16)
    return high, (value - high.astype(jnp.float32)).astype(jnp.bfloat16)


def dot(left, right, contract=((1,), (0,))):
    return lax.dot_general(left, right, (contract, ((), ())), preferred_element_type=jnp.float32)


def split_dot(left, right, contract):
    left_high, left_rest = halves(left)
    right_high, right_rest = halves(right)
    return (
        dot(left_high, right_high, contract)
        + dot(left_high, right_rest, contract)
        + dot(left_rest, right_high, contract)
    )


def stacked(value, outs):
    high, rest = halves(value)
    for dim, out in enumerate(outs):
        for part, piece in enumerate((high, rest, high)):
            out[part * WIDTH : (part + 1) * WIDTH, :] = piece[columns(dim), :]


def operator_kernel(fine, *outs):
    stacked(fine[...], outs)


def smoother_kernel(inverse, four, coarse_four, two, coarse_two, *refs):
    *outs, right, left = refs
    right[...] = jnp.zeros_like(right)
    left[...] = jnp.zeros_like(left)
    start = 0
    for prolong, coarse in ((four, coarse_four), (two, coarse_two)):
        rows = slice(start, start + prolong.shape[0])
        left[rows, :] = prolong[...]
        right[rows, :] = split_dot(coarse[...], prolong[...], ((1,), (0,)))
        start += rounded(prolong.shape[0])
    corrections = split_dot(left[...], right[...], ((0,), (0,)))
    stacked(0.5 * (inverse[...] + corrections), outs)


def rounded(count):
    return (count + 7) // 8 * 8


def first_kernel(layout, load, orient, boundary, *refs):
    turns = len(layout.turns())
    weights, refs = refs[:4], refs[4:]
    outs, (masks, keeps), fetched, refs = refs[:turns], refs[turns : turns + 2], *cut_at(refs, turns)
    staged, codes, fixed, arrived = refs
    small = [
        pltpu.make_async_copy(source, target, arrived.at[number])
        for number, (source, target) in enumerate(((orient, codes), (boundary, fixed)))
    ]
    strips = [
        pltpu.make_async_copy(
            load.at[:, columns(dim)], staged.at[:, columns(dim)], arrived.at[2 + dim]
        )
        for dim in range(3)
    ]
    fetches = [
        pltpu.make_async_copy(source, target, arrived.at[5 + number])
        for number, (source, target) in enumerate(zip(weights, fetched))
    ]
    for copy in small + strips + fetches:
        copy.start()
    here = places()
    for copy in small:
        copy.wait()
    tabulate(layout, here, codes, fixed, masks, keeps)
    for dim in range(3):
        strips[dim].wait()
        pack(
            layout,
            here,
            dim,
            lambda element, dim: staged[layout.rows(element), columns(dim)],
            table(layout, masks),
            outs,
        )
    for copy in fetches:
        copy.wait()


def cut_at(refs, turns):
    return refs[turns + 2 : turns + 6], refs[turns + 6 :]


def tabulate(layout, here, codes, boundary, masks, keeps):
    low = lax.broadcasted_iota(jnp.int32, (1, WIDTH), 1) < FACE
    for element in layout.elements():
        number = layout.number(element)
        for dim in range(3):
            mask = flip_mask(codes[(dim,) + element])
            masks[number : number + 1, columns(dim)] = jnp.full((1, WIDTH), mask, jnp.int32)
            at_start = (here[dim] == 0) & (element[dim] == 0)
            at_end = (here[dim] == layout.sizes[dim] - 1) & (element[dim] == layout.counts[dim] - 1)
            fixed_low = jnp.where(at_start, boundary[element + (2 * dim,)], 0)
            fixed_top = jnp.where(at_end, boundary[element + (2 * dim + 1,)], 0)
            fixed = jnp.where(low, fixed_low, fixed_top)
            keeps[number : number + 1, columns(dim)] = 1.0 - fixed.astype(jnp.float32)


def table(layout, ref):
    def row(element, dim):
        number = layout.number(element)
        return ref[number : number + 1, columns(dim)]

    return row


def scales(layout, kind, ref):
    def row(element, dim):
        value = ref[element[0], element[1], element[2] : element[2] + 1, columns(dim)]
        return value if kind == "operator" else 1.0 / value

    return row


def put_split(split, rows, value):
    high, rest = halves(value)
    for part, piece in enumerate((high, high, rest)):
        split[rows, part * WIDTH : (part + 1) * WIDTH] = piece


def taken(layout, dims, refs, order=TURNS):
    turns = layout.turns(dims, order)
    return dict(zip(turns, refs)), refs[len(turns) :]


def combined(kind, begun, result):
    if begun is None:
        return result
    return begun - result if kind == "operator" else begun + result


def strip_kernel(layout, kind, dim, local, value, *refs):
    messages, refs = (None, refs) if local else taken(layout, (dim,), refs)
    masks, keeps, scaling, matrix, *before, out, split, summed = refs
    begun = before[0] if before else None
    here = places()
    factor = scales(layout, kind, scaling)

    def emit(element, result):
        put_split(split, layout.rows(element), result * factor(element, dim))

    def assembled(slab):
        assemble(
            layout,
            here,
            dim,
            lambda element, dim: value[layout.rows(element), columns(dim)],
            messages,
            table(layout, masks),
            table(layout, keeps),
            emit,
            slab,
        )

    if dim == 0:
        assembled(None)
    count = layout.counts[0]
    height = value.shape[0] // count
    for slab in range(count):
        if dim != 0:
            assembled(slab)
        rows = slice(slab * height, (slab + 1) * height)
        summed[rows, :] = dot(split[rows, :], matrix[...])
        for element in layout.layer(0, slab):
            for each in range(3):
                at = (layout.rows(element), columns(each))
                result = summed[at] * factor(element, each)
                out[at] = combined(kind, None if begun is None else begun[at], result)


def faces_kernel(layout, kind, *refs):
    messages, refs = taken(layout, (LATE,), refs)
    masks, scaling, matrix, begun, *refs = refs
    out, *sent, split, summed = refs
    here = places()
    factor = scales(layout, kind, scaling)
    lane = lanes(layout)
    low = lane < FACE
    outside = received(layout, here, LATE, messages)
    mask_of = table(layout, masks)
    edge = layout.edge(LATE)
    for number, element in enumerate(edge):
        start = element[:LATE] + (0,) + element[LATE + 1 :]
        where = layout.layer(LATE, 0).index(start)
        from_below, from_above = unpacked(lane, outside, where, mask_of(start, LATE))
        lower = from_below if element[LATE] == 0 else 0.0
        upper = from_above if element[LATE] == layout.counts[LATE] - 1 else 0.0
        rows = slice(number * layout.species, (number + 1) * layout.species)
        put_split(split, rows, jnp.where(low, lower, upper) * factor(element, LATE))
    summed[...] = dot(split[...], matrix[...])
    for element in layout.elements():
        for dim in range(3):
            at = (layout.rows(element), columns(dim))
            if element in edge:
                number = edge.index(element)
                rows = slice(number * layout.species, (number + 1) * layout.species)
                result = summed[rows, columns(dim)] * factor(element, dim)
                out[at] = combined(kind, begun[at], result)
            else:
                out[at] = begun[at]
    for dim in range(3):
        pack(
            layout,
            here,
            dim,
            lambda element, dim: out[layout.rows(element), columns(dim)],
            mask_of,
            sent,
        )


def assembled_strips(layout, dims, value, messages, masks, keeps, ready):
    for place, dim in enumerate(dims):

        def emit(element, result):
            ready[layout.rows(element), place * WIDTH : (place + 1) * WIDTH] = result

        assemble(
            layout,
            places(),
            dim,
            lambda element, dim: value[layout.rows(element), columns(dim)],
            messages,
            table(layout, masks),
            table(layout, keeps),
            emit,
        )


def last_early_kernel(layout, value, *refs):
    messages, (masks, keeps, ready) = taken(layout, LAST_EARLY, refs, LAST_TURNS)
    assembled_strips(layout, LAST_EARLY, value, messages, masks, keeps, ready)


def last_late_kernel(layout, begun, value, *refs):
    messages, (masks, keeps, out, ready, left) = taken(layout, (LAST_LATE,), refs, LAST_TURNS)

    def copies(source, done, first):
        return [
            pltpu.make_async_copy(
                source.at[:, place * WIDTH : (place + 1) * WIDTH],
                out.at[:, columns(dim)],
                left.at[first + place],
            )
            for place, dim in enumerate(done)
        ]

    started = copies(begun, LAST_EARLY, 0)
    for copy in started:
        copy.start()
    assembled_strips(layout, (LAST_LATE,), value, messages, masks, keeps, ready)
    rest = copies(ready, (LAST_LATE,), len(LAST_EARLY))
    for copy in rest:
        copy.start()
    for copy in started + rest:
        copy.wait()


def in_vmem(count):
    return [pl.BlockSpec(memory_space=pltpu.VMEM)] * count


def in_hbm(count):
    return [pl.BlockSpec(memory_space=pltpu.HBM)] * count


PARAMS = pltpu.CompilerParams(vmem_limit_bytes=VMEM_LIMIT)


def kept_in_hbm(*values):
    return [pltpu.with_memory_space_constraint(value, pltpu.HBM) for value in values]


def cost(flops, size):
    return pl.CostEstimate(flops=flops, bytes_accessed=size, transcendentals=0)


def partners(layout, dim, parity):
    sizes = layout.sizes
    swap = {}
    for place in np.ndindex(*sizes):
        other = list(place)
        lower = place[dim] % 2 == parity
        at = place[dim] + (1 if lower else -1)
        if 0 <= at < sizes[dim]:
            other[dim] = at
        elif dim != 1 and sizes[1] % 2 == 0:
            other[1] = place[1] ^ 1
        elif sizes[dim] % 2 == 0:
            other[dim] = sizes[dim] - 1 - place[dim]
        swap[place] = tuple(other)
    return [
        (int(np.ravel_multi_index(place, sizes)), int(np.ravel_multi_index(other, sizes)))
        for place, other in swap.items()
    ]


def exchange(layout, messages, order=TURNS):
    given = dict(zip(layout.turns(), messages))
    return {
        turn: lax.ppermute(given[turn], AXES, partners(layout, *turn))
        for turn in order
        if turn in given
    }


def body(
    load_raw,
    scaling,
    fine_matrix,
    fine_inverse,
    prolong_four,
    coarse_four,
    prolong_two,
    coarse_two,
    orient,
    boundary,
):
    counts, species, nodes = load_raw.shape[:3], load_raw.shape[3], load_raw.shape[4]
    layout = Layout(counts, species, tuple(lax.axis_size(axis) for axis in AXES))
    load = load_raw.reshape(-1, nodes)
    rows = load.shape[0]
    turns = layout.turns()
    message_shapes = tuple(layout.message(dim) for dim, _ in turns)
    last_shapes = tuple(layout.message(dim, True) for dim, _ in turns)
    whole = jax.ShapeDtypeStruct(load.shape, jnp.float32)
    matrix_shapes = (jax.ShapeDtypeStruct((3 * WIDTH, nodes), jnp.bfloat16),) * 3
    elements = len(layout.elements())
    tables = tuple(jax.ShapeDtypeStruct((elements, nodes), kind) for kind in (jnp.int32, jnp.float32))
    weights = (prolong_four.T, coarse_four, prolong_two.T, coarse_two)
    sides = jnp.transpose(boundary, (1, 2, 3, 0))

    sent = pl.pallas_call(
        functools.partial(first_kernel, layout),
        out_shape=message_shapes
        + tables
        + tuple(jax.ShapeDtypeStruct(weight.shape, weight.dtype) for weight in weights),
        in_specs=in_hbm(7),
        out_specs=tuple(in_vmem(len(turns) + 6)),
        scratch_shapes=[
            pltpu.VMEM(load.shape, jnp.float32),
            pltpu.SMEM(orient.shape, jnp.int32),
            pltpu.SMEM(sides.shape, jnp.int32),
            pltpu.SemaphoreType.DMA((9,)),
        ],
        compiler_params=PARAMS,
        name="pack",
    )(*kept_in_hbm(load, orient, sides, *weights))
    masks, keeps, *weights = sent[len(turns) :]

    stack = (rounded(prolong_four.shape[1]) + rounded(prolong_two.shape[1]), nodes)
    smoother = pl.pallas_call(
        smoother_kernel,
        out_shape=matrix_shapes,
        in_specs=in_vmem(5),
        out_specs=tuple(in_vmem(3)),
        scratch_shapes=[pltpu.VMEM(stack, jnp.float32), pltpu.VMEM(stack, jnp.float32)],
        compiler_params=PARAMS,
        cost_estimate=cost(2 * nodes * nodes * nodes, 8 * nodes * nodes),
        name="smoother",
    )(fine_inverse, *weights)
    operator = pl.pallas_call(
        operator_kernel,
        out_shape=matrix_shapes,
        in_specs=in_vmem(1),
        out_specs=tuple(in_vmem(3)),
        compiler_params=PARAMS,
        cost_estimate=cost(0, 10 * nodes * nodes),
        name="operator",
    )(fine_matrix)

    def stage(kind, value, messages, matrix, begun, shapes=message_shapes):
        estimate = cost(6 * rows * WIDTH * nodes, 8 * rows * nodes)
        for dim, local in ((LATE, True),) + tuple((dim, False) for dim in EARLY):
            mine = [] if local else [messages[turn] for turn in layout.turns((dim,))]
            before = () if begun is None else (begun,)
            begun = pl.pallas_call(
                functools.partial(strip_kernel, layout, kind, dim, local),
                out_shape=whole,
                in_specs=in_vmem(5 + len(mine) + len(before)),
                out_specs=in_vmem(1)[0],
                scratch_shapes=[
                    pltpu.VMEM((rows, 3 * WIDTH), jnp.bfloat16),
                    pltpu.VMEM(load.shape, jnp.float32),
                ],
                compiler_params=PARAMS,
                cost_estimate=estimate,
                name="{}_{}".format(kind, dim),
            )(value, *mine, masks, keeps, scaling, matrix[dim], *before)
        mine = [messages[turn] for turn in layout.turns((LATE,))]
        height = len(layout.edge(LATE)) * species
        result, *sent = pl.pallas_call(
            functools.partial(faces_kernel, layout, kind),
            out_shape=(whole,) + shapes,
            in_specs=in_vmem(4 + len(mine)),
            out_specs=tuple(in_vmem(1 + len(turns))),
            scratch_shapes=[
                pltpu.VMEM((height, 3 * WIDTH), jnp.bfloat16),
                pltpu.VMEM((height, nodes), jnp.float32),
            ],
            compiler_params=PARAMS,
            cost_estimate=estimate,
            name="{}_faces".format(kind),
        )(*mine, masks, scaling, matrix[LATE], begun)
        return result, sent

    first, sent = stage("smooth", load, exchange(layout, sent), smoother, None)
    left, sent = stage("operator", first, exchange(layout, sent), operator, load)
    total, sent = stage("smooth_more", left, exchange(layout, sent), smoother, first, last_shapes)
    messages = exchange(layout, sent, LAST_TURNS)
    early = [messages[turn] for turn in layout.turns(LAST_EARLY, LAST_TURNS)]
    late = [messages[turn] for turn in layout.turns((LAST_LATE,), LAST_TURNS)]
    cut = len(LAST_EARLY) * WIDTH
    begun = pl.pallas_call(
        functools.partial(last_early_kernel, layout),
        out_shape=jax.ShapeDtypeStruct((rows, cut), jnp.float32),
        in_specs=in_vmem(3 + len(early)),
        out_specs=in_vmem(1)[0],
        compiler_params=PARAMS,
        cost_estimate=cost(0, 8 * rows * cut),
        name="last_early",
    )(total, *early, masks, keeps)
    result = pl.pallas_call(
        functools.partial(last_late_kernel, layout),
        out_shape=whole,
        in_specs=in_vmem(4 + len(late)),
        out_specs=in_hbm(1)[0],
        scratch_shapes=[
            pltpu.VMEM((rows, nodes - cut), jnp.float32),
            pltpu.SemaphoreType.DMA((3,)),
        ],
        compiler_params=PARAMS,
        cost_estimate=cost(0, 8 * rows * nodes),
        name="last_late",
    )(begun, total, *late, masks, keeps)
    return result.reshape(load_raw.shape)


def solution(mesh):
    in_specs = (
        P("ex", "ey", "ez", None, None),
        P("ex", "ey", "ez", None),
        P(),
        P(),
        P(),
        P(),
        P(),
        P(),
        P(None, "ex", "ey", "ez"),
        P(None, "ex", "ey", "ez"),
    )
    out_specs = P("ex", "ey", "ez", None, None)
    return jax.shard_map(body, mesh=mesh, in_specs=in_specs, out_specs=out_specs, check_vma=False)
```

```python
import functools

import jax
import jax.numpy as jnp
from jax import lax
from jax.experimental import pallas as pl
from jax.experimental.pallas import tpu as pltpu
import numpy as np
from jax.sharding import PartitionSpec as P

FACE_SIDE = 8
FACE = FACE_SIDE * FACE_SIDE
WIDTH = 2 * FACE
AXES = ("ex", "ey", "ez")
TURNS = ((1, 1), (0, 1), (0, 0), (1, 0), (2, 1), (2, 0))
EARLY = (1, 0)
LATE = 2
VMEM_LIMIT = 24 * 1024 * 1024


class Layout:
    def __init__(self, counts, species, sizes):
        self.counts = counts
        self.species = species
        self.sizes = sizes

    def elements(self):
        spans = [range(count) for count in self.counts]
        return [(i, j, k) for i in spans[0] for j in spans[1] for k in spans[2]]

    def number(self, element):
        return (element[0] * self.counts[1] + element[1]) * self.counts[2] + element[2]

    def rows(self, element):
        start = self.number(element) * self.species
        return slice(start, start + self.species)

    def layer(self, dim, position):
        return [element for element in self.elements() if element[dim] == position]

    def pairs(self, dim):
        return (len(self.layer(dim, 0)) + 1) // 2

    def pair_rows(self, pair):
        return slice(pair * self.species, (pair + 1) * self.species)

    def turns(self, dims=(0, 1, 2)):
        return [
            (dim, parity) for dim, parity in TURNS if dim in dims and self.sizes[dim] > 1 + parity
        ]

    def edge(self, dim):
        ends = (0, self.counts[dim] - 1)
        return [element for element in self.elements() if element[dim] in ends]

    def blocks(self):
        height = self.counts[2] * self.species
        return [
            slice(part * height, (part + 1) * height) for part in range(self.counts[0] * self.counts[1])
        ]

    def message(self, dim):
        return jax.ShapeDtypeStruct((self.pairs(dim) * self.species, WIDTH), jnp.float32)


def columns(dim):
    return slice(dim * WIDTH, (dim + 1) * WIDTH)


def lanes(layout):
    return lax.broadcasted_iota(jnp.int32, (layout.species, WIDTH), 1)


def picked(value, index):
    return jnp.take_along_axis(value, index, axis=1, mode="promise_in_bounds")


def flip_mask(code):
    reach = FACE_SIDE - 1
    return (code & 1) * (reach * FACE_SIDE) + (code >> 1) * reach


def places():
    return [lax.axis_index(axis) for axis in AXES]


def pack(layout, here, dim, load_block, mask_of, outs):
    turns = [(turn, out) for turn, out in zip(layout.turns(), outs) if turn[0] == dim]
    if not turns:
        return
    lane = lanes(layout)
    low = lane < FACE
    even = (here[dim] & 1) == 0
    first = layout.layer(dim, 0)
    last = layout.layer(dim, layout.counts[dim] - 1)
    for pair in range(layout.pairs(dim)):
        sides = []
        for half in range(2):
            where = min(2 * pair + half, len(first) - 1)
            upper = load_block(last[where], dim)
            lower = load_block(first[where], dim)
            lower = picked(lower, lane ^ mask_of(first[where], dim) ^ (half * FACE))
            if half == 0:
                upper = pltpu.roll(upper, FACE, 1)
            sides.append((upper, lower))
        up = jnp.where(low, sides[0][0], sides[1][0])
        down = jnp.where(low, sides[0][1], sides[1][1])
        for (_, parity), out in turns:
            is_lower = even if parity == 0 else jnp.logical_not(even)
            out[layout.pair_rows(pair), :] = jnp.where(is_lower, up, down)


def received(layout, here, dim, messages):
    even = (here[dim] & 1) == 0
    at_start = here[dim] == 0
    at_end = here[dim] == layout.sizes[dim] - 1
    zero = jnp.zeros((layout.species, WIDTH), jnp.float32)
    found = []
    for pair in range(layout.pairs(dim)):
        first, second = [
            messages[dim, parity][layout.pair_rows(pair), :] if (dim, parity) in messages else zero
            for parity in range(2)
        ]
        below = jnp.where(at_start, 0.0, jnp.where(even, second, first))
        above = jnp.where(at_end, 0.0, jnp.where(even, first, second))
        found.append((below, above))
    return found


def unpacked(lane, outside, where, mask):
    below, above = outside[where // 2]
    half = (where % 2) * FACE
    from_below = picked(below, lane ^ mask ^ half)
    from_above = pltpu.roll(above, FACE, 1) if half == 0 else above
    return from_below, from_above


def assemble(layout, here, dim, load_block, messages, mask_of, keep_of, emit, slab=None):
    lane = lanes(layout)
    low = lane < FACE
    count = layout.counts[dim]
    outside = None if messages is None else received(layout, here, dim, messages)
    zero = jnp.zeros((layout.species, WIDTH), jnp.float32)
    for where, start in enumerate(layout.layer(dim, 0)):
        if slab not in (None, start[0]):
            continue
        line = [start[:dim] + (step,) + start[dim + 1 :] for step in range(count)]
        blocks = [load_block(element, dim) for element in line]
        if outside is None:
            from_below, from_above = zero, zero
        else:
            from_below, from_above = unpacked(lane, outside, where, mask_of(start, dim))
        turned = [from_below]
        for step, element in list(enumerate(line))[1:]:
            shared = jnp.where(low, blocks[step], blocks[step - 1])
            turned.append(picked(shared, lane ^ mask_of(element, dim) ^ FACE))
        turned.append(from_above)
        for step, element in enumerate(line):
            value = blocks[step] + jnp.where(low, turned[step], turned[step + 1])
            if step in (0, count - 1):
                value = value * keep_of(element, dim)
            emit(element, value)


def halves(value):
    high = value.astype(jnp.bfloat16)
    return high, (value - high.astype(jnp.float32)).astype(jnp.bfloat16)


def dot(left, right, contract=((1,), (0,))):
    return lax.dot_general(left, right, (contract, ((), ())), preferred_element_type=jnp.float32)


def split_dot(left, right, contract):
    left_high, left_rest = halves(left)
    right_high, right_rest = halves(right)
    return (
        dot(left_high, right_high, contract)
        + dot(left_high, right_rest, contract)
        + dot(left_rest, right_high, contract)
    )


def stacked(value, outs):
    high, rest = halves(value)
    for dim, out in enumerate(outs):
        for part, piece in enumerate((high, rest, high)):
            out[part * WIDTH : (part + 1) * WIDTH, :] = piece[columns(dim), :]


def operator_kernel(fine, *outs):
    stacked(fine[...], outs)


def smoother_kernel(inverse, four, coarse_four, two, coarse_two, *refs):
    *outs, right, left = refs
    right[...] = jnp.zeros_like(right)
    left[...] = jnp.zeros_like(left)
    start = 0
    for prolong, coarse in ((four, coarse_four), (two, coarse_two)):
        rows = slice(start, start + prolong.shape[0])
        left[rows, :] = prolong[...]
        right[rows, :] = split_dot(coarse[...], prolong[...], ((1,), (0,)))
        start += rounded(prolong.shape[0])
    corrections = split_dot(left[...], right[...], ((0,), (0,)))
    stacked(0.5 * (inverse[...] + corrections), outs)


def rounded(count):
    return (count + 7) // 8 * 8


def first_kernel(layout, load, orient, boundary, *refs):
    turns = len(layout.turns())
    weights, refs = refs[:4], refs[4:]
    outs, (masks, keeps), fetched, refs = refs[:turns], refs[turns : turns + 2], *cut_at(refs, turns)
    staged, codes, fixed, arrived = refs
    small = [
        pltpu.make_async_copy(source, target, arrived.at[number])
        for number, (source, target) in enumerate(((orient, codes), (boundary, fixed)))
    ]
    fetches = [
        pltpu.make_async_copy(source, target, arrived.at[2 + number])
        for number, (source, target) in enumerate(zip(weights, fetched))
    ]
    blocks = layout.blocks()
    strips = [
        [
            pltpu.make_async_copy(
                load.at[rows, columns(dim)],
                staged.at[rows, columns(dim)],
                arrived.at[6 + dim * len(blocks) + part],
            )
            for part, rows in enumerate(blocks)
        ]
        for dim in range(3)
    ]
    for copy in small + sum(strips, []) + fetches:
        copy.start()
    here = places()
    for copy in small:
        copy.wait()
    tabulate(layout, here, codes, fixed, masks, keeps)
    for dim in range(3):
        for copy in strips[dim]:
            copy.wait()
        pack(
            layout,
            here,
            dim,
            lambda element, dim: staged[layout.rows(element), columns(dim)],
            table(layout, masks),
            outs,
        )
    for copy in fetches:
        copy.wait()


def cut_at(refs, turns):
    return refs[turns + 2 : turns + 6], refs[turns + 6 :]


def tabulate(layout, here, codes, boundary, masks, keeps):
    low = lax.broadcasted_iota(jnp.int32, (1, WIDTH), 1) < FACE
    for element in layout.elements():
        number = layout.number(element)
        for dim in range(3):
            mask = flip_mask(codes[(dim,) + element])
            masks[number : number + 1, columns(dim)] = jnp.full((1, WIDTH), mask, jnp.int32)
            at_start = (here[dim] == 0) & (element[dim] == 0)
            at_end = (here[dim] == layout.sizes[dim] - 1) & (element[dim] == layout.counts[dim] - 1)
            fixed_low = jnp.where(at_start, boundary[element + (2 * dim,)], 0)
            fixed_top = jnp.where(at_end, boundary[element + (2 * dim + 1,)], 0)
            fixed = jnp.where(low, fixed_low, fixed_top)
            keeps[number : number + 1, columns(dim)] = 1.0 - fixed.astype(jnp.float32)


def table(layout, ref):
    def row(element, dim):
        number = layout.number(element)
        return ref[number : number + 1, columns(dim)]

    return row


def scales(layout, kind, ref):
    def row(element, dim):
        value = ref[element[0], element[1], element[2] : element[2] + 1, columns(dim)]
        return value if kind == "operator" else 1.0 / value

    return row


def put_split(split, rows, value):
    high, rest = halves(value)
    for part, piece in enumerate((high, high, rest)):
        split[rows, part * WIDTH : (part + 1) * WIDTH] = piece


def taken(layout, dims, refs):
    turns = layout.turns(dims)
    return dict(zip(turns, refs)), refs[len(turns) :]


def combined(kind, begun, result):
    if begun is None:
        return result
    return begun - result if kind == "operator" else begun + result


def strip_kernel(layout, kind, dim, local, value, *refs):
    messages, refs = (None, refs) if local else taken(layout, (dim,), refs)
    masks, keeps, scaling, matrix, *before, out, split, summed = refs
    begun = before[0] if before else None
    here = places()
    factor = scales(layout, kind, scaling)

    def emit(element, result):
        put_split(split, layout.rows(element), result * factor(element, dim))

    def assembled(slab):
        assemble(
            layout,
            here,
            dim,
            lambda element, dim: value[layout.rows(element), columns(dim)],
            messages,
            table(layout, masks),
            table(layout, keeps),
            emit,
            slab,
        )

    if dim == 0:
        assembled(None)
    count = layout.counts[0]
    height = value.shape[0] // count
    for slab in range(count):
        if dim != 0:
            assembled(slab)
        rows = slice(slab * height, (slab + 1) * height)
        summed[rows, :] = dot(split[rows, :], matrix[...])
        for element in layout.layer(0, slab):
            for each in range(3):
                at = (layout.rows(element), columns(each))
                result = summed[at] * factor(element, each)
                out[at] = combined(kind, None if begun is None else begun[at], result)


def faces_kernel(layout, kind, *refs):
    messages, refs = taken(layout, (LATE,), refs)
    masks, scaling, matrix, begun, *refs = refs
    out, *sent, split, summed = refs
    here = places()
    factor = scales(layout, kind, scaling)
    lane = lanes(layout)
    low = lane < FACE
    outside = received(layout, here, LATE, messages)
    mask_of = table(layout, masks)
    edge = layout.edge(LATE)
    for number, element in enumerate(edge):
        start = element[:LATE] + (0,) + element[LATE + 1 :]
        where = layout.layer(LATE, 0).index(start)
        from_below, from_above = unpacked(lane, outside, where, mask_of(start, LATE))
        lower = from_below if element[LATE] == 0 else 0.0
        upper = from_above if element[LATE] == layout.counts[LATE] - 1 else 0.0
        rows = slice(number * layout.species, (number + 1) * layout.species)
        put_split(split, rows, jnp.where(low, lower, upper) * factor(element, LATE))
    summed[...] = dot(split[...], matrix[...])
    for element in layout.elements():
        for dim in range(3):
            at = (layout.rows(element), columns(dim))
            if element in edge:
                number = edge.index(element)
                rows = slice(number * layout.species, (number + 1) * layout.species)
                result = summed[rows, columns(dim)] * factor(element, dim)
                out[at] = combined(kind, begun[at], result)
            else:
                out[at] = begun[at]
    for dim in range(3):
        pack(
            layout,
            here,
            dim,
            lambda element, dim: out[layout.rows(element), columns(dim)],
            mask_of,
            sent,
        )


def last_early_kernel(layout, value, *refs):
    messages, (masks, keeps, ready) = taken(layout, EARLY, refs)
    for dim in range(3):

        def emit(element, result):
            ready[layout.rows(element), columns(dim)] = result

        assemble(
            layout,
            places(),
            dim,
            lambda element, dim: value[layout.rows(element), columns(dim)],
            None if dim == LATE else messages,
            table(layout, masks),
            table(layout, keeps),
            emit,
        )


def last_late_kernel(layout, begun, *refs):
    messages, (masks, out, ready, left) = taken(layout, (LATE,), refs)
    blocks = layout.blocks()

    def copy(source, dim, part):
        at = (blocks[part], columns(dim))
        return pltpu.make_async_copy(
            source.at[at], out.at[at], left.at[dim * len(blocks) + part]
        )

    copies = [copy(begun, dim, part) for dim in EARLY for part in range(len(blocks))]
    for each in copies:
        each.start()
    lane = lanes(layout)
    low = lane < FACE
    outside = received(layout, places(), LATE, messages)
    lines = layout.layer(LATE, 0)
    for part in range(len(blocks)):
        start = lines[part]
        mask = table(layout, masks)(start, LATE)
        from_below, from_above = unpacked(lane, outside, part, mask)
        for step in range(layout.counts[LATE]):
            at = (layout.rows(start[:LATE] + (step,)), columns(LATE))
            value = begun[at]
            if step == 0:
                value += jnp.where(low, from_below, 0.0)
            if step == layout.counts[LATE] - 1:
                value += jnp.where(low, 0.0, from_above)
            ready[layout.rows(start[:LATE] + (step,)), :] = value
        late = pltpu.make_async_copy(
            ready.at[blocks[part], :],
            out.at[blocks[part], columns(LATE)],
            left.at[LATE * len(blocks) + part],
        )
        late.start()
        copies.append(late)
    for each in copies:
        each.wait()


def in_vmem(count):
    return [pl.BlockSpec(memory_space=pltpu.VMEM)] * count


def in_hbm(count):
    return [pl.BlockSpec(memory_space=pltpu.HBM)] * count


PARAMS = pltpu.CompilerParams(vmem_limit_bytes=VMEM_LIMIT)


def kept_in_hbm(*values):
    return [pltpu.with_memory_space_constraint(value, pltpu.HBM) for value in values]


def cost(flops, size):
    return pl.CostEstimate(flops=flops, bytes_accessed=size, transcendentals=0)


def partners(layout, dim, parity):
    sizes = layout.sizes
    swap = {}
    for place in np.ndindex(*sizes):
        other = list(place)
        lower = place[dim] % 2 == parity
        at = place[dim] + (1 if lower else -1)
        if 0 <= at < sizes[dim]:
            other[dim] = at
        elif dim != 1 and sizes[1] % 2 == 0:
            other[1] = place[1] ^ 1
        elif sizes[dim] % 2 == 0:
            other[dim] = sizes[dim] - 1 - place[dim]
        swap[place] = tuple(other)
    return [
        (int(np.ravel_multi_index(place, sizes)), int(np.ravel_multi_index(other, sizes)))
        for place, other in swap.items()
    ]


def exchange(layout, messages):
    return {
        turn: lax.ppermute(message, AXES, partners(layout, *turn))
        for turn, message in zip(layout.turns(), messages)
    }


def body(
    load_raw,
    scaling,
    fine_matrix,
    fine_inverse,
    prolong_four,
    coarse_four,
    prolong_two,
    coarse_two,
    orient,
    boundary,
):
    counts, species, nodes = load_raw.shape[:3], load_raw.shape[3], load_raw.shape[4]
    layout = Layout(counts, species, tuple(lax.axis_size(axis) for axis in AXES))
    load = load_raw.reshape(-1, nodes)
    rows = load.shape[0]
    turns = layout.turns()
    message_shapes = tuple(layout.message(dim) for dim, _ in turns)
    whole = jax.ShapeDtypeStruct(load.shape, jnp.float32)
    matrix_shapes = (jax.ShapeDtypeStruct((3 * WIDTH, nodes), jnp.bfloat16),) * 3
    elements = len(layout.elements())
    tables = tuple(jax.ShapeDtypeStruct((elements, nodes), kind) for kind in (jnp.int32, jnp.float32))
    weights = (prolong_four.T, coarse_four, prolong_two.T, coarse_two)
    sides = jnp.transpose(boundary, (1, 2, 3, 0))

    sent = pl.pallas_call(
        functools.partial(first_kernel, layout),
        out_shape=message_shapes
        + tables
        + tuple(jax.ShapeDtypeStruct(weight.shape, weight.dtype) for weight in weights),
        in_specs=in_hbm(7),
        out_specs=tuple(in_vmem(len(turns) + 6)),
        scratch_shapes=[
            pltpu.VMEM(load.shape, jnp.float32),
            pltpu.SMEM(orient.shape, jnp.int32),
            pltpu.SMEM(sides.shape, jnp.int32),
            pltpu.SemaphoreType.DMA((6 + 3 * len(layout.blocks()),)),
        ],
        compiler_params=PARAMS,
        name="pack",
    )(*kept_in_hbm(load, orient, sides, *weights))
    masks, keeps, *weights = sent[len(turns) :]

    stack = (rounded(prolong_four.shape[1]) + rounded(prolong_two.shape[1]), nodes)
    smoother = pl.pallas_call(
        smoother_kernel,
        out_shape=matrix_shapes,
        in_specs=in_vmem(5),
        out_specs=tuple(in_vmem(3)),
        scratch_shapes=[pltpu.VMEM(stack, jnp.float32), pltpu.VMEM(stack, jnp.float32)],
        compiler_params=PARAMS,
        cost_estimate=cost(2 * nodes * nodes * nodes, 8 * nodes * nodes),
        name="smoother",
    )(fine_inverse, *weights)
    operator = pl.pallas_call(
        operator_kernel,
        out_shape=matrix_shapes,
        in_specs=in_vmem(1),
        out_specs=tuple(in_vmem(3)),
        compiler_params=PARAMS,
        cost_estimate=cost(0, 10 * nodes * nodes),
        name="operator",
    )(fine_matrix)

    def stage(kind, value, messages, matrix, begun):
        estimate = cost(6 * rows * WIDTH * nodes, 8 * rows * nodes)
        for dim, local in ((LATE, True),) + tuple((dim, False) for dim in EARLY):
            mine = [] if local else [messages[turn] for turn in layout.turns((dim,))]
            before = () if begun is None else (begun,)
            begun = pl.pallas_call(
                functools.partial(strip_kernel, layout, kind, dim, local),
                out_shape=whole,
                in_specs=in_vmem(5 + len(mine) + len(before)),
                out_specs=in_vmem(1)[0],
                scratch_shapes=[
                    pltpu.VMEM((rows, 3 * WIDTH), jnp.bfloat16),
                    pltpu.VMEM(load.shape, jnp.float32),
                ],
                compiler_params=PARAMS,
                cost_estimate=estimate,
                name="{}_{}".format(kind, dim),
            )(value, *mine, masks, keeps, scaling, matrix[dim], *before)
        mine = [messages[turn] for turn in layout.turns((LATE,))]
        height = len(layout.edge(LATE)) * species
        result, *sent = pl.pallas_call(
            functools.partial(faces_kernel, layout, kind),
            out_shape=(whole,) + message_shapes,
            in_specs=in_vmem(4 + len(mine)),
            out_specs=tuple(in_vmem(1 + len(turns))),
            scratch_shapes=[
                pltpu.VMEM((height, 3 * WIDTH), jnp.bfloat16),
                pltpu.VMEM((height, nodes), jnp.float32),
            ],
            compiler_params=PARAMS,
            cost_estimate=estimate,
            name="{}_faces".format(kind),
        )(*mine, masks, scaling, matrix[LATE], begun)
        return result, sent

    first, sent = stage("smooth", load, exchange(layout, sent), smoother, None)
    left, sent = stage("operator", first, exchange(layout, sent), operator, load)
    total, sent = stage("smooth_more", left, exchange(layout, sent), smoother, first)
    messages = exchange(layout, sent)
    early = [messages[turn] for turn in layout.turns(EARLY)]
    late = [messages[turn] for turn in layout.turns((LATE,))]
    begun = pl.pallas_call(
        functools.partial(last_early_kernel, layout),
        out_shape=whole,
        in_specs=in_vmem(3 + len(early)),
        out_specs=in_vmem(1)[0],
        compiler_params=PARAMS,
        cost_estimate=cost(0, 8 * rows * nodes),
        name="last_early",
    )(total, *early, masks, keeps)
    result = pl.pallas_call(
        functools.partial(last_late_kernel, layout),
        out_shape=whole,
        in_specs=in_vmem(2 + len(late)),
        out_specs=in_hbm(1)[0],
        scratch_shapes=[
            pltpu.VMEM((rows, WIDTH), jnp.float32),
            pltpu.SemaphoreType.DMA((3 * len(layout.blocks()),)),
        ],
        compiler_params=PARAMS,
        cost_estimate=cost(0, 8 * rows * nodes),
        name="last_late",
    )(begun, *late, masks)
    return result.reshape(load_raw.shape)


def solution(mesh):
    in_specs = (
        P("ex", "ey", "ez", None, None),
        P("ex", "ey", "ez", None),
        P(),
        P(),
        P(),
        P(),
        P(),
        P(),
        P(None, "ex", "ey", "ez"),
        P(None, "ex", "ey", "ez"),
    )
    out_specs = P("ex", "ey", "ez", None, None)
    return jax.shard_map(body, mesh=mesh, in_specs=in_specs, out_specs=out_specs, check_vma=False)
```

```python
import functools

import jax
import jax.numpy as jnp
from jax import lax
from jax.experimental import pallas as pl
from jax.experimental.pallas import tpu as pltpu
import numpy as np
from jax.sharding import PartitionSpec as P

FACE_SIDE = 8
FACE = FACE_SIDE * FACE_SIDE
WIDTH = 2 * FACE
AXES = ("ex", "ey", "ez")
TURNS = ((1, 1), (0, 1), (0, 0), (1, 0), (2, 1), (2, 0))
DIMS = (0, 1, 2)
EARLY = (1, 0)
LATE = 2
VMEM_LIMIT = 24 * 1024 * 1024


class Layout:
    def __init__(self, counts, species, sizes):
        self.counts = counts
        self.species = species
        self.sizes = sizes

    def elements(self):
        spans = [range(count) for count in self.counts]
        return [(i, j, k) for i in spans[0] for j in spans[1] for k in spans[2]]

    def number(self, element):
        return (element[0] * self.counts[1] + element[1]) * self.counts[2] + element[2]

    def rows(self, element):
        start = self.number(element) * self.species
        return slice(start, start + self.species)

    def layer(self, dim, position):
        return [element for element in self.elements() if element[dim] == position]

    def pairs(self, dim):
        return (len(self.layer(dim, 0)) + 1) // 2

    def pair_rows(self, pair):
        return slice(pair * self.species, (pair + 1) * self.species)

    def turns(self, dims=(0, 1, 2)):
        return [
            (dim, parity) for dim, parity in TURNS if dim in dims and self.sizes[dim] > 1 + parity
        ]

    def sides(self, dim):
        return self.layer(dim, 0), self.layer(dim, self.counts[dim] - 1)

    def message(self, dim):
        return jax.ShapeDtypeStruct((self.pairs(dim) * self.species, WIDTH), jnp.float32)


def columns(dim):
    return slice(dim * WIDTH, (dim + 1) * WIDTH)


def lanes(layout):
    return lax.broadcasted_iota(jnp.int32, (layout.species, WIDTH), 1)


def picked(value, index):
    return jnp.take_along_axis(value, index, axis=1, mode="promise_in_bounds")


def flip_mask(code):
    reach = FACE_SIDE - 1
    return (code & 1) * (reach * FACE_SIDE) + (code >> 1) * reach


def places():
    return [lax.axis_index(axis) for axis in AXES]


def pack(layout, here, dim, load_block, mask_of, outs):
    turns = [(turn, out) for turn, out in zip(layout.turns(), outs) if turn[0] == dim]
    if not turns:
        return
    lane = lanes(layout)
    low = lane < FACE
    even = (here[dim] & 1) == 0
    first = layout.layer(dim, 0)
    last = layout.layer(dim, layout.counts[dim] - 1)
    for pair in range(layout.pairs(dim)):
        sides = []
        for half in range(2):
            where = min(2 * pair + half, len(first) - 1)
            upper = load_block(last[where], dim)
            lower = load_block(first[where], dim)
            lower = picked(lower, lane ^ mask_of(first[where], dim) ^ (half * FACE))
            if half == 0:
                upper = pltpu.roll(upper, FACE, 1)
            sides.append((upper, lower))
        up = jnp.where(low, sides[0][0], sides[1][0])
        down = jnp.where(low, sides[0][1], sides[1][1])
        for (_, parity), out in turns:
            is_lower = even if parity == 0 else jnp.logical_not(even)
            out[layout.pair_rows(pair), :] = jnp.where(is_lower, up, down)


def received(layout, here, dim, messages):
    even = (here[dim] & 1) == 0
    at_start = here[dim] == 0
    at_end = here[dim] == layout.sizes[dim] - 1
    zero = jnp.zeros((layout.species, WIDTH), jnp.float32)
    found = []
    for pair in range(layout.pairs(dim)):
        first, second = [
            messages[dim, parity][layout.pair_rows(pair), :] if (dim, parity) in messages else zero
            for parity in range(2)
        ]
        below = jnp.where(at_start, 0.0, jnp.where(even, second, first))
        above = jnp.where(at_end, 0.0, jnp.where(even, first, second))
        found.append((below, above))
    return found


def unpacked(lane, outside, where, mask):
    below, above = outside[where // 2]
    half = (where % 2) * FACE
    inside = lane & (FACE - 1)
    return picked(below, (inside ^ mask) + half), picked(above, inside + half)


def assemble(layout, here, dim, load_block, messages, mask_of, keep_of, emit, slab=None):
    lane = lanes(layout)
    low = lane < FACE
    count = layout.counts[dim]
    outside = None if messages is None else received(layout, here, dim, messages)
    zero = jnp.zeros((layout.species, WIDTH), jnp.float32)
    for where, start in enumerate(layout.layer(dim, 0)):
        if slab not in (None, start[0]):
            continue
        line = [start[:dim] + (step,) + start[dim + 1 :] for step in range(count)]
        blocks = [load_block(element, dim) for element in line]
        if outside is None:
            from_below, from_above = zero, zero
        else:
            from_below, from_above = unpacked(lane, outside, where, mask_of(start, dim))
        turned = [from_below]
        for step, element in list(enumerate(line))[1:]:
            shared = jnp.where(low, blocks[step], blocks[step - 1])
            turned.append(picked(shared, lane ^ mask_of(element, dim) ^ FACE))
        turned.append(from_above)
        for step, element in enumerate(line):
            value = blocks[step] + jnp.where(low, turned[step], turned[step + 1])
            if step in (0, count - 1):
                value = value * keep_of(element, dim)
            emit(element, value)


def halves(value):
    high = value.astype(jnp.bfloat16)
    return high, (value - high.astype(jnp.float32)).astype(jnp.bfloat16)


def dot(left, right, contract=((1,), (0,))):
    return lax.dot_general(left, right, (contract, ((), ())), preferred_element_type=jnp.float32)


def split_dot(left, right, contract):
    left_high, left_rest = halves(left)
    right_high, right_rest = halves(right)
    return (
        dot(left_high, right_high, contract)
        + dot(left_high, right_rest, contract)
        + dot(left_rest, right_high, contract)
    )


def stacked(value, local, faces):
    high, rest = halves(value)
    size = value.shape[0]
    for part, piece in enumerate((high, rest, high)):
        local[part * size : (part + 1) * size, :] = piece
    for number in range(faces.shape[0]):
        rows = slice(number * FACE, (number + 1) * FACE)
        for part, piece in enumerate((high, high, rest)):
            faces[number, part * FACE : (part + 1) * FACE, :] = piece[rows, :]
        faces[number, 3 * FACE :, :] = jnp.zeros((FACE, value.shape[1]), jnp.bfloat16)


def operator_kernel(fine, *outs):
    stacked(fine[...], *outs)


def smoother_kernel(inverse, four, coarse_four, two, coarse_two, *refs):
    *outs, right, left = refs
    right[...] = jnp.zeros_like(right)
    left[...] = jnp.zeros_like(left)
    start = 0
    for prolong, coarse in ((four, coarse_four), (two, coarse_two)):
        rows = slice(start, start + prolong.shape[0])
        left[rows, :] = prolong[...]
        right[rows, :] = split_dot(coarse[...], prolong[...], ((1,), (0,)))
        start += rounded(prolong.shape[0])
    corrections = split_dot(left[...], right[...], ((0,), (0,)))
    stacked(0.5 * (inverse[...] + corrections), *outs)


def rounded(count):
    return (count + 7) // 8 * 8


def first_kernel(layout, load, orient, boundary, *refs):
    turns = len(layout.turns())
    weights, refs = refs[:4], refs[4:]
    outs, (masks, keeps), fetched, refs = refs[:turns], refs[turns : turns + 2], *cut_at(refs, turns)
    staged, codes, fixed, arrived = refs
    small = [
        pltpu.make_async_copy(source, target, arrived.at[number])
        for number, (source, target) in enumerate(((orient, codes), (boundary, fixed)))
    ]
    strips = [
        pltpu.make_async_copy(
            load.at[:, columns(dim)], staged.at[:, columns(dim)], arrived.at[2 + dim]
        )
        for dim in range(3)
    ]
    fetches = [
        pltpu.make_async_copy(source, target, arrived.at[5 + number])
        for number, (source, target) in enumerate(zip(weights, fetched))
    ]
    for copy in small + strips + fetches:
        copy.start()
    here = places()
    for copy in small:
        copy.wait()
    tabulate(layout, here, codes, fixed, masks, keeps)
    for dim in range(3):
        strips[dim].wait()
        pack(
            layout,
            here,
            dim,
            lambda element, dim: staged[layout.rows(element), columns(dim)],
            table(layout, masks),
            outs,
        )
    for copy in fetches:
        copy.wait()


def cut_at(refs, turns):
    return refs[turns + 2 : turns + 6], refs[turns + 6 :]


def tabulate(layout, here, codes, boundary, masks, keeps):
    low = lax.broadcasted_iota(jnp.int32, (1, WIDTH), 1) < FACE
    for element in layout.elements():
        number = layout.number(element)
        for dim in range(3):
            mask = flip_mask(codes[(dim,) + element])
            masks[number : number + 1, columns(dim)] = jnp.full((1, WIDTH), mask, jnp.int32)
            at_start = (here[dim] == 0) & (element[dim] == 0)
            at_end = (here[dim] == layout.sizes[dim] - 1) & (element[dim] == layout.counts[dim] - 1)
            fixed_low = jnp.where(at_start, boundary[element + (2 * dim,)], 0)
            fixed_top = jnp.where(at_end, boundary[element + (2 * dim + 1,)], 0)
            fixed = jnp.where(low, fixed_low, fixed_top)
            keeps[number : number + 1, columns(dim)] = 1.0 - fixed.astype(jnp.float32)


def table(layout, ref):
    def row(element, dim):
        number = layout.number(element)
        return ref[number : number + 1, columns(dim)]

    return row


def scales(layout, kind, ref):
    def row(element, dim):
        value = ref[element[0], element[1], element[2] : element[2] + 1, columns(dim)]
        return value if kind == "operator" else 1.0 / value

    return row


def taken(layout, dims, refs):
    turns = layout.turns(dims)
    return dict(zip(turns, refs)), refs[len(turns) :]


def combined(kind, begun, result):
    if begun is None:
        return result
    return begun - result if kind == "operator" else begun + result


def local_kernel(layout, kind, value, masks, keeps, scaling, matrix, *refs):
    *before, out, split, summed = refs
    begun = before[0] if before else None
    here = places()
    factor = scales(layout, kind, scaling)
    nodes = value.shape[1]

    def assembled(dim, slab):
        def emit(element, result):
            high, rest = halves(result * factor(element, dim))
            for part, piece in enumerate((high, high, rest)):
                start = part * nodes + dim * WIDTH
                split[layout.rows(element), start : start + WIDTH] = piece

        assemble(
            layout,
            here,
            dim,
            lambda element, dim: value[layout.rows(element), columns(dim)],
            None,
            table(layout, masks),
            table(layout, keeps),
            emit,
            slab,
        )

    assembled(0, None)
    count = layout.counts[0]
    height = value.shape[0] // count
    for slab in range(count):
        assembled(1, slab)
        assembled(2, slab)
        rows = slice(slab * height, (slab + 1) * height)
        summed[rows, :] = dot(split[rows, :], matrix[...])
        for element in layout.layer(0, slab):
            for dim in DIMS:
                at = (layout.rows(element), columns(dim))
                result = summed[at] * factor(element, dim)
                out[at] = combined(kind, None if begun is None else begun[at], result)


def combined(kind, begun, result):
    if begun is None:
        return result
    return begun - result if kind == "operator" else begun + result


def strips_kernel(layout, kind, dims, local, value, *refs):
    messages, refs = (None, refs) if local else taken(layout, dims, refs)
    masks, keeps, scaling, matrix, *before, out, split, summed = refs
    begun = before[0] if before else None
    here = places()
    factor = scales(layout, kind, scaling)

    def assembled(place, slab):
        dim = dims[place]

        def emit(element, result):
            scaled = result * factor(element, dim)
            put_split(split, layout.rows(element), place, len(dims), scaled)

        assemble(
            layout,
            here,
            dim,
            lambda element, dim: value[layout.rows(element), columns(dim)],
            messages,
            table(layout, masks),
            table(layout, keeps),
            emit,
            slab,
        )

    if 0 in dims:
        assembled(dims.index(0), None)
    count = layout.counts[0]
    height = value.shape[0] // count
    for slab in range(count):
        for place, dim in enumerate(dims):
            if dim != 0:
                assembled(place, slab)
        rows = slice(slab * height, (slab + 1) * height)
        summed[rows, :] = dot(split[rows, :], matrix[...])
        for element in layout.layer(0, slab):
            for each in range(3):
                at = (layout.rows(element), columns(each))
                result = summed[at] * factor(element, each)
                out[at] = combined(kind, None if begun is None else begun[at], result)


def combined(kind, begun, result):
    if begun is None:
        return result
    return begun - result if kind == "operator" else begun + result


def outside_faces(layout, here, dims, messages, masks):
    lane = lanes(layout)
    for dim in dims:
        outside = received(layout, here, dim, messages)
        lower, upper = layout.sides(dim)
        for where, element in enumerate(lower):
            mask = table(layout, masks)(element, dim)
            from_below, from_above = unpacked(lane, outside, where, mask)
            yield 2 * dim, where, element, from_below
            yield 2 * dim + 1, where, upper[where], from_above


def faces_kernel(layout, kind, *refs):
    messages, refs = taken(layout, DIMS, refs)
    masks, scaling, faces, begun, *refs = refs
    turns = len(layout.turns())
    out, sent, scratch = refs[0], refs[1 : 1 + turns], refs[1 + turns :]
    splits, sums = scratch[:6], scratch[6:]
    here = places()
    factor = scales(layout, kind, scaling)
    low = lanes(layout) < FACE
    row_low = low[:1]

    def both(row, side):
        turned = pltpu.roll(row, FACE, 1)
        return jnp.where(row_low, turned, row) if side else jnp.where(row_low, row, turned)

    share = {}
    for number, where, element, face in outside_faces(layout, here, DIMS, messages, masks):
        value = face * both(factor(element, number // 2), number % 2)
        high = value.astype(jnp.bfloat16).astype(jnp.float32)
        rows = layout.pair_rows(where)
        splits[number][rows, :WIDTH] = jnp.where(low, high, value - high).astype(jnp.bfloat16)
        splits[number][rows, WIDTH:] = jnp.where(low, high, 0.0).astype(jnp.bfloat16)
        share.setdefault(element, []).append((number, rows))
    for number in range(6):
        sums[number][...] = dot(splits[number][...], faces[number])
    for element in layout.elements():
        for dim in DIMS:
            at = (layout.rows(element), columns(dim))
            parts = [sums[number][rows, columns(dim)] for number, rows in share.get(element, ())]
            if parts:
                result = sum(parts[1:], parts[0]) * factor(element, dim)
                out[at] = combined(kind, begun[at], result)
            else:
                out[at] = begun[at]
    for dim in DIMS:
        pack(
            layout,
            here,
            dim,
            lambda element, dim: out[layout.rows(element), columns(dim)],
            table(layout, masks),
            sent,
        )


def last_early_kernel(layout, value, *refs):
    messages, (masks, keeps, ready) = taken(layout, EARLY, refs)
    for dim in DIMS:

        def emit(element, result):
            ready[layout.rows(element), columns(dim)] = result

        assemble(
            layout,
            places(),
            dim,
            lambda element, dim: value[layout.rows(element), columns(dim)],
            None if dim == LATE else messages,
            table(layout, masks),
            table(layout, keeps),
            emit,
        )


def last_late_kernel(layout, begun, *refs):
    messages, (masks, out, ready, left) = taken(layout, (LATE,), refs)
    low = lanes(layout) < FACE

    def copy(source, dim):
        return pltpu.make_async_copy(source, out.at[:, columns(dim)], left.at[dim])

    copies = [copy(begun.at[:, columns(dim)], dim) for dim in EARLY]
    for each in copies:
        each.start()
    added = {}
    for number, _, element, face in outside_faces(layout, places(), (LATE,), messages, masks):
        part = jnp.where(low, 0.0, face) if number % 2 else jnp.where(low, face, 0.0)
        added[element] = added[element] + part if element in added else part
    for element in layout.elements():
        value = begun[layout.rows(element), columns(LATE)]
        ready[layout.rows(element), :] = value + added[element] if element in added else value
    copies.append(copy(ready, LATE))
    copies[-1].start()
    for each in copies:
        each.wait()


def in_vmem(count):
    return [pl.BlockSpec(memory_space=pltpu.VMEM)] * count


def in_hbm(count):
    return [pl.BlockSpec(memory_space=pltpu.HBM)] * count


PARAMS = pltpu.CompilerParams(vmem_limit_bytes=VMEM_LIMIT)


def kept_in_hbm(*values):
    return [pltpu.with_memory_space_constraint(value, pltpu.HBM) for value in values]


def cost(flops, size):
    return pl.CostEstimate(flops=flops, bytes_accessed=size, transcendentals=0)


def partners(layout, dim, parity):
    sizes = layout.sizes
    swap = {}
    for place in np.ndindex(*sizes):
        other = list(place)
        lower = place[dim] % 2 == parity
        at = place[dim] + (1 if lower else -1)
        if 0 <= at < sizes[dim]:
            other[dim] = at
        elif dim != 1 and sizes[1] % 2 == 0:
            other[1] = place[1] ^ 1
        elif sizes[dim] % 2 == 0:
            other[dim] = sizes[dim] - 1 - place[dim]
        swap[place] = tuple(other)
    return [
        (int(np.ravel_multi_index(place, sizes)), int(np.ravel_multi_index(other, sizes)))
        for place, other in swap.items()
    ]


def exchange(layout, messages):
    return {
        turn: lax.ppermute(message, AXES, partners(layout, *turn))
        for turn, message in zip(layout.turns(), messages)
    }


def body(
    load_raw,
    scaling,
    fine_matrix,
    fine_inverse,
    prolong_four,
    coarse_four,
    prolong_two,
    coarse_two,
    orient,
    boundary,
):
    counts, species, nodes = load_raw.shape[:3], load_raw.shape[3], load_raw.shape[4]
    layout = Layout(counts, species, tuple(lax.axis_size(axis) for axis in AXES))
    load = load_raw.reshape(-1, nodes)
    rows = load.shape[0]
    turns = layout.turns()
    message_shapes = tuple(layout.message(dim) for dim, _ in turns)
    whole = jax.ShapeDtypeStruct(load.shape, jnp.float32)
    matrix_shapes = (
        jax.ShapeDtypeStruct((3 * nodes, nodes), jnp.bfloat16),
        jax.ShapeDtypeStruct((2 * len(DIMS), 4 * FACE, nodes), jnp.bfloat16),
    )
    elements = len(layout.elements())
    tables = tuple(jax.ShapeDtypeStruct((elements, nodes), kind) for kind in (jnp.int32, jnp.float32))
    weights = (prolong_four.T, coarse_four, prolong_two.T, coarse_two)
    sides = jnp.transpose(boundary, (1, 2, 3, 0))

    sent = pl.pallas_call(
        functools.partial(first_kernel, layout),
        out_shape=message_shapes
        + tables
        + tuple(jax.ShapeDtypeStruct(weight.shape, weight.dtype) for weight in weights),
        in_specs=in_hbm(7),
        out_specs=tuple(in_vmem(len(turns) + 6)),
        scratch_shapes=[
            pltpu.VMEM(load.shape, jnp.float32),
            pltpu.SMEM(orient.shape, jnp.int32),
            pltpu.SMEM(sides.shape, jnp.int32),
            pltpu.SemaphoreType.DMA((9,)),
        ],
        compiler_params=PARAMS,
        name="pack",
    )(*kept_in_hbm(load, orient, sides, *weights))
    masks, keeps, *weights = sent[len(turns) :]

    stack = (rounded(prolong_four.shape[1]) + rounded(prolong_two.shape[1]), nodes)
    smoother = pl.pallas_call(
        smoother_kernel,
        out_shape=matrix_shapes,
        in_specs=in_vmem(5),
        out_specs=tuple(in_vmem(2)),
        scratch_shapes=[pltpu.VMEM(stack, jnp.float32), pltpu.VMEM(stack, jnp.float32)],
        compiler_params=PARAMS,
        cost_estimate=cost(2 * nodes * nodes * nodes, 8 * nodes * nodes),
        name="smoother",
    )(fine_inverse, *weights)
    operator = pl.pallas_call(
        operator_kernel,
        out_shape=matrix_shapes,
        in_specs=in_vmem(1),
        out_specs=tuple(in_vmem(2)),
        compiler_params=PARAMS,
        cost_estimate=cost(0, 10 * nodes * nodes),
        name="operator",
    )(fine_matrix)

    def stage(kind, value, messages, matrix, begun):
        before = () if begun is None else (begun,)
        begun = pl.pallas_call(
            functools.partial(local_kernel, layout, kind),
            out_shape=whole,
            in_specs=in_vmem(5 + len(before)),
            out_specs=in_vmem(1)[0],
            scratch_shapes=[
                pltpu.VMEM((rows, 3 * nodes), jnp.bfloat16),
                pltpu.VMEM(load.shape, jnp.float32),
            ],
            compiler_params=PARAMS,
            cost_estimate=cost(2 * rows * nodes * nodes, 0),
            name=kind + "_local",
        )(value, masks, keeps, scaling, matrix[0], *before)
        mine = [messages[turn] for turn in turns]
        heights = [len(side) * species for dim in DIMS for side in layout.sides(dim)]
        result, *sent = pl.pallas_call(
            functools.partial(faces_kernel, layout, kind),
            out_shape=(whole,) + message_shapes,
            in_specs=in_vmem(4 + len(mine)),
            out_specs=tuple(in_vmem(1 + len(turns))),
            scratch_shapes=[pltpu.VMEM((height, 4 * FACE), jnp.bfloat16) for height in heights]
            + [pltpu.VMEM((height, nodes), jnp.float32) for height in heights],
            compiler_params=PARAMS,
            cost_estimate=cost(8 * FACE * sum(heights) * nodes, 12 * rows * nodes),
            name=kind + "_faces",
        )(*mine, masks, scaling, matrix[1], begun)
        return result, sent

    first, sent = stage("smooth", load, exchange(layout, sent), smoother, None)
    left, sent = stage("operator", first, exchange(layout, sent), operator, load)
    total, sent = stage("smooth_more", left, exchange(layout, sent), smoother, first)
    messages = exchange(layout, sent)
    early = [messages[turn] for turn in layout.turns(EARLY)]
    late = [messages[turn] for turn in layout.turns((LATE,))]
    begun = pl.pallas_call(
        functools.partial(last_early_kernel, layout),
        out_shape=whole,
        in_specs=in_vmem(3 + len(early)),
        out_specs=in_vmem(1)[0],
        compiler_params=PARAMS,
        cost_estimate=cost(0, 8 * rows * nodes),
        name="last_early",
    )(total, *early, masks, keeps)
    result = pl.pallas_call(
        functools.partial(last_late_kernel, layout),
        out_shape=whole,
        in_specs=in_vmem(2 + len(late)),
        out_specs=in_hbm(1)[0],
        scratch_shapes=[pltpu.VMEM((rows, WIDTH), jnp.float32), pltpu.SemaphoreType.DMA((3,))],
        compiler_params=PARAMS,
        cost_estimate=cost(0, 8 * rows * nodes),
        name="last_late",
    )(begun, *late, masks)
    return result.reshape(load_raw.shape)


def solution(mesh):
    in_specs = (
        P("ex", "ey", "ez", None, None),
        P("ex", "ey", "ez", None),
        P(),
        P(),
        P(),
        P(),
        P(),
        P(),
        P(None, "ex", "ey", "ez"),
        P(None, "ex", "ey", "ez"),
    )
    out_specs = P("ex", "ey", "ez", None, None)
    return jax.shard_map(body, mesh=mesh, in_specs=in_specs, out_specs=out_specs, check_vma=False)
```

```python
import functools

import jax
import jax.numpy as jnp
from jax import lax
from jax.experimental import pallas as pl
from jax.experimental.pallas import tpu as pltpu
import numpy as np
from jax.sharding import PartitionSpec as P

FACE_SIDE = 8
FACE = FACE_SIDE * FACE_SIDE
WIDTH = 2 * FACE
AXES = ("ex", "ey", "ez")
TURNS = ((1, 1), (0, 1), (0, 0), (1, 0), (2, 1), (2, 0))
DIMS = (0, 1, 2)
EARLY = (1, 0)
LATE = 2
FETCHED = 5
VMEM_LIMIT = 24 * 1024 * 1024


class Layout:
    def __init__(self, counts, species, sizes):
        self.counts = counts
        self.species = species
        self.sizes = sizes

    def elements(self):
        spans = [range(count) for count in self.counts]
        return [(i, j, k) for i in spans[0] for j in spans[1] for k in spans[2]]

    def number(self, element):
        return (element[0] * self.counts[1] + element[1]) * self.counts[2] + element[2]

    def rows(self, element):
        start = self.number(element) * self.species
        return slice(start, start + self.species)

    def layer(self, dim, position):
        return [element for element in self.elements() if element[dim] == position]

    def pairs(self, dim):
        return (len(self.layer(dim, 0)) + 1) // 2

    def pair_rows(self, pair):
        return slice(pair * self.species, (pair + 1) * self.species)

    def turns(self, dims=(0, 1, 2)):
        return [
            (dim, parity) for dim, parity in TURNS if dim in dims and self.sizes[dim] > 1 + parity
        ]

    def sides(self, dim):
        return self.layer(dim, 0), self.layer(dim, self.counts[dim] - 1)

    def message(self, dim):
        return jax.ShapeDtypeStruct((self.pairs(dim) * self.species, WIDTH), jnp.float32)


def columns(dim):
    return slice(dim * WIDTH, (dim + 1) * WIDTH)


def lanes(layout):
    return lax.broadcasted_iota(jnp.int32, (layout.species, WIDTH), 1)


def picked(value, index):
    return jnp.take_along_axis(value, index, axis=1, mode="promise_in_bounds")


def flip_mask(code):
    reach = FACE_SIDE - 1
    return (code & 1) * (reach * FACE_SIDE) + (code >> 1) * reach


def places():
    return [lax.axis_index(axis) for axis in AXES]


def pack(layout, here, dim, load_block, mask_of, outs):
    turns = [(turn, out) for turn, out in zip(layout.turns(), outs) if turn[0] == dim]
    if not turns:
        return
    lane = lanes(layout)
    low = lane < FACE
    even = (here[dim] & 1) == 0
    first = layout.layer(dim, 0)
    last = layout.layer(dim, layout.counts[dim] - 1)
    for pair in range(layout.pairs(dim)):
        sides = []
        for half in range(2):
            where = min(2 * pair + half, len(first) - 1)
            upper = load_block(last[where], dim)
            lower = load_block(first[where], dim)
            lower = picked(lower, lane ^ mask_of(first[where], dim) ^ (half * FACE))
            if half == 0:
                upper = pltpu.roll(upper, FACE, 1)
            sides.append((upper, lower))
        up = jnp.where(low, sides[0][0], sides[1][0])
        down = jnp.where(low, sides[0][1], sides[1][1])
        for (_, parity), out in turns:
            is_lower = even if parity == 0 else jnp.logical_not(even)
            out[layout.pair_rows(pair), :] = jnp.where(is_lower, up, down)


def received(layout, here, dim, messages):
    even = (here[dim] & 1) == 0
    at_start = here[dim] == 0
    at_end = here[dim] == layout.sizes[dim] - 1
    zero = jnp.zeros((layout.species, WIDTH), jnp.float32)
    found = []
    for pair in range(layout.pairs(dim)):
        first, second = [
            messages[dim, parity][layout.pair_rows(pair), :] if (dim, parity) in messages else zero
            for parity in range(2)
        ]
        below = jnp.where(at_start, 0.0, jnp.where(even, second, first))
        above = jnp.where(at_end, 0.0, jnp.where(even, first, second))
        found.append((below, above))
    return found


def unpacked(lane, outside, where, mask):
    below, above = outside[where // 2]
    half = (where % 2) * FACE
    inside = lane & (FACE - 1)
    return picked(below, (inside ^ mask) + half), picked(above, inside + half)


def assemble(layout, here, dim, load_block, messages, mask_of, keep_of, emit, slab=None):
    lane = lanes(layout)
    low = lane < FACE
    count = layout.counts[dim]
    outside = None if messages is None else received(layout, here, dim, messages)
    zero = jnp.zeros((layout.species, WIDTH), jnp.float32)
    for where, start in enumerate(layout.layer(dim, 0)):
        if slab not in (None, start[0]):
            continue
        line = [start[:dim] + (step,) + start[dim + 1 :] for step in range(count)]
        blocks = [load_block(element, dim) for element in line]
        if outside is None:
            from_below, from_above = zero, zero
        else:
            from_below, from_above = unpacked(lane, outside, where, mask_of(start, dim))
        turned = [from_below]
        for step, element in list(enumerate(line))[1:]:
            shared = jnp.where(low, blocks[step], blocks[step - 1])
            turned.append(picked(shared, lane ^ mask_of(element, dim) ^ FACE))
        turned.append(from_above)
        for step, element in enumerate(line):
            value = blocks[step] + jnp.where(low, turned[step], turned[step + 1])
            if step in (0, count - 1):
                value = value * keep_of(element, dim)
            emit(element, value)


def halves(value):
    high = value.astype(jnp.bfloat16)
    return high, (value - high.astype(jnp.float32)).astype(jnp.bfloat16)


def dot(left, right, contract=((1,), (0,))):
    return lax.dot_general(left, right, (contract, ((), ())), preferred_element_type=jnp.float32)


def split_dot(left, right, contract):
    left_high, left_rest = halves(left)
    right_high, right_rest = halves(right)
    return (
        dot(left_high, right_high, contract)
        + dot(left_high, right_rest, contract)
        + dot(left_rest, right_high, contract)
    )


def stacked(value, local, faces):
    high, rest = halves(value)
    size = value.shape[0]
    for part, piece in enumerate((high, rest, high)):
        local[part * size : (part + 1) * size, :] = piece
    for number in range(faces.shape[0]):
        rows = slice(number * FACE, (number + 1) * FACE)
        for part, piece in enumerate((high, high, rest)):
            faces[number, part * FACE : (part + 1) * FACE, :] = piece[rows, :]
        faces[number, 3 * FACE :, :] = jnp.zeros((FACE, value.shape[1]), jnp.bfloat16)


def operator_kernel(fine, *outs):
    stacked(fine[...], *outs)


def smoother_kernel(inverse, four, coarse_four, two, coarse_two, *refs):
    *outs, right, left = refs
    right[...] = jnp.zeros_like(right)
    left[...] = jnp.zeros_like(left)
    start = 0
    for prolong, coarse in ((four, coarse_four), (two, coarse_two)):
        rows = slice(start, start + prolong.shape[0])
        left[rows, :] = prolong[...]
        right[rows, :] = split_dot(coarse[...], prolong[...], ((1,), (0,)))
        start += rounded(prolong.shape[0])
    corrections = split_dot(left[...], right[...], ((0,), (0,)))
    stacked(0.5 * (inverse[...] + corrections), *outs)


def rounded(count):
    return (count + 7) // 8 * 8


def first_kernel(layout, load, orient, boundary, *refs):
    turns = len(layout.turns())
    small, refs = refs[:FETCHED], refs[FETCHED:]
    outs, masks, keeps, staged = refs[:turns], *refs[turns : turns + 3]
    fetched, (codes, fixed, arrived) = refs[turns + 3 : turns + 3 + FETCHED], refs[-3:]
    scalars = [
        pltpu.make_async_copy(source, target, arrived.at[number])
        for number, (source, target) in enumerate(((orient, codes), (boundary, fixed)))
    ]
    strips = [
        pltpu.make_async_copy(
            load.at[:, columns(dim)], staged.at[:, columns(dim)], arrived.at[2 + dim]
        )
        for dim in DIMS
    ]
    fetches = [
        pltpu.make_async_copy(source, target, arrived.at[5 + number])
        for number, (source, target) in enumerate(zip(small, fetched))
    ]
    for copy in scalars + strips + fetches:
        copy.start()
    here = places()
    for copy in scalars:
        copy.wait()
    tabulate(layout, here, codes, fixed, masks, keeps)
    for dim in DIMS:
        strips[dim].wait()
        pack(
            layout,
            here,
            dim,
            lambda element, dim: staged[layout.rows(element), columns(dim)],
            table(layout, masks),
            outs,
        )
    for copy in fetches:
        copy.wait()


def tabulate(layout, here, codes, boundary, masks, keeps):
    low = lax.broadcasted_iota(jnp.int32, (1, WIDTH), 1) < FACE
    for element in layout.elements():
        number = layout.number(element)
        for dim in range(3):
            mask = flip_mask(codes[(dim,) + element])
            masks[number : number + 1, columns(dim)] = jnp.full((1, WIDTH), mask, jnp.int32)
            at_start = (here[dim] == 0) & (element[dim] == 0)
            at_end = (here[dim] == layout.sizes[dim] - 1) & (element[dim] == layout.counts[dim] - 1)
            fixed_low = jnp.where(at_start, boundary[element + (2 * dim,)], 0)
            fixed_top = jnp.where(at_end, boundary[element + (2 * dim + 1,)], 0)
            fixed = jnp.where(low, fixed_low, fixed_top)
            keeps[number : number + 1, columns(dim)] = 1.0 - fixed.astype(jnp.float32)


def table(layout, ref):
    def row(element, dim):
        number = layout.number(element)
        return ref[number : number + 1, columns(dim)]

    return row


def scales(layout, kind, ref):
    def row(element, dim):
        value = ref[element[0], element[1], element[2] : element[2] + 1, columns(dim)]
        return value if kind == "operator" else 1.0 / value

    return row


def taken(layout, dims, refs):
    turns = layout.turns(dims)
    return dict(zip(turns, refs)), refs[len(turns) :]


def combined(kind, begun, result):
    if begun is None:
        return result
    return begun - result if kind == "operator" else begun + result


def local_kernel(layout, kind, value, masks, keeps, scaling, matrix, *refs):
    *before, out, split, summed = refs
    begun = before[0] if before else None
    here = places()
    factor = scales(layout, kind, scaling)
    nodes = value.shape[1]

    def assembled(dim, slab):
        def emit(element, result):
            high, rest = halves(result * factor(element, dim))
            for part, piece in enumerate((high, high, rest)):
                start = part * nodes + dim * WIDTH
                split[layout.rows(element), start : start + WIDTH] = piece

        assemble(
            layout,
            here,
            dim,
            lambda element, dim: value[layout.rows(element), columns(dim)],
            None,
            table(layout, masks),
            table(layout, keeps),
            emit,
            slab,
        )

    assembled(0, None)
    count = layout.counts[0]
    height = value.shape[0] // count
    for slab in range(count):
        assembled(1, slab)
        assembled(2, slab)
        rows = slice(slab * height, (slab + 1) * height)
        summed[rows, :] = dot(split[rows, :], matrix[...])
        for element in layout.layer(0, slab):
            for dim in DIMS:
                at = (layout.rows(element), columns(dim))
                result = summed[at] * factor(element, dim)
                out[at] = combined(kind, None if begun is None else begun[at], result)


def combined(kind, begun, result):
    if begun is None:
        return result
    return begun - result if kind == "operator" else begun + result


def strips_kernel(layout, kind, dims, local, value, *refs):
    messages, refs = (None, refs) if local else taken(layout, dims, refs)
    masks, keeps, scaling, matrix, *before, out, split, summed = refs
    begun = before[0] if before else None
    here = places()
    factor = scales(layout, kind, scaling)

    def assembled(place, slab):
        dim = dims[place]

        def emit(element, result):
            scaled = result * factor(element, dim)
            put_split(split, layout.rows(element), place, len(dims), scaled)

        assemble(
            layout,
            here,
            dim,
            lambda element, dim: value[layout.rows(element), columns(dim)],
            messages,
            table(layout, masks),
            table(layout, keeps),
            emit,
            slab,
        )

    if 0 in dims:
        assembled(dims.index(0), None)
    count = layout.counts[0]
    height = value.shape[0] // count
    for slab in range(count):
        for place, dim in enumerate(dims):
            if dim != 0:
                assembled(place, slab)
        rows = slice(slab * height, (slab + 1) * height)
        summed[rows, :] = dot(split[rows, :], matrix[...])
        for element in layout.layer(0, slab):
            for each in range(3):
                at = (layout.rows(element), columns(each))
                result = summed[at] * factor(element, each)
                out[at] = combined(kind, None if begun is None else begun[at], result)


def combined(kind, begun, result):
    if begun is None:
        return result
    return begun - result if kind == "operator" else begun + result


def outside_faces(layout, here, dims, messages, masks):
    lane = lanes(layout)
    for dim in dims:
        outside = received(layout, here, dim, messages)
        lower, upper = layout.sides(dim)
        for where, element in enumerate(lower):
            mask = table(layout, masks)(element, dim)
            from_below, from_above = unpacked(lane, outside, where, mask)
            yield 2 * dim, where, element, from_below
            yield 2 * dim + 1, where, upper[where], from_above


def faces_kernel(layout, kind, *refs):
    messages, refs = taken(layout, DIMS, refs)
    masks, scaling, faces, begun, *refs = refs
    turns = len(layout.turns())
    out, sent, scratch = refs[0], refs[1 : 1 + turns], refs[1 + turns :]
    splits, sums = scratch[:6], scratch[6:]
    here = places()
    factor = scales(layout, kind, scaling)
    low = lanes(layout) < FACE
    row_low = low[:1]

    def both(row, side):
        turned = pltpu.roll(row, FACE, 1)
        return jnp.where(row_low, turned, row) if side else jnp.where(row_low, row, turned)

    share = {}
    for number, where, element, face in outside_faces(layout, here, DIMS, messages, masks):
        value = face * both(factor(element, number // 2), number % 2)
        high = value.astype(jnp.bfloat16).astype(jnp.float32)
        rows = layout.pair_rows(where)
        splits[number][rows, :WIDTH] = jnp.where(low, high, value - high).astype(jnp.bfloat16)
        splits[number][rows, WIDTH:] = jnp.where(low, high, 0.0).astype(jnp.bfloat16)
        share.setdefault(element, []).append((number, rows))
    for number in range(6):
        sums[number][...] = dot(splits[number][...], faces[number])
    for element in layout.elements():
        for dim in DIMS:
            at = (layout.rows(element), columns(dim))
            parts = [sums[number][rows, columns(dim)] for number, rows in share.get(element, ())]
            if parts:
                result = sum(parts[1:], parts[0]) * factor(element, dim)
                out[at] = combined(kind, begun[at], result)
            else:
                out[at] = begun[at]
    for dim in DIMS:
        pack(
            layout,
            here,
            dim,
            lambda element, dim: out[layout.rows(element), columns(dim)],
            table(layout, masks),
            sent,
        )


def last_early_kernel(layout, value, *refs):
    messages, (masks, keeps, ready) = taken(layout, EARLY, refs)
    for dim in DIMS:

        def emit(element, result):
            ready[layout.rows(element), columns(dim)] = result

        assemble(
            layout,
            places(),
            dim,
            lambda element, dim: value[layout.rows(element), columns(dim)],
            None if dim == LATE else messages,
            table(layout, masks),
            table(layout, keeps),
            emit,
        )


def last_late_kernel(layout, begun, *refs):
    messages, (masks, out, ready, left) = taken(layout, (LATE,), refs)
    low = lanes(layout) < FACE

    def copy(source, dim):
        return pltpu.make_async_copy(source, out.at[:, columns(dim)], left.at[dim])

    copies = [copy(begun.at[:, columns(dim)], dim) for dim in EARLY]
    for each in copies:
        each.start()
    added = {}
    for number, _, element, face in outside_faces(layout, places(), (LATE,), messages, masks):
        part = jnp.where(low, 0.0, face) if number % 2 else jnp.where(low, face, 0.0)
        added[element] = added[element] + part if element in added else part
    for element in layout.elements():
        value = begun[layout.rows(element), columns(LATE)]
        ready[layout.rows(element), :] = value + added[element] if element in added else value
    copies.append(copy(ready, LATE))
    copies[-1].start()
    for each in copies:
        each.wait()


def in_vmem(count):
    return [pl.BlockSpec(memory_space=pltpu.VMEM)] * count


def in_hbm(count):
    return [pl.BlockSpec(memory_space=pltpu.HBM)] * count


PARAMS = pltpu.CompilerParams(vmem_limit_bytes=VMEM_LIMIT)


def kept_in_hbm(*values):
    return [pltpu.with_memory_space_constraint(value, pltpu.HBM) for value in values]


def cost(flops, size):
    return pl.CostEstimate(flops=flops, bytes_accessed=size, transcendentals=0)


def partners(layout, dim, parity):
    sizes = layout.sizes
    swap = {}
    for place in np.ndindex(*sizes):
        other = list(place)
        lower = place[dim] % 2 == parity
        at = place[dim] + (1 if lower else -1)
        if 0 <= at < sizes[dim]:
            other[dim] = at
        elif dim != 1 and sizes[1] % 2 == 0:
            other[1] = place[1] ^ 1
        elif sizes[dim] % 2 == 0:
            other[dim] = sizes[dim] - 1 - place[dim]
        swap[place] = tuple(other)
    return [
        (int(np.ravel_multi_index(place, sizes)), int(np.ravel_multi_index(other, sizes)))
        for place, other in swap.items()
    ]


def exchange(layout, messages):
    return {
        turn: lax.ppermute(message, AXES, partners(layout, *turn))
        for turn, message in zip(layout.turns(), messages)
    }


def body(
    load_raw,
    scaling,
    fine_matrix,
    fine_inverse,
    prolong_four,
    coarse_four,
    prolong_two,
    coarse_two,
    orient,
    boundary,
):
    counts, species, nodes = load_raw.shape[:3], load_raw.shape[3], load_raw.shape[4]
    layout = Layout(counts, species, tuple(lax.axis_size(axis) for axis in AXES))
    load = load_raw.reshape(-1, nodes)
    rows = load.shape[0]
    turns = layout.turns()
    message_shapes = tuple(layout.message(dim) for dim, _ in turns)
    whole = jax.ShapeDtypeStruct(load.shape, jnp.float32)
    matrix_shapes = (
        jax.ShapeDtypeStruct((3 * nodes, nodes), jnp.bfloat16),
        jax.ShapeDtypeStruct((2 * len(DIMS), 4 * FACE, nodes), jnp.bfloat16),
    )
    elements = len(layout.elements())
    tables = tuple(jax.ShapeDtypeStruct((elements, nodes), kind) for kind in (jnp.int32, jnp.float32))
    small = (scaling, prolong_four.T, coarse_four, prolong_two.T, coarse_two)
    sides = jnp.transpose(boundary, (1, 2, 3, 0))

    *sent, masks, keeps, load, scaling, four, coarse_four, two, coarse_two = pl.pallas_call(
        functools.partial(first_kernel, layout),
        out_shape=message_shapes
        + tables
        + (whole,)
        + tuple(jax.ShapeDtypeStruct(each.shape, each.dtype) for each in small),
        in_specs=in_hbm(3 + FETCHED),
        out_specs=tuple(in_vmem(len(turns) + 3 + FETCHED)),
        scratch_shapes=[
            pltpu.SMEM(orient.shape, jnp.int32),
            pltpu.SMEM(sides.shape, jnp.int32),
            pltpu.SemaphoreType.DMA((5 + FETCHED,)),
        ],
        compiler_params=PARAMS,
        name="pack",
    )(*kept_in_hbm(load, orient, sides, *small))

    stack = (rounded(prolong_four.shape[1]) + rounded(prolong_two.shape[1]), nodes)
    smoother = pl.pallas_call(
        smoother_kernel,
        out_shape=matrix_shapes,
        in_specs=in_vmem(5),
        out_specs=tuple(in_vmem(2)),
        scratch_shapes=[pltpu.VMEM(stack, jnp.float32), pltpu.VMEM(stack, jnp.float32)],
        compiler_params=PARAMS,
        cost_estimate=cost(2 * nodes * nodes * nodes, 8 * nodes * nodes),
        name="smoother",
    )(fine_inverse, four, coarse_four, two, coarse_two)
    operator = pl.pallas_call(
        operator_kernel,
        out_shape=matrix_shapes,
        in_specs=in_vmem(1),
        out_specs=tuple(in_vmem(2)),
        compiler_params=PARAMS,
        cost_estimate=cost(0, 10 * nodes * nodes),
        name="operator",
    )(fine_matrix)

    def stage(kind, value, messages, matrix, begun):
        before = () if begun is None else (begun,)
        begun = pl.pallas_call(
            functools.partial(local_kernel, layout, kind),
            out_shape=whole,
            in_specs=in_vmem(5 + len(before)),
            out_specs=in_vmem(1)[0],
            scratch_shapes=[
                pltpu.VMEM((rows, 3 * nodes), jnp.bfloat16),
                pltpu.VMEM(load.shape, jnp.float32),
            ],
            compiler_params=PARAMS,
            cost_estimate=cost(2 * rows * nodes * nodes, 0),
            name=kind + "_local",
        )(value, masks, keeps, scaling, matrix[0], *before)
        mine = [messages[turn] for turn in turns]
        heights = [len(side) * species for dim in DIMS for side in layout.sides(dim)]
        result, *sent = pl.pallas_call(
            functools.partial(faces_kernel, layout, kind),
            out_shape=(whole,) + message_shapes,
            in_specs=in_vmem(4 + len(mine)),
            out_specs=tuple(in_vmem(1 + len(turns))),
            scratch_shapes=[pltpu.VMEM((height, 4 * FACE), jnp.bfloat16) for height in heights]
            + [pltpu.VMEM((height, nodes), jnp.float32) for height in heights],
            compiler_params=PARAMS,
            cost_estimate=cost(8 * FACE * sum(heights) * nodes, 12 * rows * nodes),
            name=kind + "_faces",
        )(*mine, masks, scaling, matrix[1], begun)
        return result, sent

    first, sent = stage("smooth", load, exchange(layout, sent), smoother, None)
    left, sent = stage("operator", first, exchange(layout, sent), operator, load)
    total, sent = stage("smooth_more", left, exchange(layout, sent), smoother, first)
    messages = exchange(layout, sent)
    early = [messages[turn] for turn in layout.turns(EARLY)]
    late = [messages[turn] for turn in layout.turns((LATE,))]
    begun = pl.pallas_call(
        functools.partial(last_early_kernel, layout),
        out_shape=whole,
        in_specs=in_vmem(3 + len(early)),
        out_specs=in_vmem(1)[0],
        compiler_params=PARAMS,
        cost_estimate=cost(0, 8 * rows * nodes),
        name="last_early",
    )(total, *early, masks, keeps)
    result = pl.pallas_call(
        functools.partial(last_late_kernel, layout),
        out_shape=whole,
        in_specs=in_vmem(2 + len(late)),
        out_specs=in_hbm(1)[0],
        scratch_shapes=[pltpu.VMEM((rows, WIDTH), jnp.float32), pltpu.SemaphoreType.DMA((3,))],
        compiler_params=PARAMS,
        cost_estimate=cost(0, 8 * rows * nodes),
        name="last_late",
    )(begun, *late, masks)
    return result.reshape(load_raw.shape)


def solution(mesh):
    in_specs = (
        P("ex", "ey", "ez", None, None),
        P("ex", "ey", "ez", None),
        P(),
        P(),
        P(),
        P(),
        P(),
        P(),
        P(None, "ex", "ey", "ez"),
        P(None, "ex", "ey", "ez"),
    )
    out_specs = P("ex", "ey", "ez", None, None)
    return jax.shard_map(body, mesh=mesh, in_specs=in_specs, out_specs=out_specs, check_vma=False)
```

```python
import functools

import jax
import jax.numpy as jnp
from jax import lax
from jax.experimental import pallas as pl
from jax.experimental.pallas import tpu as pltpu
import numpy as np
from jax.sharding import PartitionSpec as P

FACE_SIDE = 8
FACE = FACE_SIDE * FACE_SIDE
WIDTH = 2 * FACE
AXES = ("ex", "ey", "ez")
TURNS = ((1, 1), (0, 0), (0, 1), (1, 0), (2, 1), (2, 0))
DIMS = (0, 1, 2)
EARLY = (1, 0)
LATE = 2
FETCHED = 5
VMEM_LIMIT = 24 * 1024 * 1024


class Layout:
    def __init__(self, counts, species, sizes):
        self.counts = counts
        self.species = species
        self.sizes = sizes

    def elements(self):
        spans = [range(count) for count in self.counts]
        return [(i, j, k) for i in spans[0] for j in spans[1] for k in spans[2]]

    def number(self, element):
        return (element[0] * self.counts[1] + element[1]) * self.counts[2] + element[2]

    def rows(self, element):
        start = self.number(element) * self.species
        return slice(start, start + self.species)

    def layer(self, dim, position):
        return [element for element in self.elements() if element[dim] == position]

    def pairs(self, dim):
        return (len(self.layer(dim, 0)) + 1) // 2

    def pair_rows(self, pair):
        return slice(pair * self.species, (pair + 1) * self.species)

    def turns(self, dims=(0, 1, 2)):
        return [
            (dim, parity) for dim, parity in TURNS if dim in dims and self.sizes[dim] > 1 + parity
        ]

    def sides(self, dim):
        return self.layer(dim, 0), self.layer(dim, self.counts[dim] - 1)

    def message(self, dim):
        return jax.ShapeDtypeStruct((self.pairs(dim) * self.species, WIDTH), jnp.float32)


def columns(dim):
    return slice(dim * WIDTH, (dim + 1) * WIDTH)


def lanes(layout):
    return lax.broadcasted_iota(jnp.int32, (layout.species, WIDTH), 1)


def picked(value, index):
    return jnp.take_along_axis(value, index, axis=1, mode="promise_in_bounds")


def flip_mask(code):
    reach = FACE_SIDE - 1
    return (code & 1) * (reach * FACE_SIDE) + (code >> 1) * reach


def places():
    return [lax.axis_index(axis) for axis in AXES]


def pack(layout, here, dim, load_block, mask_of, outs):
    turns = [(turn, out) for turn, out in zip(layout.turns(), outs) if turn[0] == dim]
    if not turns:
        return
    lane = lanes(layout)
    low = lane < FACE
    even = (here[dim] & 1) == 0
    first = layout.layer(dim, 0)
    last = layout.layer(dim, layout.counts[dim] - 1)
    for pair in range(layout.pairs(dim)):
        sides = []
        for half in range(2):
            where = min(2 * pair + half, len(first) - 1)
            upper = load_block(last[where], dim)
            lower = load_block(first[where], dim)
            lower = picked(lower, lane ^ mask_of(first[where], dim) ^ (half * FACE))
            if half == 0:
                upper = pltpu.roll(upper, FACE, 1)
            sides.append((upper, lower))
        up = jnp.where(low, sides[0][0], sides[1][0])
        down = jnp.where(low, sides[0][1], sides[1][1])
        for (_, parity), out in turns:
            is_lower = even if parity == 0 else jnp.logical_not(even)
            out[layout.pair_rows(pair), :] = jnp.where(is_lower, up, down)


def received(layout, here, dim, messages):
    even = (here[dim] & 1) == 0
    at_start = here[dim] == 0
    at_end = here[dim] == layout.sizes[dim] - 1
    zero = jnp.zeros((layout.species, WIDTH), jnp.float32)
    found = []
    for pair in range(layout.pairs(dim)):
        first, second = [
            messages[dim, parity][layout.pair_rows(pair), :] if (dim, parity) in messages else zero
            for parity in range(2)
        ]
        below = jnp.where(at_start, 0.0, jnp.where(even, second, first))
        above = jnp.where(at_end, 0.0, jnp.where(even, first, second))
        found.append((below, above))
    return found


def unpacked(lane, outside, where, mask):
    below, above = outside[where // 2]
    half = (where % 2) * FACE
    inside = lane & (FACE - 1)
    return picked(below, (inside ^ mask) + half), picked(above, inside + half)


def assemble(layout, here, dim, load_block, messages, mask_of, keep_of, emit, slab=None):
    lane = lanes(layout)
    low = lane < FACE
    count = layout.counts[dim]
    outside = None if messages is None else received(layout, here, dim, messages)
    zero = jnp.zeros((layout.species, WIDTH), jnp.float32)
    for where, start in enumerate(layout.layer(dim, 0)):
        if slab not in (None, start[0]):
            continue
        line = [start[:dim] + (step,) + start[dim + 1 :] for step in range(count)]
        blocks = [load_block(element, dim) for element in line]
        if outside is None:
            from_below, from_above = zero, zero
        else:
            from_below, from_above = unpacked(lane, outside, where, mask_of(start, dim))
        turned = [from_below]
        for step, element in list(enumerate(line))[1:]:
            shared = jnp.where(low, blocks[step], blocks[step - 1])
            turned.append(picked(shared, lane ^ mask_of(element, dim) ^ FACE))
        turned.append(from_above)
        for step, element in enumerate(line):
            value = blocks[step] + jnp.where(low, turned[step], turned[step + 1])
            if step in (0, count - 1):
                value = value * keep_of(element, dim)
            emit(element, value)


def halves(value):
    high = value.astype(jnp.bfloat16)
    return high, (value - high.astype(jnp.float32)).astype(jnp.bfloat16)


def dot(left, right, contract=((1,), (0,))):
    return lax.dot_general(left, right, (contract, ((), ())), preferred_element_type=jnp.float32)


def split_dot(left, right, contract):
    left_high, left_rest = halves(left)
    right_high, right_rest = halves(right)
    return (
        dot(left_high, right_high, contract)
        + dot(left_high, right_rest, contract)
        + dot(left_rest, right_high, contract)
    )


def stacked(value, local, faces):
    high, rest = halves(value)
    size = value.shape[0]
    for part, piece in enumerate((high, rest, high)):
        local[part * size : (part + 1) * size, :] = piece
    for number in range(faces.shape[0]):
        rows = slice(number * FACE, (number + 1) * FACE)
        for part, piece in enumerate((high, high, rest)):
            faces[number, part * FACE : (part + 1) * FACE, :] = piece[rows, :]
        faces[number, 3 * FACE :, :] = jnp.zeros((FACE, value.shape[1]), jnp.bfloat16)


def operator_kernel(fine, *outs):
    stacked(fine[...], *outs)


def smoother_kernel(inverse, four, coarse_four, two, coarse_two, *refs):
    *outs, right, left = refs
    right[...] = jnp.zeros_like(right)
    left[...] = jnp.zeros_like(left)
    start = 0
    for prolong, coarse in ((four, coarse_four), (two, coarse_two)):
        rows = slice(start, start + prolong.shape[0])
        left[rows, :] = prolong[...]
        right[rows, :] = split_dot(coarse[...], prolong[...], ((1,), (0,)))
        start += rounded(prolong.shape[0])
    corrections = split_dot(left[...], right[...], ((0,), (0,)))
    stacked(0.5 * (inverse[...] + corrections), *outs)


def rounded(count):
    return (count + 7) // 8 * 8


def first_kernel(layout, load, orient, boundary, *refs):
    turns = len(layout.turns())
    small, refs = refs[:FETCHED], refs[FETCHED:]
    outs, masks, keeps, staged = refs[:turns], *refs[turns : turns + 3]
    fetched, (codes, fixed, arrived) = refs[turns + 3 : turns + 3 + FETCHED], refs[-3:]
    scalars = [
        pltpu.make_async_copy(source, target, arrived.at[number])
        for number, (source, target) in enumerate(((orient, codes), (boundary, fixed)))
    ]
    strips = [
        pltpu.make_async_copy(
            load.at[:, columns(dim)], staged.at[:, columns(dim)], arrived.at[2 + dim]
        )
        for dim in DIMS
    ]
    fetches = [
        pltpu.make_async_copy(source, target, arrived.at[5 + number])
        for number, (source, target) in enumerate(zip(small, fetched))
    ]
    for copy in scalars + strips + fetches:
        copy.start()
    here = places()
    for copy in scalars:
        copy.wait()
    tabulate(layout, here, codes, fixed, masks, keeps)
    for dim in DIMS:
        strips[dim].wait()
        pack(
            layout,
            here,
            dim,
            lambda element, dim: staged[layout.rows(element), columns(dim)],
            table(layout, masks),
            outs,
        )
    for copy in fetches:
        copy.wait()


def tabulate(layout, here, codes, boundary, masks, keeps):
    low = lax.broadcasted_iota(jnp.int32, (1, WIDTH), 1) < FACE
    for element in layout.elements():
        number = layout.number(element)
        for dim in range(3):
            mask = flip_mask(codes[(dim,) + element])
            masks[number : number + 1, columns(dim)] = jnp.full((1, WIDTH), mask, jnp.int32)
            at_start = (here[dim] == 0) & (element[dim] == 0)
            at_end = (here[dim] == layout.sizes[dim] - 1) & (element[dim] == layout.counts[dim] - 1)
            fixed_low = jnp.where(at_start, boundary[element + (2 * dim,)], 0)
            fixed_top = jnp.where(at_end, boundary[element + (2 * dim + 1,)], 0)
            fixed = jnp.where(low, fixed_low, fixed_top)
            keeps[number : number + 1, columns(dim)] = 1.0 - fixed.astype(jnp.float32)


def table(layout, ref):
    def row(element, dim):
        number = layout.number(element)
        return ref[number : number + 1, columns(dim)]

    return row


def scales(layout, kind, ref):
    def row(element, dim):
        value = ref[element[0], element[1], element[2] : element[2] + 1, columns(dim)]
        return value if kind == "operator" else 1.0 / value

    return row


def taken(layout, dims, refs):
    turns = layout.turns(dims)
    return dict(zip(turns, refs)), refs[len(turns) :]


def combined(kind, begun, result):
    if begun is None:
        return result
    return begun - result if kind == "operator" else begun + result


def local_kernel(layout, kind, value, masks, keeps, scaling, matrix, *refs):
    *before, out, split, summed = refs
    begun = before[0] if before else None
    here = places()
    factor = scales(layout, kind, scaling)
    nodes = value.shape[1]

    def assembled(dim, slab):
        def emit(element, result):
            high, rest = halves(result * factor(element, dim))
            for part, piece in enumerate((high, high, rest)):
                start = part * nodes + dim * WIDTH
                split[layout.rows(element), start : start + WIDTH] = piece

        assemble(
            layout,
            here,
            dim,
            lambda element, dim: value[layout.rows(element), columns(dim)],
            None,
            table(layout, masks),
            table(layout, keeps),
            emit,
            slab,
        )

    assembled(0, None)
    count = layout.counts[0]
    height = value.shape[0] // count
    for slab in range(count):
        assembled(1, slab)
        assembled(2, slab)
        rows = slice(slab * height, (slab + 1) * height)
        summed[rows, :] = dot(split[rows, :], matrix[...])
        for element in layout.layer(0, slab):
            for dim in DIMS:
                at = (layout.rows(element), columns(dim))
                result = summed[at] * factor(element, dim)
                out[at] = combined(kind, None if begun is None else begun[at], result)


def combined(kind, begun, result):
    if begun is None:
        return result
    return begun - result if kind == "operator" else begun + result


def strips_kernel(layout, kind, dims, local, value, *refs):
    messages, refs = (None, refs) if local else taken(layout, dims, refs)
    masks, keeps, scaling, matrix, *before, out, split, summed = refs
    begun = before[0] if before else None
    here = places()
    factor = scales(layout, kind, scaling)

    def assembled(place, slab):
        dim = dims[place]

        def emit(element, result):
            scaled = result * factor(element, dim)
            put_split(split, layout.rows(element), place, len(dims), scaled)

        assemble(
            layout,
            here,
            dim,
            lambda element, dim: value[layout.rows(element), columns(dim)],
            messages,
            table(layout, masks),
            table(layout, keeps),
            emit,
            slab,
        )

    if 0 in dims:
        assembled(dims.index(0), None)
    count = layout.counts[0]
    height = value.shape[0] // count
    for slab in range(count):
        for place, dim in enumerate(dims):
            if dim != 0:
                assembled(place, slab)
        rows = slice(slab * height, (slab + 1) * height)
        summed[rows, :] = dot(split[rows, :], matrix[...])
        for element in layout.layer(0, slab):
            for each in range(3):
                at = (layout.rows(element), columns(each))
                result = summed[at] * factor(element, each)
                out[at] = combined(kind, None if begun is None else begun[at], result)


def combined(kind, begun, result):
    if begun is None:
        return result
    return begun - result if kind == "operator" else begun + result


def outside_faces(layout, here, dims, messages, masks):
    lane = lanes(layout)
    for dim in dims:
        outside = received(layout, here, dim, messages)
        lower, upper = layout.sides(dim)
        for where, element in enumerate(lower):
            mask = table(layout, masks)(element, dim)
            from_below, from_above = unpacked(lane, outside, where, mask)
            yield 2 * dim, where, element, from_below
            yield 2 * dim + 1, where, upper[where], from_above


def faces_kernel(layout, kind, dims, *refs):
    messages, refs = taken(layout, dims, refs)
    masks, scaling, faces, begun, out, *refs = refs
    turns = len(layout.turns()) if LATE in dims else 0
    sent, scratch = refs[:turns], refs[turns:]
    count = 2 * len(dims)
    splits, sums = scratch[:count], scratch[count:]
    here = places()
    factor = scales(layout, kind, scaling)
    low = lanes(layout) < FACE
    row_low = low[:1]

    def both(row, side):
        turned = pltpu.roll(row, FACE, 1)
        return jnp.where(row_low, turned, row) if side else jnp.where(row_low, row, turned)

    share = {}
    for place, dim in enumerate(dims):
        for number, where, element, face in outside_faces(layout, here, (dim,), messages, masks):
            side = number % 2
            value = face * both(factor(element, dim), side)
            high = value.astype(jnp.bfloat16).astype(jnp.float32)
            rows = layout.pair_rows(where)
            split = splits[2 * place + side]
            split[rows, :WIDTH] = jnp.where(low, value, value - high).astype(jnp.bfloat16)
            split[rows, WIDTH:] = jnp.where(low, value, 0.0).astype(jnp.bfloat16)
            share.setdefault(element, []).append((2 * place + side, rows))
        for side in range(2):
            at = 2 * place + side
            sums[at][...] = dot(splits[at][...], faces[2 * dim + side])
    for element in layout.elements():
        for dim in DIMS:
            at = (layout.rows(element), columns(dim))
            parts = [sums[number][rows, columns(dim)] for number, rows in share.get(element, ())]
            if parts:
                result = sum(parts[1:], parts[0]) * factor(element, dim)
                out[at] = combined(kind, begun[at], result)
            else:
                out[at] = begun[at]
    if sent:
        for dim in DIMS:
            pack(
                layout,
                here,
                dim,
                lambda element, dim: out[layout.rows(element), columns(dim)],
                table(layout, masks),
                sent,
            )


def last_early_kernel(layout, value, *refs):
    messages, (masks, keeps, ready) = taken(layout, EARLY, refs)
    for dim in DIMS:

        def emit(element, result):
            ready[layout.rows(element), columns(dim)] = result

        assemble(
            layout,
            places(),
            dim,
            lambda element, dim: value[layout.rows(element), columns(dim)],
            None if dim == LATE else messages,
            table(layout, masks),
            table(layout, keeps),
            emit,
        )


def last_late_kernel(layout, begun, *refs):
    messages, (masks, out, ready, left) = taken(layout, (LATE,), refs)
    low = lanes(layout) < FACE

    def copy(source, dim):
        return pltpu.make_async_copy(source, out.at[:, columns(dim)], left.at[dim])

    copies = [copy(begun.at[:, columns(dim)], dim) for dim in EARLY]
    for each in copies:
        each.start()
    added = {}
    for number, _, element, face in outside_faces(layout, places(), (LATE,), messages, masks):
        part = jnp.where(low, 0.0, face) if number % 2 else jnp.where(low, face, 0.0)
        added[element] = added[element] + part if element in added else part
    for element in layout.elements():
        value = begun[layout.rows(element), columns(LATE)]
        ready[layout.rows(element), :] = value + added[element] if element in added else value
    copies.append(copy(ready, LATE))
    copies[-1].start()
    for each in copies:
        each.wait()


def in_vmem(count):
    return [pl.BlockSpec(memory_space=pltpu.VMEM)] * count


def in_hbm(count):
    return [pl.BlockSpec(memory_space=pltpu.HBM)] * count


PARAMS = pltpu.CompilerParams(vmem_limit_bytes=VMEM_LIMIT)


def kept_in_hbm(*values):
    return [pltpu.with_memory_space_constraint(value, pltpu.HBM) for value in values]


def cost(flops, size):
    return pl.CostEstimate(flops=flops, bytes_accessed=size, transcendentals=0)


def partners(layout, dim, parity):
    sizes = layout.sizes
    swap = {}
    for place in np.ndindex(*sizes):
        other = list(place)
        lower = place[dim] % 2 == parity
        at = place[dim] + (1 if lower else -1)
        if 0 <= at < sizes[dim]:
            other[dim] = at
        elif dim != 1 and sizes[1] % 2 == 0:
            other[1] = place[1] ^ 1
        elif sizes[dim] % 2 == 0:
            other[dim] = sizes[dim] - 1 - place[dim]
        swap[place] = tuple(other)
    return [
        (int(np.ravel_multi_index(place, sizes)), int(np.ravel_multi_index(other, sizes)))
        for place, other in swap.items()
    ]


def exchange(layout, messages):
    return {
        turn: lax.ppermute(message, AXES, partners(layout, *turn))
        for turn, message in zip(layout.turns(), messages)
    }


def body(
    load_raw,
    scaling,
    fine_matrix,
    fine_inverse,
    prolong_four,
    coarse_four,
    prolong_two,
    coarse_two,
    orient,
    boundary,
):
    counts, species, nodes = load_raw.shape[:3], load_raw.shape[3], load_raw.shape[4]
    layout = Layout(counts, species, tuple(lax.axis_size(axis) for axis in AXES))
    load = load_raw.reshape(-1, nodes)
    rows = load.shape[0]
    turns = layout.turns()
    message_shapes = tuple(layout.message(dim) for dim, _ in turns)
    whole = jax.ShapeDtypeStruct(load.shape, jnp.float32)
    matrix_shapes = (
        jax.ShapeDtypeStruct((3 * nodes, nodes), jnp.bfloat16),
        jax.ShapeDtypeStruct((2 * len(DIMS), 4 * FACE, nodes), jnp.bfloat16),
    )
    elements = len(layout.elements())
    tables = tuple(jax.ShapeDtypeStruct((elements, nodes), kind) for kind in (jnp.int32, jnp.float32))
    small = (scaling, prolong_four.T, coarse_four, prolong_two.T, coarse_two)
    sides = jnp.transpose(boundary, (1, 2, 3, 0))

    *sent, masks, keeps, load, scaling, four, coarse_four, two, coarse_two = pl.pallas_call(
        functools.partial(first_kernel, layout),
        out_shape=message_shapes
        + tables
        + (whole,)
        + tuple(jax.ShapeDtypeStruct(each.shape, each.dtype) for each in small),
        in_specs=in_hbm(3 + FETCHED),
        out_specs=tuple(in_vmem(len(turns) + 3 + FETCHED)),
        scratch_shapes=[
            pltpu.SMEM(orient.shape, jnp.int32),
            pltpu.SMEM(sides.shape, jnp.int32),
            pltpu.SemaphoreType.DMA((5 + FETCHED,)),
        ],
        compiler_params=PARAMS,
        name="pack",
    )(*kept_in_hbm(load, orient, sides, *small))

    stack = (rounded(prolong_four.shape[1]) + rounded(prolong_two.shape[1]), nodes)
    smoother = pl.pallas_call(
        smoother_kernel,
        out_shape=matrix_shapes,
        in_specs=in_vmem(5),
        out_specs=tuple(in_vmem(2)),
        scratch_shapes=[pltpu.VMEM(stack, jnp.float32), pltpu.VMEM(stack, jnp.float32)],
        compiler_params=PARAMS,
        cost_estimate=cost(2 * nodes * nodes * nodes, 8 * nodes * nodes),
        name="smoother",
    )(fine_inverse, four, coarse_four, two, coarse_two)
    operator = pl.pallas_call(
        operator_kernel,
        out_shape=matrix_shapes,
        in_specs=in_vmem(1),
        out_specs=tuple(in_vmem(2)),
        compiler_params=PARAMS,
        cost_estimate=cost(0, 10 * nodes * nodes),
        name="operator",
    )(fine_matrix)

    def stage(kind, value, messages, matrix, begun):
        before = () if begun is None else (begun,)
        begun = pl.pallas_call(
            functools.partial(local_kernel, layout, kind),
            out_shape=whole,
            in_specs=in_vmem(5 + len(before)),
            out_specs=in_vmem(1)[0],
            scratch_shapes=[
                pltpu.VMEM((rows, 3 * nodes), jnp.bfloat16),
                pltpu.VMEM(load.shape, jnp.float32),
            ],
            compiler_params=PARAMS,
            cost_estimate=cost(rows * nodes, 0),
            name=kind + "_local",
        )(value, masks, keeps, scaling, matrix[0], *before)
        for dims in (EARLY, (LATE,)):
            mine = [messages[turn] for turn in layout.turns(dims)]
            heights = [len(side) * species for dim in dims for side in layout.sides(dim)]
            shapes = message_shapes if LATE in dims else ()
            begun, *sent = pl.pallas_call(
                functools.partial(faces_kernel, layout, kind, dims),
                out_shape=(whole,) + shapes,
                in_specs=in_vmem(4 + len(mine)),
                out_specs=tuple(in_vmem(1 + len(shapes))),
                scratch_shapes=[pltpu.VMEM((height, 4 * FACE), jnp.bfloat16) for height in heights]
                + [pltpu.VMEM((height, nodes), jnp.float32) for height in heights],
                compiler_params=PARAMS,
                cost_estimate=cost(0, 0),
                name=kind + ("_faces_late" if shapes else "_faces_early"),
            )(*mine, masks, scaling, matrix[1], begun)
        return begun, sent

    first, sent = stage("smooth", load, exchange(layout, sent), smoother, None)
    left, sent = stage("operator", first, exchange(layout, sent), operator, load)
    total, sent = stage("smooth_more", left, exchange(layout, sent), smoother, first)
    messages = exchange(layout, sent)
    early = [messages[turn] for turn in layout.turns(EARLY)]
    late = [messages[turn] for turn in layout.turns((LATE,))]
    begun = pl.pallas_call(
        functools.partial(last_early_kernel, layout),
        out_shape=whole,
        in_specs=in_vmem(3 + len(early)),
        out_specs=in_vmem(1)[0],
        compiler_params=PARAMS,
        cost_estimate=cost(0, 8 * rows * nodes),
        name="last_early",
    )(total, *early, masks, keeps)
    result = pl.pallas_call(
        functools.partial(last_late_kernel, layout),
        out_shape=whole,
        in_specs=in_vmem(2 + len(late)),
        out_specs=in_hbm(1)[0],
        scratch_shapes=[pltpu.VMEM((rows, WIDTH), jnp.float32), pltpu.SemaphoreType.DMA((3,))],
        compiler_params=PARAMS,
        cost_estimate=cost(0, 8 * rows * nodes),
        name="last_late",
    )(begun, *late, masks)
    return result.reshape(load_raw.shape)


def solution(mesh):
    in_specs = (
        P("ex", "ey", "ez", None, None),
        P("ex", "ey", "ez", None),
        P(),
        P(),
        P(),
        P(),
        P(),
        P(),
        P(None, "ex", "ey", "ez"),
        P(None, "ex", "ey", "ez"),
    )
    out_specs = P("ex", "ey", "ez", None, None)
    return jax.shard_map(body, mesh=mesh, in_specs=in_specs, out_specs=out_specs, check_vma=False)
```

```python
import functools

import jax
import jax.numpy as jnp
from jax import lax
from jax.experimental import pallas as pl
from jax.experimental.pallas import tpu as pltpu
import numpy as np
from jax.sharding import PartitionSpec as P

FACE_SIDE = 8
FACE = FACE_SIDE * FACE_SIDE
WIDTH = 2 * FACE
AXES = ("ex", "ey", "ez")
TURNS = ((1, 1), (0, 0), (0, 1), (1, 0), (2, 1), (2, 0))
FIRST_TURNS = ((1, 1), (0, 1), (0, 0), (1, 0), (2, 1), (2, 0))
DIMS = (0, 1, 2)
EARLY = (1, 0)
LATE = 2
FETCHED = 5
VMEM_LIMIT = 24 * 1024 * 1024


class Layout:
    def __init__(self, counts, species, sizes):
        self.counts = counts
        self.species = species
        self.sizes = sizes

    def elements(self):
        spans = [range(count) for count in self.counts]
        return [(i, j, k) for i in spans[0] for j in spans[1] for k in spans[2]]

    def number(self, element):
        return (element[0] * self.counts[1] + element[1]) * self.counts[2] + element[2]

    def rows(self, element):
        start = self.number(element) * self.species
        return slice(start, start + self.species)

    def layer(self, dim, position):
        return [element for element in self.elements() if element[dim] == position]

    def pairs(self, dim):
        return (len(self.layer(dim, 0)) + 1) // 2

    def pair_rows(self, pair):
        return slice(pair * self.species, (pair + 1) * self.species)

    def turns(self, dims=(0, 1, 2), order=TURNS):
        return [
            (dim, parity) for dim, parity in order if dim in dims and self.sizes[dim] > 1 + parity
        ]

    def sides(self, dim):
        return self.layer(dim, 0), self.layer(dim, self.counts[dim] - 1)

    def message(self, dim):
        return jax.ShapeDtypeStruct((self.pairs(dim) * self.species, WIDTH), jnp.float32)


def columns(dim):
    return slice(dim * WIDTH, (dim + 1) * WIDTH)


def lanes(layout):
    return lax.broadcasted_iota(jnp.int32, (layout.species, WIDTH), 1)


def picked(value, index):
    return jnp.take_along_axis(value, index, axis=1, mode="promise_in_bounds")


def flip_mask(code):
    reach = FACE_SIDE - 1
    return (code & 1) * (reach * FACE_SIDE) + (code >> 1) * reach


def places():
    return [lax.axis_index(axis) for axis in AXES]


def pack(layout, here, dim, load_block, mask_of, outs):
    turns = [(turn, out) for turn, out in zip(layout.turns(), outs) if turn[0] == dim]
    if not turns:
        return
    lane = lanes(layout)
    low = lane < FACE
    even = (here[dim] & 1) == 0
    first = layout.layer(dim, 0)
    last = layout.layer(dim, layout.counts[dim] - 1)
    for pair in range(layout.pairs(dim)):
        sides = []
        for half in range(2):
            where = min(2 * pair + half, len(first) - 1)
            upper = load_block(last[where], dim)
            lower = load_block(first[where], dim)
            lower = picked(lower, lane ^ mask_of(first[where], dim) ^ (half * FACE))
            if half == 0:
                upper = pltpu.roll(upper, FACE, 1)
            sides.append((upper, lower))
        up = jnp.where(low, sides[0][0], sides[1][0])
        down = jnp.where(low, sides[0][1], sides[1][1])
        for (_, parity), out in turns:
            is_lower = even if parity == 0 else jnp.logical_not(even)
            out[layout.pair_rows(pair), :] = jnp.where(is_lower, up, down)


def received(layout, here, dim, messages):
    even = (here[dim] & 1) == 0
    at_start = here[dim] == 0
    at_end = here[dim] == layout.sizes[dim] - 1
    zero = jnp.zeros((layout.species, WIDTH), jnp.float32)
    found = []
    for pair in range(layout.pairs(dim)):
        first, second = [
            messages[dim, parity][layout.pair_rows(pair), :] if (dim, parity) in messages else zero
            for parity in range(2)
        ]
        below = jnp.where(at_start, 0.0, jnp.where(even, second, first))
        above = jnp.where(at_end, 0.0, jnp.where(even, first, second))
        found.append((below, above))
    return found


def unpacked(lane, outside, where, mask):
    below, above = outside[where // 2]
    half = (where % 2) * FACE
    inside = lane & (FACE - 1)
    return picked(below, (inside ^ mask) + half), picked(above, inside + half)


def assemble(layout, here, dim, load_block, messages, mask_of, keep_of, emit, slab=None):
    lane = lanes(layout)
    low = lane < FACE
    count = layout.counts[dim]
    outside = None if messages is None else received(layout, here, dim, messages)
    zero = jnp.zeros((layout.species, WIDTH), jnp.float32)
    for where, start in enumerate(layout.layer(dim, 0)):
        if slab not in (None, start[0]):
            continue
        line = [start[:dim] + (step,) + start[dim + 1 :] for step in range(count)]
        blocks = [load_block(element, dim) for element in line]
        if outside is None:
            from_below, from_above = zero, zero
        else:
            from_below, from_above = unpacked(lane, outside, where, mask_of(start, dim))
        turned = [from_below]
        for step, element in list(enumerate(line))[1:]:
            shared = jnp.where(low, blocks[step], blocks[step - 1])
            turned.append(picked(shared, lane ^ mask_of(element, dim) ^ FACE))
        turned.append(from_above)
        for step, element in enumerate(line):
            value = blocks[step] + jnp.where(low, turned[step], turned[step + 1])
            if step in (0, count - 1):
                value = value * keep_of(element, dim)
            emit(element, value)


def halves(value):
    high = value.astype(jnp.bfloat16)
    return high, (value - high.astype(jnp.float32)).astype(jnp.bfloat16)


def dot(left, right, contract=((1,), (0,))):
    return lax.dot_general(left, right, (contract, ((), ())), preferred_element_type=jnp.float32)


def split_dot(left, right, contract):
    left_high, left_rest = halves(left)
    right_high, right_rest = halves(right)
    return (
        dot(left_high, right_high, contract)
        + dot(left_high, right_rest, contract)
        + dot(left_rest, right_high, contract)
    )


def stacked(value, local, faces):
    high, rest = halves(value)
    size = value.shape[0]
    for part, piece in enumerate((high, rest, high)):
        local[part * size : (part + 1) * size, :] = piece
    for number in range(faces.shape[0]):
        rows = slice(number * FACE, (number + 1) * FACE)
        for part, piece in enumerate((high, high, rest)):
            faces[number, part * FACE : (part + 1) * FACE, :] = piece[rows, :]
        faces[number, 3 * FACE :, :] = jnp.zeros((FACE, value.shape[1]), jnp.bfloat16)


def operator_kernel(fine, *outs):
    stacked(fine[...], *outs)


def smoother_kernel(inverse, four, coarse_four, two, coarse_two, *refs):
    *outs, right, left = refs
    right[...] = jnp.zeros_like(right)
    left[...] = jnp.zeros_like(left)
    start = 0
    for prolong, coarse in ((four, coarse_four), (two, coarse_two)):
        rows = slice(start, start + prolong.shape[0])
        left[rows, :] = prolong[...]
        right[rows, :] = split_dot(coarse[...], prolong[...], ((1,), (0,)))
        start += rounded(prolong.shape[0])
    corrections = split_dot(left[...], right[...], ((0,), (0,)))
    stacked(0.5 * (inverse[...] + corrections), *outs)


def rounded(count):
    return (count + 7) // 8 * 8


def first_kernel(layout, load, orient, boundary, *refs):
    turns = len(layout.turns())
    small, refs = refs[:FETCHED], refs[FETCHED:]
    outs, masks, keeps, staged = refs[:turns], *refs[turns : turns + 3]
    fetched, (codes, fixed, arrived) = refs[turns + 3 : turns + 3 + FETCHED], refs[-3:]
    scalars = [
        pltpu.make_async_copy(source, target, arrived.at[number])
        for number, (source, target) in enumerate(((orient, codes), (boundary, fixed)))
    ]
    strips = [
        pltpu.make_async_copy(
            load.at[:, columns(dim)], staged.at[:, columns(dim)], arrived.at[2 + dim]
        )
        for dim in DIMS
    ]
    fetches = [
        pltpu.make_async_copy(source, target, arrived.at[5 + number])
        for number, (source, target) in enumerate(zip(small, fetched))
    ]
    for copy in scalars + strips + fetches:
        copy.start()
    here = places()
    for copy in scalars:
        copy.wait()
    tabulate(layout, here, codes, fixed, masks, keeps)
    for dim in DIMS:
        strips[dim].wait()
        pack(
            layout,
            here,
            dim,
            lambda element, dim: staged[layout.rows(element), columns(dim)],
            table(layout, masks),
            outs,
        )
    for copy in fetches:
        copy.wait()


def tabulate(layout, here, codes, boundary, masks, keeps):
    low = lax.broadcasted_iota(jnp.int32, (1, WIDTH), 1) < FACE
    for element in layout.elements():
        number = layout.number(element)
        for dim in range(3):
            mask = flip_mask(codes[(dim,) + element])
            masks[number : number + 1, columns(dim)] = jnp.full((1, WIDTH), mask, jnp.int32)
            at_start = (here[dim] == 0) & (element[dim] == 0)
            at_end = (here[dim] == layout.sizes[dim] - 1) & (element[dim] == layout.counts[dim] - 1)
            fixed_low = jnp.where(at_start, boundary[element + (2 * dim,)], 0)
            fixed_top = jnp.where(at_end, boundary[element + (2 * dim + 1,)], 0)
            fixed = jnp.where(low, fixed_low, fixed_top)
            keeps[number : number + 1, columns(dim)] = 1.0 - fixed.astype(jnp.float32)


def table(layout, ref):
    def row(element, dim):
        number = layout.number(element)
        return ref[number : number + 1, columns(dim)]

    return row


def scales(layout, kind, ref):
    def row(element, dim):
        value = ref[element[0], element[1], element[2] : element[2] + 1, columns(dim)]
        return value if kind == "operator" else 1.0 / value

    return row


def taken(layout, dims, refs, order=TURNS):
    turns = layout.turns(dims, order)
    return dict(zip(turns, refs)), refs[len(turns) :]


def combined(kind, begun, result):
    if begun is None:
        return result
    return begun - result if kind == "operator" else begun + result


def local_kernel(layout, kind, value, masks, keeps, scaling, matrix, *refs):
    *before, out, split, summed = refs
    begun = before[0] if before else None
    here = places()
    factor = scales(layout, kind, scaling)
    nodes = value.shape[1]

    def assembled(dim, slab):
        def emit(element, result):
            high, rest = halves(result * factor(element, dim))
            for part, piece in enumerate((high, high, rest)):
                start = part * nodes + dim * WIDTH
                split[layout.rows(element), start : start + WIDTH] = piece

        assemble(
            layout,
            here,
            dim,
            lambda element, dim: value[layout.rows(element), columns(dim)],
            None,
            table(layout, masks),
            table(layout, keeps),
            emit,
            slab,
        )

    assembled(0, None)
    count = layout.counts[0]
    height = value.shape[0] // count
    for slab in range(count):
        assembled(1, slab)
        assembled(2, slab)
        rows = slice(slab * height, (slab + 1) * height)
        summed[rows, :] = dot(split[rows, :], matrix[...])
        for element in layout.layer(0, slab):
            for dim in DIMS:
                at = (layout.rows(element), columns(dim))
                result = summed[at] * factor(element, dim)
                out[at] = combined(kind, None if begun is None else begun[at], result)


def combined(kind, begun, result):
    if begun is None:
        return result
    return begun - result if kind == "operator" else begun + result


def strips_kernel(layout, kind, dims, local, value, *refs):
    messages, refs = (None, refs) if local else taken(layout, dims, refs)
    masks, keeps, scaling, matrix, *before, out, split, summed = refs
    begun = before[0] if before else None
    here = places()
    factor = scales(layout, kind, scaling)

    def assembled(place, slab):
        dim = dims[place]

        def emit(element, result):
            scaled = result * factor(element, dim)
            put_split(split, layout.rows(element), place, len(dims), scaled)

        assemble(
            layout,
            here,
            dim,
            lambda element, dim: value[layout.rows(element), columns(dim)],
            messages,
            table(layout, masks),
            table(layout, keeps),
            emit,
            slab,
        )

    if 0 in dims:
        assembled(dims.index(0), None)
    count = layout.counts[0]
    height = value.shape[0] // count
    for slab in range(count):
        for place, dim in enumerate(dims):
            if dim != 0:
                assembled(place, slab)
        rows = slice(slab * height, (slab + 1) * height)
        summed[rows, :] = dot(split[rows, :], matrix[...])
        for element in layout.layer(0, slab):
            for each in range(3):
                at = (layout.rows(element), columns(each))
                result = summed[at] * factor(element, each)
                out[at] = combined(kind, None if begun is None else begun[at], result)


def combined(kind, begun, result):
    if begun is None:
        return result
    return begun - result if kind == "operator" else begun + result


def outside_faces(layout, here, dims, messages, masks):
    lane = lanes(layout)
    for dim in dims:
        outside = received(layout, here, dim, messages)
        lower, upper = layout.sides(dim)
        for where, element in enumerate(lower):
            mask = table(layout, masks)(element, dim)
            from_below, from_above = unpacked(lane, outside, where, mask)
            yield 2 * dim, where, element, from_below
            yield 2 * dim + 1, where, upper[where], from_above


def faces_kernel(layout, kind, dims, order, *refs):
    messages, refs = taken(layout, dims, refs, order)
    masks, scaling, faces, begun, out, *refs = refs
    turns = len(layout.turns()) if LATE in dims else 0
    sent, scratch = refs[:turns], refs[turns:]
    count = 2 * len(dims)
    splits, sums = scratch[:count], scratch[count:]
    here = places()
    factor = scales(layout, kind, scaling)
    low = lanes(layout) < FACE
    row_low = low[:1]

    def both(row, side):
        turned = pltpu.roll(row, FACE, 1)
        return jnp.where(row_low, turned, row) if side else jnp.where(row_low, row, turned)

    share = {}
    for place, dim in enumerate(dims):
        for number, where, element, face in outside_faces(layout, here, (dim,), messages, masks):
            side = number % 2
            value = face * both(factor(element, dim), side)
            high = value.astype(jnp.bfloat16).astype(jnp.float32)
            rows = layout.pair_rows(where)
            split = splits[2 * place + side]
            split[rows, :WIDTH] = jnp.where(low, value, value - high).astype(jnp.bfloat16)
            split[rows, WIDTH:] = jnp.where(low, value, 0.0).astype(jnp.bfloat16)
            share.setdefault(element, []).append((2 * place + side, rows))
        for side in range(2):
            at = 2 * place + side
            sums[at][...] = dot(splits[at][...], faces[2 * dim + side])
    for element in layout.elements():
        for dim in DIMS:
            at = (layout.rows(element), columns(dim))
            parts = [sums[number][rows, columns(dim)] for number, rows in share.get(element, ())]
            if parts:
                result = sum(parts[1:], parts[0]) * factor(element, dim)
                out[at] = combined(kind, begun[at], result)
            else:
                out[at] = begun[at]
    if sent:
        for dim in DIMS:
            pack(
                layout,
                here,
                dim,
                lambda element, dim: out[layout.rows(element), columns(dim)],
                table(layout, masks),
                sent,
            )


def last_early_kernel(layout, value, *refs):
    messages, (masks, keeps, ready) = taken(layout, EARLY, refs)
    for dim in DIMS:

        def emit(element, result):
            ready[layout.rows(element), columns(dim)] = result

        assemble(
            layout,
            places(),
            dim,
            lambda element, dim: value[layout.rows(element), columns(dim)],
            None if dim == LATE else messages,
            table(layout, masks),
            table(layout, keeps),
            emit,
        )


def last_late_kernel(layout, begun, *refs):
    messages, (masks, out, ready, left) = taken(layout, (LATE,), refs)
    low = lanes(layout) < FACE

    def copy(source, dim):
        return pltpu.make_async_copy(source, out.at[:, columns(dim)], left.at[dim])

    copies = [copy(begun.at[:, columns(dim)], dim) for dim in EARLY]
    for each in copies:
        each.start()
    added = {}
    for number, _, element, face in outside_faces(layout, places(), (LATE,), messages, masks):
        part = jnp.where(low, 0.0, face) if number % 2 else jnp.where(low, face, 0.0)
        added[element] = added[element] + part if element in added else part
    for element in layout.elements():
        value = begun[layout.rows(element), columns(LATE)]
        ready[layout.rows(element), :] = value + added[element] if element in added else value
    copies.append(copy(ready, LATE))
    copies[-1].start()
    for each in copies:
        each.wait()


def in_vmem(count):
    return [pl.BlockSpec(memory_space=pltpu.VMEM)] * count


def in_hbm(count):
    return [pl.BlockSpec(memory_space=pltpu.HBM)] * count


PARAMS = pltpu.CompilerParams(vmem_limit_bytes=VMEM_LIMIT)


def kept_in_hbm(*values):
    return [pltpu.with_memory_space_constraint(value, pltpu.HBM) for value in values]


def cost(flops, size):
    return pl.CostEstimate(flops=flops, bytes_accessed=size, transcendentals=0)


def partners(layout, dim, parity):
    sizes = layout.sizes
    swap = {}
    for place in np.ndindex(*sizes):
        other = list(place)
        lower = place[dim] % 2 == parity
        at = place[dim] + (1 if lower else -1)
        if 0 <= at < sizes[dim]:
            other[dim] = at
        elif dim != 1 and sizes[1] % 2 == 0:
            other[1] = place[1] ^ 1
        elif sizes[dim] % 2 == 0:
            other[dim] = sizes[dim] - 1 - place[dim]
        swap[place] = tuple(other)
    return [
        (int(np.ravel_multi_index(place, sizes)), int(np.ravel_multi_index(other, sizes)))
        for place, other in swap.items()
    ]


def exchange(layout, messages, order=TURNS):
    given = dict(zip(layout.turns(), messages))
    return {
        turn: lax.ppermute(given[turn], AXES, partners(layout, *turn))
        for turn in order
        if turn in given
    }


def body(
    load_raw,
    scaling,
    fine_matrix,
    fine_inverse,
    prolong_four,
    coarse_four,
    prolong_two,
    coarse_two,
    orient,
    boundary,
):
    counts, species, nodes = load_raw.shape[:3], load_raw.shape[3], load_raw.shape[4]
    layout = Layout(counts, species, tuple(lax.axis_size(axis) for axis in AXES))
    load = load_raw.reshape(-1, nodes)
    rows = load.shape[0]
    turns = layout.turns()
    message_shapes = tuple(layout.message(dim) for dim, _ in turns)
    whole = jax.ShapeDtypeStruct(load.shape, jnp.float32)
    matrix_shapes = (
        jax.ShapeDtypeStruct((3 * nodes, nodes), jnp.bfloat16),
        jax.ShapeDtypeStruct((2 * len(DIMS), 4 * FACE, nodes), jnp.bfloat16),
    )
    elements = len(layout.elements())
    tables = tuple(jax.ShapeDtypeStruct((elements, nodes), kind) for kind in (jnp.int32, jnp.float32))
    small = (scaling, prolong_four.T, coarse_four, prolong_two.T, coarse_two)
    sides = jnp.transpose(boundary, (1, 2, 3, 0))

    *sent, masks, keeps, load, scaling, four, coarse_four, two, coarse_two = pl.pallas_call(
        functools.partial(first_kernel, layout),
        out_shape=message_shapes
        + tables
        + (whole,)
        + tuple(jax.ShapeDtypeStruct(each.shape, each.dtype) for each in small),
        in_specs=in_hbm(3 + FETCHED),
        out_specs=tuple(in_vmem(len(turns) + 3 + FETCHED)),
        scratch_shapes=[
            pltpu.SMEM(orient.shape, jnp.int32),
            pltpu.SMEM(sides.shape, jnp.int32),
            pltpu.SemaphoreType.DMA((5 + FETCHED,)),
        ],
        compiler_params=PARAMS,
        name="pack",
    )(*kept_in_hbm(load, orient, sides, *small))

    stack = (rounded(prolong_four.shape[1]) + rounded(prolong_two.shape[1]), nodes)
    smoother = pl.pallas_call(
        smoother_kernel,
        out_shape=matrix_shapes,
        in_specs=in_vmem(5),
        out_specs=tuple(in_vmem(2)),
        scratch_shapes=[pltpu.VMEM(stack, jnp.float32), pltpu.VMEM(stack, jnp.float32)],
        compiler_params=PARAMS,
        cost_estimate=cost(2 * nodes * nodes * nodes, 8 * nodes * nodes),
        name="smoother",
    )(fine_inverse, four, coarse_four, two, coarse_two)
    operator = pl.pallas_call(
        operator_kernel,
        out_shape=matrix_shapes,
        in_specs=in_vmem(1),
        out_specs=tuple(in_vmem(2)),
        compiler_params=PARAMS,
        cost_estimate=cost(0, 10 * nodes * nodes),
        name="operator",
    )(fine_matrix)

    def stage(kind, value, sent, matrix, begun, order=TURNS):
        messages = exchange(layout, sent, order)
        before = () if begun is None else (begun,)
        begun = pl.pallas_call(
            functools.partial(local_kernel, layout, kind),
            out_shape=whole,
            in_specs=in_vmem(5 + len(before)),
            out_specs=in_vmem(1)[0],
            scratch_shapes=[
                pltpu.VMEM((rows, 3 * nodes), jnp.bfloat16),
                pltpu.VMEM(load.shape, jnp.float32),
            ],
            compiler_params=PARAMS,
            cost_estimate=cost(rows * nodes, 0),
            name=kind + "_local",
        )(value, masks, keeps, scaling, matrix[0], *before)
        for dims in (EARLY, (LATE,)):
            mine = [messages[turn] for turn in layout.turns(dims, order)]
            heights = [len(side) * species for dim in dims for side in layout.sides(dim)]
            shapes = message_shapes if LATE in dims else ()
            begun, *sent = pl.pallas_call(
                functools.partial(faces_kernel, layout, kind, dims, order),
                out_shape=(whole,) + shapes,
                in_specs=in_vmem(4 + len(mine)),
                out_specs=tuple(in_vmem(1 + len(shapes))),
                scratch_shapes=[pltpu.VMEM((height, 4 * FACE), jnp.bfloat16) for height in heights]
                + [pltpu.VMEM((height, nodes), jnp.float32) for height in heights],
                compiler_params=PARAMS,
                cost_estimate=cost(0, 0),
                name=kind + ("_faces_late" if shapes else "_faces_early"),
            )(*mine, masks, scaling, matrix[1], begun)
        return begun, sent

    first, sent = stage("smooth", load, sent, smoother, None, FIRST_TURNS)
    left, sent = stage("operator", first, sent, operator, load)
    total, sent = stage("smooth_more", left, sent, smoother, first)
    messages = exchange(layout, sent)
    early = [messages[turn] for turn in layout.turns(EARLY)]
    late = [messages[turn] for turn in layout.turns((LATE,))]
    begun = pl.pallas_call(
        functools.partial(last_early_kernel, layout),
        out_shape=whole,
        in_specs=in_vmem(3 + len(early)),
        out_specs=in_vmem(1)[0],
        compiler_params=PARAMS,
        cost_estimate=cost(0, 8 * rows * nodes),
        name="last_early",
    )(total, *early, masks, keeps)
    result = pl.pallas_call(
        functools.partial(last_late_kernel, layout),
        out_shape=whole,
        in_specs=in_vmem(2 + len(late)),
        out_specs=in_hbm(1)[0],
        scratch_shapes=[pltpu.VMEM((rows, WIDTH), jnp.float32), pltpu.SemaphoreType.DMA((3,))],
        compiler_params=PARAMS,
        cost_estimate=cost(0, 8 * rows * nodes),
        name="last_late",
    )(begun, *late, masks)
    return result.reshape(load_raw.shape)


def solution(mesh):
    in_specs = (
        P("ex", "ey", "ez", None, None),
        P("ex", "ey", "ez", None),
        P(),
        P(),
        P(),
        P(),
        P(),
        P(),
        P(None, "ex", "ey", "ez"),
        P(None, "ex", "ey", "ez"),
    )
    out_specs = P("ex", "ey", "ez", None, None)
    return jax.shard_map(body, mesh=mesh, in_specs=in_specs, out_specs=out_specs, check_vma=False)
```

```python
import functools

import jax
import jax.numpy as jnp
from jax import lax
from jax.experimental import pallas as pl
from jax.experimental.pallas import tpu as pltpu
import numpy as np
from jax.sharding import PartitionSpec as P

FACE_SIDE = 8
FACE = FACE_SIDE * FACE_SIDE
WIDTH = 2 * FACE
AXES = ("ex", "ey", "ez")
TURNS = ((1, 1), (0, 0), (0, 1), (1, 0), (2, 1), (2, 0))
FIRST_TURNS = ((1, 1), (0, 1), (0, 0), (1, 0), (2, 1), (2, 0))
DIMS = (0, 1, 2)
EARLY = (1, 0)
LATE = 2
FETCHED = 5
VMEM_LIMIT = 24 * 1024 * 1024


class Layout:
    def __init__(self, counts, species, sizes):
        self.counts = counts
        self.species = species
        self.sizes = sizes

    def elements(self):
        spans = [range(count) for count in self.counts]
        return [(i, j, k) for i in spans[0] for j in spans[1] for k in spans[2]]

    def number(self, element):
        return (element[0] * self.counts[1] + element[1]) * self.counts[2] + element[2]

    def rows(self, element):
        start = self.number(element) * self.species
        return slice(start, start + self.species)

    def layer(self, dim, position):
        return [element for element in self.elements() if element[dim] == position]

    def pairs(self, dim):
        return (len(self.layer(dim, 0)) + 1) // 2

    def pair_rows(self, pair):
        return slice(pair * self.species, (pair + 1) * self.species)

    def turns(self, dims=(0, 1, 2), order=TURNS):
        return [
            (dim, parity) for dim, parity in order if dim in dims and self.sizes[dim] > 1 + parity
        ]

    def edge(self):
        ends = (0, self.counts[LATE] - 1)
        return [element for element in self.elements() if element[LATE] in ends]

    def sides(self, dim):
        return self.layer(dim, 0), self.layer(dim, self.counts[dim] - 1)

    def message(self, dim):
        return jax.ShapeDtypeStruct((self.pairs(dim) * self.species, WIDTH), jnp.float32)


def columns(dim):
    return slice(dim * WIDTH, (dim + 1) * WIDTH)


def lanes(layout):
    return lax.broadcasted_iota(jnp.int32, (layout.species, WIDTH), 1)


def picked(value, index):
    return jnp.take_along_axis(value, index, axis=1, mode="promise_in_bounds")


def flip_mask(code):
    reach = FACE_SIDE - 1
    return (code & 1) * (reach * FACE_SIDE) + (code >> 1) * reach


def places():
    return [lax.axis_index(axis) for axis in AXES]


def pack(layout, here, dim, load_block, mask_of, outs):
    turns = [(turn, out) for turn, out in zip(layout.turns(), outs) if turn[0] == dim]
    if not turns:
        return
    lane = lanes(layout)
    low = lane < FACE
    even = (here[dim] & 1) == 0
    first = layout.layer(dim, 0)
    last = layout.layer(dim, layout.counts[dim] - 1)
    for pair in range(layout.pairs(dim)):
        sides = []
        for half in range(2):
            where = min(2 * pair + half, len(first) - 1)
            upper = load_block(last[where], dim)
            lower = load_block(first[where], dim)
            lower = picked(lower, lane ^ mask_of(first[where], dim) ^ (half * FACE))
            if half == 0:
                upper = pltpu.roll(upper, FACE, 1)
            sides.append((upper, lower))
        up = jnp.where(low, sides[0][0], sides[1][0])
        down = jnp.where(low, sides[0][1], sides[1][1])
        for (_, parity), out in turns:
            is_lower = even if parity == 0 else jnp.logical_not(even)
            out[layout.pair_rows(pair), :] = jnp.where(is_lower, up, down)


def received(layout, here, dim, messages):
    even = (here[dim] & 1) == 0
    at_start = here[dim] == 0
    at_end = here[dim] == layout.sizes[dim] - 1
    zero = jnp.zeros((layout.species, WIDTH), jnp.float32)
    found = []
    for pair in range(layout.pairs(dim)):
        first, second = [
            messages[dim, parity][layout.pair_rows(pair), :] if (dim, parity) in messages else zero
            for parity in range(2)
        ]
        below = jnp.where(at_start, 0.0, jnp.where(even, second, first))
        above = jnp.where(at_end, 0.0, jnp.where(even, first, second))
        found.append((below, above))
    return found


def unpacked(lane, outside, where, mask):
    below, above = outside[where // 2]
    half = (where % 2) * FACE
    inside = lane & (FACE - 1)
    return picked(below, (inside ^ mask) + half), picked(above, inside + half)


def assemble(layout, here, dim, load_block, messages, mask_of, keep_of, emit, slab=None):
    lane = lanes(layout)
    low = lane < FACE
    count = layout.counts[dim]
    outside = None if messages is None else received(layout, here, dim, messages)
    zero = jnp.zeros((layout.species, WIDTH), jnp.float32)
    for where, start in enumerate(layout.layer(dim, 0)):
        if slab not in (None, start[0]):
            continue
        line = [start[:dim] + (step,) + start[dim + 1 :] for step in range(count)]
        blocks = [load_block(element, dim) for element in line]
        if outside is None:
            from_below, from_above = zero, zero
        else:
            from_below, from_above = unpacked(lane, outside, where, mask_of(start, dim))
        turned = [from_below]
        for step, element in list(enumerate(line))[1:]:
            shared = jnp.where(low, blocks[step], blocks[step - 1])
            turned.append(picked(shared, lane ^ mask_of(element, dim) ^ FACE))
        turned.append(from_above)
        for step, element in enumerate(line):
            value = blocks[step] + jnp.where(low, turned[step], turned[step + 1])
            if step in (0, count - 1):
                value = value * keep_of(element, dim)
            emit(element, value)


def halves(value):
    high = value.astype(jnp.bfloat16)
    return high, (value - high.astype(jnp.float32)).astype(jnp.bfloat16)


def dot(left, right, contract=((1,), (0,))):
    return lax.dot_general(left, right, (contract, ((), ())), preferred_element_type=jnp.float32)


def split_dot(left, right, contract):
    left_high, left_rest = halves(left)
    right_high, right_rest = halves(right)
    return (
        dot(left_high, right_high, contract)
        + dot(left_high, right_rest, contract)
        + dot(left_rest, right_high, contract)
    )


def stacked(value, local, faces):
    high, rest = halves(value)
    size = value.shape[0]
    for part, piece in enumerate((high, rest, high)):
        local[part * size : (part + 1) * size, :] = piece
    for number in range(faces.shape[0]):
        rows = slice(number * FACE, (number + 1) * FACE)
        for part, piece in enumerate((high, high, rest)):
            faces[number, part * FACE : (part + 1) * FACE, :] = piece[rows, :]
        faces[number, 3 * FACE :, :] = jnp.zeros((FACE, value.shape[1]), jnp.bfloat16)


def operator_kernel(fine, *outs):
    stacked(fine[...], *outs)


def smoother_kernel(inverse, four, coarse_four, two, coarse_two, *refs):
    *outs, right, left = refs
    right[...] = jnp.zeros_like(right)
    left[...] = jnp.zeros_like(left)
    start = 0
    for prolong, coarse in ((four, coarse_four), (two, coarse_two)):
        rows = slice(start, start + prolong.shape[0])
        left[rows, :] = prolong[...]
        right[rows, :] = split_dot(coarse[...], prolong[...], ((1,), (0,)))
        start += rounded(prolong.shape[0])
    corrections = split_dot(left[...], right[...], ((0,), (0,)))
    stacked(0.5 * (inverse[...] + corrections), *outs)


def rounded(count):
    return (count + 7) // 8 * 8


def first_kernel(layout, load, orient, boundary, *refs):
    turns = len(layout.turns())
    small, refs = refs[:FETCHED], refs[FETCHED:]
    outs, masks, keeps, staged = refs[:turns], *refs[turns : turns + 3]
    fetched, (codes, fixed, arrived) = refs[turns + 3 : turns + 3 + FETCHED], refs[-3:]
    scalars = [
        pltpu.make_async_copy(source, target, arrived.at[number])
        for number, (source, target) in enumerate(((orient, codes), (boundary, fixed)))
    ]
    strips = [
        pltpu.make_async_copy(
            load.at[:, columns(dim)], staged.at[:, columns(dim)], arrived.at[2 + dim]
        )
        for dim in DIMS
    ]
    fetches = [
        pltpu.make_async_copy(source, target, arrived.at[5 + number])
        for number, (source, target) in enumerate(zip(small, fetched))
    ]
    for copy in scalars + strips + fetches:
        copy.start()
    here = places()
    for copy in scalars:
        copy.wait()
    tabulate(layout, here, codes, fixed, masks, keeps)
    for dim in DIMS:
        strips[dim].wait()
        pack(
            layout,
            here,
            dim,
            lambda element, dim: staged[layout.rows(element), columns(dim)],
            table(layout, masks),
            outs,
        )
    for copy in fetches:
        copy.wait()


def tabulate(layout, here, codes, boundary, masks, keeps):
    low = lax.broadcasted_iota(jnp.int32, (1, WIDTH), 1) < FACE
    for element in layout.elements():
        number = layout.number(element)
        for dim in range(3):
            mask = flip_mask(codes[(dim,) + element])
            masks[number : number + 1, columns(dim)] = jnp.full((1, WIDTH), mask, jnp.int32)
            at_start = (here[dim] == 0) & (element[dim] == 0)
            at_end = (here[dim] == layout.sizes[dim] - 1) & (element[dim] == layout.counts[dim] - 1)
            fixed_low = jnp.where(at_start, boundary[element + (2 * dim,)], 0)
            fixed_top = jnp.where(at_end, boundary[element + (2 * dim + 1,)], 0)
            fixed = jnp.where(low, fixed_low, fixed_top)
            keeps[number : number + 1, columns(dim)] = 1.0 - fixed.astype(jnp.float32)


def table(layout, ref):
    def row(element, dim):
        number = layout.number(element)
        return ref[number : number + 1, columns(dim)]

    return row


def scales(layout, kind, ref):
    def row(element, dim):
        value = ref[element[0], element[1], element[2] : element[2] + 1, columns(dim)]
        return value if kind == "operator" else 1.0 / value

    return row


def taken(layout, dims, refs, order=TURNS):
    turns = layout.turns(dims, order)
    return dict(zip(turns, refs)), refs[len(turns) :]


def combined(kind, begun, result):
    if begun is None:
        return result
    return begun - result if kind == "operator" else begun + result


def reader(layout, whole, edges=None):
    edge = [] if edges is None else layout.edge()

    def block(element, dim):
        if element in edge:
            return edges[layout.pair_rows(edge.index(element)), columns(dim)]
        return whole[layout.rows(element), columns(dim)]

    return block


def local_kernel(layout, kind, given, *refs):
    value, begun, refs = refs[: given[0]], refs[given[0] : sum(given)], refs[sum(given) :]
    masks, keeps, scaling, matrix, out, split, summed = refs
    value = reader(layout, *value)
    begun = reader(layout, *begun) if begun else None
    here = places()
    factor = scales(layout, kind, scaling)
    nodes = out.shape[1]

    def assembled(dim, slab):
        def emit(element, result):
            high, rest = halves(result * factor(element, dim))
            for part, piece in enumerate((high, high, rest)):
                start = part * nodes + dim * WIDTH
                split[layout.rows(element), start : start + WIDTH] = piece

        assemble(
            layout,
            here,
            dim,
            value,
            None,
            table(layout, masks),
            table(layout, keeps),
            emit,
            slab,
        )

    assembled(0, None)
    count = layout.counts[0]
    height = out.shape[0] // count
    for slab in range(count):
        assembled(1, slab)
        assembled(2, slab)
        rows = slice(slab * height, (slab + 1) * height)
        summed[rows, :] = dot(split[rows, :], matrix[...])
        for element in layout.layer(0, slab):
            for dim in DIMS:
                at = (layout.rows(element), columns(dim))
                result = summed[at] * factor(element, dim)
                out[at] = combined(kind, begun and begun(element, dim), result)


def combined(kind, begun, result):
    if begun is None:
        return result
    return begun - result if kind == "operator" else begun + result


def strips_kernel(layout, kind, dims, local, value, *refs):
    messages, refs = (None, refs) if local else taken(layout, dims, refs)
    masks, keeps, scaling, matrix, *before, out, split, summed = refs
    begun = before[0] if before else None
    here = places()
    factor = scales(layout, kind, scaling)

    def assembled(place, slab):
        dim = dims[place]

        def emit(element, result):
            scaled = result * factor(element, dim)
            put_split(split, layout.rows(element), place, len(dims), scaled)

        assemble(
            layout,
            here,
            dim,
            lambda element, dim: value[layout.rows(element), columns(dim)],
            messages,
            table(layout, masks),
            table(layout, keeps),
            emit,
            slab,
        )

    if 0 in dims:
        assembled(dims.index(0), None)
    count = layout.counts[0]
    height = value.shape[0] // count
    for slab in range(count):
        for place, dim in enumerate(dims):
            if dim != 0:
                assembled(place, slab)
        rows = slice(slab * height, (slab + 1) * height)
        summed[rows, :] = dot(split[rows, :], matrix[...])
        for element in layout.layer(0, slab):
            for each in range(3):
                at = (layout.rows(element), columns(each))
                result = summed[at] * factor(element, each)
                out[at] = combined(kind, None if begun is None else begun[at], result)


def combined(kind, begun, result):
    if begun is None:
        return result
    return begun - result if kind == "operator" else begun + result


def outside_faces(layout, here, dims, messages, masks):
    lane = lanes(layout)
    for dim in dims:
        outside = received(layout, here, dim, messages)
        lower, upper = layout.sides(dim)
        for where, element in enumerate(lower):
            mask = table(layout, masks)(element, dim)
            from_below, from_above = unpacked(lane, outside, where, mask)
            yield 2 * dim, where, element, from_below
            yield 2 * dim + 1, where, upper[where], from_above


def put_faces(layout, here, dim, messages, masks, factor, splits):
    low = lanes(layout) < FACE
    row_low = low[:1]
    for number, where, element, face in outside_faces(layout, here, (dim,), messages, masks):
        row = factor(element, dim)
        turned = pltpu.roll(row, FACE, 1)
        side = number % 2
        value = face * (jnp.where(row_low, turned, row) if side else jnp.where(row_low, row, turned))
        high = value.astype(jnp.bfloat16).astype(jnp.float32)
        rows = layout.pair_rows(where)
        splits[side][rows, :WIDTH] = jnp.where(low, value, value - high).astype(jnp.bfloat16)
        splits[side][rows, WIDTH:] = jnp.where(low, value, 0.0).astype(jnp.bfloat16)


def early_faces_kernel(layout, kind, order, *refs):
    messages, refs = taken(layout, EARLY, refs, order)
    masks, scaling, faces, begun, out, *scratch = refs
    count = 2 * len(EARLY)
    splits, sums = scratch[:count], scratch[count:]
    here = places()
    factor = scales(layout, kind, scaling)
    share = {}
    for place, dim in enumerate(EARLY):
        put_faces(layout, here, dim, messages, masks, factor, splits[2 * place : 2 * place + 2])
        for side, elements in enumerate(layout.sides(dim)):
            at = 2 * place + side
            sums[at][...] = dot(splits[at][...], faces[2 * dim + side])
            for where, element in enumerate(elements):
                share.setdefault(element, []).append((at, layout.pair_rows(where)))
    for element in layout.elements():
        for dim in DIMS:
            at = (layout.rows(element), columns(dim))
            parts = [sums[number][rows, columns(dim)] for number, rows in share.get(element, ())]
            if parts:
                result = sum(parts[1:], parts[0]) * factor(element, dim)
                out[at] = combined(kind, begun[at], result)
            else:
                out[at] = begun[at]


def late_faces_kernel(layout, kind, order, *refs):
    messages, refs = taken(layout, (LATE,), refs, order)
    masks, scaling, faces, begun, out, *refs = refs
    sent, splits = refs[: len(layout.turns())], refs[len(layout.turns()) :]
    here = places()
    factor = scales(layout, kind, scaling)
    put_faces(layout, here, LATE, messages, masks, factor, splits)
    edge = layout.edge()
    done = set()
    for side, elements in enumerate(layout.sides(LATE)):
        product = dot(splits[side][...], faces[2 * LATE + side])
        for where, element in enumerate(elements):
            rows = layout.pair_rows(edge.index(element))
            for dim in DIMS:
                part = product[layout.pair_rows(where), columns(dim)] * factor(element, dim)
                at = (rows, columns(dim))
                base = out[at] if element in done else begun[layout.rows(element), columns(dim)]
                out[at] = combined(kind, base, part)
            done.add(element)
    for dim in DIMS:
        pack(layout, here, dim, reader(layout, begun, out), table(layout, masks), sent)


def last_early_kernel(layout, whole, edges, *refs):
    value = reader(layout, whole, edges)
    messages, (masks, keeps, ready) = taken(layout, EARLY, refs)
    for dim in DIMS:

        def emit(element, result):
            ready[layout.rows(element), columns(dim)] = result

        assemble(
            layout,
            places(),
            dim,
            value,
            None if dim == LATE else messages,
            table(layout, masks),
            table(layout, keeps),
            emit,
        )


def last_late_kernel(layout, begun, *refs):
    messages, (masks, out, ready, left) = taken(layout, (LATE,), refs)
    low = lanes(layout) < FACE

    def copy(source, dim):
        return pltpu.make_async_copy(source, out.at[:, columns(dim)], left.at[dim])

    copies = [copy(begun.at[:, columns(dim)], dim) for dim in EARLY]
    for each in copies:
        each.start()
    added = {}
    for number, _, element, face in outside_faces(layout, places(), (LATE,), messages, masks):
        part = jnp.where(low, 0.0, face) if number % 2 else jnp.where(low, face, 0.0)
        added[element] = added[element] + part if element in added else part
    for element in layout.elements():
        value = begun[layout.rows(element), columns(LATE)]
        ready[layout.rows(element), :] = value + added[element] if element in added else value
    copies.append(copy(ready, LATE))
    copies[-1].start()
    for each in copies:
        each.wait()


def in_vmem(count):
    return [pl.BlockSpec(memory_space=pltpu.VMEM)] * count


def in_hbm(count):
    return [pl.BlockSpec(memory_space=pltpu.HBM)] * count


PARAMS = pltpu.CompilerParams(vmem_limit_bytes=VMEM_LIMIT)


def kept_in_hbm(*values):
    return [pltpu.with_memory_space_constraint(value, pltpu.HBM) for value in values]


def cost(flops, size):
    return pl.CostEstimate(flops=flops, bytes_accessed=size, transcendentals=0)


def partners(layout, dim, parity):
    sizes = layout.sizes
    swap = {}
    for place in np.ndindex(*sizes):
        other = list(place)
        lower = place[dim] % 2 == parity
        at = place[dim] + (1 if lower else -1)
        if 0 <= at < sizes[dim]:
            other[dim] = at
        elif dim != 1 and sizes[1] % 2 == 0:
            other[1] = place[1] ^ 1
        elif sizes[dim] % 2 == 0:
            other[dim] = sizes[dim] - 1 - place[dim]
        swap[place] = tuple(other)
    return [
        (int(np.ravel_multi_index(place, sizes)), int(np.ravel_multi_index(other, sizes)))
        for place, other in swap.items()
    ]


def exchange(layout, messages, order=TURNS):
    given = dict(zip(layout.turns(), messages))
    return {
        turn: lax.ppermute(given[turn], AXES, partners(layout, *turn))
        for turn in order
        if turn in given
    }


def body(
    load_raw,
    scaling,
    fine_matrix,
    fine_inverse,
    prolong_four,
    coarse_four,
    prolong_two,
    coarse_two,
    orient,
    boundary,
):
    counts, species, nodes = load_raw.shape[:3], load_raw.shape[3], load_raw.shape[4]
    layout = Layout(counts, species, tuple(lax.axis_size(axis) for axis in AXES))
    load = load_raw.reshape(-1, nodes)
    rows = load.shape[0]
    turns = layout.turns()
    message_shapes = tuple(layout.message(dim) for dim, _ in turns)
    whole = jax.ShapeDtypeStruct(load.shape, jnp.float32)
    matrix_shapes = (
        jax.ShapeDtypeStruct((3 * nodes, nodes), jnp.bfloat16),
        jax.ShapeDtypeStruct((2 * len(DIMS), 4 * FACE, nodes), jnp.bfloat16),
    )
    elements = len(layout.elements())
    tables = tuple(jax.ShapeDtypeStruct((elements, nodes), kind) for kind in (jnp.int32, jnp.float32))
    small = (scaling, prolong_four.T, coarse_four, prolong_two.T, coarse_two)
    sides = jnp.transpose(boundary, (1, 2, 3, 0))

    *sent, masks, keeps, load, scaling, four, coarse_four, two, coarse_two = pl.pallas_call(
        functools.partial(first_kernel, layout),
        out_shape=message_shapes
        + tables
        + (whole,)
        + tuple(jax.ShapeDtypeStruct(each.shape, each.dtype) for each in small),
        in_specs=in_hbm(3 + FETCHED),
        out_specs=tuple(in_vmem(len(turns) + 3 + FETCHED)),
        scratch_shapes=[
            pltpu.SMEM(orient.shape, jnp.int32),
            pltpu.SMEM(sides.shape, jnp.int32),
            pltpu.SemaphoreType.DMA((5 + FETCHED,)),
        ],
        compiler_params=PARAMS,
        name="pack",
    )(*kept_in_hbm(load, orient, sides, *small))

    stack = (rounded(prolong_four.shape[1]) + rounded(prolong_two.shape[1]), nodes)
    smoother = pl.pallas_call(
        smoother_kernel,
        out_shape=matrix_shapes,
        in_specs=in_vmem(5),
        out_specs=tuple(in_vmem(2)),
        scratch_shapes=[pltpu.VMEM(stack, jnp.float32), pltpu.VMEM(stack, jnp.float32)],
        compiler_params=PARAMS,
        cost_estimate=cost(2 * nodes * nodes * nodes, 8 * nodes * nodes),
        name="smoother",
    )(fine_inverse, four, coarse_four, two, coarse_two)
    operator = pl.pallas_call(
        operator_kernel,
        out_shape=matrix_shapes,
        in_specs=in_vmem(1),
        out_specs=tuple(in_vmem(2)),
        compiler_params=PARAMS,
        cost_estimate=cost(0, 10 * nodes * nodes),
        name="operator",
    )(fine_matrix)

    def scratch(dims):
        heights = [len(side) * species for dim in dims for side in layout.sides(dim)]
        splits = [pltpu.VMEM((height, 4 * FACE), jnp.bfloat16) for height in heights]
        return splits, [pltpu.VMEM((height, nodes), jnp.float32) for height in heights]

    edges = jax.ShapeDtypeStruct((len(layout.edge()) * species, nodes), jnp.float32)

    def stage(kind, value, sent, matrix, begun, order=TURNS):
        messages = exchange(layout, sent, order)
        begun = pl.pallas_call(
            functools.partial(local_kernel, layout, kind, (len(value), len(begun))),
            out_shape=whole,
            in_specs=in_vmem(4 + len(value) + len(begun)),
            out_specs=in_vmem(1)[0],
            scratch_shapes=[
                pltpu.VMEM((rows, 3 * nodes), jnp.bfloat16),
                pltpu.VMEM(load.shape, jnp.float32),
            ],
            compiler_params=PARAMS,
            cost_estimate=cost(rows * nodes, 0),
            name=kind + "_local",
        )(*value, *begun, masks, keeps, scaling, matrix[0])
        mine = [messages[turn] for turn in layout.turns(EARLY, order)]
        splits, sums = scratch(EARLY)
        begun = pl.pallas_call(
            functools.partial(early_faces_kernel, layout, kind, order),
            out_shape=whole,
            in_specs=in_vmem(4 + len(mine)),
            out_specs=in_vmem(1)[0],
            scratch_shapes=splits + sums,
            compiler_params=PARAMS,
            cost_estimate=cost(0, 0),
            name=kind + "_faces_early",
        )(*mine, masks, scaling, matrix[1], begun)
        mine = [messages[turn] for turn in layout.turns((LATE,), order)]
        changed, *sent = pl.pallas_call(
            functools.partial(late_faces_kernel, layout, kind, order),
            out_shape=(edges,) + message_shapes,
            in_specs=in_vmem(4 + len(mine)),
            out_specs=tuple(in_vmem(1 + len(turns))),
            scratch_shapes=scratch((LATE,))[0],
            compiler_params=PARAMS,
            cost_estimate=cost(0, 0),
            name=kind + "_faces_late",
        )(*mine, masks, scaling, matrix[1], begun)
        return (begun, changed), sent

    first, sent = stage("smooth", (load,), sent, smoother, (), FIRST_TURNS)
    left, sent = stage("operator", first, sent, operator, (load,))
    total, sent = stage("smooth_more", left, sent, smoother, first)
    messages = exchange(layout, sent)
    early = [messages[turn] for turn in layout.turns(EARLY)]
    late = [messages[turn] for turn in layout.turns((LATE,))]
    begun = pl.pallas_call(
        functools.partial(last_early_kernel, layout),
        out_shape=whole,
        in_specs=in_vmem(4 + len(early)),
        out_specs=in_vmem(1)[0],
        compiler_params=PARAMS,
        cost_estimate=cost(0, 8 * rows * nodes),
        name="last_early",
    )(*total, *early, masks, keeps)
    result = pl.pallas_call(
        functools.partial(last_late_kernel, layout),
        out_shape=whole,
        in_specs=in_vmem(2 + len(late)),
        out_specs=in_hbm(1)[0],
        scratch_shapes=[pltpu.VMEM((rows, WIDTH), jnp.float32), pltpu.SemaphoreType.DMA((3,))],
        compiler_params=PARAMS,
        cost_estimate=cost(0, 8 * rows * nodes),
        name="last_late",
    )(begun, *late, masks)
    return result.reshape(load_raw.shape)


def solution(mesh):
    in_specs = (
        P("ex", "ey", "ez", None, None),
        P("ex", "ey", "ez", None),
        P(),
        P(),
        P(),
        P(),
        P(),
        P(),
        P(None, "ex", "ey", "ez"),
        P(None, "ex", "ey", "ez"),
    )
    out_specs = P("ex", "ey", "ez", None, None)
    return jax.shard_map(body, mesh=mesh, in_specs=in_specs, out_specs=out_specs, check_vma=False)
```

```python
import functools

import jax
import jax.numpy as jnp
from jax import lax
from jax.experimental import pallas as pl
from jax.experimental.pallas import tpu as pltpu
import numpy as np
from jax.sharding import PartitionSpec as P

FACE_SIDE = 8
FACE = FACE_SIDE * FACE_SIDE
WIDTH = 2 * FACE
AXES = ("ex", "ey", "ez")
TURNS = ((1, 1), (0, 0), (0, 1), (1, 0), (2, 1), (2, 0))
FIRST_TURNS = ((1, 1), (0, 1), (0, 0), (1, 0), (2, 1), (2, 0))
DIMS = (0, 1, 2)
EARLY = (1, 0)
LATE = 2
FETCHED = 5
VMEM_LIMIT = 24 * 1024 * 1024


class Layout:
    def __init__(self, counts, species, sizes):
        self.counts = counts
        self.species = species
        self.sizes = sizes

    def elements(self):
        spans = [range(count) for count in self.counts]
        return [(i, j, k) for i in spans[0] for j in spans[1] for k in spans[2]]

    def number(self, element):
        return (element[0] * self.counts[1] + element[1]) * self.counts[2] + element[2]

    def rows(self, element):
        start = self.number(element) * self.species
        return slice(start, start + self.species)

    def layer(self, dim, position):
        return [element for element in self.elements() if element[dim] == position]

    def pairs(self, dim):
        return (len(self.layer(dim, 0)) + 1) // 2

    def pair_rows(self, pair):
        return slice(pair * self.species, (pair + 1) * self.species)

    def turns(self, dims=(0, 1, 2), order=TURNS):
        return [
            (dim, parity) for dim, parity in order if dim in dims and self.sizes[dim] > 1 + parity
        ]

    def edge(self):
        ends = (0, self.counts[LATE] - 1)
        return [element for element in self.elements() if element[LATE] in ends]

    def sides(self, dim):
        return self.layer(dim, 0), self.layer(dim, self.counts[dim] - 1)

    def message(self, dim):
        return jax.ShapeDtypeStruct((self.pairs(dim) * self.species, WIDTH), jnp.float32)


def columns(dim):
    return slice(dim * WIDTH, (dim + 1) * WIDTH)


def lanes(layout):
    return lax.broadcasted_iota(jnp.int32, (layout.species, WIDTH), 1)


def picked(value, index):
    return jnp.take_along_axis(value, index, axis=1, mode="promise_in_bounds")


def flip_mask(code):
    reach = FACE_SIDE - 1
    return (code & 1) * (reach * FACE_SIDE) + (code >> 1) * reach


def places():
    return [lax.axis_index(axis) for axis in AXES]


def pack(layout, here, dim, load_block, mask_of, outs):
    turns = [(turn, out) for turn, out in zip(layout.turns(), outs) if turn[0] == dim]
    if not turns:
        return
    lane = lanes(layout)
    low = lane < FACE
    even = (here[dim] & 1) == 0
    first = layout.layer(dim, 0)
    last = layout.layer(dim, layout.counts[dim] - 1)
    for pair in range(layout.pairs(dim)):
        sides = []
        for half in range(2):
            where = min(2 * pair + half, len(first) - 1)
            upper = load_block(last[where], dim)
            lower = load_block(first[where], dim)
            lower = picked(lower, lane ^ mask_of(first[where], dim) ^ (half * FACE))
            if half == 0:
                upper = pltpu.roll(upper, FACE, 1)
            sides.append((upper, lower))
        up = jnp.where(low, sides[0][0], sides[1][0])
        down = jnp.where(low, sides[0][1], sides[1][1])
        for (_, parity), out in turns:
            is_lower = even if parity == 0 else jnp.logical_not(even)
            out[layout.pair_rows(pair), :] = jnp.where(is_lower, up, down)


def received(layout, here, dim, messages):
    even = (here[dim] & 1) == 0
    at_start = here[dim] == 0
    at_end = here[dim] == layout.sizes[dim] - 1
    zero = jnp.zeros((layout.species, WIDTH), jnp.float32)
    found = []
    for pair in range(layout.pairs(dim)):
        first, second = [
            messages[dim, parity][layout.pair_rows(pair), :] if (dim, parity) in messages else zero
            for parity in range(2)
        ]
        below = jnp.where(at_start, 0.0, jnp.where(even, second, first))
        above = jnp.where(at_end, 0.0, jnp.where(even, first, second))
        found.append((below, above))
    return found


def unpacked(lane, outside, where, mask):
    below, above = outside[where // 2]
    half = (where % 2) * FACE
    inside = lane & (FACE - 1)
    return picked(below, (inside ^ mask) + half), picked(above, inside + half)


def assemble(layout, here, dim, load_block, messages, mask_of, keep_of, emit, slab=None):
    lane = lanes(layout)
    low = lane < FACE
    count = layout.counts[dim]
    outside = None if messages is None else received(layout, here, dim, messages)
    zero = jnp.zeros((layout.species, WIDTH), jnp.float32)
    for where, start in enumerate(layout.layer(dim, 0)):
        if slab not in (None, start[0]):
            continue
        line = [start[:dim] + (step,) + start[dim + 1 :] for step in range(count)]
        blocks = [load_block(element, dim) for element in line]
        if outside is None:
            from_below, from_above = zero, zero
        else:
            from_below, from_above = unpacked(lane, outside, where, mask_of(start, dim))
        turned = [from_below]
        for step, element in list(enumerate(line))[1:]:
            shared = jnp.where(low, blocks[step], blocks[step - 1])
            turned.append(picked(shared, lane ^ mask_of(element, dim) ^ FACE))
        turned.append(from_above)
        for step, element in enumerate(line):
            value = blocks[step] + jnp.where(low, turned[step], turned[step + 1])
            if step in (0, count - 1):
                value = value * keep_of(element, dim)
            emit(element, value)


def halves(value):
    high = value.astype(jnp.bfloat16)
    return high, (value - high.astype(jnp.float32)).astype(jnp.bfloat16)


def dot(left, right, contract=((1,), (0,))):
    return lax.dot_general(left, right, (contract, ((), ())), preferred_element_type=jnp.float32)


def split_dot(left, right, contract):
    left_high, left_rest = halves(left)
    right_high, right_rest = halves(right)
    return (
        dot(left_high, right_high, contract)
        + dot(left_high, right_rest, contract)
        + dot(left_rest, right_high, contract)
    )


def stacked(value, local, faces):
    high, rest = halves(value)
    size = value.shape[0]
    for part, piece in enumerate((high, rest, high)):
        local[part * size : (part + 1) * size, :] = piece
    for number in range(faces.shape[0]):
        rows = slice(number * FACE, (number + 1) * FACE)
        for part, piece in enumerate((high, high, rest)):
            faces[number, part * FACE : (part + 1) * FACE, :] = piece[rows, :]
        faces[number, 3 * FACE :, :] = jnp.zeros((FACE, value.shape[1]), jnp.bfloat16)


def operator_kernel(fine, *outs):
    stacked(fine[...], *outs)


def smoother_kernel(inverse, four, coarse_four, two, coarse_two, *refs):
    *outs, right, left = refs
    right[...] = jnp.zeros_like(right)
    left[...] = jnp.zeros_like(left)
    start = 0
    for prolong, coarse in ((four, coarse_four), (two, coarse_two)):
        rows = slice(start, start + prolong.shape[0])
        left[rows, :] = prolong[...]
        right[rows, :] = split_dot(coarse[...], prolong[...], ((1,), (0,)))
        start += rounded(prolong.shape[0])
    corrections = split_dot(left[...], right[...], ((0,), (0,)))
    stacked(0.5 * (inverse[...] + corrections), *outs)


def rounded(count):
    return (count + 7) // 8 * 8


def first_kernel(layout, load, orient, boundary, *refs):
    turns = len(layout.turns())
    small, refs = refs[:FETCHED], refs[FETCHED:]
    outs, masks, keeps, staged = refs[:turns], *refs[turns : turns + 3]
    fetched, (codes, fixed, arrived) = refs[turns + 3 : turns + 3 + FETCHED], refs[-3:]
    scalars = [
        pltpu.make_async_copy(source, target, arrived.at[number])
        for number, (source, target) in enumerate(((orient, codes), (boundary, fixed)))
    ]
    strips = [
        pltpu.make_async_copy(
            load.at[:, columns(dim)], staged.at[:, columns(dim)], arrived.at[2 + dim]
        )
        for dim in DIMS
    ]
    fetches = [
        pltpu.make_async_copy(source, target, arrived.at[5 + number])
        for number, (source, target) in enumerate(zip(small, fetched))
    ]
    for copy in scalars + strips + fetches:
        copy.start()
    here = places()
    scalars[0].wait()
    tabulate_masks(layout, codes, masks)
    scalars[1].wait()
    tabulate_keeps(layout, here, fixed, keeps)
    for dim in DIMS:
        strips[dim].wait()
        pack(
            layout,
            here,
            dim,
            lambda element, dim: staged[layout.rows(element), columns(dim)],
            table(layout, masks),
            outs,
        )
    for copy in fetches:
        copy.wait()


def tabulate_masks(layout, codes, masks):
    for element in layout.elements():
        number = layout.number(element)
        for dim in DIMS:
            code = jnp.full((1, WIDTH), codes[(dim,) + element], jnp.int32)
            masks[number : number + 1, columns(dim)] = flip_mask(code)


def tabulate_keeps(layout, here, boundary, keeps):
    low = lax.broadcasted_iota(jnp.int32, (1, WIDTH), 1) < FACE
    for dim in DIMS:
        first = jnp.where(here[dim] == 0, 1, 0)
        last = jnp.where(here[dim] == layout.sizes[dim] - 1, 1, 0)
        for element in layout.elements():
            number = layout.number(element)
            keep = jnp.ones((1, WIDTH), jnp.float32)
            if element[dim] == 0:
                fixed = first * boundary[element + (2 * dim,)]
                keep = jnp.where(low, 1.0 - jnp.full((1, WIDTH), fixed, jnp.float32), keep)
            if element[dim] == layout.counts[dim] - 1:
                fixed = last * boundary[element + (2 * dim + 1,)]
                keep = jnp.where(low, keep, 1.0 - jnp.full((1, WIDTH), fixed, jnp.float32))
            keeps[number : number + 1, columns(dim)] = keep


def table(layout, ref):
    def row(element, dim):
        number = layout.number(element)
        return ref[number : number + 1, columns(dim)]

    return row


def scales(layout, kind, ref):
    def row(element, dim):
        value = ref[element[0], element[1], element[2] : element[2] + 1, columns(dim)]
        return value if kind == "operator" else 1.0 / value

    return row


def taken(layout, dims, refs, order=TURNS):
    turns = layout.turns(dims, order)
    return dict(zip(turns, refs)), refs[len(turns) :]


def combined(kind, begun, result):
    if begun is None:
        return result
    return begun - result if kind == "operator" else begun + result


def reader(layout, whole, edges=None):
    edge = [] if edges is None else layout.edge()

    def block(element, dim):
        if element in edge:
            return edges[layout.pair_rows(edge.index(element)), columns(dim)]
        return whole[layout.rows(element), columns(dim)]

    return block


def local_kernel(layout, kind, given, *refs):
    value, begun, refs = refs[: given[0]], refs[given[0] : sum(given)], refs[sum(given) :]
    masks, keeps, scaling, matrix, out, split, summed = refs
    value = reader(layout, *value)
    begun = reader(layout, *begun) if begun else None
    here = places()
    factor = scales(layout, kind, scaling)
    nodes = out.shape[1]

    def assembled(dim, slab):
        def emit(element, result):
            high, rest = halves(result * factor(element, dim))
            for part, piece in enumerate((high, high, rest)):
                start = part * nodes + dim * WIDTH
                split[layout.rows(element), start : start + WIDTH] = piece

        assemble(
            layout,
            here,
            dim,
            value,
            None,
            table(layout, masks),
            table(layout, keeps),
            emit,
            slab,
        )

    assembled(0, None)
    count = layout.counts[0]
    height = out.shape[0] // count
    for slab in range(count):
        assembled(1, slab)
        assembled(2, slab)
        rows = slice(slab * height, (slab + 1) * height)
        summed[rows, :] = dot(split[rows, :], matrix[...])
        for element in layout.layer(0, slab):
            for dim in DIMS:
                at = (layout.rows(element), columns(dim))
                result = summed[at] * factor(element, dim)
                out[at] = combined(kind, begun and begun(element, dim), result)


def combined(kind, begun, result):
    if begun is None:
        return result
    return begun - result if kind == "operator" else begun + result


def strips_kernel(layout, kind, dims, local, value, *refs):
    messages, refs = (None, refs) if local else taken(layout, dims, refs)
    masks, keeps, scaling, matrix, *before, out, split, summed = refs
    begun = before[0] if before else None
    here = places()
    factor = scales(layout, kind, scaling)

    def assembled(place, slab):
        dim = dims[place]

        def emit(element, result):
            scaled = result * factor(element, dim)
            put_split(split, layout.rows(element), place, len(dims), scaled)

        assemble(
            layout,
            here,
            dim,
            lambda element, dim: value[layout.rows(element), columns(dim)],
            messages,
            table(layout, masks),
            table(layout, keeps),
            emit,
            slab,
        )

    if 0 in dims:
        assembled(dims.index(0), None)
    count = layout.counts[0]
    height = value.shape[0] // count
    for slab in range(count):
        for place, dim in enumerate(dims):
            if dim != 0:
                assembled(place, slab)
        rows = slice(slab * height, (slab + 1) * height)
        summed[rows, :] = dot(split[rows, :], matrix[...])
        for element in layout.layer(0, slab):
            for each in range(3):
                at = (layout.rows(element), columns(each))
                result = summed[at] * factor(element, each)
                out[at] = combined(kind, None if begun is None else begun[at], result)


def combined(kind, begun, result):
    if begun is None:
        return result
    return begun - result if kind == "operator" else begun + result


def outside_faces(layout, here, dims, messages, masks):
    lane = lanes(layout)
    for dim in dims:
        outside = received(layout, here, dim, messages)
        lower, upper = layout.sides(dim)
        for where, element in enumerate(lower):
            mask = table(layout, masks)(element, dim)
            from_below, from_above = unpacked(lane, outside, where, mask)
            yield 2 * dim, where, element, from_below
            yield 2 * dim + 1, where, upper[where], from_above


def put_faces(layout, here, dim, messages, masks, factor, splits):
    low = lanes(layout) < FACE
    row_low = low[:1]
    for number, where, element, face in outside_faces(layout, here, (dim,), messages, masks):
        row = factor(element, dim)
        turned = pltpu.roll(row, FACE, 1)
        side = number % 2
        value = face * (jnp.where(row_low, turned, row) if side else jnp.where(row_low, row, turned))
        high = value.astype(jnp.bfloat16).astype(jnp.float32)
        rows = layout.pair_rows(where)
        splits[side][rows, :WIDTH] = jnp.where(low, value, value - high).astype(jnp.bfloat16)
        splits[side][rows, WIDTH:] = jnp.where(low, value, 0.0).astype(jnp.bfloat16)


def early_faces_kernel(layout, kind, order, *refs):
    messages, refs = taken(layout, EARLY, refs, order)
    masks, scaling, faces, begun, out, *scratch = refs
    count = 2 * len(EARLY)
    splits, sums = scratch[:count], scratch[count:]
    here = places()
    factor = scales(layout, kind, scaling)
    share = {}
    for place, dim in enumerate(EARLY):
        put_faces(layout, here, dim, messages, masks, factor, splits[2 * place : 2 * place + 2])
        for side, elements in enumerate(layout.sides(dim)):
            at = 2 * place + side
            sums[at][...] = dot(splits[at][...], faces[2 * dim + side])
            for where, element in enumerate(elements):
                share.setdefault(element, []).append((at, layout.pair_rows(where)))
    for element in layout.elements():
        for dim in DIMS:
            at = (layout.rows(element), columns(dim))
            parts = [sums[number][rows, columns(dim)] for number, rows in share.get(element, ())]
            if parts:
                result = sum(parts[1:], parts[0]) * factor(element, dim)
                out[at] = combined(kind, begun[at], result)
            else:
                out[at] = begun[at]


def late_faces_kernel(layout, kind, order, *refs):
    messages, refs = taken(layout, (LATE,), refs, order)
    masks, scaling, faces, begun, out, *refs = refs
    sent, splits = refs[: len(layout.turns())], refs[len(layout.turns()) :]
    here = places()
    factor = scales(layout, kind, scaling)
    put_faces(layout, here, LATE, messages, masks, factor, splits)
    edge = layout.edge()
    done = set()
    for side, elements in enumerate(layout.sides(LATE)):
        product = dot(splits[side][...], faces[2 * LATE + side])
        for where, element in enumerate(elements):
            rows = layout.pair_rows(edge.index(element))
            for dim in DIMS:
                part = product[layout.pair_rows(where), columns(dim)] * factor(element, dim)
                at = (rows, columns(dim))
                base = out[at] if element in done else begun[layout.rows(element), columns(dim)]
                out[at] = combined(kind, base, part)
            done.add(element)
    for dim in DIMS:
        pack(layout, here, dim, reader(layout, begun, out), table(layout, masks), sent)


def last_early_kernel(layout, whole, edges, *refs):
    value = reader(layout, whole, edges)
    messages, (masks, keeps, ready) = taken(layout, EARLY, refs)
    for dim in DIMS:

        def emit(element, result):
            ready[layout.rows(element), columns(dim)] = result

        assemble(
            layout,
            places(),
            dim,
            value,
            None if dim == LATE else messages,
            table(layout, masks),
            table(layout, keeps),
            emit,
        )


def last_late_kernel(layout, begun, *refs):
    messages, (masks, out, ready, left) = taken(layout, (LATE,), refs)
    low = lanes(layout) < FACE

    def copy(source, dim):
        return pltpu.make_async_copy(source, out.at[:, columns(dim)], left.at[dim])

    copies = [copy(begun.at[:, columns(dim)], dim) for dim in EARLY]
    for each in copies:
        each.start()
    added = {}
    for number, _, element, face in outside_faces(layout, places(), (LATE,), messages, masks):
        part = jnp.where(low, 0.0, face) if number % 2 else jnp.where(low, face, 0.0)
        added[element] = added[element] + part if element in added else part
    for element in layout.elements():
        value = begun[layout.rows(element), columns(LATE)]
        ready[layout.rows(element), :] = value + added[element] if element in added else value
    copies.append(copy(ready, LATE))
    copies[-1].start()
    for each in copies:
        each.wait()


def in_vmem(count):
    return [pl.BlockSpec(memory_space=pltpu.VMEM)] * count


def in_hbm(count):
    return [pl.BlockSpec(memory_space=pltpu.HBM)] * count


PARAMS = pltpu.CompilerParams(vmem_limit_bytes=VMEM_LIMIT)


def kept_in_hbm(*values):
    return [pltpu.with_memory_space_constraint(value, pltpu.HBM) for value in values]


def cost(flops, size):
    return pl.CostEstimate(flops=flops, bytes_accessed=size, transcendentals=0)


def partners(layout, dim, parity):
    sizes = layout.sizes
    swap = {}
    for place in np.ndindex(*sizes):
        other = list(place)
        lower = place[dim] % 2 == parity
        at = place[dim] + (1 if lower else -1)
        if 0 <= at < sizes[dim]:
            other[dim] = at
        elif dim != 1 and sizes[1] % 2 == 0:
            other[1] = place[1] ^ 1
        elif sizes[dim] % 2 == 0:
            other[dim] = sizes[dim] - 1 - place[dim]
        swap[place] = tuple(other)
    return [
        (int(np.ravel_multi_index(place, sizes)), int(np.ravel_multi_index(other, sizes)))
        for place, other in swap.items()
    ]


def exchange(layout, messages, order=TURNS):
    given = dict(zip(layout.turns(), messages))
    return {
        turn: lax.ppermute(given[turn], AXES, partners(layout, *turn))
        for turn in order
        if turn in given
    }


def body(
    load_raw,
    scaling,
    fine_matrix,
    fine_inverse,
    prolong_four,
    coarse_four,
    prolong_two,
    coarse_two,
    orient,
    boundary,
):
    counts, species, nodes = load_raw.shape[:3], load_raw.shape[3], load_raw.shape[4]
    layout = Layout(counts, species, tuple(lax.axis_size(axis) for axis in AXES))
    load = load_raw.reshape(-1, nodes)
    rows = load.shape[0]
    turns = layout.turns()
    message_shapes = tuple(layout.message(dim) for dim, _ in turns)
    whole = jax.ShapeDtypeStruct(load.shape, jnp.float32)
    matrix_shapes = (
        jax.ShapeDtypeStruct((3 * nodes, nodes), jnp.bfloat16),
        jax.ShapeDtypeStruct((2 * len(DIMS), 4 * FACE, nodes), jnp.bfloat16),
    )
    elements = len(layout.elements())
    tables = tuple(jax.ShapeDtypeStruct((elements, nodes), kind) for kind in (jnp.int32, jnp.float32))
    small = (scaling, prolong_four.T, coarse_four, prolong_two.T, coarse_two)
    sides = jnp.transpose(boundary, (1, 2, 3, 0))

    *sent, masks, keeps, load, scaling, four, coarse_four, two, coarse_two = pl.pallas_call(
        functools.partial(first_kernel, layout),
        out_shape=message_shapes
        + tables
        + (whole,)
        + tuple(jax.ShapeDtypeStruct(each.shape, each.dtype) for each in small),
        in_specs=in_hbm(3 + FETCHED),
        out_specs=tuple(in_vmem(len(turns) + 3 + FETCHED)),
        scratch_shapes=[
            pltpu.SMEM(orient.shape, jnp.int32),
            pltpu.SMEM(sides.shape, jnp.int32),
            pltpu.SemaphoreType.DMA((5 + FETCHED,)),
        ],
        compiler_params=PARAMS,
        name="pack",
    )(*kept_in_hbm(load, orient, sides, *small))

    stack = (rounded(prolong_four.shape[1]) + rounded(prolong_two.shape[1]), nodes)
    smoother = pl.pallas_call(
        smoother_kernel,
        out_shape=matrix_shapes,
        in_specs=in_vmem(5),
        out_specs=tuple(in_vmem(2)),
        scratch_shapes=[pltpu.VMEM(stack, jnp.float32), pltpu.VMEM(stack, jnp.float32)],
        compiler_params=PARAMS,
        cost_estimate=cost(2 * nodes * nodes * nodes, 8 * nodes * nodes),
        name="smoother",
    )(fine_inverse, four, coarse_four, two, coarse_two)
    operator = pl.pallas_call(
        operator_kernel,
        out_shape=matrix_shapes,
        in_specs=in_vmem(1),
        out_specs=tuple(in_vmem(2)),
        compiler_params=PARAMS,
        cost_estimate=cost(0, 10 * nodes * nodes),
        name="operator",
    )(fine_matrix)

    def scratch(dims):
        heights = [len(side) * species for dim in dims for side in layout.sides(dim)]
        splits = [pltpu.VMEM((height, 4 * FACE), jnp.bfloat16) for height in heights]
        return splits, [pltpu.VMEM((height, nodes), jnp.float32) for height in heights]

    edges = jax.ShapeDtypeStruct((len(layout.edge()) * species, nodes), jnp.float32)

    def stage(kind, value, sent, matrix, begun, order=TURNS):
        messages = exchange(layout, sent, order)
        begun = pl.pallas_call(
            functools.partial(local_kernel, layout, kind, (len(value), len(begun))),
            out_shape=whole,
            in_specs=in_vmem(4 + len(value) + len(begun)),
            out_specs=in_vmem(1)[0],
            scratch_shapes=[
                pltpu.VMEM((rows, 3 * nodes), jnp.bfloat16),
                pltpu.VMEM(load.shape, jnp.float32),
            ],
            compiler_params=PARAMS,
            cost_estimate=cost(rows * nodes, 0),
            name=kind + "_local",
        )(*value, *begun, masks, keeps, scaling, matrix[0])
        mine = [messages[turn] for turn in layout.turns(EARLY, order)]
        splits, sums = scratch(EARLY)
        begun = pl.pallas_call(
            functools.partial(early_faces_kernel, layout, kind, order),
            out_shape=whole,
            in_specs=in_vmem(4 + len(mine)),
            out_specs=in_vmem(1)[0],
            scratch_shapes=splits + sums,
            compiler_params=PARAMS,
            cost_estimate=cost(0, 0),
            name=kind + "_faces_early",
        )(*mine, masks, scaling, matrix[1], begun)
        mine = [messages[turn] for turn in layout.turns((LATE,), order)]
        changed, *sent = pl.pallas_call(
            functools.partial(late_faces_kernel, layout, kind, order),
            out_shape=(edges,) + message_shapes,
            in_specs=in_vmem(4 + len(mine)),
            out_specs=tuple(in_vmem(1 + len(turns))),
            scratch_shapes=scratch((LATE,))[0],
            compiler_params=PARAMS,
            cost_estimate=cost(0, 0),
            name=kind + "_faces_late",
        )(*mine, masks, scaling, matrix[1], begun)
        return (begun, changed), sent

    first, sent = stage("smooth", (load,), sent, smoother, (), FIRST_TURNS)
    left, sent = stage("operator", first, sent, operator, (load,))
    total, sent = stage("smooth_more", left, sent, smoother, first)
    messages = exchange(layout, sent)
    early = [messages[turn] for turn in layout.turns(EARLY)]
    late = [messages[turn] for turn in layout.turns((LATE,))]
    begun = pl.pallas_call(
        functools.partial(last_early_kernel, layout),
        out_shape=whole,
        in_specs=in_vmem(4 + len(early)),
        out_specs=in_vmem(1)[0],
        compiler_params=PARAMS,
        cost_estimate=cost(0, 8 * rows * nodes),
        name="last_early",
    )(*total, *early, masks, keeps)
    result = pl.pallas_call(
        functools.partial(last_late_kernel, layout),
        out_shape=whole,
        in_specs=in_vmem(2 + len(late)),
        out_specs=in_hbm(1)[0],
        scratch_shapes=[pltpu.VMEM((rows, WIDTH), jnp.float32), pltpu.SemaphoreType.DMA((3,))],
        compiler_params=PARAMS,
        cost_estimate=cost(0, 8 * rows * nodes),
        name="last_late",
    )(begun, *late, masks)
    return result.reshape(load_raw.shape)


def solution(mesh):
    in_specs = (
        P("ex", "ey", "ez", None, None),
        P("ex", "ey", "ez", None),
        P(),
        P(),
        P(),
        P(),
        P(),
        P(),
        P(None, "ex", "ey", "ez"),
        P(None, "ex", "ey", "ez"),
    )
    out_specs = P("ex", "ey", "ez", None, None)
    return jax.shard_map(body, mesh=mesh, in_specs=in_specs, out_specs=out_specs, check_vma=False)
```

```python
import functools

import jax
import jax.numpy as jnp
from jax import lax
from jax.experimental import pallas as pl
from jax.experimental.pallas import tpu as pltpu
import numpy as np
from jax.sharding import PartitionSpec as P

FACE_SIDE = 8
FACE = FACE_SIDE * FACE_SIDE
WIDTH = 2 * FACE
AXES = ("ex", "ey", "ez")
TURNS = ((1, 1), (0, 0), (0, 1), (1, 0), (2, 1), (2, 0))
FIRST_TURNS = ((1, 1), (0, 1), (0, 0), (1, 0), (2, 1), (2, 0))
DIMS = (0, 1, 2)
EARLY = (1, 0)
LATE = 2
FETCHED = 5
VMEM_LIMIT = 24 * 1024 * 1024


class Layout:
    def __init__(self, counts, species, sizes):
        self.counts = counts
        self.species = species
        self.sizes = sizes

    def elements(self):
        spans = [range(count) for count in self.counts]
        return [(i, j, k) for i in spans[0] for j in spans[1] for k in spans[2]]

    def number(self, element):
        return (element[0] * self.counts[1] + element[1]) * self.counts[2] + element[2]

    def rows(self, element):
        start = self.number(element) * self.species
        return slice(start, start + self.species)

    def layer(self, dim, position):
        found = [element for element in self.elements() if element[dim] == position]
        return sorted(found, key=lambda element: (element[:LATE], element not in self.edge()))

    def pairs(self, dim):
        return (len(self.layer(dim, 0)) + 1) // 2

    def early_pairs(self, dim):
        first, edge = self.layer(dim, 0), self.edge()
        ends = [(2 * pair, min(2 * pair + 1, len(first) - 1)) for pair in range(self.pairs(dim))]
        if dim == LATE:
            return []
        return [
            pair
            for pair, places in enumerate(ends)
            if not any(first[place] in edge for place in places)
        ]

    def pair_rows(self, pair):
        return slice(pair * self.species, (pair + 1) * self.species)

    def turns(self, dims=(0, 1, 2), order=TURNS):
        return [
            (dim, parity) for dim, parity in order if dim in dims and self.sizes[dim] > 1 + parity
        ]

    def edge(self):
        ends = (0, self.counts[LATE] - 1)
        return [element for element in self.elements() if element[LATE] in ends]

    def sides(self, dim):
        return self.layer(dim, 0), self.layer(dim, self.counts[dim] - 1)

    def message(self, dim):
        return jax.ShapeDtypeStruct((self.pairs(dim) * self.species, WIDTH), jnp.float32)


def columns(dim):
    return slice(dim * WIDTH, (dim + 1) * WIDTH)


def lanes(layout):
    return lax.broadcasted_iota(jnp.int32, (layout.species, WIDTH), 1)


def picked(value, index):
    return jnp.take_along_axis(value, index, axis=1, mode="promise_in_bounds")


def flip_mask(code):
    reach = FACE_SIDE - 1
    return (code & 1) * (reach * FACE_SIDE) + (code >> 1) * reach


def places():
    return [lax.axis_index(axis) for axis in AXES]


def pack(layout, here, dim, load_block, mask_of, outs, only=None):
    turns = [(turn, out) for turn, out in zip(layout.turns(), outs) if turn[0] == dim]
    if not turns:
        return
    lane = lanes(layout)
    low = lane < FACE
    even = (here[dim] & 1) == 0
    first = layout.layer(dim, 0)
    last = layout.layer(dim, layout.counts[dim] - 1)
    for pair in range(layout.pairs(dim)) if only is None else only:
        sides = []
        for half in range(2):
            where = min(2 * pair + half, len(first) - 1)
            upper = load_block(last[where], dim)
            lower = load_block(first[where], dim)
            lower = picked(lower, lane ^ mask_of(first[where], dim) ^ (half * FACE))
            if half == 0:
                upper = pltpu.roll(upper, FACE, 1)
            sides.append((upper, lower))
        up = jnp.where(low, sides[0][0], sides[1][0])
        down = jnp.where(low, sides[0][1], sides[1][1])
        for (_, parity), out in turns:
            is_lower = even if parity == 0 else jnp.logical_not(even)
            out[layout.pair_rows(pair), :] = jnp.where(is_lower, up, down)


def received(layout, here, dim, messages):
    even = (here[dim] & 1) == 0
    at_start = here[dim] == 0
    at_end = here[dim] == layout.sizes[dim] - 1
    zero = jnp.zeros((layout.species, WIDTH), jnp.float32)
    found = []
    for pair in range(layout.pairs(dim)):
        first, second = [
            messages[dim, parity][layout.pair_rows(pair), :] if (dim, parity) in messages else zero
            for parity in range(2)
        ]
        below = jnp.where(at_start, 0.0, jnp.where(even, second, first))
        above = jnp.where(at_end, 0.0, jnp.where(even, first, second))
        found.append((below, above))
    return found


def unpacked(lane, outside, where, mask):
    below, above = outside[where // 2]
    half = (where % 2) * FACE
    inside = lane & (FACE - 1)
    return picked(below, (inside ^ mask) + half), picked(above, inside + half)


def assemble(layout, here, dim, load_block, messages, mask_of, keep_of, emit, slab=None):
    lane = lanes(layout)
    low = lane < FACE
    count = layout.counts[dim]
    outside = None if messages is None else received(layout, here, dim, messages)
    zero = jnp.zeros((layout.species, WIDTH), jnp.float32)
    for where, start in enumerate(layout.layer(dim, 0)):
        if slab not in (None, start[0]):
            continue
        line = [start[:dim] + (step,) + start[dim + 1 :] for step in range(count)]
        blocks = [load_block(element, dim) for element in line]
        if outside is None:
            from_below, from_above = zero, zero
        else:
            from_below, from_above = unpacked(lane, outside, where, mask_of(start, dim))
        turned = [from_below]
        for step, element in list(enumerate(line))[1:]:
            shared = jnp.where(low, blocks[step], blocks[step - 1])
            turned.append(picked(shared, lane ^ mask_of(element, dim) ^ FACE))
        turned.append(from_above)
        for step, element in enumerate(line):
            value = blocks[step] + jnp.where(low, turned[step], turned[step + 1])
            if step in (0, count - 1):
                value = value * keep_of(element, dim)
            emit(element, value)


def halves(value):
    high = value.astype(jnp.bfloat16)
    return high, (value - high.astype(jnp.float32)).astype(jnp.bfloat16)


def dot(left, right, contract=((1,), (0,))):
    return lax.dot_general(left, right, (contract, ((), ())), preferred_element_type=jnp.float32)


def split_dot(left, right, contract):
    left_high, left_rest = halves(left)
    right_high, right_rest = halves(right)
    return (
        dot(left_high, right_high, contract)
        + dot(left_high, right_rest, contract)
        + dot(left_rest, right_high, contract)
    )


def stacked(value, local, faces):
    high, rest = halves(value)
    size = value.shape[0]
    for part, piece in enumerate((high, rest, high)):
        local[part * size : (part + 1) * size, :] = piece
    for number in range(faces.shape[0]):
        rows = slice(number * FACE, (number + 1) * FACE)
        for part, piece in enumerate((high, high, rest)):
            faces[number, part * FACE : (part + 1) * FACE, :] = piece[rows, :]
        faces[number, 3 * FACE :, :] = jnp.zeros((FACE, value.shape[1]), jnp.bfloat16)


def operator_kernel(fine, *outs):
    stacked(fine[...], *outs)


def smoother_kernel(inverse, four, coarse_four, two, coarse_two, *refs):
    *outs, right, left = refs
    right[...] = jnp.zeros_like(right)
    left[...] = jnp.zeros_like(left)
    start = 0
    for prolong, coarse in ((four, coarse_four), (two, coarse_two)):
        rows = slice(start, start + prolong.shape[0])
        left[rows, :] = prolong[...]
        right[rows, :] = split_dot(coarse[...], prolong[...], ((1,), (0,)))
        start += rounded(prolong.shape[0])
    corrections = split_dot(left[...], right[...], ((0,), (0,)))
    stacked(0.5 * (inverse[...] + corrections), *outs)


def rounded(count):
    return (count + 7) // 8 * 8


def first_kernel(layout, load, orient, boundary, *refs):
    turns = len(layout.turns())
    small, refs = refs[:FETCHED], refs[FETCHED:]
    outs, masks, keeps, staged = refs[:turns], *refs[turns : turns + 3]
    fetched, (codes, fixed, arrived) = refs[turns + 3 : turns + 3 + FETCHED], refs[-3:]
    scalars = [
        pltpu.make_async_copy(source, target, arrived.at[number])
        for number, (source, target) in enumerate(((orient, codes), (boundary, fixed)))
    ]
    strips = [
        pltpu.make_async_copy(
            load.at[:, columns(dim)], staged.at[:, columns(dim)], arrived.at[2 + dim]
        )
        for dim in DIMS
    ]
    fetches = [
        pltpu.make_async_copy(source, target, arrived.at[5 + number])
        for number, (source, target) in enumerate(zip(small, fetched))
    ]
    for copy in scalars + strips + fetches:
        copy.start()
    here = places()
    scalars[0].wait()
    tabulate_masks(layout, codes, masks)
    scalars[1].wait()
    tabulate_keeps(layout, here, fixed, keeps)
    for dim in DIMS:
        strips[dim].wait()
        pack(
            layout,
            here,
            dim,
            lambda element, dim: staged[layout.rows(element), columns(dim)],
            table(layout, masks),
            outs,
        )
    for copy in fetches:
        copy.wait()


def tabulate_masks(layout, codes, masks):
    for element in layout.elements():
        number = layout.number(element)
        for dim in DIMS:
            code = jnp.full((1, WIDTH), codes[(dim,) + element], jnp.int32)
            masks[number : number + 1, columns(dim)] = flip_mask(code)


def tabulate_keeps(layout, here, boundary, keeps):
    low = lax.broadcasted_iota(jnp.int32, (1, WIDTH), 1) < FACE
    for dim in DIMS:
        first = jnp.where(here[dim] == 0, 1, 0)
        last = jnp.where(here[dim] == layout.sizes[dim] - 1, 1, 0)
        for element in layout.elements():
            number = layout.number(element)
            keep = jnp.ones((1, WIDTH), jnp.float32)
            if element[dim] == 0:
                fixed = first * boundary[element + (2 * dim,)]
                keep = jnp.where(low, 1.0 - jnp.full((1, WIDTH), fixed, jnp.float32), keep)
            if element[dim] == layout.counts[dim] - 1:
                fixed = last * boundary[element + (2 * dim + 1,)]
                keep = jnp.where(low, keep, 1.0 - jnp.full((1, WIDTH), fixed, jnp.float32))
            keeps[number : number + 1, columns(dim)] = keep


def table(layout, ref):
    def row(element, dim):
        number = layout.number(element)
        return ref[number : number + 1, columns(dim)]

    return row


def scales(layout, kind, ref):
    def row(element, dim):
        value = ref[element[0], element[1], element[2] : element[2] + 1, columns(dim)]
        return value if kind == "operator" else 1.0 / value

    return row


def taken(layout, dims, refs, order=TURNS):
    turns = layout.turns(dims, order)
    return dict(zip(turns, refs)), refs[len(turns) :]


def combined(kind, begun, result):
    if begun is None:
        return result
    return begun - result if kind == "operator" else begun + result


def reader(layout, whole, edges=None):
    edge = [] if edges is None else layout.edge()

    def block(element, dim):
        if element in edge:
            return edges[layout.pair_rows(edge.index(element)), columns(dim)]
        return whole[layout.rows(element), columns(dim)]

    return block


def local_kernel(layout, kind, given, *refs):
    value, begun, refs = refs[: given[0]], refs[given[0] : sum(given)], refs[sum(given) :]
    masks, keeps, scaling, matrix, out, split, summed = refs
    value = reader(layout, *value)
    begun = reader(layout, *begun) if begun else None
    here = places()
    factor = scales(layout, kind, scaling)
    nodes = out.shape[1]

    def assembled(dim, slab):
        def emit(element, result):
            high, rest = halves(result * factor(element, dim))
            for part, piece in enumerate((high, high, rest)):
                start = part * nodes + dim * WIDTH
                split[layout.rows(element), start : start + WIDTH] = piece

        assemble(
            layout,
            here,
            dim,
            value,
            None,
            table(layout, masks),
            table(layout, keeps),
            emit,
            slab,
        )

    assembled(0, None)
    count = layout.counts[0]
    height = out.shape[0] // count
    for slab in range(count):
        assembled(1, slab)
        assembled(2, slab)
        rows = slice(slab * height, (slab + 1) * height)
        summed[rows, :] = dot(split[rows, :], matrix[...])
        for element in layout.layer(0, slab):
            for dim in DIMS:
                at = (layout.rows(element), columns(dim))
                result = summed[at] * factor(element, dim)
                out[at] = combined(kind, begun and begun(element, dim), result)


def combined(kind, begun, result):
    if begun is None:
        return result
    return begun - result if kind == "operator" else begun + result


def strips_kernel(layout, kind, dims, local, value, *refs):
    messages, refs = (None, refs) if local else taken(layout, dims, refs)
    masks, keeps, scaling, matrix, *before, out, split, summed = refs
    begun = before[0] if before else None
    here = places()
    factor = scales(layout, kind, scaling)

    def assembled(place, slab):
        dim = dims[place]

        def emit(element, result):
            scaled = result * factor(element, dim)
            put_split(split, layout.rows(element), place, len(dims), scaled)

        assemble(
            layout,
            here,
            dim,
            lambda element, dim: value[layout.rows(element), columns(dim)],
            messages,
            table(layout, masks),
            table(layout, keeps),
            emit,
            slab,
        )

    if 0 in dims:
        assembled(dims.index(0), None)
    count = layout.counts[0]
    height = value.shape[0] // count
    for slab in range(count):
        for place, dim in enumerate(dims):
            if dim != 0:
                assembled(place, slab)
        rows = slice(slab * height, (slab + 1) * height)
        summed[rows, :] = dot(split[rows, :], matrix[...])
        for element in layout.layer(0, slab):
            for each in range(3):
                at = (layout.rows(element), columns(each))
                result = summed[at] * factor(element, each)
                out[at] = combined(kind, None if begun is None else begun[at], result)


def combined(kind, begun, result):
    if begun is None:
        return result
    return begun - result if kind == "operator" else begun + result


def outside_faces(layout, here, dims, messages, masks):
    lane = lanes(layout)
    for dim in dims:
        outside = received(layout, here, dim, messages)
        lower, upper = layout.sides(dim)
        for where, element in enumerate(lower):
            mask = table(layout, masks)(element, dim)
            from_below, from_above = unpacked(lane, outside, where, mask)
            yield 2 * dim, where, element, from_below
            yield 2 * dim + 1, where, upper[where], from_above


def put_faces(layout, here, dim, messages, masks, factor, splits):
    low = lanes(layout) < FACE
    row_low = low[:1]
    for number, where, element, face in outside_faces(layout, here, (dim,), messages, masks):
        row = factor(element, dim)
        turned = pltpu.roll(row, FACE, 1)
        side = number % 2
        value = face * (jnp.where(row_low, turned, row) if side else jnp.where(row_low, row, turned))
        high = value.astype(jnp.bfloat16).astype(jnp.float32)
        rows = layout.pair_rows(where)
        splits[side][rows, :WIDTH] = jnp.where(low, value, value - high).astype(jnp.bfloat16)
        splits[side][rows, WIDTH:] = jnp.where(low, value, 0.0).astype(jnp.bfloat16)


def early_faces_kernel(layout, kind, order, *refs):
    messages, refs = taken(layout, EARLY, refs, order)
    turns, count = len(layout.turns(EARLY)), 2 * len(EARLY)
    masks, scaling, faces, begun, out, *refs = refs
    ready, splits, sums = refs[:turns], refs[turns : turns + count], refs[turns + count :]
    here = places()
    factor = scales(layout, kind, scaling)
    share = {}
    for place, dim in enumerate(EARLY):
        put_faces(layout, here, dim, messages, masks, factor, splits[2 * place : 2 * place + 2])
        for side, elements in enumerate(layout.sides(dim)):
            at = 2 * place + side
            sums[at][...] = dot(splits[at][...], faces[2 * dim + side])
            for where, element in enumerate(elements):
                share.setdefault(element, []).append((at, layout.pair_rows(where)))
    for element in layout.elements():
        for dim in DIMS:
            at = (layout.rows(element), columns(dim))
            parts = [sums[number][rows, columns(dim)] for number, rows in share.get(element, ())]
            if parts:
                result = sum(parts[1:], parts[0]) * factor(element, dim)
                out[at] = combined(kind, begun[at], result)
            else:
                out[at] = begun[at]
    outs = dict(zip(layout.turns(EARLY), ready))
    for dim in EARLY:
        pack(
            layout,
            here,
            dim,
            reader(layout, out),
            table(layout, masks),
            [outs.get(turn) for turn in layout.turns()],
            layout.early_pairs(dim),
        )


def late_faces_kernel(layout, kind, order, *refs):
    messages, refs = taken(layout, (LATE,), refs, order)
    ready, refs = taken(layout, EARLY, refs)
    masks, scaling, faces, begun, out, *refs = refs
    sent, splits = refs[: len(layout.turns())], refs[len(layout.turns()) :]
    here = places()
    factor = scales(layout, kind, scaling)
    put_faces(layout, here, LATE, messages, masks, factor, splits)
    edge = layout.edge()
    done = set()
    for side, elements in enumerate(layout.sides(LATE)):
        product = dot(splits[side][...], faces[2 * LATE + side])
        for where, element in enumerate(elements):
            rows = layout.pair_rows(edge.index(element))
            for dim in DIMS:
                part = product[layout.pair_rows(where), columns(dim)] * factor(element, dim)
                at = (rows, columns(dim))
                base = out[at] if element in done else begun[layout.rows(element), columns(dim)]
                out[at] = combined(kind, base, part)
            done.add(element)
    for turn, message in zip(layout.turns(), sent):
        for pair in layout.early_pairs(turn[0]):
            rows = layout.pair_rows(pair)
            message[rows, :] = ready[turn][rows, :]
    for dim in DIMS:
        early = layout.early_pairs(dim)
        only = [pair for pair in range(layout.pairs(dim)) if pair not in early]
        pack(layout, here, dim, reader(layout, begun, out), table(layout, masks), sent, only)


def last_early_kernel(layout, whole, edges, *refs):
    value = reader(layout, whole, edges)
    messages, (masks, keeps, ready) = taken(layout, EARLY, refs)
    for dim in DIMS:

        def emit(element, result):
            ready[layout.rows(element), columns(dim)] = result

        assemble(
            layout,
            places(),
            dim,
            value,
            None if dim == LATE else messages,
            table(layout, masks),
            table(layout, keeps),
            emit,
        )


def last_late_kernel(layout, begun, *refs):
    messages, (masks, out, ready, left) = taken(layout, (LATE,), refs)
    low = lanes(layout) < FACE

    def copy(source, dim):
        return pltpu.make_async_copy(source, out.at[:, columns(dim)], left.at[dim])

    copies = [copy(begun.at[:, columns(dim)], dim) for dim in EARLY]
    for each in copies:
        each.start()
    added = {}
    for number, _, element, face in outside_faces(layout, places(), (LATE,), messages, masks):
        part = jnp.where(low, 0.0, face) if number % 2 else jnp.where(low, face, 0.0)
        added[element] = added[element] + part if element in added else part
    for element in layout.elements():
        value = begun[layout.rows(element), columns(LATE)]
        ready[layout.rows(element), :] = value + added[element] if element in added else value
    copies.append(copy(ready, LATE))
    copies[-1].start()
    for each in copies:
        each.wait()


def in_vmem(count):
    return [pl.BlockSpec(memory_space=pltpu.VMEM)] * count


def in_hbm(count):
    return [pl.BlockSpec(memory_space=pltpu.HBM)] * count


PARAMS = pltpu.CompilerParams(vmem_limit_bytes=VMEM_LIMIT)


def kept_in_hbm(*values):
    return [pltpu.with_memory_space_constraint(value, pltpu.HBM) for value in values]


def cost(flops, size):
    return pl.CostEstimate(flops=flops, bytes_accessed=size, transcendentals=0)


def partners(layout, dim, parity):
    sizes = layout.sizes
    swap = {}
    for place in np.ndindex(*sizes):
        other = list(place)
        lower = place[dim] % 2 == parity
        at = place[dim] + (1 if lower else -1)
        if 0 <= at < sizes[dim]:
            other[dim] = at
        elif dim != 1 and sizes[1] % 2 == 0:
            other[1] = place[1] ^ 1
        elif sizes[dim] % 2 == 0:
            other[dim] = sizes[dim] - 1 - place[dim]
        swap[place] = tuple(other)
    return [
        (int(np.ravel_multi_index(place, sizes)), int(np.ravel_multi_index(other, sizes)))
        for place, other in swap.items()
    ]


def exchange(layout, messages, order=TURNS):
    given = dict(zip(layout.turns(), messages))
    return {
        turn: lax.ppermute(given[turn], AXES, partners(layout, *turn))
        for turn in order
        if turn in given
    }


def body(
    load_raw,
    scaling,
    fine_matrix,
    fine_inverse,
    prolong_four,
    coarse_four,
    prolong_two,
    coarse_two,
    orient,
    boundary,
):
    counts, species, nodes = load_raw.shape[:3], load_raw.shape[3], load_raw.shape[4]
    layout = Layout(counts, species, tuple(lax.axis_size(axis) for axis in AXES))
    load = load_raw.reshape(-1, nodes)
    rows = load.shape[0]
    turns = layout.turns()
    message_shapes = tuple(layout.message(dim) for dim, _ in turns)
    whole = jax.ShapeDtypeStruct(load.shape, jnp.float32)
    matrix_shapes = (
        jax.ShapeDtypeStruct((3 * nodes, nodes), jnp.bfloat16),
        jax.ShapeDtypeStruct((2 * len(DIMS), 4 * FACE, nodes), jnp.bfloat16),
    )
    elements = len(layout.elements())
    tables = tuple(jax.ShapeDtypeStruct((elements, nodes), kind) for kind in (jnp.int32, jnp.float32))
    small = (scaling, prolong_four.T, coarse_four, prolong_two.T, coarse_two)
    sides = jnp.transpose(boundary, (1, 2, 3, 0))

    *sent, masks, keeps, load, scaling, four, coarse_four, two, coarse_two = pl.pallas_call(
        functools.partial(first_kernel, layout),
        out_shape=message_shapes
        + tables
        + (whole,)
        + tuple(jax.ShapeDtypeStruct(each.shape, each.dtype) for each in small),
        in_specs=in_hbm(3 + FETCHED),
        out_specs=tuple(in_vmem(len(turns) + 3 + FETCHED)),
        scratch_shapes=[
            pltpu.SMEM(orient.shape, jnp.int32),
            pltpu.SMEM(sides.shape, jnp.int32),
            pltpu.SemaphoreType.DMA((5 + FETCHED,)),
        ],
        compiler_params=PARAMS,
        name="pack",
    )(*kept_in_hbm(load, orient, sides, *small))

    stack = (rounded(prolong_four.shape[1]) + rounded(prolong_two.shape[1]), nodes)
    smoother = pl.pallas_call(
        smoother_kernel,
        out_shape=matrix_shapes,
        in_specs=in_vmem(5),
        out_specs=tuple(in_vmem(2)),
        scratch_shapes=[pltpu.VMEM(stack, jnp.float32), pltpu.VMEM(stack, jnp.float32)],
        compiler_params=PARAMS,
        cost_estimate=cost(2 * nodes * nodes * nodes, 8 * nodes * nodes),
        name="smoother",
    )(fine_inverse, four, coarse_four, two, coarse_two)
    operator = pl.pallas_call(
        operator_kernel,
        out_shape=matrix_shapes,
        in_specs=in_vmem(1),
        out_specs=tuple(in_vmem(2)),
        compiler_params=PARAMS,
        cost_estimate=cost(0, 10 * nodes * nodes),
        name="operator",
    )(fine_matrix)

    def scratch(dims):
        heights = [len(side) * species for dim in dims for side in layout.sides(dim)]
        splits = [pltpu.VMEM((height, 4 * FACE), jnp.bfloat16) for height in heights]
        return splits, [pltpu.VMEM((height, nodes), jnp.float32) for height in heights]

    edges = jax.ShapeDtypeStruct((len(layout.edge()) * species, nodes), jnp.float32)

    def stage(kind, value, sent, matrix, begun, order=TURNS):
        messages = exchange(layout, sent, order)
        begun = pl.pallas_call(
            functools.partial(local_kernel, layout, kind, (len(value), len(begun))),
            out_shape=whole,
            in_specs=in_vmem(4 + len(value) + len(begun)),
            out_specs=in_vmem(1)[0],
            scratch_shapes=[
                pltpu.VMEM((rows, 3 * nodes), jnp.bfloat16),
                pltpu.VMEM(load.shape, jnp.float32),
            ],
            compiler_params=PARAMS,
            cost_estimate=cost(rows * nodes, 0),
            name=kind + "_local",
        )(*value, *begun, masks, keeps, scaling, matrix[0])
        mine = [messages[turn] for turn in layout.turns(EARLY, order)]
        splits, sums = scratch(EARLY)
        early_turns = layout.turns(EARLY)
        begun, *ready = pl.pallas_call(
            functools.partial(early_faces_kernel, layout, kind, order),
            out_shape=(whole,) + tuple(layout.message(dim) for dim, _ in early_turns),
            in_specs=in_vmem(4 + len(mine)),
            out_specs=tuple(in_vmem(1 + len(early_turns))),
            scratch_shapes=splits + sums,
            compiler_params=PARAMS,
            cost_estimate=cost(0, 0),
            name=kind + "_faces_early",
        )(*mine, masks, scaling, matrix[1], begun)
        mine = [messages[turn] for turn in layout.turns((LATE,), order)]
        changed, *sent = pl.pallas_call(
            functools.partial(late_faces_kernel, layout, kind, order),
            out_shape=(edges,) + message_shapes,
            in_specs=in_vmem(4 + len(mine) + len(ready)),
            out_specs=tuple(in_vmem(1 + len(turns))),
            scratch_shapes=scratch((LATE,))[0],
            compiler_params=PARAMS,
            cost_estimate=cost(0, 0),
            name=kind + "_faces_late",
        )(*mine, *ready, masks, scaling, matrix[1], begun)
        return (begun, changed), sent

    first, sent = stage("smooth", (load,), sent, smoother, (), FIRST_TURNS)
    left, sent = stage("operator", first, sent, operator, (load,))
    total, sent = stage("smooth_more", left, sent, smoother, first)
    messages = exchange(layout, sent)
    early = [messages[turn] for turn in layout.turns(EARLY)]
    late = [messages[turn] for turn in layout.turns((LATE,))]
    begun = pl.pallas_call(
        functools.partial(last_early_kernel, layout),
        out_shape=whole,
        in_specs=in_vmem(4 + len(early)),
        out_specs=in_vmem(1)[0],
        compiler_params=PARAMS,
        cost_estimate=cost(0, 8 * rows * nodes),
        name="last_early",
    )(*total, *early, masks, keeps)
    result = pl.pallas_call(
        functools.partial(last_late_kernel, layout),
        out_shape=whole,
        in_specs=in_vmem(2 + len(late)),
        out_specs=in_hbm(1)[0],
        scratch_shapes=[pltpu.VMEM((rows, WIDTH), jnp.float32), pltpu.SemaphoreType.DMA((3,))],
        compiler_params=PARAMS,
        cost_estimate=cost(0, 8 * rows * nodes),
        name="last_late",
    )(begun, *late, masks)
    return result.reshape(load_raw.shape)


def solution(mesh):
    in_specs = (
        P("ex", "ey", "ez", None, None),
        P("ex", "ey", "ez", None),
        P(),
        P(),
        P(),
        P(),
        P(),
        P(),
        P(None, "ex", "ey", "ez"),
        P(None, "ex", "ey", "ez"),
    )
    out_specs = P("ex", "ey", "ez", None, None)
    return jax.shard_map(body, mesh=mesh, in_specs=in_specs, out_specs=out_specs, check_vma=False)
```

```python
import functools

import jax
import jax.numpy as jnp
from jax import lax
from jax.experimental import pallas as pl
from jax.experimental.pallas import tpu as pltpu
import numpy as np
from jax.sharding import PartitionSpec as P

FACE_SIDE = 8
FACE = FACE_SIDE * FACE_SIDE
WIDTH = 2 * FACE
AXES = ("ex", "ey", "ez")
TURNS = ((1, 1), (0, 0), (0, 1), (1, 0), (2, 1), (2, 0))
FIRST_TURNS = ((1, 1), (0, 1), (0, 0), (1, 0), (2, 1), (2, 0))
DIMS = (0, 1, 2)
EARLY = (1, 0)
LATE = 2
FETCHED = 4
VMEM_LIMIT = 24 * 1024 * 1024


class Layout:
    def __init__(self, counts, species, sizes):
        self.counts = counts
        self.species = species
        self.sizes = sizes

    def elements(self):
        spans = [range(count) for count in self.counts]
        return [(i, j, k) for i in spans[0] for j in spans[1] for k in spans[2]]

    def number(self, element):
        return (element[0] * self.counts[1] + element[1]) * self.counts[2] + element[2]

    def rows(self, element):
        start = self.number(element) * self.species
        return slice(start, start + self.species)

    def layer(self, dim, position):
        return [element for element in self.elements() if element[dim] == position]

    def pairs(self, dim):
        return (len(self.layer(dim, 0)) + 1) // 2

    def pair_rows(self, pair):
        return slice(pair * self.species, (pair + 1) * self.species)

    def turns(self, dims=(0, 1, 2), order=TURNS):
        return [
            (dim, parity) for dim, parity in order if dim in dims and self.sizes[dim] > 1 + parity
        ]

    def edge(self):
        ends = (0, self.counts[LATE] - 1)
        return [element for element in self.elements() if element[LATE] in ends]

    def sides(self, dim):
        return self.layer(dim, 0), self.layer(dim, self.counts[dim] - 1)

    def message(self, dim):
        return jax.ShapeDtypeStruct((self.pairs(dim) * self.species, WIDTH), jnp.float32)


def columns(dim):
    return slice(dim * WIDTH, (dim + 1) * WIDTH)


def lanes(layout):
    return lax.broadcasted_iota(jnp.int32, (layout.species, WIDTH), 1)


def picked(value, index):
    return jnp.take_along_axis(value, index, axis=1, mode="promise_in_bounds")


def flip_mask(code):
    reach = FACE_SIDE - 1
    return (code & 1) * (reach * FACE_SIDE) + (code >> 1) * reach


def places():
    return [lax.axis_index(axis) for axis in AXES]


def pack(layout, here, dim, load_block, mask_of, outs):
    turns = [(turn, out) for turn, out in zip(layout.turns(), outs) if turn[0] == dim]
    if not turns:
        return
    lane = lanes(layout)
    low = lane < FACE
    even = (here[dim] & 1) == 0
    first = layout.layer(dim, 0)
    last = layout.layer(dim, layout.counts[dim] - 1)
    for pair in range(layout.pairs(dim)):
        sides = []
        for half in range(2):
            where = min(2 * pair + half, len(first) - 1)
            upper = load_block(last[where], dim)
            lower = load_block(first[where], dim)
            lower = picked(lower, lane ^ mask_of(first[where], dim) ^ (half * FACE))
            if half == 0:
                upper = pltpu.roll(upper, FACE, 1)
            sides.append((upper, lower))
        up = jnp.where(low, sides[0][0], sides[1][0])
        down = jnp.where(low, sides[0][1], sides[1][1])
        for (_, parity), out in turns:
            is_lower = even if parity == 0 else jnp.logical_not(even)
            out[layout.pair_rows(pair), :] = jnp.where(is_lower, up, down)


def received(layout, here, dim, messages):
    even = (here[dim] & 1) == 0
    at_start = here[dim] == 0
    at_end = here[dim] == layout.sizes[dim] - 1
    zero = jnp.zeros((layout.species, WIDTH), jnp.float32)
    found = []
    for pair in range(layout.pairs(dim)):
        first, second = [
            messages[dim, parity][layout.pair_rows(pair), :] if (dim, parity) in messages else zero
            for parity in range(2)
        ]
        below = jnp.where(at_start, 0.0, jnp.where(even, second, first))
        above = jnp.where(at_end, 0.0, jnp.where(even, first, second))
        found.append((below, above))
    return found


def unpacked(lane, outside, where, mask):
    below, above = outside[where // 2]
    half = (where % 2) * FACE
    inside = lane & (FACE - 1)
    return picked(below, (inside ^ mask) + half), picked(above, inside + half)


def assemble(layout, here, dim, load_block, messages, mask_of, keep_of, emit, slab=None):
    lane = lanes(layout)
    low = lane < FACE
    count = layout.counts[dim]
    outside = None if messages is None else received(layout, here, dim, messages)
    zero = jnp.zeros((layout.species, WIDTH), jnp.float32)
    for where, start in enumerate(layout.layer(dim, 0)):
        if slab not in (None, start[0]):
            continue
        line = [start[:dim] + (step,) + start[dim + 1 :] for step in range(count)]
        blocks = [load_block(element, dim) for element in line]
        if outside is None:
            from_below, from_above = zero, zero
        else:
            from_below, from_above = unpacked(lane, outside, where, mask_of(start, dim))
        turned = [from_below]
        for step, element in list(enumerate(line))[1:]:
            shared = jnp.where(low, blocks[step], blocks[step - 1])
            turned.append(picked(shared, lane ^ mask_of(element, dim) ^ FACE))
        turned.append(from_above)
        for step, element in enumerate(line):
            value = blocks[step] + jnp.where(low, turned[step], turned[step + 1])
            if step in (0, count - 1):
                value = value * keep_of(element, dim)
            emit(element, value)


def halves(value):
    high = value.astype(jnp.bfloat16)
    return high, (value - high.astype(jnp.float32)).astype(jnp.bfloat16)


def dot(left, right, contract=((1,), (0,))):
    return lax.dot_general(left, right, (contract, ((), ())), preferred_element_type=jnp.float32)


def split_dot(left, right, contract):
    left_high, left_rest = halves(left)
    right_high, right_rest = halves(right)
    return (
        dot(left_high, right_high, contract)
        + dot(left_high, right_rest, contract)
        + dot(left_rest, right_high, contract)
    )


def stacked(value, local, faces):
    high, rest = halves(value)
    size = value.shape[0]
    for part, piece in enumerate((high, rest, high)):
        local[part * size : (part + 1) * size, :] = piece
    for number in range(faces.shape[0]):
        rows = slice(number * FACE, (number + 1) * FACE)
        for part, piece in enumerate((high, high, rest)):
            faces[number, part * FACE : (part + 1) * FACE, :] = piece[rows, :]
        faces[number, 3 * FACE :, :] = jnp.zeros((FACE, value.shape[1]), jnp.bfloat16)


def operator_kernel(fine, *outs):
    stacked(fine[...], *outs)


def smoother_kernel(inverse, four, coarse_four, two, coarse_two, *refs):
    *outs, right, left = refs
    right[...] = jnp.zeros_like(right)
    left[...] = jnp.zeros_like(left)
    start = 0
    for prolong, coarse in ((four, coarse_four), (two, coarse_two)):
        rows = slice(start, start + prolong.shape[0])
        left[rows, :] = prolong[...]
        right[rows, :] = split_dot(coarse[...], prolong[...], ((1,), (0,)))
        start += rounded(prolong.shape[0])
    corrections = split_dot(left[...], right[...], ((0,), (0,)))
    stacked(0.5 * (inverse[...] + corrections), *outs)


def rounded(count):
    return (count + 7) // 8 * 8


def first_kernel(layout, load, orient, boundary, *refs):
    turns = len(layout.turns())
    small, refs = refs[:FETCHED], refs[FETCHED:]
    outs, masks, keeps, staged = refs[:turns], *refs[turns : turns + 3]
    fetched, (codes, fixed, arrived) = refs[turns + 3 : turns + 3 + FETCHED], refs[-3:]
    scalars = [
        pltpu.make_async_copy(source, target, arrived.at[number])
        for number, (source, target) in enumerate(((orient, codes), (boundary, fixed)))
    ]
    strips = [
        pltpu.make_async_copy(
            load.at[:, columns(dim)], staged.at[:, columns(dim)], arrived.at[2 + dim]
        )
        for dim in DIMS
    ]
    fetches = [
        pltpu.make_async_copy(source, target, arrived.at[5 + number])
        for number, (source, target) in enumerate(zip(small, fetched))
    ]
    for copy in scalars + strips + fetches:
        copy.start()
    here = places()
    scalars[0].wait()
    tabulate_masks(layout, codes, masks)
    scalars[1].wait()
    tabulate_keeps(layout, here, fixed, keeps)
    for dim in DIMS:
        strips[dim].wait()
        pack(
            layout,
            here,
            dim,
            lambda element, dim: staged[layout.rows(element), columns(dim)],
            table(layout, masks),
            outs,
        )
    for copy in fetches:
        copy.wait()


def tabulate_masks(layout, codes, masks):
    for element in layout.elements():
        number = layout.number(element)
        for dim in DIMS:
            code = jnp.full((1, WIDTH), codes[(dim,) + element], jnp.int32)
            masks[number : number + 1, columns(dim)] = flip_mask(code)


def tabulate_keeps(layout, here, boundary, keeps):
    low = lax.broadcasted_iota(jnp.int32, (1, WIDTH), 1) < FACE
    for dim in DIMS:
        first = jnp.where(here[dim] == 0, 1, 0)
        last = jnp.where(here[dim] == layout.sizes[dim] - 1, 1, 0)
        for element in layout.elements():
            number = layout.number(element)
            keep = jnp.ones((1, WIDTH), jnp.float32)
            if element[dim] == 0:
                fixed = first * boundary[element + (2 * dim,)]
                keep = jnp.where(low, 1.0 - jnp.full((1, WIDTH), fixed, jnp.float32), keep)
            if element[dim] == layout.counts[dim] - 1:
                fixed = last * boundary[element + (2 * dim + 1,)]
                keep = jnp.where(low, keep, 1.0 - jnp.full((1, WIDTH), fixed, jnp.float32))
            keeps[number : number + 1, columns(dim)] = keep


def table(layout, ref):
    def row(element, dim):
        number = layout.number(element)
        return ref[number : number + 1, columns(dim)]

    return row


def scales(layout, kind, ref):
    def row(element, dim):
        value = ref[element[0], element[1], element[2] : element[2] + 1, columns(dim)]
        return value if kind == "operator" else 1.0 / value

    return row


def taken(layout, dims, refs, order=TURNS):
    turns = layout.turns(dims, order)
    return dict(zip(turns, refs)), refs[len(turns) :]


def combined(kind, begun, result):
    if begun is None:
        return result
    return begun - result if kind == "operator" else begun + result


def reader(layout, whole, edges=None):
    edge = [] if edges is None else layout.edge()

    def block(element, dim):
        if element in edge:
            return edges[layout.pair_rows(edge.index(element)), columns(dim)]
        return whole[layout.rows(element), columns(dim)]

    return block


def local_kernel(layout, kind, given, *refs):
    value, begun, refs = refs[: given[0]], refs[given[0] : sum(given)], refs[sum(given) :]
    masks, keeps, scaling, matrix, out, split, summed = refs
    value = reader(layout, *value)
    begun = reader(layout, *begun) if begun else None
    here = places()
    factor = scales(layout, kind, scaling)
    nodes = out.shape[1]

    def assembled(dim, slab):
        def emit(element, result):
            high, rest = halves(result * factor(element, dim))
            for part, piece in enumerate((high, high, rest)):
                start = part * nodes + dim * WIDTH
                split[layout.rows(element), start : start + WIDTH] = piece

        assemble(
            layout,
            here,
            dim,
            value,
            None,
            table(layout, masks),
            table(layout, keeps),
            emit,
            slab,
        )

    assembled(0, None)
    count = layout.counts[0]
    height = out.shape[0] // count
    for slab in range(count):
        assembled(1, slab)
        assembled(2, slab)
        rows = slice(slab * height, (slab + 1) * height)
        summed[rows, :] = dot(split[rows, :], matrix[...])
        for element in layout.layer(0, slab):
            for dim in DIMS:
                at = (layout.rows(element), columns(dim))
                result = summed[at] * factor(element, dim)
                out[at] = combined(kind, begun and begun(element, dim), result)


def combined(kind, begun, result):
    if begun is None:
        return result
    return begun - result if kind == "operator" else begun + result


def strips_kernel(layout, kind, dims, local, value, *refs):
    messages, refs = (None, refs) if local else taken(layout, dims, refs)
    masks, keeps, scaling, matrix, *before, out, split, summed = refs
    begun = before[0] if before else None
    here = places()
    factor = scales(layout, kind, scaling)

    def assembled(place, slab):
        dim = dims[place]

        def emit(element, result):
            scaled = result * factor(element, dim)
            put_split(split, layout.rows(element), place, len(dims), scaled)

        assemble(
            layout,
            here,
            dim,
            lambda element, dim: value[layout.rows(element), columns(dim)],
            messages,
            table(layout, masks),
            table(layout, keeps),
            emit,
            slab,
        )

    if 0 in dims:
        assembled(dims.index(0), None)
    count = layout.counts[0]
    height = value.shape[0] // count
    for slab in range(count):
        for place, dim in enumerate(dims):
            if dim != 0:
                assembled(place, slab)
        rows = slice(slab * height, (slab + 1) * height)
        summed[rows, :] = dot(split[rows, :], matrix[...])
        for element in layout.layer(0, slab):
            for each in range(3):
                at = (layout.rows(element), columns(each))
                result = summed[at] * factor(element, each)
                out[at] = combined(kind, None if begun is None else begun[at], result)


def combined(kind, begun, result):
    if begun is None:
        return result
    return begun - result if kind == "operator" else begun + result


def outside_faces(layout, here, dims, messages, masks):
    lane = lanes(layout)
    for dim in dims:
        outside = received(layout, here, dim, messages)
        lower, upper = layout.sides(dim)
        for where, element in enumerate(lower):
            mask = table(layout, masks)(element, dim)
            from_below, from_above = unpacked(lane, outside, where, mask)
            yield 2 * dim, where, element, from_below
            yield 2 * dim + 1, where, upper[where], from_above


def put_faces(layout, here, dim, messages, masks, factor, splits):
    low = lanes(layout) < FACE
    row_low = low[:1]
    for number, where, element, face in outside_faces(layout, here, (dim,), messages, masks):
        row = factor(element, dim)
        turned = pltpu.roll(row, FACE, 1)
        side = number % 2
        value = face * (jnp.where(row_low, turned, row) if side else jnp.where(row_low, row, turned))
        high = value.astype(jnp.bfloat16).astype(jnp.float32)
        rows = layout.pair_rows(where)
        splits[side][rows, :WIDTH] = jnp.where(low, value, value - high).astype(jnp.bfloat16)
        splits[side][rows, WIDTH:] = jnp.where(low, value, 0.0).astype(jnp.bfloat16)


def early_faces_kernel(layout, kind, order, *refs):
    messages, refs = taken(layout, EARLY, refs, order)
    masks, scaling, faces, begun, out, *scratch = refs
    count = 2 * len(EARLY)
    splits, sums = scratch[:count], scratch[count:]
    here = places()
    factor = scales(layout, kind, scaling)
    share = {}
    for place, dim in enumerate(EARLY):
        put_faces(layout, here, dim, messages, masks, factor, splits[2 * place : 2 * place + 2])
        for side, elements in enumerate(layout.sides(dim)):
            at = 2 * place + side
            sums[at][...] = dot(splits[at][...], faces[2 * dim + side])
            for where, element in enumerate(elements):
                share.setdefault(element, []).append((at, layout.pair_rows(where)))
    for element in layout.elements():
        for dim in DIMS:
            at = (layout.rows(element), columns(dim))
            parts = [sums[number][rows, columns(dim)] for number, rows in share.get(element, ())]
            if parts:
                result = sum(parts[1:], parts[0]) * factor(element, dim)
                out[at] = combined(kind, begun[at], result)
            else:
                out[at] = begun[at]


def late_faces_kernel(layout, kind, order, *refs):
    messages, refs = taken(layout, (LATE,), refs, order)
    masks, scaling, faces, begun, out, *refs = refs
    sent, splits = refs[: len(layout.turns())], refs[len(layout.turns()) :]
    here = places()
    factor = scales(layout, kind, scaling)
    put_faces(layout, here, LATE, messages, masks, factor, splits)
    edge = layout.edge()
    done = set()
    for side, elements in enumerate(layout.sides(LATE)):
        product = dot(splits[side][...], faces[2 * LATE + side])
        for where, element in enumerate(elements):
            rows = layout.pair_rows(edge.index(element))
            for dim in DIMS:
                part = product[layout.pair_rows(where), columns(dim)] * factor(element, dim)
                at = (rows, columns(dim))
                base = out[at] if element in done else begun[layout.rows(element), columns(dim)]
                out[at] = combined(kind, base, part)
            done.add(element)
    for dim in DIMS:
        pack(layout, here, dim, reader(layout, begun, out), table(layout, masks), sent)


def last_early_kernel(layout, whole, edges, *refs):
    value = reader(layout, whole, edges)
    messages, (masks, keeps, ready) = taken(layout, EARLY, refs)
    for dim in DIMS:

        def emit(element, result):
            ready[layout.rows(element), columns(dim)] = result

        assemble(
            layout,
            places(),
            dim,
            value,
            None if dim == LATE else messages,
            table(layout, masks),
            table(layout, keeps),
            emit,
        )


def last_late_kernel(layout, begun, *refs):
    messages, (masks, out, ready, left) = taken(layout, (LATE,), refs)
    low = lanes(layout) < FACE

    cut = len(EARLY) * WIDTH
    early = pltpu.make_async_copy(begun.at[:, :cut], out.at[:, :cut], left.at[0])
    early.start()
    added = {}
    for number, _, element, face in outside_faces(layout, places(), (LATE,), messages, masks):
        part = jnp.where(low, 0.0, face) if number % 2 else jnp.where(low, face, 0.0)
        added[element] = added[element] + part if element in added else part
    for element in layout.elements():
        value = begun[layout.rows(element), columns(LATE)]
        ready[layout.rows(element), :] = value + added[element] if element in added else value
    late = pltpu.make_async_copy(ready, out.at[:, cut:], left.at[1])
    late.start()
    early.wait()
    late.wait()


def in_vmem(count):
    return [pl.BlockSpec(memory_space=pltpu.VMEM)] * count


def in_hbm(count):
    return [pl.BlockSpec(memory_space=pltpu.HBM)] * count


PARAMS = pltpu.CompilerParams(vmem_limit_bytes=VMEM_LIMIT)


def kept_in_hbm(*values):
    return [pltpu.with_memory_space_constraint(value, pltpu.HBM) for value in values]


def cost(flops, size):
    return pl.CostEstimate(flops=flops, bytes_accessed=size, transcendentals=0)


def partners(layout, dim, parity):
    sizes = layout.sizes
    swap = {}
    for place in np.ndindex(*sizes):
        other = list(place)
        lower = place[dim] % 2 == parity
        at = place[dim] + (1 if lower else -1)
        if 0 <= at < sizes[dim]:
            other[dim] = at
        elif dim != 1 and sizes[1] % 2 == 0:
            other[1] = place[1] ^ 1
        elif sizes[dim] % 2 == 0:
            other[dim] = sizes[dim] - 1 - place[dim]
        swap[place] = tuple(other)
    return [
        (int(np.ravel_multi_index(place, sizes)), int(np.ravel_multi_index(other, sizes)))
        for place, other in swap.items()
    ]


def exchange(layout, messages, order=TURNS):
    given = dict(zip(layout.turns(), messages))
    return {
        turn: lax.ppermute(given[turn], AXES, partners(layout, *turn))
        for turn in order
        if turn in given
    }


def body(
    load_raw,
    scaling,
    fine_matrix,
    fine_inverse,
    prolong_four,
    coarse_four,
    prolong_two,
    coarse_two,
    orient,
    boundary,
):
    counts, species, nodes = load_raw.shape[:3], load_raw.shape[3], load_raw.shape[4]
    layout = Layout(counts, species, tuple(lax.axis_size(axis) for axis in AXES))
    load = load_raw.reshape(-1, nodes)
    rows = load.shape[0]
    turns = layout.turns()
    message_shapes = tuple(layout.message(dim) for dim, _ in turns)
    whole = jax.ShapeDtypeStruct(load.shape, jnp.float32)
    matrix_shapes = (
        jax.ShapeDtypeStruct((3 * nodes, nodes), jnp.bfloat16),
        jax.ShapeDtypeStruct((2 * len(DIMS), 4 * FACE, nodes), jnp.bfloat16),
    )
    elements = len(layout.elements())
    tables = tuple(jax.ShapeDtypeStruct((elements, nodes), kind) for kind in (jnp.int32, jnp.float32))
    small = (scaling, coarse_four, prolong_two.T, coarse_two)
    sides = jnp.transpose(boundary, (1, 2, 3, 0))

    *sent, masks, keeps, load, scaling, coarse_four, two, coarse_two = pl.pallas_call(
        functools.partial(first_kernel, layout),
        out_shape=message_shapes
        + tables
        + (whole,)
        + tuple(jax.ShapeDtypeStruct(each.shape, each.dtype) for each in small),
        in_specs=in_hbm(3 + FETCHED),
        out_specs=tuple(in_vmem(len(turns) + 3 + FETCHED)),
        scratch_shapes=[
            pltpu.SMEM(orient.shape, jnp.int32),
            pltpu.SMEM(sides.shape, jnp.int32),
            pltpu.SemaphoreType.DMA((5 + FETCHED,)),
        ],
        compiler_params=PARAMS,
        name="pack",
    )(*kept_in_hbm(load, orient, sides, *small))

    stack = (rounded(prolong_four.shape[1]) + rounded(prolong_two.shape[1]), nodes)
    smoother = pl.pallas_call(
        smoother_kernel,
        out_shape=matrix_shapes,
        in_specs=in_vmem(5),
        out_specs=tuple(in_vmem(2)),
        scratch_shapes=[pltpu.VMEM(stack, jnp.float32), pltpu.VMEM(stack, jnp.float32)],
        compiler_params=PARAMS,
        cost_estimate=cost(2 * nodes * nodes * nodes, 8 * nodes * nodes),
        name="smoother",
    )(fine_inverse, prolong_four.T, coarse_four, two, coarse_two)
    operator = pl.pallas_call(
        operator_kernel,
        out_shape=matrix_shapes,
        in_specs=in_vmem(1),
        out_specs=tuple(in_vmem(2)),
        compiler_params=PARAMS,
        cost_estimate=cost(0, 10 * nodes * nodes),
        name="operator",
    )(fine_matrix)

    def scratch(dims):
        heights = [len(side) * species for dim in dims for side in layout.sides(dim)]
        splits = [pltpu.VMEM((height, 4 * FACE), jnp.bfloat16) for height in heights]
        return splits, [pltpu.VMEM((height, nodes), jnp.float32) for height in heights]

    edges = jax.ShapeDtypeStruct((len(layout.edge()) * species, nodes), jnp.float32)

    def stage(kind, value, sent, matrix, begun, order=TURNS):
        messages = exchange(layout, sent, order)
        begun = pl.pallas_call(
            functools.partial(local_kernel, layout, kind, (len(value), len(begun))),
            out_shape=whole,
            in_specs=in_vmem(4 + len(value) + len(begun)),
            out_specs=in_vmem(1)[0],
            scratch_shapes=[
                pltpu.VMEM((rows, 3 * nodes), jnp.bfloat16),
                pltpu.VMEM(load.shape, jnp.float32),
            ],
            compiler_params=PARAMS,
            cost_estimate=cost(rows * nodes, 0),
            name=kind + "_local",
        )(*value, *begun, masks, keeps, scaling, matrix[0])
        mine = [messages[turn] for turn in layout.turns(EARLY, order)]
        splits, sums = scratch(EARLY)
        begun = pl.pallas_call(
            functools.partial(early_faces_kernel, layout, kind, order),
            out_shape=whole,
            in_specs=in_vmem(4 + len(mine)),
            out_specs=in_vmem(1)[0],
            scratch_shapes=splits + sums,
            compiler_params=PARAMS,
            cost_estimate=cost(0, 0),
            name=kind + "_faces_early",
        )(*mine, masks, scaling, matrix[1], begun)
        mine = [messages[turn] for turn in layout.turns((LATE,), order)]
        changed, *sent = pl.pallas_call(
            functools.partial(late_faces_kernel, layout, kind, order),
            out_shape=(edges,) + message_shapes,
            in_specs=in_vmem(4 + len(mine)),
            out_specs=tuple(in_vmem(1 + len(turns))),
            scratch_shapes=scratch((LATE,))[0],
            compiler_params=PARAMS,
            cost_estimate=cost(0, 0),
            name=kind + "_faces_late",
        )(*mine, masks, scaling, matrix[1], begun)
        return (begun, changed), sent

    first, sent = stage("smooth", (load,), sent, smoother, (), FIRST_TURNS)
    left, sent = stage("operator", first, sent, operator, (load,))
    total, sent = stage("smooth_more", left, sent, smoother, first)
    messages = exchange(layout, sent)
    early = [messages[turn] for turn in layout.turns(EARLY)]
    late = [messages[turn] for turn in layout.turns((LATE,))]
    begun = pl.pallas_call(
        functools.partial(last_early_kernel, layout),
        out_shape=whole,
        in_specs=in_vmem(4 + len(early)),
        out_specs=in_vmem(1)[0],
        compiler_params=PARAMS,
        cost_estimate=cost(0, 8 * rows * nodes),
        name="last_early",
    )(*total, *early, masks, keeps)
    result = pl.pallas_call(
        functools.partial(last_late_kernel, layout),
        out_shape=whole,
        in_specs=in_vmem(2 + len(late)),
        out_specs=in_hbm(1)[0],
        scratch_shapes=[pltpu.VMEM((rows, WIDTH), jnp.float32), pltpu.SemaphoreType.DMA((2,))],
        compiler_params=PARAMS,
        cost_estimate=cost(0, 8 * rows * nodes),
        name="last_late",
    )(begun, *late, masks)
    return result.reshape(load_raw.shape)


def solution(mesh):
    in_specs = (
        P("ex", "ey", "ez", None, None),
        P("ex", "ey", "ez", None),
        P(),
        P(),
        P(),
        P(),
        P(),
        P(),
        P(None, "ex", "ey", "ez"),
        P(None, "ex", "ey", "ez"),
    )
    out_specs = P("ex", "ey", "ez", None, None)
    return jax.shard_map(body, mesh=mesh, in_specs=in_specs, out_specs=out_specs, check_vma=False)
```

```python
import functools

import jax
import jax.numpy as jnp
from jax import lax
from jax.experimental import pallas as pl
from jax.experimental.pallas import tpu as pltpu
import numpy as np
from jax.sharding import PartitionSpec as P

FACE_SIDE = 8
FACE = FACE_SIDE * FACE_SIDE
WIDTH = 2 * FACE
AXES = ("ex", "ey", "ez")
TURNS = ((1, 1), (0, 0), (0, 1), (1, 0), (2, 1), (2, 0))
FIRST_TURNS = ((1, 1), (0, 1), (0, 0), (1, 0), (2, 1), (2, 0))
DIMS = (0, 1, 2)
EARLY = (1, 0)
LATE = 2
FETCHED = 5
VMEM_LIMIT = 24 * 1024 * 1024


class Layout:
    def __init__(self, counts, species, sizes):
        self.counts = counts
        self.species = species
        self.sizes = sizes

    def elements(self):
        spans = [range(count) for count in self.counts]
        return [(i, j, k) for i in spans[0] for j in spans[1] for k in spans[2]]

    def number(self, element):
        return (element[0] * self.counts[1] + element[1]) * self.counts[2] + element[2]

    def rows(self, element):
        start = self.number(element) * self.species
        return slice(start, start + self.species)

    def layer(self, dim, position):
        return [element for element in self.elements() if element[dim] == position]

    def pairs(self, dim):
        return (len(self.layer(dim, 0)) + 1) // 2

    def pair_rows(self, pair):
        return slice(pair * self.species, (pair + 1) * self.species)

    def turns(self, dims=(0, 1, 2), order=TURNS):
        return [
            (dim, parity) for dim, parity in order if dim in dims and self.sizes[dim] > 1 + parity
        ]

    def edge(self):
        ends = (0, self.counts[LATE] - 1)
        return [element for element in self.elements() if element[LATE] in ends]

    def sides(self, dim):
        return self.layer(dim, 0), self.layer(dim, self.counts[dim] - 1)

    def message(self, dim):
        return jax.ShapeDtypeStruct((self.pairs(dim) * self.species, WIDTH), jnp.float32)


def columns(dim):
    return slice(dim * WIDTH, (dim + 1) * WIDTH)


def lanes(layout):
    return lax.broadcasted_iota(jnp.int32, (layout.species, WIDTH), 1)


def picked(value, index):
    return jnp.take_along_axis(value, index, axis=1, mode="promise_in_bounds")


def flip_mask(code):
    reach = FACE_SIDE - 1
    return (code & 1) * (reach * FACE_SIDE) + (code >> 1) * reach


def places():
    return [lax.axis_index(axis) for axis in AXES]


def pack(layout, here, dim, load_block, mask_of, outs):
    turns = [(turn, out) for turn, out in zip(layout.turns(), outs) if turn[0] == dim]
    if not turns:
        return
    lane = lanes(layout)
    low = lane < FACE
    even = (here[dim] & 1) == 0
    first = layout.layer(dim, 0)
    last = layout.layer(dim, layout.counts[dim] - 1)
    for pair in range(layout.pairs(dim)):
        sides = []
        for half in range(2):
            where = min(2 * pair + half, len(first) - 1)
            upper = load_block(last[where], dim)
            lower = load_block(first[where], dim)
            lower = picked(lower, lane ^ mask_of(first[where], dim) ^ (half * FACE))
            if half == 0:
                upper = pltpu.roll(upper, FACE, 1)
            sides.append((upper, lower))
        up = jnp.where(low, sides[0][0], sides[1][0])
        down = jnp.where(low, sides[0][1], sides[1][1])
        for (_, parity), out in turns:
            is_lower = even if parity == 0 else jnp.logical_not(even)
            out[layout.pair_rows(pair), :] = jnp.where(is_lower, up, down)


def received(layout, here, dim, messages):
    even = (here[dim] & 1) == 0
    at_start = here[dim] == 0
    at_end = here[dim] == layout.sizes[dim] - 1
    zero = jnp.zeros((layout.species, WIDTH), jnp.float32)
    found = []
    for pair in range(layout.pairs(dim)):
        first, second = [
            messages[dim, parity][layout.pair_rows(pair), :] if (dim, parity) in messages else zero
            for parity in range(2)
        ]
        below = jnp.where(at_start, 0.0, jnp.where(even, second, first))
        above = jnp.where(at_end, 0.0, jnp.where(even, first, second))
        found.append((below, above))
    return found


def unpacked(lane, outside, where, mask):
    below, above = outside[where // 2]
    half = (where % 2) * FACE
    inside = lane & (FACE - 1)
    return picked(below, (inside ^ mask) + half), picked(above, inside + half)


def assemble(layout, here, dim, load_block, messages, mask_of, keep_of, emit, slab=None):
    lane = lanes(layout)
    low = lane < FACE
    count = layout.counts[dim]
    outside = None if messages is None else received(layout, here, dim, messages)
    zero = jnp.zeros((layout.species, WIDTH), jnp.float32)
    for where, start in enumerate(layout.layer(dim, 0)):
        if slab not in (None, start[0]):
            continue
        line = [start[:dim] + (step,) + start[dim + 1 :] for step in range(count)]
        blocks = [load_block(element, dim) for element in line]
        if outside is None:
            from_below, from_above = zero, zero
        else:
            from_below, from_above = unpacked(lane, outside, where, mask_of(start, dim))
        turned = [from_below]
        for step, element in list(enumerate(line))[1:]:
            shared = jnp.where(low, blocks[step], blocks[step - 1])
            turned.append(picked(shared, lane ^ mask_of(element, dim) ^ FACE))
        turned.append(from_above)
        for step, element in enumerate(line):
            value = blocks[step] + jnp.where(low, turned[step], turned[step + 1])
            if step in (0, count - 1):
                value = value * keep_of(element, dim)
            emit(element, value)


def halves(value):
    high = value.astype(jnp.bfloat16)
    return high, (value - high.astype(jnp.float32)).astype(jnp.bfloat16)


def dot(left, right, contract=((1,), (0,))):
    return lax.dot_general(left, right, (contract, ((), ())), preferred_element_type=jnp.float32)


def split_dot(left, right, contract):
    left_high, left_rest = halves(left)
    right_high, right_rest = halves(right)
    return (
        dot(left_high, right_high, contract)
        + dot(left_high, right_rest, contract)
        + dot(left_rest, right_high, contract)
    )


def stacked(value, local, faces):
    high, rest = halves(value)
    size = value.shape[0]
    for part, piece in enumerate((high, rest, high)):
        local[part * size : (part + 1) * size, :] = piece
    for number in range(faces.shape[0]):
        rows = slice(number * FACE, (number + 1) * FACE)
        for part, piece in enumerate((high, high, rest)):
            faces[number, part * FACE : (part + 1) * FACE, :] = piece[rows, :]
        faces[number, 3 * FACE :, :] = jnp.zeros((FACE, value.shape[1]), jnp.bfloat16)


def operator_kernel(fine, *outs):
    stacked(fine[...], *outs)


def smoother_kernel(inverse, four, coarse_four, two, coarse_two, *refs):
    *outs, right, left = refs
    right[...] = jnp.zeros_like(right)
    left[...] = jnp.zeros_like(left)
    start = 0
    for prolong, coarse in ((four, coarse_four), (two, coarse_two)):
        rows = slice(start, start + prolong.shape[0])
        left[rows, :] = prolong[...]
        right[rows, :] = split_dot(coarse[...], prolong[...], ((1,), (0,)))
        start += rounded(prolong.shape[0])
    corrections = split_dot(left[...], right[...], ((0,), (0,)))
    stacked(0.5 * (inverse[...] + corrections), *outs)


def rounded(count):
    return (count + 7) // 8 * 8


def first_kernel(layout, load, orient, boundary, *refs):
    turns = len(layout.turns())
    small, refs = refs[:FETCHED], refs[FETCHED:]
    outs, masks, keeps, staged = refs[:turns], *refs[turns : turns + 3]
    fetched, (codes, fixed, arrived) = refs[turns + 3 : turns + 3 + FETCHED], refs[-3:]
    scalars = [
        pltpu.make_async_copy(source, target, arrived.at[number])
        for number, (source, target) in enumerate(((orient, codes), (boundary, fixed)))
    ]
    strips = [
        pltpu.make_async_copy(
            load.at[:, columns(dim)], staged.at[:, columns(dim)], arrived.at[2 + dim]
        )
        for dim in DIMS
    ]
    fetches = [
        pltpu.make_async_copy(source, target, arrived.at[5 + number])
        for number, (source, target) in enumerate(zip(small, fetched))
    ]
    for copy in scalars + strips + fetches:
        copy.start()
    here = places()
    scalars[0].wait()
    tabulate_masks(layout, codes, masks)
    scalars[1].wait()
    tabulate_keeps(layout, here, fixed, keeps)
    for dim in DIMS:
        strips[dim].wait()
        pack(
            layout,
            here,
            dim,
            lambda element, dim: staged[layout.rows(element), columns(dim)],
            table(layout, masks),
            outs,
        )
    for copy in fetches:
        copy.wait()


def tabulate_masks(layout, codes, masks):
    for element in layout.elements():
        number = layout.number(element)
        for dim in DIMS:
            code = jnp.full((1, WIDTH), codes[(dim,) + element], jnp.int32)
            masks[number : number + 1, columns(dim)] = flip_mask(code)


def tabulate_keeps(layout, here, boundary, keeps):
    low = lax.broadcasted_iota(jnp.int32, (1, WIDTH), 1) < FACE
    for dim in DIMS:
        first = jnp.where(here[dim] == 0, 1, 0)
        last = jnp.where(here[dim] == layout.sizes[dim] - 1, 1, 0)
        for element in layout.elements():
            number = layout.number(element)
            keep = jnp.ones((1, WIDTH), jnp.float32)
            if element[dim] == 0:
                fixed = first * boundary[element + (2 * dim,)]
                keep = jnp.where(low, 1.0 - jnp.full((1, WIDTH), fixed, jnp.float32), keep)
            if element[dim] == layout.counts[dim] - 1:
                fixed = last * boundary[element + (2 * dim + 1,)]
                keep = jnp.where(low, keep, 1.0 - jnp.full((1, WIDTH), fixed, jnp.float32))
            keeps[number : number + 1, columns(dim)] = keep


def table(layout, ref):
    def row(element, dim):
        number = layout.number(element)
        return ref[number : number + 1, columns(dim)]

    return row


def scales(layout, kind, ref):
    def row(element, dim):
        value = ref[element[0], element[1], element[2] : element[2] + 1, columns(dim)]
        return value if kind == "operator" else 1.0 / value

    return row


def taken(layout, dims, refs, order=TURNS):
    turns = layout.turns(dims, order)
    return dict(zip(turns, refs)), refs[len(turns) :]


def combined(kind, begun, result):
    if begun is None:
        return result
    return begun - result if kind == "operator" else begun + result


def reader(layout, whole, edges=None):
    edge = [] if edges is None else layout.edge()

    def block(element, dim):
        if element in edge:
            return edges[layout.pair_rows(edge.index(element)), columns(dim)]
        return whole[layout.rows(element), columns(dim)]

    return block


def local_kernel(layout, kind, given, *refs):
    value, begun, refs = refs[: given[0]], refs[given[0] : sum(given)], refs[sum(given) :]
    masks, keeps, scaling, matrix, out, split, summed = refs
    value = reader(layout, *value)
    begun = reader(layout, *begun) if begun else None
    here = places()
    factor = scales(layout, kind, scaling)
    nodes = out.shape[1]

    def assembled(dim, slab):
        def emit(element, result):
            high, rest = halves(result * factor(element, dim))
            for part, piece in enumerate((high, high, rest)):
                start = part * nodes + dim * WIDTH
                split[layout.rows(element), start : start + WIDTH] = piece

        assemble(
            layout,
            here,
            dim,
            value,
            None,
            table(layout, masks),
            table(layout, keeps),
            emit,
            slab,
        )

    assembled(0, None)
    count = layout.counts[0]
    height = out.shape[0] // count
    for slab in range(count):
        assembled(1, slab)
        assembled(2, slab)
        rows = slice(slab * height, (slab + 1) * height)
        summed[rows, :] = dot(split[rows, :], matrix[...])
        for element in layout.layer(0, slab):
            for dim in DIMS:
                at = (layout.rows(element), columns(dim))
                result = summed[at] * factor(element, dim)
                out[at] = combined(kind, begun and begun(element, dim), result)


def combined(kind, begun, result):
    if begun is None:
        return result
    return begun - result if kind == "operator" else begun + result


def strips_kernel(layout, kind, dims, local, value, *refs):
    messages, refs = (None, refs) if local else taken(layout, dims, refs)
    masks, keeps, scaling, matrix, *before, out, split, summed = refs
    begun = before[0] if before else None
    here = places()
    factor = scales(layout, kind, scaling)

    def assembled(place, slab):
        dim = dims[place]

        def emit(element, result):
            scaled = result * factor(element, dim)
            put_split(split, layout.rows(element), place, len(dims), scaled)

        assemble(
            layout,
            here,
            dim,
            lambda element, dim: value[layout.rows(element), columns(dim)],
            messages,
            table(layout, masks),
            table(layout, keeps),
            emit,
            slab,
        )

    if 0 in dims:
        assembled(dims.index(0), None)
    count = layout.counts[0]
    height = value.shape[0] // count
    for slab in range(count):
        for place, dim in enumerate(dims):
            if dim != 0:
                assembled(place, slab)
        rows = slice(slab * height, (slab + 1) * height)
        summed[rows, :] = dot(split[rows, :], matrix[...])
        for element in layout.layer(0, slab):
            for each in range(3):
                at = (layout.rows(element), columns(each))
                result = summed[at] * factor(element, each)
                out[at] = combined(kind, None if begun is None else begun[at], result)


def combined(kind, begun, result):
    if begun is None:
        return result
    return begun - result if kind == "operator" else begun + result


def outside_faces(layout, here, dims, messages, masks):
    lane = lanes(layout)
    for dim in dims:
        outside = received(layout, here, dim, messages)
        lower, upper = layout.sides(dim)
        for where, element in enumerate(lower):
            mask = table(layout, masks)(element, dim)
            from_below, from_above = unpacked(lane, outside, where, mask)
            yield 2 * dim, where, element, from_below
            yield 2 * dim + 1, where, upper[where], from_above


def put_faces(layout, here, dim, messages, masks, factor, splits):
    low = lanes(layout) < FACE
    row_low = low[:1]
    for number, where, element, face in outside_faces(layout, here, (dim,), messages, masks):
        row = factor(element, dim)
        turned = pltpu.roll(row, FACE, 1)
        side = number % 2
        value = face * (jnp.where(row_low, turned, row) if side else jnp.where(row_low, row, turned))
        high = value.astype(jnp.bfloat16).astype(jnp.float32)
        rows = layout.pair_rows(where)
        splits[side][rows, :WIDTH] = jnp.where(low, value, value - high).astype(jnp.bfloat16)
        splits[side][rows, WIDTH:] = jnp.where(low, value, 0.0).astype(jnp.bfloat16)


def early_faces_kernel(layout, kind, order, *refs):
    messages, refs = taken(layout, EARLY, refs, order)
    masks, scaling, faces, begun, out, *scratch = refs
    count = 2 * len(EARLY)
    splits, sums = scratch[:count], scratch[count:]
    here = places()
    factor = scales(layout, kind, scaling)
    share = {}
    for place, dim in enumerate(EARLY):
        put_faces(layout, here, dim, messages, masks, factor, splits[2 * place : 2 * place + 2])
        for side, elements in enumerate(layout.sides(dim)):
            at = 2 * place + side
            sums[at][...] = dot(splits[at][...], faces[2 * dim + side])
            for where, element in enumerate(elements):
                share.setdefault(element, []).append((at, layout.pair_rows(where)))
    for element in layout.elements():
        for dim in DIMS:
            at = (layout.rows(element), columns(dim))
            parts = [sums[number][rows, columns(dim)] for number, rows in share.get(element, ())]
            if parts:
                result = sum(parts[1:], parts[0]) * factor(element, dim)
                out[at] = combined(kind, begun[at], result)
            else:
                out[at] = begun[at]


def late_faces_kernel(layout, kind, order, *refs):
    messages, refs = taken(layout, (LATE,), refs, order)
    masks, scaling, faces, begun, out, *refs = refs
    *sent, split = refs
    here = places()
    factor = scales(layout, kind, scaling)
    height, depth = split.shape[0] // 2, split.shape[1] // 2
    parts = [(slice(side * height, (side + 1) * height), side * depth) for side in range(2)]
    views = []
    for rows, start in parts:
        views.append(split.at[rows, start : start + depth])
        split[rows, depth - start : 2 * depth - start] = jnp.zeros((height, depth), jnp.bfloat16)
    put_faces(layout, here, LATE, messages, masks, factor, views)
    both = faces[2 * LATE : 2 * LATE + 2]
    products = dot(split[...], both.reshape(2 * depth, both.shape[2]))
    edge = layout.edge()
    done = set()
    for side, elements in enumerate(layout.sides(LATE)):
        product = products[parts[side][0], :]
        for where, element in enumerate(elements):
            rows = layout.pair_rows(edge.index(element))
            for dim in DIMS:
                part = product[layout.pair_rows(where), columns(dim)] * factor(element, dim)
                at = (rows, columns(dim))
                base = out[at] if element in done else begun[layout.rows(element), columns(dim)]
                out[at] = combined(kind, base, part)
            done.add(element)
    for dim in DIMS:
        pack(layout, here, dim, reader(layout, begun, out), table(layout, masks), sent)


def last_early_kernel(layout, whole, edges, *refs):
    value = reader(layout, whole, edges)
    messages, (masks, keeps, ready) = taken(layout, EARLY, refs)
    for dim in DIMS:

        def emit(element, result):
            ready[layout.rows(element), columns(dim)] = result

        assemble(
            layout,
            places(),
            dim,
            value,
            None if dim == LATE else messages,
            table(layout, masks),
            table(layout, keeps),
            emit,
        )


def last_late_kernel(layout, begun, *refs):
    messages, (masks, out, ready, left) = taken(layout, (LATE,), refs)
    low = lanes(layout) < FACE

    cut = len(EARLY) * WIDTH
    early = pltpu.make_async_copy(begun.at[:, :cut], out.at[:, :cut], left.at[0])
    early.start()
    added = {}
    for number, _, element, face in outside_faces(layout, places(), (LATE,), messages, masks):
        part = jnp.where(low, 0.0, face) if number % 2 else jnp.where(low, face, 0.0)
        added[element] = added[element] + part if element in added else part
    for element in layout.elements():
        value = begun[layout.rows(element), columns(LATE)]
        ready[layout.rows(element), :] = value + added[element] if element in added else value
    late = pltpu.make_async_copy(ready, out.at[:, cut:], left.at[1])
    late.start()
    early.wait()
    late.wait()


def in_vmem(count):
    return [pl.BlockSpec(memory_space=pltpu.VMEM)] * count


def in_hbm(count):
    return [pl.BlockSpec(memory_space=pltpu.HBM)] * count


PARAMS = pltpu.CompilerParams(vmem_limit_bytes=VMEM_LIMIT)


def kept_in_hbm(*values):
    return [pltpu.with_memory_space_constraint(value, pltpu.HBM) for value in values]


def cost(flops, size):
    return pl.CostEstimate(flops=flops, bytes_accessed=size, transcendentals=0)


def partners(layout, dim, parity):
    sizes = layout.sizes
    swap = {}
    for place in np.ndindex(*sizes):
        other = list(place)
        lower = place[dim] % 2 == parity
        at = place[dim] + (1 if lower else -1)
        if 0 <= at < sizes[dim]:
            other[dim] = at
        elif dim != 1 and sizes[1] % 2 == 0:
            other[1] = place[1] ^ 1
        elif sizes[dim] % 2 == 0:
            other[dim] = sizes[dim] - 1 - place[dim]
        swap[place] = tuple(other)
    return [
        (int(np.ravel_multi_index(place, sizes)), int(np.ravel_multi_index(other, sizes)))
        for place, other in swap.items()
    ]


def exchange(layout, messages, order=TURNS):
    given = dict(zip(layout.turns(), messages))
    return {
        turn: lax.ppermute(given[turn], AXES, partners(layout, *turn))
        for turn in order
        if turn in given
    }


def body(
    load_raw,
    scaling,
    fine_matrix,
    fine_inverse,
    prolong_four,
    coarse_four,
    prolong_two,
    coarse_two,
    orient,
    boundary,
):
    counts, species, nodes = load_raw.shape[:3], load_raw.shape[3], load_raw.shape[4]
    layout = Layout(counts, species, tuple(lax.axis_size(axis) for axis in AXES))
    load = load_raw.reshape(-1, nodes)
    rows = load.shape[0]
    turns = layout.turns()
    message_shapes = tuple(layout.message(dim) for dim, _ in turns)
    whole = jax.ShapeDtypeStruct(load.shape, jnp.float32)
    matrix_shapes = (
        jax.ShapeDtypeStruct((3 * nodes, nodes), jnp.bfloat16),
        jax.ShapeDtypeStruct((2 * len(DIMS), 4 * FACE, nodes), jnp.bfloat16),
    )
    elements = len(layout.elements())
    tables = tuple(jax.ShapeDtypeStruct((elements, nodes), kind) for kind in (jnp.int32, jnp.float32))
    small = (scaling, prolong_four.T, coarse_four, prolong_two.T, coarse_two)
    sides = jnp.transpose(boundary, (1, 2, 3, 0))

    *sent, masks, keeps, load, scaling, four, coarse_four, two, coarse_two = pl.pallas_call(
        functools.partial(first_kernel, layout),
        out_shape=message_shapes
        + tables
        + (whole,)
        + tuple(jax.ShapeDtypeStruct(each.shape, each.dtype) for each in small),
        in_specs=in_hbm(3 + FETCHED),
        out_specs=tuple(in_vmem(len(turns) + 3 + FETCHED)),
        scratch_shapes=[
            pltpu.SMEM(orient.shape, jnp.int32),
            pltpu.SMEM(sides.shape, jnp.int32),
            pltpu.SemaphoreType.DMA((5 + FETCHED,)),
        ],
        compiler_params=PARAMS,
        name="pack",
    )(*kept_in_hbm(load, orient, sides, *small))

    stack = (rounded(prolong_four.shape[1]) + rounded(prolong_two.shape[1]), nodes)
    smoother = pl.pallas_call(
        smoother_kernel,
        out_shape=matrix_shapes,
        in_specs=in_vmem(5),
        out_specs=tuple(in_vmem(2)),
        scratch_shapes=[pltpu.VMEM(stack, jnp.float32), pltpu.VMEM(stack, jnp.float32)],
        compiler_params=PARAMS,
        cost_estimate=cost(2 * nodes * nodes * nodes, 8 * nodes * nodes),
        name="smoother",
    )(fine_inverse, four, coarse_four, two, coarse_two)
    operator = pl.pallas_call(
        operator_kernel,
        out_shape=matrix_shapes,
        in_specs=in_vmem(1),
        out_specs=tuple(in_vmem(2)),
        compiler_params=PARAMS,
        cost_estimate=cost(0, 10 * nodes * nodes),
        name="operator",
    )(fine_matrix)

    def scratch(dims):
        heights = [len(side) * species for dim in dims for side in layout.sides(dim)]
        splits = [pltpu.VMEM((height, 4 * FACE), jnp.bfloat16) for height in heights]
        return splits, [pltpu.VMEM((height, nodes), jnp.float32) for height in heights]

    edges = jax.ShapeDtypeStruct((len(layout.edge()) * species, nodes), jnp.float32)

    def stage(kind, value, sent, matrix, begun, order=TURNS):
        messages = exchange(layout, sent, order)
        begun = pl.pallas_call(
            functools.partial(local_kernel, layout, kind, (len(value), len(begun))),
            out_shape=whole,
            in_specs=in_vmem(4 + len(value) + len(begun)),
            out_specs=in_vmem(1)[0],
            scratch_shapes=[
                pltpu.VMEM((rows, 3 * nodes), jnp.bfloat16),
                pltpu.VMEM(load.shape, jnp.float32),
            ],
            compiler_params=PARAMS,
            cost_estimate=cost(rows * nodes, 0),
            name=kind + "_local",
        )(*value, *begun, masks, keeps, scaling, matrix[0])
        mine = [messages[turn] for turn in layout.turns(EARLY, order)]
        splits, sums = scratch(EARLY)
        begun = pl.pallas_call(
            functools.partial(early_faces_kernel, layout, kind, order),
            out_shape=whole,
            in_specs=in_vmem(4 + len(mine)),
            out_specs=in_vmem(1)[0],
            scratch_shapes=splits + sums,
            compiler_params=PARAMS,
            cost_estimate=cost(0, 0),
            name=kind + "_faces_early",
        )(*mine, masks, scaling, matrix[1], begun)
        mine = [messages[turn] for turn in layout.turns((LATE,), order)]
        height = len(layout.sides(LATE)[0]) * species
        changed, *sent = pl.pallas_call(
            functools.partial(late_faces_kernel, layout, kind, order),
            out_shape=(edges,) + message_shapes,
            in_specs=in_vmem(4 + len(mine)),
            out_specs=tuple(in_vmem(1 + len(turns))),
            scratch_shapes=[pltpu.VMEM((2 * height, 8 * FACE), jnp.bfloat16)],
            compiler_params=PARAMS,
            cost_estimate=cost(0, 0),
            name=kind + "_faces_late",
        )(*mine, masks, scaling, matrix[1], begun)
        return (begun, changed), sent

    first, sent = stage("smooth", (load,), sent, smoother, (), FIRST_TURNS)
    left, sent = stage("operator", first, sent, operator, (load,))
    total, sent = stage("smooth_more", left, sent, smoother, first)
    messages = exchange(layout, sent)
    early = [messages[turn] for turn in layout.turns(EARLY)]
    late = [messages[turn] for turn in layout.turns((LATE,))]
    begun = pl.pallas_call(
        functools.partial(last_early_kernel, layout),
        out_shape=whole,
        in_specs=in_vmem(4 + len(early)),
        out_specs=in_vmem(1)[0],
        compiler_params=PARAMS,
        cost_estimate=cost(0, 8 * rows * nodes),
        name="last_early",
    )(*total, *early, masks, keeps)
    result = pl.pallas_call(
        functools.partial(last_late_kernel, layout),
        out_shape=whole,
        in_specs=in_vmem(2 + len(late)),
        out_specs=in_hbm(1)[0],
        scratch_shapes=[pltpu.VMEM((rows, WIDTH), jnp.float32), pltpu.SemaphoreType.DMA((2,))],
        compiler_params=PARAMS,
        cost_estimate=cost(0, 8 * rows * nodes),
        name="last_late",
    )(begun, *late, masks)
    return result.reshape(load_raw.shape)


def solution(mesh):
    in_specs = (
        P("ex", "ey", "ez", None, None),
        P("ex", "ey", "ez", None),
        P(),
        P(),
        P(),
        P(),
        P(),
        P(),
        P(None, "ex", "ey", "ez"),
        P(None, "ex", "ey", "ez"),
    )
    out_specs = P("ex", "ey", "ez", None, None)
    return jax.shard_map(body, mesh=mesh, in_specs=in_specs, out_specs=out_specs, check_vma=False)
```

```python
import functools

import jax
import jax.numpy as jnp
from jax import lax
from jax.experimental import pallas as pl
from jax.experimental.pallas import tpu as pltpu
import numpy as np
from jax.sharding import PartitionSpec as P

FACE_SIDE = 8
FACE = FACE_SIDE * FACE_SIDE
WIDTH = 2 * FACE
AXES = ("ex", "ey", "ez")
TURNS = ((1, 1), (0, 0), (0, 1), (1, 0), (2, 1), (2, 0))
FIRST_TURNS = ((1, 1), (0, 1), (0, 0), (1, 0), (2, 1), (2, 0))
DIMS = (0, 1, 2)
EARLY = (1, 0)
LATE = 2
FETCHED = 5
VMEM_LIMIT = 24 * 1024 * 1024


class Layout:
    def __init__(self, counts, species, sizes):
        self.counts = counts
        self.species = species
        self.sizes = sizes

    def elements(self):
        spans = [range(count) for count in self.counts]
        return [(i, j, k) for i in spans[0] for j in spans[1] for k in spans[2]]

    def number(self, element):
        return (element[0] * self.counts[1] + element[1]) * self.counts[2] + element[2]

    def rows(self, element):
        start = self.number(element) * self.species
        return slice(start, start + self.species)

    def layer(self, dim, position):
        return [element for element in self.elements() if element[dim] == position]

    def pairs(self, dim):
        return (len(self.layer(dim, 0)) + 1) // 2

    def pair_rows(self, pair):
        return slice(pair * self.species, (pair + 1) * self.species)

    def turns(self, dims=(0, 1, 2), order=TURNS):
        return [
            (dim, parity) for dim, parity in order if dim in dims and self.sizes[dim] > 1 + parity
        ]

    def edge(self):
        ends = (0, self.counts[LATE] - 1)
        return [element for element in self.elements() if element[LATE] in ends]

    def sides(self, dim):
        return self.layer(dim, 0), self.layer(dim, self.counts[dim] - 1)

    def message(self, dim):
        return jax.ShapeDtypeStruct((self.pairs(dim) * self.species, WIDTH), jnp.float32)


def columns(dim):
    return slice(dim * WIDTH, (dim + 1) * WIDTH)


def lanes(layout):
    return lax.broadcasted_iota(jnp.int32, (layout.species, WIDTH), 1)


def picked(value, index):
    return jnp.take_along_axis(value, index, axis=1, mode="promise_in_bounds")


def flip_mask(code):
    reach = FACE_SIDE - 1
    return (code & 1) * (reach * FACE_SIDE) + (code >> 1) * reach


def places():
    return [lax.axis_index(axis) for axis in AXES]


def write_flags(layout, here, flags):
    for dim in DIMS:
        tests = ((here[dim] & 1) == 0, here[dim] == 0, here[dim] == layout.sizes[dim] - 1)
        for number, test in enumerate(tests):
            row = 3 * dim + number
            flags[row : row + 1, :] = jnp.full((1, WIDTH), jnp.where(test, 1, 0), jnp.int32)


def flagged(layout, flags, dim):
    rows = [flags[3 * dim + number : 3 * dim + number + 1, :] for number in range(3)]
    return [jnp.broadcast_to(row, (layout.species, WIDTH)) == 1 for row in rows]


def pack(layout, here, dim, load_block, mask_of, outs):
    turns = [(turn, out) for turn, out in zip(layout.turns(), outs) if turn[0] == dim]
    if not turns:
        return
    lane = lanes(layout)
    low = lane < FACE
    even = flagged(layout, here, dim)[0]
    first = layout.layer(dim, 0)
    last = layout.layer(dim, layout.counts[dim] - 1)
    for pair in range(layout.pairs(dim)):
        sides = []
        for half in range(2):
            where = min(2 * pair + half, len(first) - 1)
            upper = load_block(last[where], dim)
            lower = load_block(first[where], dim)
            lower = picked(lower, lane ^ mask_of(first[where], dim) ^ (half * FACE))
            if half == 0:
                upper = pltpu.roll(upper, FACE, 1)
            sides.append((upper, lower))
        up = jnp.where(low, sides[0][0], sides[1][0])
        down = jnp.where(low, sides[0][1], sides[1][1])
        for (_, parity), out in turns:
            is_lower = even if parity == 0 else jnp.logical_not(even)
            out[layout.pair_rows(pair), :] = jnp.where(is_lower, up, down)


def received(layout, here, dim, messages):
    even, at_start, at_end = flagged(layout, here, dim)
    zero = jnp.zeros((layout.species, WIDTH), jnp.float32)
    found = []
    for pair in range(layout.pairs(dim)):
        first, second = [
            messages[dim, parity][layout.pair_rows(pair), :] if (dim, parity) in messages else zero
            for parity in range(2)
        ]
        below = jnp.where(at_start, 0.0, jnp.where(even, second, first))
        above = jnp.where(at_end, 0.0, jnp.where(even, first, second))
        found.append((below, above))
    return found


def unpacked(lane, outside, where, mask):
    below, above = outside[where // 2]
    half = (where % 2) * FACE
    inside = lane & (FACE - 1)
    return picked(below, (inside ^ mask) + half), picked(above, inside + half)


def assemble(layout, here, dim, load_block, messages, mask_of, keep_of, emit, slab=None):
    lane = lanes(layout)
    low = lane < FACE
    count = layout.counts[dim]
    outside = None if messages is None else received(layout, here, dim, messages)
    zero = jnp.zeros((layout.species, WIDTH), jnp.float32)
    for where, start in enumerate(layout.layer(dim, 0)):
        if slab not in (None, start[0]):
            continue
        line = [start[:dim] + (step,) + start[dim + 1 :] for step in range(count)]
        blocks = [load_block(element, dim) for element in line]
        if outside is None:
            from_below, from_above = zero, zero
        else:
            from_below, from_above = unpacked(lane, outside, where, mask_of(start, dim))
        turned = [from_below]
        for step, element in list(enumerate(line))[1:]:
            shared = jnp.where(low, blocks[step], blocks[step - 1])
            turned.append(picked(shared, lane ^ mask_of(element, dim) ^ FACE))
        turned.append(from_above)
        for step, element in enumerate(line):
            value = blocks[step] + jnp.where(low, turned[step], turned[step + 1])
            if step in (0, count - 1):
                value = value * keep_of(element, dim)
            emit(element, value)


def halves(value):
    high = value.astype(jnp.bfloat16)
    return high, (value - high.astype(jnp.float32)).astype(jnp.bfloat16)


def dot(left, right, contract=((1,), (0,))):
    return lax.dot_general(left, right, (contract, ((), ())), preferred_element_type=jnp.float32)


def split_dot(left, right, contract):
    left_high, left_rest = halves(left)
    right_high, right_rest = halves(right)
    return (
        dot(left_high, right_high, contract)
        + dot(left_high, right_rest, contract)
        + dot(left_rest, right_high, contract)
    )


def stacked(value, local, faces):
    high, rest = halves(value)
    size = value.shape[0]
    for part, piece in enumerate((high, rest, high)):
        local[part * size : (part + 1) * size, :] = piece
    for number in range(faces.shape[0]):
        rows = slice(number * FACE, (number + 1) * FACE)
        for part, piece in enumerate((high, high, rest)):
            faces[number, part * FACE : (part + 1) * FACE, :] = piece[rows, :]
        faces[number, 3 * FACE :, :] = jnp.zeros((FACE, value.shape[1]), jnp.bfloat16)


def operator_kernel(fine, *outs):
    stacked(fine[...], *outs)


def smoother_kernel(inverse, four, coarse_four, two, coarse_two, *refs):
    *outs, right, left = refs
    right[...] = jnp.zeros_like(right)
    left[...] = jnp.zeros_like(left)
    start = 0
    for prolong, coarse in ((four, coarse_four), (two, coarse_two)):
        rows = slice(start, start + prolong.shape[0])
        left[rows, :] = prolong[...]
        right[rows, :] = split_dot(coarse[...], prolong[...], ((1,), (0,)))
        start += rounded(prolong.shape[0])
    corrections = split_dot(left[...], right[...], ((0,), (0,)))
    stacked(0.5 * (inverse[...] + corrections), *outs)


def rounded(count):
    return (count + 7) // 8 * 8


def first_kernel(layout, load, orient, boundary, *refs):
    turns = len(layout.turns())
    small, refs = refs[:FETCHED], refs[FETCHED:]
    outs, masks, keeps, staged, flags = refs[:turns], *refs[turns : turns + 4]
    fetched, (codes, fixed, arrived) = refs[turns + 4 : turns + 4 + FETCHED], refs[-3:]
    scalars = [
        pltpu.make_async_copy(source, target, arrived.at[number])
        for number, (source, target) in enumerate(((orient, codes), (boundary, fixed)))
    ]
    strips = [
        pltpu.make_async_copy(
            load.at[:, columns(dim)], staged.at[:, columns(dim)], arrived.at[2 + dim]
        )
        for dim in DIMS
    ]
    fetches = [
        pltpu.make_async_copy(source, target, arrived.at[5 + number])
        for number, (source, target) in enumerate(zip(small, fetched))
    ]
    for copy in scalars + strips + fetches:
        copy.start()
    here = places()
    write_flags(layout, here, flags)
    scalars[0].wait()
    tabulate_masks(layout, codes, masks)
    scalars[1].wait()
    tabulate_keeps(layout, here, fixed, keeps)
    for dim in DIMS:
        strips[dim].wait()
        pack(
            layout,
            flags,
            dim,
            lambda element, dim: staged[layout.rows(element), columns(dim)],
            table(layout, masks),
            outs,
        )
    for copy in fetches:
        copy.wait()


def tabulate_masks(layout, codes, masks):
    for element in layout.elements():
        number = layout.number(element)
        for dim in DIMS:
            code = jnp.full((1, WIDTH), codes[(dim,) + element], jnp.int32)
            masks[number : number + 1, columns(dim)] = flip_mask(code)


def tabulate_keeps(layout, here, boundary, keeps):
    low = lax.broadcasted_iota(jnp.int32, (1, WIDTH), 1) < FACE
    for dim in DIMS:
        first = jnp.where(here[dim] == 0, 1, 0)
        last = jnp.where(here[dim] == layout.sizes[dim] - 1, 1, 0)
        for element in layout.elements():
            number = layout.number(element)
            keep = jnp.ones((1, WIDTH), jnp.float32)
            if element[dim] == 0:
                fixed = first * boundary[element + (2 * dim,)]
                keep = jnp.where(low, 1.0 - jnp.full((1, WIDTH), fixed, jnp.float32), keep)
            if element[dim] == layout.counts[dim] - 1:
                fixed = last * boundary[element + (2 * dim + 1,)]
                keep = jnp.where(low, keep, 1.0 - jnp.full((1, WIDTH), fixed, jnp.float32))
            keeps[number : number + 1, columns(dim)] = keep


def table(layout, ref):
    def row(element, dim):
        number = layout.number(element)
        return ref[number : number + 1, columns(dim)]

    return row


def scales(layout, kind, ref):
    def row(element, dim):
        value = ref[element[0], element[1], element[2] : element[2] + 1, columns(dim)]
        return value if kind == "operator" else 1.0 / value

    return row


def taken(layout, dims, refs, order=TURNS):
    turns = layout.turns(dims, order)
    return dict(zip(turns, refs)), refs[len(turns) :]


def combined(kind, begun, result):
    if begun is None:
        return result
    return begun - result if kind == "operator" else begun + result


def reader(layout, whole, edges=None):
    edge = [] if edges is None else layout.edge()

    def block(element, dim):
        if element in edge:
            return edges[layout.pair_rows(edge.index(element)), columns(dim)]
        return whole[layout.rows(element), columns(dim)]

    return block


def local_kernel(layout, kind, given, *refs):
    value, begun, refs = refs[: given[0]], refs[given[0] : sum(given)], refs[sum(given) :]
    masks, keeps, scaling, matrix, out, split, summed = refs
    value = reader(layout, *value)
    begun = reader(layout, *begun) if begun else None
    here = None
    factor = scales(layout, kind, scaling)
    nodes = out.shape[1]

    def assembled(dim, slab):
        def emit(element, result):
            high, rest = halves(result * factor(element, dim))
            for part, piece in enumerate((high, high, rest)):
                start = part * nodes + dim * WIDTH
                split[layout.rows(element), start : start + WIDTH] = piece

        assemble(
            layout,
            here,
            dim,
            value,
            None,
            table(layout, masks),
            table(layout, keeps),
            emit,
            slab,
        )

    assembled(0, None)
    count = layout.counts[0]
    height = out.shape[0] // count
    for slab in range(count):
        assembled(1, slab)
        assembled(2, slab)
        rows = slice(slab * height, (slab + 1) * height)
        summed[rows, :] = dot(split[rows, :], matrix[...])
        for element in layout.layer(0, slab):
            for dim in DIMS:
                at = (layout.rows(element), columns(dim))
                result = summed[at] * factor(element, dim)
                out[at] = combined(kind, begun and begun(element, dim), result)


def combined(kind, begun, result):
    if begun is None:
        return result
    return begun - result if kind == "operator" else begun + result


def strips_kernel(layout, kind, dims, local, value, *refs):
    messages, refs = (None, refs) if local else taken(layout, dims, refs)
    masks, keeps, scaling, matrix, *before, out, split, summed = refs
    begun = before[0] if before else None
    here = places()
    factor = scales(layout, kind, scaling)

    def assembled(place, slab):
        dim = dims[place]

        def emit(element, result):
            scaled = result * factor(element, dim)
            put_split(split, layout.rows(element), place, len(dims), scaled)

        assemble(
            layout,
            here,
            dim,
            lambda element, dim: value[layout.rows(element), columns(dim)],
            messages,
            table(layout, masks),
            table(layout, keeps),
            emit,
            slab,
        )

    if 0 in dims:
        assembled(dims.index(0), None)
    count = layout.counts[0]
    height = value.shape[0] // count
    for slab in range(count):
        for place, dim in enumerate(dims):
            if dim != 0:
                assembled(place, slab)
        rows = slice(slab * height, (slab + 1) * height)
        summed[rows, :] = dot(split[rows, :], matrix[...])
        for element in layout.layer(0, slab):
            for each in range(3):
                at = (layout.rows(element), columns(each))
                result = summed[at] * factor(element, each)
                out[at] = combined(kind, None if begun is None else begun[at], result)


def combined(kind, begun, result):
    if begun is None:
        return result
    return begun - result if kind == "operator" else begun + result


def outside_faces(layout, here, dims, messages, masks):
    lane = lanes(layout)
    for dim in dims:
        outside = received(layout, here, dim, messages)
        lower, upper = layout.sides(dim)
        for where, element in enumerate(lower):
            mask = table(layout, masks)(element, dim)
            from_below, from_above = unpacked(lane, outside, where, mask)
            yield 2 * dim, where, element, from_below
            yield 2 * dim + 1, where, upper[where], from_above


def put_faces(layout, here, dim, messages, masks, factor, splits):
    low = lanes(layout) < FACE
    row_low = low[:1]
    for number, where, element, face in outside_faces(layout, here, (dim,), messages, masks):
        row = factor(element, dim)
        turned = pltpu.roll(row, FACE, 1)
        side = number % 2
        value = face * (jnp.where(row_low, turned, row) if side else jnp.where(row_low, row, turned))
        high = value.astype(jnp.bfloat16).astype(jnp.float32)
        rows = layout.pair_rows(where)
        splits[side][rows, :WIDTH] = jnp.where(low, value, value - high).astype(jnp.bfloat16)
        splits[side][rows, WIDTH:] = jnp.where(low, value, 0.0).astype(jnp.bfloat16)


def early_faces_kernel(layout, kind, order, *refs):
    messages, refs = taken(layout, EARLY, refs, order)
    here, masks, scaling, faces, begun, out, *scratch = refs
    count = 2 * len(EARLY)
    splits, sums = scratch[:count], scratch[count:]
    factor = scales(layout, kind, scaling)
    share = {}
    for place, dim in enumerate(EARLY):
        put_faces(layout, here, dim, messages, masks, factor, splits[2 * place : 2 * place + 2])
        for side, elements in enumerate(layout.sides(dim)):
            at = 2 * place + side
            sums[at][...] = dot(splits[at][...], faces[2 * dim + side])
            for where, element in enumerate(elements):
                share.setdefault(element, []).append((at, layout.pair_rows(where)))
    for element in layout.elements():
        for dim in DIMS:
            at = (layout.rows(element), columns(dim))
            parts = [sums[number][rows, columns(dim)] for number, rows in share.get(element, ())]
            if parts:
                result = sum(parts[1:], parts[0]) * factor(element, dim)
                out[at] = combined(kind, begun[at], result)
            else:
                out[at] = begun[at]


def late_faces_kernel(layout, kind, order, *refs):
    messages, refs = taken(layout, (LATE,), refs, order)
    here, masks, scaling, faces, begun, out, *refs = refs
    sent, splits = refs[: len(layout.turns())], refs[len(layout.turns()) :]
    factor = scales(layout, kind, scaling)
    put_faces(layout, here, LATE, messages, masks, factor, splits)
    edge = layout.edge()
    done = set()
    for side, elements in enumerate(layout.sides(LATE)):
        product = dot(splits[side][...], faces[2 * LATE + side])
        for where, element in enumerate(elements):
            rows = layout.pair_rows(edge.index(element))
            for dim in DIMS:
                part = product[layout.pair_rows(where), columns(dim)] * factor(element, dim)
                at = (rows, columns(dim))
                base = out[at] if element in done else begun[layout.rows(element), columns(dim)]
                out[at] = combined(kind, base, part)
            done.add(element)
    for dim in DIMS:
        pack(layout, here, dim, reader(layout, begun, out), table(layout, masks), sent)


def last_early_kernel(layout, whole, edges, *refs):
    value = reader(layout, whole, edges)
    messages, (here, masks, keeps, ready) = taken(layout, EARLY, refs)
    for dim in DIMS:

        def emit(element, result):
            ready[layout.rows(element), columns(dim)] = result

        assemble(
            layout,
            here,
            dim,
            value,
            None if dim == LATE else messages,
            table(layout, masks),
            table(layout, keeps),
            emit,
        )


def last_late_kernel(layout, begun, *refs):
    messages, (here, masks, out, ready, left) = taken(layout, (LATE,), refs)
    low = lanes(layout) < FACE

    def copy(source, dim):
        return pltpu.make_async_copy(source, out.at[:, columns(dim)], left.at[dim])

    copies = [copy(begun.at[:, columns(dim)], dim) for dim in EARLY]
    for each in copies:
        each.start()
    added = {}
    for number, _, element, face in outside_faces(layout, here, (LATE,), messages, masks):
        part = jnp.where(low, 0.0, face) if number % 2 else jnp.where(low, face, 0.0)
        added[element] = added[element] + part if element in added else part
    for element in layout.elements():
        value = begun[layout.rows(element), columns(LATE)]
        ready[layout.rows(element), :] = value + added[element] if element in added else value
    copies.append(copy(ready, LATE))
    copies[-1].start()
    for each in copies:
        each.wait()


def in_vmem(count):
    return [pl.BlockSpec(memory_space=pltpu.VMEM)] * count


def in_hbm(count):
    return [pl.BlockSpec(memory_space=pltpu.HBM)] * count


PARAMS = pltpu.CompilerParams(vmem_limit_bytes=VMEM_LIMIT)


def kept_in_hbm(*values):
    return [pltpu.with_memory_space_constraint(value, pltpu.HBM) for value in values]


def cost(flops, size):
    return pl.CostEstimate(flops=flops, bytes_accessed=size, transcendentals=0)


def partners(layout, dim, parity):
    sizes = layout.sizes
    swap = {}
    for place in np.ndindex(*sizes):
        other = list(place)
        lower = place[dim] % 2 == parity
        at = place[dim] + (1 if lower else -1)
        if 0 <= at < sizes[dim]:
            other[dim] = at
        elif dim != 1 and sizes[1] % 2 == 0:
            other[1] = place[1] ^ 1
        elif sizes[dim] % 2 == 0:
            other[dim] = sizes[dim] - 1 - place[dim]
        swap[place] = tuple(other)
    return [
        (int(np.ravel_multi_index(place, sizes)), int(np.ravel_multi_index(other, sizes)))
        for place, other in swap.items()
    ]


def exchange(layout, messages, order=TURNS):
    given = dict(zip(layout.turns(), messages))
    return {
        turn: lax.ppermute(given[turn], AXES, partners(layout, *turn))
        for turn in order
        if turn in given
    }


def body(
    load_raw,
    scaling,
    fine_matrix,
    fine_inverse,
    prolong_four,
    coarse_four,
    prolong_two,
    coarse_two,
    orient,
    boundary,
):
    counts, species, nodes = load_raw.shape[:3], load_raw.shape[3], load_raw.shape[4]
    layout = Layout(counts, species, tuple(lax.axis_size(axis) for axis in AXES))
    load = load_raw.reshape(-1, nodes)
    rows = load.shape[0]
    turns = layout.turns()
    message_shapes = tuple(layout.message(dim) for dim, _ in turns)
    whole = jax.ShapeDtypeStruct(load.shape, jnp.float32)
    matrix_shapes = (
        jax.ShapeDtypeStruct((3 * nodes, nodes), jnp.bfloat16),
        jax.ShapeDtypeStruct((2 * len(DIMS), 4 * FACE, nodes), jnp.bfloat16),
    )
    elements = len(layout.elements())
    tables = tuple(jax.ShapeDtypeStruct((elements, nodes), kind) for kind in (jnp.int32, jnp.float32))
    small = (scaling, prolong_four.T, coarse_four, prolong_two.T, coarse_two)
    sides = jnp.transpose(boundary, (1, 2, 3, 0))

    *sent, masks, keeps, load, flags, scaling, four, coarse_four, two, coarse_two = pl.pallas_call(
        functools.partial(first_kernel, layout),
        out_shape=message_shapes
        + tables
        + (whole, jax.ShapeDtypeStruct((3 * len(DIMS), WIDTH), jnp.int32))
        + tuple(jax.ShapeDtypeStruct(each.shape, each.dtype) for each in small),
        in_specs=in_hbm(3 + FETCHED),
        out_specs=tuple(in_vmem(len(turns) + 4 + FETCHED)),
        scratch_shapes=[
            pltpu.SMEM(orient.shape, jnp.int32),
            pltpu.SMEM(sides.shape, jnp.int32),
            pltpu.SemaphoreType.DMA((5 + FETCHED,)),
        ],
        compiler_params=PARAMS,
        name="pack",
    )(*kept_in_hbm(load, orient, sides, *small))

    stack = (rounded(prolong_four.shape[1]) + rounded(prolong_two.shape[1]), nodes)
    smoother = pl.pallas_call(
        smoother_kernel,
        out_shape=matrix_shapes,
        in_specs=in_vmem(5),
        out_specs=tuple(in_vmem(2)),
        scratch_shapes=[pltpu.VMEM(stack, jnp.float32), pltpu.VMEM(stack, jnp.float32)],
        compiler_params=PARAMS,
        cost_estimate=cost(2 * nodes * nodes * nodes, 8 * nodes * nodes),
        name="smoother",
    )(fine_inverse, four, coarse_four, two, coarse_two)
    operator = pl.pallas_call(
        operator_kernel,
        out_shape=matrix_shapes,
        in_specs=in_vmem(1),
        out_specs=tuple(in_vmem(2)),
        compiler_params=PARAMS,
        cost_estimate=cost(0, 10 * nodes * nodes),
        name="operator",
    )(fine_matrix)

    def scratch(dims):
        heights = [len(side) * species for dim in dims for side in layout.sides(dim)]
        splits = [pltpu.VMEM((height, 4 * FACE), jnp.bfloat16) for height in heights]
        return splits, [pltpu.VMEM((height, nodes), jnp.float32) for height in heights]

    edges = jax.ShapeDtypeStruct((len(layout.edge()) * species, nodes), jnp.float32)

    def stage(kind, value, sent, matrix, begun, order=TURNS):
        messages = exchange(layout, sent, order)
        begun = pl.pallas_call(
            functools.partial(local_kernel, layout, kind, (len(value), len(begun))),
            out_shape=whole,
            in_specs=in_vmem(4 + len(value) + len(begun)),
            out_specs=in_vmem(1)[0],
            scratch_shapes=[
                pltpu.VMEM((rows, 3 * nodes), jnp.bfloat16),
                pltpu.VMEM(load.shape, jnp.float32),
            ],
            compiler_params=PARAMS,
            cost_estimate=cost(rows * nodes, 0),
            name=kind + "_local",
        )(*value, *begun, masks, keeps, scaling, matrix[0])
        mine = [messages[turn] for turn in layout.turns(EARLY, order)]
        splits, sums = scratch(EARLY)
        begun = pl.pallas_call(
            functools.partial(early_faces_kernel, layout, kind, order),
            out_shape=whole,
            in_specs=in_vmem(5 + len(mine)),
            out_specs=in_vmem(1)[0],
            scratch_shapes=splits + sums,
            compiler_params=PARAMS,
            cost_estimate=cost(0, 0),
            name=kind + "_faces_early",
        )(*mine, flags, masks, scaling, matrix[1], begun)
        mine = [messages[turn] for turn in layout.turns((LATE,), order)]
        changed, *sent = pl.pallas_call(
            functools.partial(late_faces_kernel, layout, kind, order),
            out_shape=(edges,) + message_shapes,
            in_specs=in_vmem(5 + len(mine)),
            out_specs=tuple(in_vmem(1 + len(turns))),
            scratch_shapes=scratch((LATE,))[0],
            compiler_params=PARAMS,
            cost_estimate=cost(0, 0),
            name=kind + "_faces_late",
        )(*mine, flags, masks, scaling, matrix[1], begun)
        return (begun, changed), sent

    first, sent = stage("smooth", (load,), sent, smoother, (), FIRST_TURNS)
    left, sent = stage("operator", first, sent, operator, (load,))
    total, sent = stage("smooth_more", left, sent, smoother, first)
    messages = exchange(layout, sent)
    early = [messages[turn] for turn in layout.turns(EARLY)]
    late = [messages[turn] for turn in layout.turns((LATE,))]
    begun = pl.pallas_call(
        functools.partial(last_early_kernel, layout),
        out_shape=whole,
        in_specs=in_vmem(5 + len(early)),
        out_specs=in_vmem(1)[0],
        compiler_params=PARAMS,
        cost_estimate=cost(0, 8 * rows * nodes),
        name="last_early",
    )(*total, *early, flags, masks, keeps)
    result = pl.pallas_call(
        functools.partial(last_late_kernel, layout),
        out_shape=whole,
        in_specs=in_vmem(3 + len(late)),
        out_specs=in_hbm(1)[0],
        scratch_shapes=[pltpu.VMEM((rows, WIDTH), jnp.float32), pltpu.SemaphoreType.DMA((3,))],
        compiler_params=PARAMS,
        cost_estimate=cost(0, 8 * rows * nodes),
        name="last_late",
    )(begun, *late, flags, masks)
    return result.reshape(load_raw.shape)


def solution(mesh):
    in_specs = (
        P("ex", "ey", "ez", None, None),
        P("ex", "ey", "ez", None),
        P(),
        P(),
        P(),
        P(),
        P(),
        P(),
        P(None, "ex", "ey", "ez"),
        P(None, "ex", "ey", "ez"),
    )
    out_specs = P("ex", "ey", "ez", None, None)
    return jax.shard_map(body, mesh=mesh, in_specs=in_specs, out_specs=out_specs, check_vma=False)
```

```python
import functools

import jax
import jax.numpy as jnp
from jax import lax
from jax.experimental import pallas as pl
from jax.experimental.pallas import tpu as pltpu
import numpy as np
from jax.sharding import PartitionSpec as P

FACE_SIDE = 8
FACE = FACE_SIDE * FACE_SIDE
WIDTH = 2 * FACE
AXES = ("ex", "ey", "ez")
TURNS = ((1, 1), (0, 0), (0, 1), (1, 0), (2, 1), (2, 0))
FIRST_TURNS = ((1, 1), (0, 1), (0, 0), (1, 0), (2, 1), (2, 0))
DIMS = (0, 1, 2)
EARLY = (1, 0)
LATE = 2
FETCHED = 5
VMEM_LIMIT = 24 * 1024 * 1024


class Layout:
    def __init__(self, counts, species, sizes):
        self.counts = counts
        self.species = species
        self.sizes = sizes

    def elements(self):
        spans = [range(count) for count in self.counts]
        return [(i, j, k) for i in spans[0] for j in spans[1] for k in spans[2]]

    def number(self, element):
        return (element[0] * self.counts[1] + element[1]) * self.counts[2] + element[2]

    def rows(self, element):
        start = self.number(element) * self.species
        return slice(start, start + self.species)

    def layer(self, dim, position):
        return [element for element in self.elements() if element[dim] == position]

    def pairs(self, dim):
        return (len(self.layer(dim, 0)) + 1) // 2

    def pair_rows(self, pair):
        return slice(pair * self.species, (pair + 1) * self.species)

    def turns(self, dims=(0, 1, 2), order=TURNS):
        return [
            (dim, parity) for dim, parity in order if dim in dims and self.sizes[dim] > 1 + parity
        ]

    def edge(self):
        ends = (0, self.counts[LATE] - 1)
        return [element for element in self.elements() if element[LATE] in ends]

    def sides(self, dim):
        return self.layer(dim, 0), self.layer(dim, self.counts[dim] - 1)

    def message(self, dim):
        return jax.ShapeDtypeStruct((self.pairs(dim) * self.species, WIDTH), jnp.float32)


def columns(dim):
    return slice(dim * WIDTH, (dim + 1) * WIDTH)


def lanes(layout):
    return lax.broadcasted_iota(jnp.int32, (layout.species, WIDTH), 1)


def picked(value, index):
    return jnp.take_along_axis(value, index, axis=1, mode="promise_in_bounds")


def flip_mask(code):
    reach = FACE_SIDE - 1
    return (code & 1) * (reach * FACE_SIDE) + (code >> 1) * reach


def places():
    return [lax.axis_index(axis) for axis in AXES]


def pack(layout, here, dim, load_block, mask_of, outs):
    turns = [(turn, out) for turn, out in zip(layout.turns(), outs) if turn[0] == dim]
    if not turns:
        return
    lane = lanes(layout)
    low = lane < FACE
    even = (here[dim] & 1) == 0
    first = layout.layer(dim, 0)
    last = layout.layer(dim, layout.counts[dim] - 1)
    for pair in range(layout.pairs(dim)):
        sides = []
        for half in range(2):
            where = min(2 * pair + half, len(first) - 1)
            upper = load_block(last[where], dim)
            lower = load_block(first[where], dim)
            lower = picked(lower, lane ^ mask_of(first[where], dim) ^ (half * FACE))
            if half == 0:
                upper = pltpu.roll(upper, FACE, 1)
            sides.append((upper, lower))
        up = jnp.where(low, sides[0][0], sides[1][0])
        down = jnp.where(low, sides[0][1], sides[1][1])
        for (_, parity), out in turns:
            is_lower = even if parity == 0 else jnp.logical_not(even)
            out[layout.pair_rows(pair), :] = jnp.where(is_lower, up, down)


def received(layout, here, dim, messages):
    even = (here[dim] & 1) == 0
    at_start = here[dim] == 0
    at_end = here[dim] == layout.sizes[dim] - 1
    zero = jnp.zeros((layout.species, WIDTH), jnp.float32)
    found = []
    for pair in range(layout.pairs(dim)):
        first, second = [
            messages[dim, parity][layout.pair_rows(pair), :] if (dim, parity) in messages else zero
            for parity in range(2)
        ]
        below = jnp.where(at_start, 0.0, jnp.where(even, second, first))
        above = jnp.where(at_end, 0.0, jnp.where(even, first, second))
        found.append((below, above))
    return found


def unpacked(lane, outside, where, mask):
    below, above = outside[where // 2]
    half = (where % 2) * FACE
    inside = lane & (FACE - 1)
    return picked(below, (inside ^ mask) + half), picked(above, inside + half)


def assemble(layout, here, dim, load_block, messages, mask_of, keep_of, emit, slab=None):
    lane = lanes(layout)
    low = lane < FACE
    count = layout.counts[dim]
    outside = None if messages is None else received(layout, here, dim, messages)
    zero = jnp.zeros((layout.species, WIDTH), jnp.float32)
    for where, start in enumerate(layout.layer(dim, 0)):
        if slab not in (None, start[0]):
            continue
        line = [start[:dim] + (step,) + start[dim + 1 :] for step in range(count)]
        blocks = [load_block(element, dim) for element in line]
        if outside is None:
            from_below, from_above = zero, zero
        else:
            from_below, from_above = unpacked(lane, outside, where, mask_of(start, dim))
        turned = [from_below]
        for step, element in list(enumerate(line))[1:]:
            shared = jnp.where(low, blocks[step], blocks[step - 1])
            turned.append(picked(shared, lane ^ mask_of(element, dim) ^ FACE))
        turned.append(from_above)
        for step, element in enumerate(line):
            value = blocks[step] + jnp.where(low, turned[step], turned[step + 1])
            if step in (0, count - 1):
                value = value * keep_of(element, dim)
            emit(element, value)


def halves(value):
    high = value.astype(jnp.bfloat16)
    return high, (value - high.astype(jnp.float32)).astype(jnp.bfloat16)


def dot(left, right, contract=((1,), (0,))):
    return lax.dot_general(left, right, (contract, ((), ())), preferred_element_type=jnp.float32)


def split_dot(left, right, contract):
    left_high, left_rest = halves(left)
    right_high, right_rest = halves(right)
    return (
        dot(left_high, right_high, contract)
        + dot(left_high, right_rest, contract)
        + dot(left_rest, right_high, contract)
    )


def stacked(value, local, faces):
    high, rest = halves(value)
    size = value.shape[0]
    for part, piece in enumerate((high, rest, high)):
        local[part * size : (part + 1) * size, :] = piece
    for number in range(faces.shape[0]):
        rows = slice(number * FACE, (number + 1) * FACE)
        for part, piece in enumerate((high, high, rest)):
            faces[number, part * FACE : (part + 1) * FACE, :] = piece[rows, :]
        faces[number, 3 * FACE :, :] = jnp.zeros((FACE, value.shape[1]), jnp.bfloat16)


def operator_kernel(fine, *outs):
    stacked(fine[...], *outs)


def smoother_kernel(inverse, four, coarse_four, two, coarse_two, *refs):
    *outs, right, left = refs
    right[...] = jnp.zeros_like(right)
    left[...] = jnp.zeros_like(left)
    start = 0
    for prolong, coarse in ((four, coarse_four), (two, coarse_two)):
        rows = slice(start, start + prolong.shape[0])
        left[rows, :] = prolong[...]
        right[rows, :] = split_dot(coarse[...], prolong[...], ((1,), (0,)))
        start += rounded(prolong.shape[0])
    corrections = split_dot(left[...], right[...], ((0,), (0,)))
    stacked(0.5 * (inverse[...] + corrections), *outs)


def rounded(count):
    return (count + 7) // 8 * 8


def first_kernel(layout, load, orient, boundary, *refs):
    turns = len(layout.turns())
    small, refs = refs[:FETCHED], refs[FETCHED:]
    outs, masks, keeps, staged = refs[:turns], *refs[turns : turns + 3]
    fetched, (codes, fixed, arrived) = refs[turns + 3 : turns + 3 + FETCHED], refs[-3:]
    scalars = [
        pltpu.make_async_copy(source, target, arrived.at[number])
        for number, (source, target) in enumerate(((orient, codes), (boundary, fixed)))
    ]
    strips = [
        pltpu.make_async_copy(
            load.at[:, columns(dim)], staged.at[:, columns(dim)], arrived.at[2 + dim]
        )
        for dim in DIMS
    ]
    fetches = [
        pltpu.make_async_copy(source, target, arrived.at[5 + number])
        for number, (source, target) in enumerate(zip(small, fetched))
    ]
    for copy in scalars + strips + fetches:
        copy.start()
    here = places()
    scalars[0].wait()
    tabulate_masks(layout, codes, masks)
    scalars[1].wait()
    tabulate_keeps(layout, here, fixed, keeps)
    for dim in DIMS:
        strips[dim].wait()
        pack(
            layout,
            here,
            dim,
            lambda element, dim: staged[layout.rows(element), columns(dim)],
            table(layout, masks),
            outs,
        )
    for copy in fetches:
        copy.wait()


def tabulate_masks(layout, codes, masks):
    for element in layout.elements():
        number = layout.number(element)
        for dim in DIMS:
            code = jnp.full((1, WIDTH), codes[(dim,) + element], jnp.int32)
            masks[number : number + 1, columns(dim)] = flip_mask(code)


def tabulate_keeps(layout, here, boundary, keeps):
    low = lax.broadcasted_iota(jnp.int32, (1, WIDTH), 1) < FACE
    for dim in DIMS:
        first = jnp.where(here[dim] == 0, 1, 0)
        last = jnp.where(here[dim] == layout.sizes[dim] - 1, 1, 0)
        for element in layout.elements():
            number = layout.number(element)
            keep = jnp.ones((1, WIDTH), jnp.float32)
            if element[dim] == 0:
                fixed = first * boundary[element + (2 * dim,)]
                keep = jnp.where(low, 1.0 - jnp.full((1, WIDTH), fixed, jnp.float32), keep)
            if element[dim] == layout.counts[dim] - 1:
                fixed = last * boundary[element + (2 * dim + 1,)]
                keep = jnp.where(low, keep, 1.0 - jnp.full((1, WIDTH), fixed, jnp.float32))
            keeps[number : number + 1, columns(dim)] = keep


def table(layout, ref):
    def row(element, dim):
        number = layout.number(element)
        return ref[number : number + 1, columns(dim)]

    return row


def scales(layout, kind, ref):
    def row(element, dim):
        value = ref[element[0], element[1], element[2] : element[2] + 1, columns(dim)]
        return value if kind == "operator" else 1.0 / value

    return row


def taken(layout, dims, refs, order=TURNS):
    turns = layout.turns(dims, order)
    return dict(zip(turns, refs)), refs[len(turns) :]


def combined(kind, begun, result):
    if begun is None:
        return result
    return begun - result if kind == "operator" else begun + result


def reader(layout, whole, edges=None):
    edge = [] if edges is None else layout.edge()

    def block(element, dim):
        if element in edge:
            return edges[layout.pair_rows(edge.index(element)), columns(dim)]
        return whole[layout.rows(element), columns(dim)]

    return block


def local_kernel(layout, kind, given, *refs):
    value, begun, refs = refs[: given[0]], refs[given[0] : sum(given)], refs[sum(given) :]
    masks, keeps, scaling, matrix, out, split, summed = refs
    value = reader(layout, *value)
    begun = reader(layout, *begun) if begun else None
    here = places()
    factor = scales(layout, kind, scaling)
    nodes = out.shape[1]

    def assembled(dim, slab):
        def emit(element, result):
            high, rest = halves(result * factor(element, dim))
            for part, piece in enumerate((high, high, rest)):
                start = part * nodes + dim * WIDTH
                split[layout.rows(element), start : start + WIDTH] = piece

        assemble(
            layout,
            here,
            dim,
            value,
            None,
            table(layout, masks),
            table(layout, keeps),
            emit,
            slab,
        )

    for dim in DIMS:
        assembled(dim, None)
    summed[...] = dot(split[...], matrix[...])
    for element in layout.elements():
        for dim in DIMS:
            at = (layout.rows(element), columns(dim))
            result = summed[at] * factor(element, dim)
            out[at] = combined(kind, begun and begun(element, dim), result)


def combined(kind, begun, result):
    if begun is None:
        return result
    return begun - result if kind == "operator" else begun + result


def reader(layout, whole, edges=None):
    edge = [] if edges is None else layout.edge()

    def block(element, dim):
        if element in edge:
            return edges[layout.pair_rows(edge.index(element)), columns(dim)]
        return whole[layout.rows(element), columns(dim)]

    return block


def local_kernel(layout, kind, given, *refs):
    value, begun, refs = refs[: given[0]], refs[given[0] : sum(given)], refs[sum(given) :]
    masks, keeps, scaling, matrix, out, split, summed = refs
    value = reader(layout, *value)
    begun = reader(layout, *begun) if begun else None
    here = places()
    factor = scales(layout, kind, scaling)
    nodes = out.shape[1]

    def assembled(dim, slab):
        def emit(element, result):
            high, rest = halves(result * factor(element, dim))
            for part, piece in enumerate((high, high, rest)):
                start = part * nodes + dim * WIDTH
                split[layout.rows(element), start : start + WIDTH] = piece

        assemble(
            layout,
            here,
            dim,
            value,
            None,
            table(layout, masks),
            table(layout, keeps),
            emit,
            slab,
        )

    assembled(0, None)
    count = layout.counts[0]
    height = out.shape[0] // count
    for slab in range(count):
        assembled(1, slab)
        assembled(2, slab)
        rows = slice(slab * height, (slab + 1) * height)
        summed[rows, :] = dot(split[rows, :], matrix[...])
        for element in layout.layer(0, slab):
            for dim in DIMS:
                at = (layout.rows(element), columns(dim))
                result = summed[at] * factor(element, dim)
                out[at] = combined(kind, begun and begun(element, dim), result)


def combined(kind, begun, result):
    if begun is None:
        return result
    return begun - result if kind == "operator" else begun + result


def strips_kernel(layout, kind, dims, local, value, *refs):
    messages, refs = (None, refs) if local else taken(layout, dims, refs)
    masks, keeps, scaling, matrix, *before, out, split, summed = refs
    begun = before[0] if before else None
    here = places()
    factor = scales(layout, kind, scaling)

    def assembled(place, slab):
        dim = dims[place]

        def emit(element, result):
            scaled = result * factor(element, dim)
            put_split(split, layout.rows(element), place, len(dims), scaled)

        assemble(
            layout,
            here,
            dim,
            lambda element, dim: value[layout.rows(element), columns(dim)],
            messages,
            table(layout, masks),
            table(layout, keeps),
            emit,
            slab,
        )

    if 0 in dims:
        assembled(dims.index(0), None)
    count = layout.counts[0]
    height = value.shape[0] // count
    for slab in range(count):
        for place, dim in enumerate(dims):
            if dim != 0:
                assembled(place, slab)
        rows = slice(slab * height, (slab + 1) * height)
        summed[rows, :] = dot(split[rows, :], matrix[...])
        for element in layout.layer(0, slab):
            for each in range(3):
                at = (layout.rows(element), columns(each))
                result = summed[at] * factor(element, each)
                out[at] = combined(kind, None if begun is None else begun[at], result)


def combined(kind, begun, result):
    if begun is None:
        return result
    return begun - result if kind == "operator" else begun + result


def outside_faces(layout, here, dims, messages, masks):
    lane = lanes(layout)
    for dim in dims:
        outside = received(layout, here, dim, messages)
        lower, upper = layout.sides(dim)
        for where, element in enumerate(lower):
            mask = table(layout, masks)(element, dim)
            from_below, from_above = unpacked(lane, outside, where, mask)
            yield 2 * dim, where, element, from_below
            yield 2 * dim + 1, where, upper[where], from_above


def put_faces(layout, here, dim, messages, masks, factor, splits):
    low = lanes(layout) < FACE
    row_low = low[:1]
    for number, where, element, face in outside_faces(layout, here, (dim,), messages, masks):
        row = factor(element, dim)
        turned = pltpu.roll(row, FACE, 1)
        side = number % 2
        value = face * (jnp.where(row_low, turned, row) if side else jnp.where(row_low, row, turned))
        high = value.astype(jnp.bfloat16).astype(jnp.float32)
        rows = layout.pair_rows(where)
        splits[side][rows, :WIDTH] = jnp.where(low, value, value - high).astype(jnp.bfloat16)
        splits[side][rows, WIDTH:] = jnp.where(low, value, 0.0).astype(jnp.bfloat16)


def early_faces_kernel(layout, kind, order, *refs):
    messages, refs = taken(layout, EARLY, refs, order)
    masks, scaling, faces, begun, out, *scratch = refs
    count = 2 * len(EARLY)
    splits, sums = scratch[:count], scratch[count:]
    here = places()
    factor = scales(layout, kind, scaling)
    share = {}
    for place, dim in enumerate(EARLY):
        put_faces(layout, here, dim, messages, masks, factor, splits[2 * place : 2 * place + 2])
        for side, elements in enumerate(layout.sides(dim)):
            at = 2 * place + side
            sums[at][...] = dot(splits[at][...], faces[2 * dim + side])
            for where, element in enumerate(elements):
                share.setdefault(element, []).append((at, layout.pair_rows(where)))
    for element in layout.elements():
        for dim in DIMS:
            at = (layout.rows(element), columns(dim))
            parts = [sums[number][rows, columns(dim)] for number, rows in share.get(element, ())]
            if parts:
                result = sum(parts[1:], parts[0]) * factor(element, dim)
                out[at] = combined(kind, begun[at], result)
            else:
                out[at] = begun[at]


def late_faces_kernel(layout, kind, order, *refs):
    messages, refs = taken(layout, (LATE,), refs, order)
    masks, scaling, faces, begun, out, *refs = refs
    sent, splits = refs[: len(layout.turns())], refs[len(layout.turns()) :]
    here = places()
    factor = scales(layout, kind, scaling)
    put_faces(layout, here, LATE, messages, masks, factor, splits)
    edge = layout.edge()
    done = set()
    for side, elements in enumerate(layout.sides(LATE)):
        product = dot(splits[side][...], faces[2 * LATE + side])
        for where, element in enumerate(elements):
            rows = layout.pair_rows(edge.index(element))
            for dim in DIMS:
                part = product[layout.pair_rows(where), columns(dim)] * factor(element, dim)
                at = (rows, columns(dim))
                base = out[at] if element in done else begun[layout.rows(element), columns(dim)]
                out[at] = combined(kind, base, part)
            done.add(element)
    for dim in DIMS:
        pack(layout, here, dim, reader(layout, begun, out), table(layout, masks), sent)


def last_early_kernel(layout, whole, edges, *refs):
    value = reader(layout, whole, edges)
    messages, (masks, keeps, ready) = taken(layout, EARLY, refs)
    for dim in DIMS:

        def emit(element, result):
            ready[layout.rows(element), columns(dim)] = result

        assemble(
            layout,
            places(),
            dim,
            value,
            None if dim == LATE else messages,
            table(layout, masks),
            table(layout, keeps),
            emit,
        )


def last_late_kernel(layout, begun, *refs):
    messages, (masks, out, ready, left) = taken(layout, (LATE,), refs)
    low = lanes(layout) < FACE

    def copy(source, dim):
        return pltpu.make_async_copy(source, out.at[:, columns(dim)], left.at[dim])

    copies = [copy(begun.at[:, columns(dim)], dim) for dim in EARLY]
    for each in copies:
        each.start()
    added = {}
    for number, _, element, face in outside_faces(layout, places(), (LATE,), messages, masks):
        part = jnp.where(low, 0.0, face) if number % 2 else jnp.where(low, face, 0.0)
        added[element] = added[element] + part if element in added else part
    for element in layout.elements():
        value = begun[layout.rows(element), columns(LATE)]
        ready[layout.rows(element), :] = value + added[element] if element in added else value
    copies.append(copy(ready, LATE))
    copies[-1].start()
    for each in copies:
        each.wait()


def in_vmem(count):
    return [pl.BlockSpec(memory_space=pltpu.VMEM)] * count


def in_hbm(count):
    return [pl.BlockSpec(memory_space=pltpu.HBM)] * count


PARAMS = pltpu.CompilerParams(vmem_limit_bytes=VMEM_LIMIT)


def kept_in_hbm(*values):
    return [pltpu.with_memory_space_constraint(value, pltpu.HBM) for value in values]


def cost(flops, size):
    return pl.CostEstimate(flops=flops, bytes_accessed=size, transcendentals=0)


def partners(layout, dim, parity):
    sizes = layout.sizes
    swap = {}
    for place in np.ndindex(*sizes):
        other = list(place)
        lower = place[dim] % 2 == parity
        at = place[dim] + (1 if lower else -1)
        if 0 <= at < sizes[dim]:
            other[dim] = at
        elif dim != 1 and sizes[1] % 2 == 0:
            other[1] = place[1] ^ 1
        elif sizes[dim] % 2 == 0:
            other[dim] = sizes[dim] - 1 - place[dim]
        swap[place] = tuple(other)
    return [
        (int(np.ravel_multi_index(place, sizes)), int(np.ravel_multi_index(other, sizes)))
        for place, other in swap.items()
    ]


def exchange(layout, messages, order=TURNS):
    given = dict(zip(layout.turns(), messages))
    return {
        turn: lax.ppermute(given[turn], AXES, partners(layout, *turn))
        for turn in order
        if turn in given
    }


def body(
    load_raw,
    scaling,
    fine_matrix,
    fine_inverse,
    prolong_four,
    coarse_four,
    prolong_two,
    coarse_two,
    orient,
    boundary,
):
    counts, species, nodes = load_raw.shape[:3], load_raw.shape[3], load_raw.shape[4]
    layout = Layout(counts, species, tuple(lax.axis_size(axis) for axis in AXES))
    load = load_raw.reshape(-1, nodes)
    rows = load.shape[0]
    turns = layout.turns()
    message_shapes = tuple(layout.message(dim) for dim, _ in turns)
    whole = jax.ShapeDtypeStruct(load.shape, jnp.float32)
    matrix_shapes = (
        jax.ShapeDtypeStruct((3 * nodes, nodes), jnp.bfloat16),
        jax.ShapeDtypeStruct((2 * len(DIMS), 4 * FACE, nodes), jnp.bfloat16),
    )
    elements = len(layout.elements())
    tables = tuple(jax.ShapeDtypeStruct((elements, nodes), kind) for kind in (jnp.int32, jnp.float32))
    small = (scaling, prolong_four.T, coarse_four, prolong_two.T, coarse_two)
    sides = jnp.transpose(boundary, (1, 2, 3, 0))

    *sent, masks, keeps, load, scaling, four, coarse_four, two, coarse_two = pl.pallas_call(
        functools.partial(first_kernel, layout),
        out_shape=message_shapes
        + tables
        + (whole,)
        + tuple(jax.ShapeDtypeStruct(each.shape, each.dtype) for each in small),
        in_specs=in_hbm(3 + FETCHED),
        out_specs=tuple(in_vmem(len(turns) + 3 + FETCHED)),
        scratch_shapes=[
            pltpu.SMEM(orient.shape, jnp.int32),
            pltpu.SMEM(sides.shape, jnp.int32),
            pltpu.SemaphoreType.DMA((5 + FETCHED,)),
        ],
        compiler_params=PARAMS,
        name="pack",
    )(*kept_in_hbm(load, orient, sides, *small))

    stack = (rounded(prolong_four.shape[1]) + rounded(prolong_two.shape[1]), nodes)
    smoother = pl.pallas_call(
        smoother_kernel,
        out_shape=matrix_shapes,
        in_specs=in_vmem(5),
        out_specs=tuple(in_vmem(2)),
        scratch_shapes=[pltpu.VMEM(stack, jnp.float32), pltpu.VMEM(stack, jnp.float32)],
        compiler_params=PARAMS,
        cost_estimate=cost(2 * nodes * nodes * nodes, 8 * nodes * nodes),
        name="smoother",
    )(fine_inverse, four, coarse_four, two, coarse_two)
    operator = pl.pallas_call(
        operator_kernel,
        out_shape=matrix_shapes,
        in_specs=in_vmem(1),
        out_specs=tuple(in_vmem(2)),
        compiler_params=PARAMS,
        cost_estimate=cost(0, 10 * nodes * nodes),
        name="operator",
    )(fine_matrix)

    def scratch(dims):
        heights = [len(side) * species for dim in dims for side in layout.sides(dim)]
        splits = [pltpu.VMEM((height, 4 * FACE), jnp.bfloat16) for height in heights]
        return splits, [pltpu.VMEM((height, nodes), jnp.float32) for height in heights]

    edges = jax.ShapeDtypeStruct((len(layout.edge()) * species, nodes), jnp.float32)

    def stage(kind, value, sent, matrix, begun, order=TURNS):
        messages = exchange(layout, sent, order)
        begun = pl.pallas_call(
            functools.partial(local_kernel, layout, kind, (len(value), len(begun))),
            out_shape=whole,
            in_specs=in_vmem(4 + len(value) + len(begun)),
            out_specs=in_vmem(1)[0],
            scratch_shapes=[
                pltpu.VMEM((rows, 3 * nodes), jnp.bfloat16),
                pltpu.VMEM(load.shape, jnp.float32),
            ],
            compiler_params=PARAMS,
            cost_estimate=cost(rows * nodes, 0),
            name=kind + "_local",
        )(*value, *begun, masks, keeps, scaling, matrix[0])
        mine = [messages[turn] for turn in layout.turns(EARLY, order)]
        splits, sums = scratch(EARLY)
        begun = pl.pallas_call(
            functools.partial(early_faces_kernel, layout, kind, order),
            out_shape=whole,
            in_specs=in_vmem(4 + len(mine)),
            out_specs=in_vmem(1)[0],
            scratch_shapes=splits + sums,
            compiler_params=PARAMS,
            cost_estimate=cost(0, 0),
            name=kind + "_faces_early",
        )(*mine, masks, scaling, matrix[1], begun)
        mine = [messages[turn] for turn in layout.turns((LATE,), order)]
        changed, *sent = pl.pallas_call(
            functools.partial(late_faces_kernel, layout, kind, order),
            out_shape=(edges,) + message_shapes,
            in_specs=in_vmem(4 + len(mine)),
            out_specs=tuple(in_vmem(1 + len(turns))),
            scratch_shapes=scratch((LATE,))[0],
            compiler_params=PARAMS,
            cost_estimate=cost(0, 0),
            name=kind + "_faces_late",
        )(*mine, masks, scaling, matrix[1], begun)
        return (begun, changed), sent

    first, sent = stage("smooth", (load,), sent, smoother, (), FIRST_TURNS)
    left, sent = stage("operator", first, sent, operator, (load,))
    total, sent = stage("smooth_more", left, sent, smoother, first)
    messages = exchange(layout, sent)
    early = [messages[turn] for turn in layout.turns(EARLY)]
    late = [messages[turn] for turn in layout.turns((LATE,))]
    begun = pl.pallas_call(
        functools.partial(last_early_kernel, layout),
        out_shape=whole,
        in_specs=in_vmem(4 + len(early)),
        out_specs=in_vmem(1)[0],
        compiler_params=PARAMS,
        cost_estimate=cost(0, 8 * rows * nodes),
        name="last_early",
    )(*total, *early, masks, keeps)
    result = pl.pallas_call(
        functools.partial(last_late_kernel, layout),
        out_shape=whole,
        in_specs=in_vmem(2 + len(late)),
        out_specs=in_hbm(1)[0],
        scratch_shapes=[pltpu.VMEM((rows, WIDTH), jnp.float32), pltpu.SemaphoreType.DMA((3,))],
        compiler_params=PARAMS,
        cost_estimate=cost(0, 8 * rows * nodes),
        name="last_late",
    )(begun, *late, masks)
    return result.reshape(load_raw.shape)


def solution(mesh):
    in_specs = (
        P("ex", "ey", "ez", None, None),
        P("ex", "ey", "ez", None),
        P(),
        P(),
        P(),
        P(),
        P(),
        P(),
        P(None, "ex", "ey", "ez"),
        P(None, "ex", "ey", "ez"),
    )
    out_specs = P("ex", "ey", "ez", None, None)
    return jax.shard_map(body, mesh=mesh, in_specs=in_specs, out_specs=out_specs, check_vma=False)
```
